32 devices in a mesh: img: 4 (over y, x), seq: 8 (over z, core).
Axes of the slice: x: 2, y: 2, z: 4, core: 2. Of those that a mesh axis runs over, the one named last changes fastest.
Arguments:
- tokens: bfloat16 [4, 2048, 384], P('img', 'seq'), may hold values from -6 to 6
- cotangent: bfloat16 [4, 2048, 384], P('img', 'seq'), may hold values from -6 to 6
- heights: int32 [4, 3], P('img'), may hold values from 1 to 120, as said below
- widths: int32 [4, 3], P('img'), may hold values from 1 to 16, as said below
- valid: int32 [4, 2048], P('img', 'seq'), may hold values 0 or 1
- norm_gain: bfloat16 [384], replicated, may hold values from 0.099609375 to 1.8984375
- in_weight: bfloat16 [384, 1536], replicated, may hold values from -0.3125 to 0.3125
- conv_weight: bfloat16 [2, 4, 768], replicated, may hold values from -3 to 3
- conv_bias: bfloat16 [2, 768], replicated, may hold values from -3 to 3
- xproj_weight: bfloat16 [2, 768, 56], replicated, may hold values from -0.21875 to 0.21875
- dt_weight: bfloat16 [2, 24, 768], replicated
- dt_bias: bfloat16 [2, 768], replicated
- a_log: bfloat16 [2, 16, 768], replicated
- skip: bfloat16 [2, 768], replicated, may hold values from 0.099609375 to 1.8984375
- out_weight: bfloat16 [768, 384], replicated, may hold values from -0.625 to 0.625
Outputs:
- output: bfloat16 [4, 2048, 384], P('img', 'seq')
- input_grad: float32 [4, 2048, 384], P('img', 'seq')
- norm_gain_grad: float32 [384], replicated
- in_weight_grad: float32 [384, 1536], replicated
- conv_weight_grad: float32 [2, 4, 768], replicated
- conv_bias_grad: float32 [2, 768], replicated
- xproj_weight_grad: float32 [2, 768, 56], replicated
- dt_weight_grad: float32 [2, 24, 768], replicated
- dt_bias_grad: float32 [2, 768], replicated
- a_log_grad: float32 [2, 16, 768], replicated
- skip_grad: float32 [2, 768], replicated
- out_weight_grad: float32 [768, 384], replicated
The draws below stay inside these ranges and needn't reach their ends.
Inputs may be any that keep to these rules, and one draw needn't show every extreme that they name: In each group one image, which one drawn from the seed, is a grid of 120 rows and 16 columns and has slots on the first and on the last block of 256 slots; the other images have sides of 1 to 8 patches; the products heights * widths of a group sum to at most 2048. `widths`: drawn together with heights.
All inputs are finite; a program needn't handle non-finite values. No bound on the sum of `valid` on one device may be relied on, other than what follows from the above.
Results may differ from the reference program's by a relative error of at most 0.014.
Values may be sent and summed in bfloat16 or wider, within the bound.
No kernel may reach another device: no remote copies, remote signals or barrier semaphores. Data moves between devices by JAX's collectives and lax.ppermute only.
A program may use at most 192 MiB of HBM per device.

```python
import math
import jax
import jax.numpy as jnp
from jax import lax

D = 384
INNER = 768
STATE = 16
RANK = 24
KCONV = 4
GRID_SIDE = 8
IMAGES = 3
SLOTS = 2048
GROUPS = 4


def grid_plan(key):
    subkeys = jax.random.split(key, 3)
    small_heights = jax.random.randint(subkeys[0], (GROUPS, IMAGES), 1, GRID_SIDE + 1)
    small_widths = jax.random.randint(subkeys[1], (GROUPS, IMAGES), 1, GRID_SIDE + 1)
    big_slot = jax.random.randint(subkeys[2], (GROUPS,), 0, IMAGES)
    is_big = jnp.arange(IMAGES, dtype=jnp.int32)[None, :] == big_slot[:, None]
    big_width = 2 * GRID_SIDE
    big_height = SLOTS // big_width - GRID_SIDE
    heights = jnp.where(is_big, big_height, small_heights).astype(jnp.int32)
    widths = jnp.where(is_big, big_width, small_widths).astype(jnp.int32)
    return (heights, widths)


def draw_heights(key, part):
    heights, widths = grid_plan(key)
    return heights


def draw_widths(key, part):
    heights, widths = grid_plan(key)
    return widths


def rate_table(key, power):
    slow_rate = 0.5 / math.sqrt(SLOTS)
    fast_rate = 1.0 / math.sqrt(8.0)
    spread = jax.random.uniform(key, (2, INNER), jnp.float32)
    return slow_rate * (fast_rate / slow_rate) ** spread ** power


def draw_a_log(key, part):
    rate_values = rate_table(key, 1.0)
    key = jax.random.fold_in(key, 11)
    factor = jax.random.uniform(key, (2, STATE, INNER), jnp.float32, -0.7, 0.7)
    return (jnp.log(rate_values)[:, None, :] + factor).astype(jnp.bfloat16)


def draw_dt_bias(key, part):
    rate_values = rate_table(key, 1.0)
    return jnp.log(jnp.expm1(rate_values)).astype(jnp.bfloat16)


def draw_dt_weight(key, part):
    key = jax.random.fold_in(key, 37)
    values = jax.random.truncated_normal(key, -4.0, 4.0, (2, RANK, INNER), jnp.float32)
    return (values * (3.0 / math.sqrt(RANK))).astype(jnp.bfloat16)


def plant(array, rng, least, largest):
    place = [jax.random.randint(jax.random.fold_in(rng, axis), (), 0, length) for axis, length in enumerate(array.shape)]
    main_axis = array.shape.index(max(array.shape))
    neighbour = place[:main_axis] + [(place[main_axis] + 1) % array.shape[main_axis]] + place[main_axis + 1:]
    return array.at[tuple(place)].set(least).at[tuple(neighbour)].set(largest)


def level_of(rng, dims, cuts, low, largest):
    level = 1.0
    for position, blocks in cuts:
        steps = jax.random.uniform(jax.random.fold_in(jax.random.fold_in(rng, 6), position), (blocks,), jnp.float32, low / len(cuts), largest / len(cuts))
        level = level * jnp.repeat(jnp.exp(steps), dims[position] // blocks).reshape((-1,) + (1,) * (len(dims) - 1 - position))
    return level


def normal_values(stream_key, shape, scale, limit, pieces=(), kind=jnp.bfloat16):
    values = scale * jax.random.normal(stream_key, shape, jnp.float32)
    if pieces:
        values = values * level_of(stream_key, shape, pieces, -0.22, 0.18)
    return jnp.clip(values, -limit, limit).astype(kind)


def setup_inputs(seed: int = 0) -> dict:
    keys = jax.random.split(jax.random.key(seed), 16)
    tokens = normal_values(keys[0], (GROUPS, SLOTS, D), 1.0, 6.0, ((0, 4), (1, 8)))
    cotangent = normal_values(keys[1], (GROUPS, SLOTS, D), 1.0, 6.0, ((0, 4), (1, 8)))
    heights = draw_heights(jax.random.fold_in(keys[15], 71), 0)
    widths = draw_widths(jax.random.fold_in(keys[15], 71), 0)
    valid = plant((jax.random.randint(keys[4], (GROUPS, SLOTS), 0, 8) < 7).astype(jnp.int32), jax.random.fold_in(keys[4], 1), 0, 1)
    norm_gain = jnp.clip(1.0 + 0.18 * jax.random.normal(keys[5], (D,), jnp.float32), 0.099609375, 1.8984375).astype(jnp.bfloat16)
    in_weight = normal_values(keys[6], (D, 2 * INNER), D ** -0.5, 0.3125)
    conv_weight = normal_values(keys[7], (2, KCONV, INNER), KCONV ** -0.5, 3.0)
    conv_bias = normal_values(keys[8], (2, INNER), 0.5, 3.0)
    xproj_weight = normal_values(keys[9], (2, INNER, RANK + 2 * STATE), INNER ** -0.5, 0.21875)
    dt_weight = draw_dt_weight(jax.random.fold_in(keys[15], 71), 0)
    dt_bias = draw_dt_bias(jax.random.fold_in(keys[15], 71), 0)
    a_log = draw_a_log(jax.random.fold_in(keys[15], 71), 0)
    skip = jnp.clip(1.0 + 0.18 * jax.random.normal(keys[13], (2, INNER), jnp.float32), 0.099609375, 1.8984375).astype(jnp.bfloat16)
    out_weight = normal_values(keys[14], (INNER, D), (INNER // 8) ** -0.5, 0.625)
    return dict(tokens=tokens, cotangent=cotangent, heights=heights, widths=widths, valid=valid, norm_gain=norm_gain, in_weight=in_weight, conv_weight=conv_weight, conv_bias=conv_bias, xproj_weight=xproj_weight, dt_weight=dt_weight, dt_bias=dt_bias, a_log=a_log, skip=skip, out_weight=out_weight)


PRECISE = lax.Precision.HIGHEST
NORM_EPS = 1e-05

@jax.custom_vjp
def low(v):
    return lax.optimization_barrier(v.astype(jnp.bfloat16)).astype(jnp.float32)

@jax.custom_vjp
def low_back(v):
    return v

def low_keep(v):
    return (low(v), None)

def low_pass(kept, grad):
    return (grad,)

def back_keep(v):
    return (v, None)

def back_low(kept, grad):
    return (low(grad),)
low.defvjp(low_keep, low_pass)
low_back.defvjp(back_keep, back_low)

def conv_way(x_value, segment, weight_taps, bias_row, direction):
    conv_reach = weight_taps.shape[0] - 1
    length = x_value.shape[0]
    x_padded = jnp.pad(x_value, ((conv_reach, conv_reach), (0, 0)))
    seg_padded = jnp.pad(segment, (conv_reach, conv_reach), constant_values=-1)
    summed = jnp.zeros_like(x_value) + bias_row[None, :]
    for tap_index in range(conv_reach + 1):
        offset = tap_index if direction == 0 else 2 * conv_reach - tap_index
        same_seg = (seg_padded[offset:offset + length] == segment).astype(x_value.dtype)
        summed = summed + weight_taps[tap_index][None, :] * x_padded[offset:offset + length] * same_seg[:, None]
    return summed

def scan_way(step_size, keep_flag, b_proj, c_proj, s_value, a_matrix):
    length = step_size.shape[0]
    block_len = math.gcd(length, 128)

    def to_blocks(values):
        return values.reshape((length // block_len, block_len) + values.shape[1:])

    @jax.checkpoint
    def block_step(state_now, block_item):

        def position_step(inner_state, row_item):
            step_row, keep_row, b_row, c_row, s_row = row_item
            inner_state = keep_row * jnp.exp(step_row[None, :] * a_matrix) * inner_state + step_row[None, :] * b_row[:, None] * s_row[None, :]
            return (inner_state, lax.optimization_barrier(jnp.sum(c_row[:, None] * inner_state, axis=0)))
        return lax.scan(position_step, state_now, block_item)
    initial = jnp.zeros(a_matrix.shape, jnp.float32)
    block_items = tuple((to_blocks(values) for values in (step_size, keep_flag, b_proj, c_proj, s_value)))
    _, y_blocks = lax.scan(block_step, initial, block_items)
    return y_blocks.reshape(step_size.shape)

def layer_forward(inputs, norm_gain, in_weight, conv_weight, conv_bias, xproj_weight, dt_weight, dt_bias, a_log, skip, out_weight, segment, live_mask):
    inv_rms = lax.rsqrt(lax.optimization_barrier(jnp.mean(inputs * inputs, axis=-1, keepdims=True)) + NORM_EPS)
    normed = low(inputs * inv_rms * norm_gain[None, :])
    x_and_z = low_back(jnp.dot(normed, in_weight, precision=PRECISE))
    x_value = low(x_and_z[:, :INNER]) * live_mask[:, None]
    z_value = x_and_z[:, INNER:]
    keep_fwd = jnp.concatenate([jnp.zeros((1,), jnp.float32), (segment[1:] == segment[:-1]).astype(jnp.float32)])
    keep_rev = jnp.concatenate([(segment[:-1] == segment[1:]).astype(jnp.float32), jnp.zeros((1,), jnp.float32)])
    summed = jnp.zeros_like(z_value)
    for direction in range(2):
        conv_out = low_back(conv_way(x_value, segment, conv_weight[direction], conv_bias[direction], direction))
        s_value = jax.nn.silu(conv_out)
        projected = low_back(jnp.dot(low(s_value), xproj_weight[direction], precision=PRECISE))
        dt_low = low(projected[:, :RANK])
        b_proj = projected[:, RANK:RANK + STATE]
        c_proj = projected[:, RANK + STATE:]
        dt_pre = low_back(jnp.dot(dt_low, dt_weight[direction], precision=PRECISE) + dt_bias[direction][None, :])
        step_size = jax.nn.softplus(dt_pre) * live_mask[:, None]
        a_matrix = -jnp.exp(a_log[direction])
        if direction == 0:
            y_out = scan_way(step_size, keep_fwd, b_proj, c_proj, s_value, a_matrix)
        else:
            y_out = jnp.flip(scan_way(jnp.flip(step_size, 0), jnp.flip(keep_rev, 0), jnp.flip(b_proj, 0), jnp.flip(c_proj, 0), jnp.flip(s_value, 0), a_matrix), 0)
        summed = summed + y_out + skip[direction][None, :] * s_value
    summed = 0.5 * summed
    gated_low = low(summed * jax.nn.silu(z_value) * live_mask[:, None])
    branch = low_back(jnp.dot(gated_low, out_weight, precision=PRECISE))
    return inputs + branch

def reference(tokens, cotangent, heights, widths, valid, norm_gain, in_weight, conv_weight, conv_bias, xproj_weight, dt_weight, dt_bias, a_log, skip, out_weight):
    weights_f32 = tuple((weight_arg.astype(jnp.float32) for weight_arg in (norm_gain, in_weight, conv_weight, conv_bias, xproj_weight, dt_weight, dt_bias, a_log, skip, out_weight)))
    positions = jnp.arange(SLOTS, dtype=jnp.int32)

    def group_step(summed_grads, group_item):
        group_tokens, group_cotan, group_heights, group_widths, group_valid = group_item
        image_ends = jnp.cumsum(group_heights * group_widths).astype(jnp.int32)
        segment = lax.optimization_barrier(jnp.sum((image_ends[None, :] <= positions[:, None]).astype(jnp.int32), axis=1)).astype(jnp.int32)
        live_mask = (group_valid * (segment < IMAGES).astype(jnp.int32)).astype(jnp.float32)

        def layer_fn(inputs, *weight_list):
            return layer_forward(inputs, *weight_list, segment, live_mask)
        result, pull_back = jax.vjp(layer_fn, group_tokens.astype(jnp.float32), *weights_f32)
        gradients = pull_back(group_cotan.astype(jnp.float32))
        summed_grads = tuple((total_grad + new_grad for total_grad, new_grad in zip(summed_grads, gradients[1:])))
        return (summed_grads, (result.astype(jnp.bfloat16), gradients[0]))
    initial = tuple((jnp.zeros_like(weight_arg) for weight_arg in weights_f32))
    summed_grads, (output, input_grad) = lax.scan(group_step, initial, (tokens, cotangent, heights, widths, valid))
    gain_grad, in_grad, conv_w_grad, conv_b_grad, xproj_grad, dt_w_grad, dt_b_grad, a_log_grad, skip_grad, out_grad = summed_grads
    return (output, input_grad, gain_grad, in_grad, conv_w_grad, conv_b_grad, xproj_grad, dt_w_grad, dt_b_grad, a_log_grad, skip_grad, out_grad)
```

```python
import functools

import jax
import jax.numpy as jnp
from jax import lax
from jax.experimental import pallas as pl
from jax.experimental.pallas import tpu as pltpu
from jax.sharding import PartitionSpec as P

NORM_EPS = 1e-05
CONTRACT_ROWS = (((0,), (0,)), ((), ()))
CONTRACT_COLS = (((1,), (1,)), ((), ()))
LOG2E = 1.4426950408889634
LN2 = 0.6931471805599453
BREAK = 1e30
CHUNKS = 8
LANES = 128
SUMMARY_STATES = 8
SUMMARY_UNROLL = 4
STATES_UNROLL = 2
ADJOINT_STATES = 8
ADJOINT_UNROLL = 2
F32 = jnp.float32
BF16 = jnp.bfloat16


def dot(a, b):
    return jnp.dot(a, b, preferred_element_type=F32)


def dot_rows(a, b):
    return lax.dot_general(a, b, CONTRACT_ROWS, preferred_element_type=F32)


def dot_cols(a, b):
    return lax.dot_general(a, b, CONTRACT_COLS, preferred_element_type=F32)


def sigmoid(v):
    return 1.0 / (1.0 + jnp.exp(-v))


def fetch(source, target, semaphore):
    copy = pltpu.make_async_copy(source, target, semaphore)
    copy.start()
    return copy


def tile_copy(source, target, semaphores, tile):
    if len(target.shape) == 3:
        return pltpu.make_async_copy(source.at[tile], target.at[tile], semaphores.at[tile])
    lanes = lanes_of(tile)
    return pltpu.make_async_copy(source.at[:, lanes], target.at[:, lanes], semaphores.at[tile])


def lanes_of(tile):
    return pl.ds(pl.multiple_of(tile * LANES, LANES), LANES)


def rows_of(j, count=CHUNKS):
    return pl.ds(pl.multiple_of(j * CHUNKS, CHUNKS), count)


def chunk_order(rows):
    row = lax.broadcasted_iota(jnp.int32, (rows, rows), 0)
    slot = lax.broadcasted_iota(jnp.int32, (rows, rows), 1)
    return slot == (row & (CHUNKS - 1)) * (rows // CHUNKS) + (row >> 3)


def image_ends(heights, widths):
    ends, total = [], 0
    for i in range(heights.shape[1]):
        total = total + heights[0, i] * widths[0, i]
        ends.append(total)
    return ends


def segment_of(places, ends):
    found = jnp.zeros_like(places)
    for end in ends:
        found = found + (places >= end).astype(jnp.int32)
    return found


def places_of(first, rows):
    row = lax.broadcasted_iota(jnp.int32, (rows, LANES), 0)
    return first + (row & (CHUNKS - 1)) * (rows // CHUNKS) + (row >> 3)


def norm_kernel(
    place, heights, widths, tokens, cotangent, valid, gain,
    normed_out, live_out, cotan_out, to_core, to_chip,
):
    rows, width = tokens.shape
    ends = image_ends(heights, widths)
    order = chunk_order(rows)
    order_low = order.astype(BF16)
    picked = jnp.where(order, jnp.broadcast_to(valid[...].astype(F32), order.shape), 0.0)
    live = dot(picked.astype(BF16), jnp.ones((rows, LANES), BF16))
    segment = segment_of(places_of(place[0], rows), ends)
    live = jnp.where(segment < heights.shape[1], live, 0.0)
    live_out[...] = live
    inputs = dot(order_low, tokens[...])
    cotan_out[...] = dot(order_low, cotangent[...]).astype(BF16)
    inv_rms = lax.rsqrt(jnp.mean(inputs * inputs, axis=-1, keepdims=True) + NORM_EPS)
    normed = inputs * inv_rms * gain[...].astype(F32)
    normed_out[0:rows, :] = normed.astype(BF16)
    live_wide = jnp.concatenate([live] * (width // LANES), axis=1)
    normed_out[rows : 2 * rows, :] = (normed * live_wide).astype(BF16)
    edge = 2 * CHUNKS
    row = lax.broadcasted_iota(jnp.int32, (edge, rows), 0)
    slot = lax.broadcasted_iota(jnp.int32, (edge, rows), 1)
    held = jnp.broadcast_to(valid[...].astype(F32), (edge, rows))
    first = jnp.where(slot == row, held, 0.0).astype(BF16)
    last = jnp.where(slot == rows - edge + row, held, 0.0).astype(BF16)
    first = dot(first, tokens[...]).astype(BF16)
    last = dot(last, tokens[...]).astype(BF16)
    even = place[1] == 0
    to_core[...] = jnp.where(even, last, first)
    to_chip[...] = jnp.where(even, first, last)


def front_kernel(
    normed, live, cotan, in_weight, out_weight, x_out, zs_out, dgz_out, dy_out,
):
    rows = cotan.shape[0]
    inner = out_weight.shape[0]
    step = 2 * LANES
    live_two = jnp.concatenate([live[...]] * 2, axis=1)
    for at in range(0, inner, step):
        x_out[:, at : at + step] = (
            dot(normed[rows : 2 * rows, :], in_weight[:, at : at + step]).astype(BF16).astype(F32)
        )
        z = dot(normed[0:rows, :], in_weight[:, inner + at : inner + at + step])
        grad = dot_cols(cotan[...], out_weight[at : at + step, :])
        gate = sigmoid(z)
        zs = z * gate * live_two
        zs_out[:, at : at + step] = zs
        dy_out[:, at : at + step] = 0.5 * grad * zs
        dgz_out[:, at : at + step] = grad * live_two * (gate * (1.0 + z * (1.0 - gate)))


def spread(values, target):
    count = values.shape[1]
    high = values.astype(BF16)
    low = (values - high.astype(F32)).astype(BF16)
    both = jnp.concatenate([high, low], axis=1)
    wide = 4 * LANES
    column = lax.broadcasted_iota(jnp.int32, (2 * count, wide), 0)
    block = lax.broadcasted_iota(jnp.int32, (2 * count, wide), 1) // LANES
    for at in range(0, count * LANES, wide):
        place = block + at // LANES
        pick = ((column == place) | (column == place + count)).astype(BF16)
        target[:, at : at + wide] = dot(both, pick)


def windows(span, up, sublane):
    sign = 1 if up else -1

    def from_before(value, by, fill):
        moved = pltpu.roll(value, (sign * by) % CHUNKS, axis=0)
        kept = sublane >= by if up else sublane < CHUNKS - by
        return jnp.where(kept, moved, fill)

    two = span + from_before(span, 1, 0.0)
    four = two + from_before(two, 2, 0.0)
    eight = four + from_before(four, 4, 0.0)
    edge = [jnp.where(sublane >= by if up else sublane < CHUNKS - by, 0.0, BREAK) for by in (1, 2, 4)]
    return (span + edge[0], two + edge[1], four + edge[2]), from_before(eight, 1, 0.0)


def chain(rate, sums, tail, up, sublane):
    sign = 1 if up else -1
    for by, span in zip((1, 2, 4), sums):
        tail = jnp.exp2(rate * span) * pltpu.roll(tail, (sign * by) % CHUNKS, axis=0) + tail
    end = CHUNKS - 1 if up else 0
    kept = sublane >= 1 if up else sublane < CHUNKS - 1
    return jnp.where(kept, pltpu.roll(tail, sign % CHUNKS, axis=0), 0.0), tail[end : end + 1]


def middle_kernel(
    place, heights, widths, from_core, from_chip, x, live, gain, in_weight, conv_weight,
    conv_bias, xproj, dt_weight, dt_bias, a_log, dy_far,
    proj_out, dtlow_out, same_out, nhalo_out, rate_out, before_out, tail_out, after_out, head_out,
    sum_out, sent_out, s_far, low_far, dsilu_far, delta_far, gate_far, xext_far,
    bc, tails, heads, spans, dy, s_out, low_out, dsilu_out, delta_out, gate_out, xext_out, moves,
    *, slots, reach,
):
    rows, inner = x.shape
    dy_here = fetch(dy_far, dy, moves.at[0])
    leaving = []
    width = from_core.shape[1]
    steps = rows // CHUNKS
    state = a_log.shape[1]
    rank = dt_weight.shape[1]
    tiles = inner // LANES
    ends = image_ends(heights, widths)
    start = place[0]
    images = heights.shape[1]
    sublane = lax.broadcasted_iota(jnp.int32, (CHUNKS, LANES), 0)

    even = place[1] == 0
    before = jnp.where(even, from_chip[...], from_core[...])
    after = jnp.where(even, from_core[...], from_chip[...])
    htok = jnp.concatenate([before[CHUNKS:], after[:CHUNKS]], axis=0)
    hrow = lax.broadcasted_iota(jnp.int32, (2 * CHUNKS, LANES), 0)
    hplace = jnp.where(hrow < CHUNKS, start - CHUNKS + hrow, start + rows + hrow - CHUNKS)
    hlive = (segment_of(hplace, ends) < images).astype(F32)
    htok = htok.astype(F32) * jnp.concatenate([hlive] * (width // LANES), axis=1)
    hinv = lax.rsqrt(jnp.mean(htok * htok, axis=-1, keepdims=True) + NORM_EPS)
    scaled = htok * hinv
    nhalo = (scaled * gain[...].astype(F32)).astype(BF16)
    nhalo_out[...] = jnp.concatenate([nhalo, scaled.astype(BF16)], axis=0)
    hx = dot(nhalo, in_weight[:, :inner]).astype(BF16).astype(F32)
    wide = lax.broadcasted_iota(jnp.int32, (CHUNKS, inner), 0)
    xext_out[reach * CHUNKS : (reach + steps) * CHUNKS, :] = x[...]
    for i in range(reach):
        at = steps - reach + i
        moved = pltpu.roll(x[at * CHUNKS : (at + 1) * CHUNKS, :], 1, axis=0)
        of = CHUNKS - reach + i
        xext_out[i * CHUNKS : (i + 1) * CHUNKS, :] = jnp.where(wide == 0, hx[of : of + 1], moved)
        moved = pltpu.roll(x[i * CHUNKS : (i + 1) * CHUNKS, :], CHUNKS - 1, axis=0)
        at = reach + steps + i
        of = CHUNKS + i
        xext_out[at * CHUNKS : (at + 1) * CHUNKS, :] = jnp.where(
            wide == CHUNKS - 1, hx[of : of + 1], moved
        )

    places = places_of(start, rows)
    segment = segment_of(places, ends)
    for k in range(1, reach + 1):
        same = (segment_of(places - k, ends) == segment) & (places >= k)
        same_out[(k - 1) * rows : k * rows, :] = same.astype(F32)
        same = (segment_of(places + k, ends) == segment) & (places + k < slots)
        same_out[(reach + k - 1) * rows : (reach + k) * rows, :] = same.astype(F32)

    taps = reach + 1
    conv_w = [conv_weight[d].astype(F32) for d in range(2)]
    conv_b = conv_bias[...].astype(F32)
    block = 32
    for tile in range(tiles):
        lanes = slice(tile * LANES, (tile + 1) * LANES)

        def conv_block(b, _):
            at = pl.multiple_of(b * block, block)
            for d in range(2):
                total = conv_b[d : d + 1, lanes] + conv_w[d][reach:taps, lanes] * (
                    xext_out[pl.ds(at + reach * CHUNKS, block), lanes]
                )
                for k in range(1, taps):
                    move = reach - k if d == 0 else reach + k
                    mask = same_out[pl.ds((d * reach + k - 1) * rows + at, block), :]
                    total = total + conv_w[d][reach - k : taps - k, lanes] * (
                        xext_out[pl.ds(at + move * CHUNKS, block), lanes] * mask
                    )
                gate = sigmoid(total)
                value = total * gate
                s_out[pl.ds(d * rows + at, block), lanes] = value
                low_out[pl.ds(d * rows + at, block), lanes] = value.astype(BF16)
                dsilu_out[pl.ds(d * rows + at, block), lanes] = gate * (1.0 + total * (1.0 - gate))
            return 0

        lax.fori_loop(0, rows // block, conv_block, 0)

    for i, (source, target) in enumerate(
        ((s_out, s_far), (low_out, low_far), (dsilu_out, dsilu_far), (xext_out, xext_far))
    ):
        leaving.append(fetch(source, target, moves.at[1 + i]))
    step = 2 * LANES
    live_two = jnp.concatenate([live[...]] * 2, axis=1)
    dt_b = dt_bias[...].astype(F32)
    for d in range(2):
        rate_out[d * state : (d + 1) * state, :] = jnp.minimum(
            -LOG2E * jnp.exp(a_log[d].astype(F32)), -1e-20
        )
        here = slice(d * rows, (d + 1) * rows)
        proj = dot_cols(low_out[here, :], xproj[d])
        proj_out[here, :] = proj
        dt_low = proj[:, :rank].astype(BF16)
        dtlow_out[here, :] = dt_low
        for at in range(0, inner, step):
            pre = dot(dt_low, dt_weight[d, :, at : at + step]) + dt_b[d : d + 1, at : at + step]
            small = jnp.exp(-jnp.abs(pre))
            log1p = jnp.where(small < 1e-4, small * (1.0 - 0.5 * small), jnp.log(1.0 + small))
            delta_out[here, at : at + step] = (jnp.maximum(pre, 0.0) + log1p) * live_two
            gate_out[here, at : at + step] = (
                jnp.where(pre >= 0.0, 1.0, small) / (1.0 + small) * live_two
            )
        leaving.append(fetch(delta_out.at[here, :], delta_far.at[here, :], moves.at[5 + d]))
        leaving.append(fetch(gate_out.at[here, :], gate_far.at[here, :], moves.at[7 + d]))
        spread(proj[:, rank:], bc)
        if d == 0:
            dy_here.wait()
        some = SUMMARY_STATES

        def scan_tile(tile, _, d=d):
            lanes = lanes_of(tile)
            for low in range(0, state, some):
                rates = [
                    jnp.broadcast_to(
                        rate_out[d * state + low + m : d * state + low + m + 1, lanes],
                        (CHUNKS, LANES),
                    )
                    for m in range(some)
                ]

                def scan_step(i, carried, d=d, low=low, rates=rates):
                    tail, lead, head, span = carried
                    j = i if d == 0 else steps - 1 - i
                    at = pl.multiple_of(j * CHUNKS, CHUNKS)
                    keep = same_out[pl.ds(d * reach * rows + at, CHUNKS), :]
                    delta = delta_out[pl.ds(d * rows + at, CHUNKS), lanes]
                    drive = delta * s_out[pl.ds(d * rows + at, CHUNKS), lanes]
                    back = dy[pl.ds(at, CHUNKS), lanes]
                    delta = jnp.where(keep > 0.0, delta, BREAK)
                    tail, lead, head = list(tail), list(lead), list(head)
                    for m in range(some):
                        b = bc[pl.ds(at, CHUNKS), (low + m) * LANES : (low + m + 1) * LANES]
                        n = state + low + m
                        c = bc[pl.ds(at, CHUNKS), n * LANES : (n + 1) * LANES]
                        decay = jnp.exp2(delta * rates[m])
                        tail[m] = decay * tail[m] + b * drive
                        lead[m] = lead[m] * decay
                        head[m] = head[m] + lead[m] * (c * back)
                    return tuple(tail), tuple(lead), tuple(head), span + delta

                zeros = tuple(jnp.zeros((CHUNKS, LANES), F32) for _ in range(some))
                ones = tuple(jnp.ones((CHUNKS, LANES), F32) for _ in range(some))
                tail, lead, head, span = lax.fori_loop(
                    0, steps, scan_step, (zeros, ones, zeros, zeros[0]), unroll=SUMMARY_UNROLL
                )
                for m in range(some):
                    tails[low + m, :, lanes] = tail[m]
                    heads[low + m, :, lanes] = head[m]
                spans[:, lanes] = span
            return 0

        lax.fori_loop(0, tiles, scan_tile, 0)

        tail_row = 0 if d == 0 else 2 * state
        head_row = 3 * state if d == 0 else state

        def chain_tile(tile, _, d=d, tail_row=tail_row, head_row=head_row):
            lanes = lanes_of(tile)
            span = spans[:, lanes]
            sums, before = windows(span, d == 0, sublane)
            sums_back, after = windows(span, d == 1, sublane)
            before_out[d * CHUNKS : (d + 1) * CHUNKS, lanes] = before
            after_out[d * CHUNKS : (d + 1) * CHUNKS, lanes] = after
            for n in range(state):
                rate = jnp.broadcast_to(
                    rate_out[d * state + n : d * state + n + 1, lanes], (CHUNKS, LANES)
                )
                carried, total = chain(rate, sums, tails[n, :, lanes], d == 0, sublane)
                tail_out[d * state + n, :, lanes] = carried
                sum_out[tail_row + n : tail_row + n + 1, lanes] = total
                carried, total = chain(rate, sums_back, heads[n, :, lanes], d == 1, sublane)
                head_out[d * state + n, :, lanes] = carried
                sum_out[head_row + n : head_row + n + 1, lanes] = total
            return 0

        lax.fori_loop(0, tiles, chain_tile, 0)
        sum_out[4 * state + d : 4 * state + d + 1, :] = jnp.sum(spans[...], axis=0, keepdims=True)
    sum_out[4 * state + 2 :, :] = jnp.zeros((sum_out.shape[0] - 4 * state - 2, inner), F32)
    sent_out[...] = packed(sum_out[...], state)
    for copy in leaving:
        copy.wait()


def packed(summary, state):
    rest = summary[4 * state :]
    high = rest.astype(BF16)
    low = (rest - high.astype(F32)).astype(BF16)
    return jnp.concatenate([summary[: 4 * state].astype(BF16), high, low], axis=0)


def leads(rate, spans, state, flip):
    parts = [jnp.exp2(rate[d * state : (d + 1) * state] * spans[d : d + 1]) for d in range(2)]
    return jnp.concatenate(parts[::-1] if flip else parts, axis=0)


def join_kernel(
    flags, got, summary, entered, rate, summary_out, entered_out, sent_out, *, state, bit, final
):
    half = 2 * state
    upper = flags[bit] == 1
    mine = summary[...]
    values = got[...].astype(F32)
    spans = mine[4 * state : 4 * state + 2]
    other = values[4 * state : 4 * state + 2] + values[4 * state + CHUNKS : 4 * state + CHUNKS + 2]
    rates = rate[...]
    if entered is None:
        entered_up = jnp.where(upper, values[:half], 0.0)
        entered_down = jnp.where(upper, 0.0, values[half : 2 * half])
        span_up = jnp.where(upper, other, 0.0)
        span_down = jnp.where(upper, 0.0, other)
    else:
        held = entered[...]
        span_up, span_down = held[2 * half : 2 * half + 2], held[2 * half + 2 : 2 * half + 4]
        entered_up = held[:half] + jnp.where(
            upper, leads(rates, span_up, state, False) * values[:half], 0.0
        )
        entered_down = held[half : 2 * half] + jnp.where(
            upper, 0.0, leads(rates, span_down, state, True) * values[half : 2 * half]
        )
        span_up = span_up + jnp.where(upper, other, 0.0)
        span_down = span_down + jnp.where(upper, 0.0, other)
    entered_out[0:half, :] = entered_up
    entered_out[half : 2 * half, :] = entered_down
    entered_out[2 * half :, :] = jnp.concatenate(
        [span_up, span_down, jnp.zeros((CHUNKS - 4, mine.shape[1]), F32)], axis=0
    )
    low_up = jnp.where(upper, values[:half], mine[:half])
    high_up = jnp.where(upper, mine[:half], values[:half])
    low_down = jnp.where(upper, values[half : 2 * half], mine[half : 2 * half])
    high_down = jnp.where(upper, mine[half : 2 * half], values[half : 2 * half])
    low_span, high_span = jnp.where(upper, other, spans), jnp.where(upper, spans, other)
    up = leads(rates, high_span, state, False) * low_up + high_up
    down = leads(rates, low_span, state, True) * high_down + low_down
    if final:
        sent_out[...] = jnp.where(flags[bit + 1] == 1, down, up).astype(BF16)
    else:
        total = jnp.concatenate(
            [up, down, spans + other, jnp.zeros((CHUNKS - 2, mine.shape[1]), F32)], axis=0
        )
        summary_out[...] = total
        sent_out[...] = packed(total, state)


def first_join(flags, got, summary, rate, *outs, state, bit, final):
    join_kernel(flags, got, summary, None, rate, *outs, state=state, bit=bit, final=final)


def state_block(j, state):
    return pl.multiple_of(j * state * CHUNKS, CHUNKS)


def states_pass(d, steps, state, rates, begin, delta, s, keep, bc, h_out, y):
    start = state_block(0 if d == 0 else steps, state)
    for n in range(state):
        h_out[pl.ds(start + n * CHUNKS, CHUNKS), :] = begin[n]

    def step(i, h):
        j = i if d == 0 else steps - 1 - i
        at = pl.multiple_of(j * CHUNKS, CHUNKS)
        here = pl.ds(at, CHUNKS)
        to = state_block(j + 1 if d == 0 else j, state)
        size = delta[here, :]
        drive = size * s[here, :]
        size = jnp.where(keep[here, :] > 0.0, size, BREAK)
        h = list(h)
        total = None if d == 0 else y[here, :]
        for n in range(state):
            b = bc[here, n * LANES : (n + 1) * LANES]
            c = bc[here, (state + n) * LANES : (state + n + 1) * LANES]
            h[n] = jnp.exp2(size * rates[n]) * h[n] + b * drive
            h_out[pl.ds(to + n * CHUNKS, CHUNKS), :] = h[n]
            total = c * h[n] if total is None else total + c * h[n]
        y[here, :] = total
        return tuple(h)

    lax.fori_loop(0, steps, step, tuple(begin), unroll=STATES_UNROLL)


def adjoint_pass(
    d, steps, state, rates, back, delta, s, gate, dy, keep, skip, bc, h_in, sums, dpre_out, ds_out,
    rows_out,
):
    some = ADJOINT_STATES
    edge = steps - 1
    skip = skip[...]
    zeros = jnp.zeros((CHUNKS, LANES), F32)
    grads = []
    for low in range(0, state, some):
        final = low + some == state

        def step(i, carried, low=low, final=final):
            g, acc, h, skip_acc, bias_acc = carried
            j = edge - i if d == 0 else i
            here = pl.ds(pl.multiple_of(j * CHUNKS, CHUNKS), CHUNKS)
            size = delta[here, :]
            value = s[here, :]
            grad = dy[here, :]
            drive = size * value
            masked = jnp.where(keep[here, :] > 0.0, size, BREAK)
            prev = state_block(j if d == 0 else j + 1, state)
            g, acc, h = list(g), list(acc), list(h)
            weighted = zeros if low == 0 else ds_out[here, :]
            rate_sum = zeros if low == 0 else dpre_out[here, :]
            for m in range(some):
                n = low + m
                b = bc[here, n * LANES : (n + 1) * LANES]
                c = bc[here, (state + n) * LANES : (state + n + 1) * LANES]
                decay = jnp.exp2(masked * rates[n])
                adjoint = c * grad + g[m]
                before = h_in[pl.ds(prev + n * CHUNKS, CHUNKS), :]
                sums[here, n * LANES : (n + 1) * LANES] += adjoint * drive
                sums[here, (state + n) * LANES : (state + n + 1) * LANES] += grad * h[m]
                g[m] = adjoint * decay
                held = g[m] * before
                weighted = weighted + adjoint * b
                rate_sum = rate_sum + held * rates[n]
                acc[m] = acc[m] + held * masked
                h[m] = before
            if final:
                ds_out[here, :] = skip * grad + size * weighted
                pre = ((LN2 * rate_sum + weighted * value) * gate[here, :]).astype(BF16).astype(F32)
                dpre_out[here, :] = pre
                bias_acc = bias_acc + pre
                skip_acc = skip_acc + grad * value
            else:
                dpre_out[here, :] = rate_sum
                ds_out[here, :] = weighted
            return tuple(g), tuple(acc), tuple(h), skip_acc, bias_acc

        last = state_block(steps if d == 0 else 0, state)
        h_last = tuple(h_in[pl.ds(last + (low + m) * CHUNKS, CHUNKS), :] for m in range(some))
        none = tuple(zeros for _ in range(some))
        _, acc, _, skip_acc, bias_acc = lax.fori_loop(
            0, steps, step, (tuple(back[low : low + some]), none, h_last, zeros, zeros),
            unroll=ADJOINT_UNROLL,
        )
        grads.extend(acc)
    for n in range(state):
        rows_out[n : n + 1, :] = jnp.sum(grads[n], axis=0, keepdims=True) * rates[n][0:1] * LN2
    rows_out[state : state + 1, :] = jnp.sum(bias_acc, axis=0, keepdims=True)
    rows_out[state + 1 : state + 2, :] = jnp.sum(skip_acc, axis=0, keepdims=True)


def lane_sums(sums, state):
    depth = 2 * state * LANES
    block = lax.broadcasted_iota(jnp.int32, (depth, LANES), 0) // LANES
    column = lax.broadcasted_iota(jnp.int32, (depth, LANES), 1)
    return dot(sums.astype(BF16), (block == column).astype(BF16))[:, : 2 * state]


def rate_tiles(rate, d, state, lanes):
    return [
        jnp.broadcast_to(rate[d * state + n : d * state + n + 1, lanes], (CHUNKS, LANES))
        for n in range(state)
    ]


def begin_tiles(rates, passed, tail, carry, at, d, state, lanes):
    passed = passed[d * CHUNKS : (d + 1) * CHUNKS, lanes]
    return [
        jnp.exp2(rates[n] * passed) * carry[at + n : at + n + 1, lanes]
        + tail[d * state + n, :, lanes]
        for n in range(state)
    ]


def slot_order(rows):
    row = lax.broadcasted_iota(jnp.int32, (rows, rows), 1)
    slot = lax.broadcasted_iota(jnp.int32, (rows, rows), 0)
    return (slot == (row & (CHUNKS - 1)) * (rows // CHUNKS) + (row >> 3)).astype(BF16)


def states_kernel(
    flags, got, entered, before, tail, rate, skip, proj, same, normed, cotan, tokens, out_weight,
    delta_far, s_far, zs_far, dgz_far,
    dz_out, out_grad, z_grad, output, carry_out, h0_far, h1_far,
    bc0, bc1, y, gated_low, delta, s, zs, dgz, h0, h1, tile_moves, out_moves, moves,
    *, reach, rank, bit,
):
    rows, inner = zs.shape
    steps = rows // CHUNKS
    state = rate.shape[0] // 2
    half = 2 * state
    tiles = inner // LANES
    for tile in range(tiles):
        tile_copy(delta_far, delta, tile_moves.at[0], tile).start()
        tile_copy(s_far, s, tile_moves.at[1], tile).start()
    zs_here = fetch(zs_far, zs, moves.at[0])
    dgz_here = fetch(dgz_far, dgz, moves.at[1])
    upper = flags[bit] == 1
    values = got[...].astype(F32)
    held = entered[...]
    rates = rate[...]
    carry_out[0:half, :] = held[:half] + jnp.where(
        upper, leads(rates, held[2 * half : 2 * half + 2], state, False) * values, 0.0
    )
    carry_out[half : 2 * half, :] = held[half : 2 * half] + jnp.where(
        upper, 0.0, leads(rates, held[2 * half + 2 : 2 * half + 4], state, True) * values
    )
    spread(proj[0:rows, rank:], bc0)
    spread(proj[rows : 2 * rows, rank:], bc1)

    def scan_tile(tile, _):
        lanes = lanes_of(tile)
        tile_copy(delta_far, delta, tile_moves.at[0], tile).wait()
        tile_copy(s_far, s, tile_moves.at[1], tile).wait()
        for d, (bc, h_out, h_far) in enumerate(((bc0, h0, h0_far), (bc1, h1, h1_far))):
            rates = rate_tiles(rate, d, state, lanes)
            begin = begin_tiles(rates, before, tail, carry_out, d * half, d, state, lanes)
            mine = slice(d * rows, (d + 1) * rows)
            states_pass(
                d, steps, state, rates, begin, delta.at[mine, lanes], s.at[mine, lanes],
                same.at[d * reach * rows : (d * reach + 1) * rows, :], bc, h_out.at[tile],
                y.at[:, lanes],
            )
            tile_copy(h_out, h_far, out_moves.at[d], tile).start()
        return 0

    lax.fori_loop(0, tiles, scan_tile, 0)
    zs_here.wait()
    dgz_here.wait()
    skips = skip[...].astype(F32)
    block = 32
    for tile in range(tiles):
        lanes = slice(tile * LANES, (tile + 1) * LANES)

        def gate_block(b, _):
            here = pl.ds(pl.multiple_of(b * block, block), block)
            there = pl.ds(pl.multiple_of(rows + b * block, block), block)
            total = 0.5 * (
                y[here, lanes] + skips[0:1, lanes] * s[here, lanes] + skips[1:2, lanes] * s[there, lanes]
            )
            gated_low[here, lanes] = (total * zs[here, lanes]).astype(BF16)
            dz_out[here, lanes] = (total * dgz[here, lanes]).astype(BF16)
            return 0

        lax.fori_loop(0, rows // block, gate_block, 0)
    folds, width = z_grad.shape[0] // normed.shape[1], normed.shape[1]
    out_grad[...] = dot_rows(gated_low[...], cotan[...])
    for i in range(folds):
        z_grad[i * width : (i + 1) * width, :] = dot_rows(
            normed[0:rows, :], dz_out[:, i * width : (i + 1) * width]
        )
    gated = dot(slot_order(rows), gated_low[...]).astype(BF16)
    output[...] = (tokens[...].astype(F32) + dot(gated, out_weight[...])).astype(BF16)
    for tile in range(tiles):
        tile_copy(h0, h0_far, out_moves.at[0], tile).wait()
        tile_copy(h1, h1_far, out_moves.at[1], tile).wait()


def adjoint_kernel(
    after, head, carry, rate, skip, proj, same, dtlow, dt_weight, xproj, conv_weight,
    delta_far, s_far, gate_far, dy_far, h_far, low_far, dsilu_far, xext_far, dx_far,
    dx_out, dc_rim, small_out,
    bc, sums, dpre, ds, rows_out, ext, delta, s, gate, dy, h, low, dsilu, xext, tile_moves, moves,
    *, d, reach, rank,
):
    rows, inner = dy.shape
    steps = rows // CHUNKS
    state = rate.shape[0] // 2
    half = 2 * state
    tiles = inner // LANES
    mine = slice(d * rows, (d + 1) * rows)
    by_tiles = (
        (delta_far.at[mine, :], delta), (s_far.at[mine, :], s), (gate_far.at[mine, :], gate),
        (dy_far, dy), (h_far, h),
    )
    for tile in range(tiles):
        for i, (source, target) in enumerate(by_tiles):
            tile_copy(source, target, tile_moves.at[i], tile).start()
    later = [
        fetch(low_far.at[mine, :], low, moves.at[0]), fetch(dsilu_far.at[mine, :], dsilu, moves.at[1]),
        fetch(xext_far, xext, moves.at[2]),
    ]
    if dx_far is not None:
        later.append(fetch(dx_far, dx_out, moves.at[3]))
    taps = reach + 1
    cols = proj.shape[1]
    keep = same.at[d * reach * rows : (d * reach + 1) * rows, :]
    spread(proj[mine, rank:], bc)
    sums[...] = jnp.zeros_like(sums)
    skips = skip[...].astype(F32)[d : d + 1]
    rows_out[...] = jnp.zeros_like(rows_out)
    at = (half if d == 0 else 0) + state

    def scan_tile(tile, _):
        lanes = lanes_of(tile)
        rates = rate_tiles(rate, d, state, lanes)
        back = begin_tiles(rates, after, head, carry, at, d, state, lanes)
        for i, (source, target) in enumerate(by_tiles):
            tile_copy(source, target, tile_moves.at[i], tile).wait()
        adjoint_pass(
            d, steps, state, rates, back, delta.at[:, lanes], s.at[:, lanes],
            gate.at[:, lanes], dy.at[:, lanes], keep, skip32.at[:, lanes], bc, h.at[tile], sums,
            dpre.at[:, lanes], ds.at[:, lanes], rows_out.at[:, lanes],
        )
        return 0

    skip32 = ext.at[0:1, :]
    skip32[...] = skips
    lax.fori_loop(0, tiles, scan_tile, 0)
    dpre_low = dpre[...].astype(BF16)
    dt_grad = dot_rows(dtlow[mine, :], dpre_low)
    dt_back = dot_cols(dpre_low, dt_weight[d])
    dproj = jnp.concatenate([dt_back, lane_sums(sums[...], state)], axis=1).astype(BF16)
    for copy in later:
        copy.wait()
    small_out[0:cols, :] = dot_rows(dproj, low[...])
    small_out[cols : cols + rank, :] = dt_grad
    base = 0 if d == 0 else reach * CHUNKS
    step = 2 * LANES
    for lane in range(0, inner, step):
        lanes = slice(lane, lane + step)
        total = ds[:, lanes] + dot(dproj, xproj[d, :, lanes])
        ext[base : base + rows, lanes] = (total * dsilu[:, lanes]).astype(BF16).astype(F32)
    wide = lax.broadcasted_iota(jnp.int32, (CHUNKS, inner), 0)
    for i in range(reach):
        if d == 0:
            moved = pltpu.roll(ext[i * CHUNKS : (i + 1) * CHUNKS, :], CHUNKS - 1, axis=0)
            ext[rows + i * CHUNKS : rows + (i + 1) * CHUNKS, :] = jnp.where(
                wide == CHUNKS - 1, 0.0, moved
            )
        else:
            moved = pltpu.roll(ext[rows + i * CHUNKS : rows + (i + 1) * CHUNKS, :], 1, axis=0)
            ext[i * CHUNKS : (i + 1) * CHUNKS, :] = jnp.where(wide == 0, 0.0, moved)

    conv_w = conv_weight[d].astype(F32)
    block = 32
    zeros = jnp.zeros((CHUNKS, LANES), F32)

    def folded(values):
        return functools.reduce(
            lambda a, b: a + b, [values[i : i + CHUNKS] for i in range(0, block, CHUNKS)]
        )

    base_row = cols + rank
    for tile in range(tiles):
        lanes = slice(tile * LANES, (tile + 1) * LANES)
        weight = conv_w[:, lanes]

        def conv_block(b, totals, lanes=lanes, weight=weight):
            here = pl.multiple_of(b * block, block)
            totals = list(totals)
            mid = ext[pl.ds(here + base, block), lanes]
            total = weight[reach:taps] * mid
            totals[reach] = totals[reach] + folded(mid * xext[pl.ds(here + reach * CHUNKS, block), lanes])
            totals[taps] = totals[taps] + folded(mid)
            for k in range(1, taps):
                past = same[pl.ds((k - 1) * rows + here, block), :]
                ahead = same[pl.ds((reach + k - 1) * rows + here, block), :]
                if d == 0:
                    given = ext[pl.ds(here + k * CHUNKS, block), lanes] * ahead
                    taken = xext[pl.ds(here + (reach - k) * CHUNKS, block), lanes] * past
                else:
                    given = ext[pl.ds(here + (reach - k) * CHUNKS, block), lanes] * past
                    taken = xext[pl.ds(here + (reach + k) * CHUNKS, block), lanes] * ahead
                total = total + weight[reach - k : taps - k] * given
                totals[reach - k] = totals[reach - k] + folded(mid * taken)
            if dx_far is not None:
                total = total + dx_out[pl.ds(here, block), lanes]
            dx_out[pl.ds(here, block), lanes] = total
            return tuple(totals)

        totals = lax.fori_loop(0, rows // block, conv_block, (zeros,) * (taps + 1))
        for i in range(taps + 1):
            at = state + 2 + i
            rows_out[at : at + 1, lanes] = jnp.sum(totals[i], axis=0, keepdims=True)

    edge = []
    for i in range(CHUNKS):
        row = jnp.zeros((1, inner), F32)
        for k in range(1, taps):
            j = i - CHUNKS + k if d == 0 else steps + i - k
            if (d == 0 and j >= 0) or (d == 1 and j < steps):
                sub = 0 if d == 0 else CHUNKS - 1
                at = (d * reach + k - 1) * rows + j * CHUNKS + sub
                mask = jnp.concatenate([same[at : at + 1, :]] * tiles, axis=1)
                at = base + j * CHUNKS + sub
                row = row + conv_w[reach - k : taps - k] * ext[at : at + 1, :] * mask
        edge.append(row)
    dc_rim[...] = jnp.concatenate(edge, axis=0)
    small_out[base_row:, :] = rows_out[0 : small_out.shape[0] - base_row, :]


def first_adjoint(*refs, **static):
    adjoint_kernel(*refs[:19], None, *refs[19:], **static)


def last_kernel(
    place, dx, rim0, rim1, small0, small1, normed, nhalo, live, dz, in_weight, tokens,
    grads, dn_out, to_core, to_chip,
    low,
):
    rows, inner = dx.shape
    width = tokens.shape[1]
    folds = inner // width
    fold = grads.shape[0] // folds
    step = 2 * LANES
    live_two = jnp.concatenate([live[...]] * 2, axis=1)
    edges = 2 * CHUNKS
    for at in range(0, inner, step):
        low[0:rows, at : at + step] = (dx[:, at : at + step] * live_two).astype(BF16)
    low[rows : rows + edges, :] = jnp.concatenate([rim0[...], rim1[...]], axis=0).astype(BF16)
    both = jnp.concatenate([normed[0:rows, :], nhalo[0:edges, :]], axis=0)
    count = small0.shape[0]
    for i in range(folds):
        lanes = slice(i * width, (i + 1) * width)
        base = i * fold
        grads[base : base + width, :] = dot_rows(both, low[:, lanes])
        grads[base + width : base + width + count, :] = small0[:, lanes]
        grads[base + width + count : base + width + 2 * count, :] = small1[:, lanes]
        grads[base + width + 2 * count : base + fold, :] = jnp.zeros(
            (fold - width - 2 * count, width), F32
        )
    back = slot_order(rows)
    dn = dot_cols(dot(back, low[0:rows, :]).astype(BF16), in_weight[:, 0:inner]) + dot_cols(
        dot(back, dz[...]).astype(BF16), in_weight[:, inner : 2 * inner]
    )
    dn_out[...] = dn
    rim = dot_cols(low[rows : rows + edges, :], in_weight[:, 0:inner])
    even = place[1] == 0
    to_core[...] = jnp.where(even, rim[CHUNKS:], rim[:CHUNKS])
    to_chip[...] = jnp.where(even, rim[:CHUNKS], rim[CHUNKS:])
    inputs = tokens[...].astype(F32)
    inv_rms = lax.rsqrt(jnp.mean(inputs * inputs, axis=-1, keepdims=True) + NORM_EPS)
    gain_row = width + 2 * count
    grads[gain_row : gain_row + 1, :] = jnp.sum(
        dn * (inputs * inv_rms), axis=0, keepdims=True
    ) + jnp.sum(rim * nhalo[edges : 2 * edges, :].astype(F32), axis=0, keepdims=True)


def finish_kernel(
    place, heights, widths, from_core, from_chip, dn, tokens, cotangent, valid, gain, input_grad
):
    rows, width = tokens.shape
    even = place[1] == 0
    before = jnp.where(even, from_chip[...], from_core[...])
    after = jnp.where(even, from_core[...], from_chip[...])
    end = image_ends(heights, widths)[-1]
    row = lax.broadcasted_iota(jnp.int32, (CHUNKS, rows), 0)
    slot = lax.broadcasted_iota(jnp.int32, (CHUNKS, rows), 1)
    alive = jnp.broadcast_to(valid[...].astype(F32), (CHUNKS, rows))
    alive = jnp.where(place[0] + slot < end, alive, 0.0)
    first = jnp.sum(jnp.where(slot == row, alive, 0.0), axis=1, keepdims=True)
    last = jnp.sum(jnp.where(slot == rows - CHUNKS + row, alive, 0.0), axis=1, keepdims=True)
    values = jnp.concatenate(
        [
            dn[0:CHUNKS, :] + first * before, dn[CHUNKS : rows - CHUNKS, :],
            dn[rows - CHUNKS : rows, :] + last * after,
        ],
        axis=0,
    )
    inputs = tokens[...].astype(F32)
    inv_rms = lax.rsqrt(jnp.mean(inputs * inputs, axis=-1, keepdims=True) + NORM_EPS)
    scaled = values * gain[...].astype(F32)
    mean = jnp.mean(scaled * inputs, axis=-1, keepdims=True)
    input_grad[...] = (
        cotangent[...].astype(F32) + inv_rms * scaled - inputs * (inv_rms * inv_rms * inv_rms) * mean
    )


def unpack_kernel(
    even, plane, first_mine, first_other, second_mine, second_other,
    in_out, conv_w, conv_b, xproj, dt_w, dt_b, a_log, skip, out_w, gain,
    left, right,
    *, count, state, rank, cols, taps,
):
    blocks = first_mine.shape[0]
    width = out_w.shape[1]
    folds = out_w.shape[0] // width

    def ordered(mine, other, into_first, into_second):
        size = mine.shape[1]
        is_even = even[0] == 0
        for k in range(blocks):
            source = plane[0] ^ k
            a, b = mine[source].astype(F32), other[source].astype(F32)
            into_first(k * size, jnp.where(is_even, a, b))
            into_second(k * size, jnp.where(is_even, b, a))

    def put_out(at, values):
        out_w[at : at + values.shape[0], :] = values

    def put_z(at, values):
        size = values.shape[0]
        column = (folds + at // width) * width
        in_out[at % width : at % width + size, column : column + width] = values

    ordered(first_mine, first_other, put_out, put_z)

    def put_left(at, values):
        left[at : at + values.shape[0], :] = values

    def put_right(at, values):
        right[at : at + values.shape[0], :] = values

    ordered(second_mine, second_other, put_left, put_right)
    for i, half in enumerate((left, right)):
        lanes = slice(i * width, (i + 1) * width)
        in_out[:, lanes] = half[0:width, :]
        for d in range(2):
            at = width + d * count
            xproj[d, :, lanes] = half[at : at + cols, :]
            at += cols
            dt_w[d, :, lanes] = half[at : at + rank, :]
            at += rank
            a_log[d, :, lanes] = half[at : at + state, :]
            dt_b[d : d + 1, lanes] = half[at + state : at + state + 1, :]
            skip[d : d + 1, lanes] = half[at + state + 1 : at + state + 2, :]
            at += state + 2
            conv_w[d, :, lanes] = half[at : at + taps, :]
            conv_b[d : d + 1, lanes] = half[at + taps : at + taps + 1, :]
    gain[...] = left[width + 2 * count : width + 2 * count + 1, :]


IN_VMEM = pl.BlockSpec(memory_space=pltpu.VMEM)
IN_SMEM = pl.BlockSpec(memory_space=pltpu.SMEM)
FAR = pl.BlockSpec(memory_space=pl.ANY)


def shape(*dims, dtype=F32):
    return jax.ShapeDtypeStruct(dims, dtype)


def scratch(*dims, dtype=F32):
    return pltpu.VMEM(dims, dtype)


def moves(*dims):
    return pltpu.SemaphoreType.DMA(dims)


def call(kernel, name, scalars, args, outs, scratches=(), far=(), far_outs=(), us=4):
    return pl.pallas_call(
        kernel,
        out_shape=list(outs) + list(far_outs),
        in_specs=[IN_SMEM] * len(scalars) + [IN_VMEM] * len(args) + [FAR] * len(far),
        out_specs=[IN_VMEM] * len(outs) + [FAR] * len(far_outs),
        scratch_shapes=list(scratches),
        compiler_params=pltpu.CompilerParams(vmem_limit_bytes=56 * 2**20),
        cost_estimate=pl.CostEstimate(flops=us * 500000000, bytes_accessed=0, transcendentals=0),
        name=name,
    )(*scalars, *args, *far)


def partner(axis, bit):
    return [(i, i ^ (1 << bit)) for i in range(lax.axis_size(axis))]


def bits_of(axis):
    return (lax.axis_size(axis) - 1).bit_length()


def other_core(values):
    return lax.ppermute(values, "seq", partner("seq", 0))


def next_chip(values):
    count = lax.axis_size("seq")
    pairs = [(i, i + 1) for i in range(1, count - 1, 2)]
    return lax.ppermute(values, "seq", pairs + [(j, i) for i, j in pairs])


def core_sum(first, second):
    even = (lax.axis_index("seq") & 1) == 0
    sent = jnp.where(even, second, first).astype(BF16)
    return jnp.where(even, first, second) + other_core(sent).astype(F32)


def plane_pairs(k):
    return [(i, i ^ k) for i in range(lax.axis_size("img"))]


def plane_sum(values):
    count = lax.axis_size("img")
    here = lax.axis_index("img")
    blocks = values.reshape(count, values.shape[0] // count, values.shape[1])

    def block(k):
        return lax.dynamic_index_in_dim(blocks, here ^ k, 0, keepdims=False)

    total = block(0)
    for k in range(1, count):
        total = total + lax.ppermute(block(k).astype(BF16), "img", plane_pairs(k)).astype(F32)
    return total


def line_step(values, bit):
    return values + lax.ppermute(values.astype(BF16), "seq", partner("seq", bit)).astype(F32)


def plane_gather(low):
    count = lax.axis_size("img")
    return jnp.stack(
        [low] + [lax.ppermute(low, "img", plane_pairs(k)) for k in range(1, count)], axis=0
    )


def tied(first, second):
    return lax.optimization_barrier((first, second))


def body(
    tokens, cotangent, heights, widths, valid, norm_gain, in_weight, conv_weight, conv_bias,
    xproj_weight, dt_weight, dt_bias, a_log, skip, out_weight,
):
    rows, width = tokens.shape[1:]
    inner = out_weight.shape[0]
    state = a_log.shape[1]
    rank = dt_weight.shape[1]
    cols = xproj_weight.shape[2]
    taps = conv_weight.shape[1]
    reach = taps - 1
    steps = rows // CHUNKS
    tiles = inner // LANES
    folds = inner // width
    position = lax.axis_index("seq")
    slots = rows * lax.axis_size("seq")
    count = bits_of("seq")
    place = jnp.stack([position * rows, position & 1]).astype(jnp.int32)
    flags = ((position >> jnp.arange(count)) & 1).astype(jnp.int32)
    tokens, cotangent = tokens[0], cotangent[0]
    gain = norm_gain.reshape(1, width)
    where_here = (place, heights, widths)
    edge = 2 * CHUNKS
    half = 2 * state

    xproj = xproj_weight.transpose(0, 2, 1)
    normed, live, cotan, to_core, to_chip = call(
        norm_kernel, "norm", where_here, (tokens, cotangent, valid, gain),
        [
            shape(2 * rows, width, dtype=BF16), shape(rows, LANES), shape(rows, width, dtype=BF16),
            shape(edge, width, dtype=BF16), shape(edge, width, dtype=BF16),
        ],
        us=2,
    )
    from_core, from_chip = other_core(to_core), next_chip(to_chip)
    x, zs, dgz, dy = call(
        front_kernel, "front", (), (normed, live, cotan, in_weight, out_weight),
        [shape(rows, inner) for _ in range(4)], us=3,
    )
    xext_rows = (steps + 2 * reach) * CHUNKS
    (
        proj, dtlow, same, nhalo, rate, before, tail, after, head, summary, sent, s, low, dsilu,
        delta, gate, xext,
    ) = call(
        functools.partial(middle_kernel, slots=slots, reach=reach), "middle", where_here,
        (
            from_core, from_chip, x, live, gain, in_weight, conv_weight, conv_bias, xproj, dt_weight,
            dt_bias, a_log,
        ),
        [
            shape(2 * rows, cols), shape(2 * rows, rank, dtype=BF16),
            shape(2 * reach * rows, LANES), shape(4 * CHUNKS, width, dtype=BF16),
            shape(half, inner), shape(2 * CHUNKS, inner), shape(half, CHUNKS, inner),
            shape(2 * CHUNKS, inner), shape(half, CHUNKS, inner), shape(2 * half + CHUNKS, inner),
            shape(2 * half + 2 * CHUNKS, inner, dtype=BF16),
        ],
        [
            scratch(rows, half * LANES), scratch(state, CHUNKS, inner),
            scratch(state, CHUNKS, inner), scratch(CHUNKS, inner), scratch(rows, inner),
            scratch(2 * rows, inner), scratch(2 * rows, inner, dtype=BF16), scratch(2 * rows, inner),
            scratch(2 * rows, inner), scratch(2 * rows, inner), scratch(xext_rows, inner), moves(9),
        ],
        (dy,),
        [
            shape(2 * rows, inner), shape(2 * rows, inner, dtype=BF16), shape(2 * rows, inner),
            shape(2 * rows, inner), shape(2 * rows, inner), shape(xext_rows, inner),
        ],
        us=16,
    )

    entered = None
    for bit in range(count - 1):
        got = lax.ppermute(sent, "seq", partner("seq", bit))
        final = bit == count - 2
        args = (got, summary) + (() if entered is None else (entered,)) + (rate,)
        summary, entered, sent = call(
            functools.partial(
                first_join if entered is None else join_kernel, state=state, bit=bit, final=final
            ),
            "join", (flags,), args,
            [
                shape(2 * half + CHUNKS, inner), shape(2 * half + CHUNKS, inner),
                shape(half if final else 2 * half + 2 * CHUNKS, inner, dtype=BF16),
            ],
            us=1,
        )
    got = lax.ppermute(sent, "seq", partner("seq", count - 1))

    held = (steps + 1) * state * CHUNKS
    dz, out_grad, z_grad, output, carry, h0, h1 = call(
        functools.partial(states_kernel, reach=reach, rank=rank, bit=count - 1), "states", (flags,),
        (
            got, entered, before, tail, rate, skip, proj, same, normed, cotan, tokens, out_weight,
        ),
        [
            shape(rows, inner, dtype=BF16), shape(inner, width), shape(inner, width),
            shape(rows, width, dtype=BF16), shape(2 * half, inner),
        ],
        [
            scratch(rows, half * LANES), scratch(rows, half * LANES), scratch(rows, inner),
            scratch(rows, inner, dtype=BF16), scratch(2 * rows, inner), scratch(2 * rows, inner),
            scratch(rows, inner), scratch(rows, inner), scratch(tiles, held, LANES),
            scratch(tiles, held, LANES), moves(2, tiles), moves(2, tiles), moves(2),
        ],
        (delta, s, zs, dgz), [shape(tiles, held, LANES), shape(tiles, held, LANES)],
        us=12,
    )
    first_sum = core_sum(out_grad, z_grad)

    small = -(-(cols + rank + state + 2 + taps + 1) // CHUNKS) * CHUNKS

    def adjoint(d, h, dx):
        args = (
            after, head, carry, rate, skip, proj, same, dtlow, dt_weight, xproj, conv_weight,
        )
        far = (delta, s, gate, dy, h, low, dsilu, xext) + (() if dx is None else (dx,))
        return call(
            functools.partial(
                first_adjoint if dx is None else adjoint_kernel, d=d, reach=reach, rank=rank
            ),
            ("adjoint_up", "adjoint_down")[d], (), args,
            [shape(rows, inner), shape(CHUNKS, inner), shape(small, inner)],
            [
                scratch(rows, half * LANES), scratch(rows, half * LANES), scratch(rows, inner),
                scratch(rows, inner), scratch(small - cols - rank, inner),
                scratch(rows + reach * CHUNKS, inner), scratch(rows, inner), scratch(rows, inner),
                scratch(rows, inner), scratch(rows, inner), scratch(tiles, held, LANES),
                scratch(rows, inner, dtype=BF16), scratch(rows, inner), scratch(xext_rows, inner),
                moves(5, tiles), moves(4),
            ],
            far, us=14,
        )

    dx, rim0, small0 = adjoint(0, h0, None)
    first_sum, dx = tied(first_sum, dx)
    first_sum = plane_sum(first_sum)
    dx, rim1, small1 = adjoint(1, h1, dx)
    first_sum, dx = tied(first_sum, dx)
    first_sum = line_step(first_sum, 1)
    fold = -(-(width + 2 * small + CHUNKS) // 64) * 64
    grads, dn, rim_core, rim_chip = call(
        last_kernel, "last", (place,),
        (dx, rim0, rim1, small0, small1, normed, nhalo, live, dz, in_weight, tokens),
        [
            shape(folds * fold, width), shape(rows, width), shape(CHUNKS, width), shape(CHUNKS, width),
        ],
        [scratch(rows + edge, inner, dtype=BF16)],
        us=4,
    )
    first_sum, grads = tied(first_sum, grads)
    second_sum = core_sum(grads[:fold], grads[fold:])
    second_sum = plane_sum(second_sum)
    for bit in range(2, count):
        first_sum = line_step(first_sum, bit)
    for bit in range(1, count):
        second_sum = line_step(second_sum, bit)
    first_mine = plane_gather(first_sum.astype(BF16))
    first_other = other_core(first_mine)
    second_mine = plane_gather(second_sum.astype(BF16))
    second_other = other_core(second_mine)

    input_grad = call(
        finish_kernel, "finish", where_here,
        (other_core(rim_core), next_chip(rim_chip), dn, tokens, cotangent, valid, gain),
        [shape(rows, width)], us=1,
    )[0]
    in_total, conv_total, bias_total, xproj_total, dtw_total, dtb_total, a_total, skip_total, out_total, gain_total = call(
        functools.partial(
            unpack_kernel, count=small, state=state, rank=rank, cols=cols, taps=taps
        ),
        "unpack", (place[1:], lax.axis_index("img").astype(jnp.int32).reshape(1)),
        (first_mine, first_other, second_mine, second_other),
        [
            shape(width, 2 * inner), shape(2, taps, inner), shape(2, inner), shape(2, cols, inner),
            shape(2, rank, inner), shape(2, inner), shape(2, state, inner), shape(2, inner),
            shape(inner, width), shape(1, width),
        ],
        [scratch(fold, width), scratch(fold, width)],
        us=2,
    )
    return (
        output[None], input_grad[None], gain_total.reshape(width), in_total, conv_total, bias_total,
        xproj_total.transpose(0, 2, 1), dtw_total, dtb_total, a_total, skip_total, out_total,
    )


def solution(mesh):
    split = P("img", "seq", None)
    placed = (split, split, P("img", None), P("img", None), P("img", "seq")) + (P(),) * 10
    return jax.shard_map(
        body,
        mesh=mesh,
        in_specs=placed,
        out_specs=(split, split) + (P(),) * 10,
        check_vma=False,
    )
```

```python
import functools

import jax
import jax.numpy as jnp
from jax import lax
from jax.experimental import pallas as pl
from jax.experimental.pallas import tpu as pltpu
from jax.sharding import PartitionSpec as P

NORM_EPS = 1e-05
CONTRACT_ROWS = (((0,), (0,)), ((), ()))
CONTRACT_COLS = (((1,), (1,)), ((), ()))
LOG2E = 1.4426950408889634
LN2 = 0.6931471805599453
BREAK = 1e30
CHUNKS = 8
LANES = 128
SUMMARY_STATES = 8
SUMMARY_UNROLL = 4
STATES_UNROLL = 4
ADJOINT_STATES = 8
ADJOINT_UNROLL = 4
F32 = jnp.float32
BF16 = jnp.bfloat16


def dot(a, b):
    return jnp.dot(a, b, preferred_element_type=F32)


def dot_rows(a, b):
    return lax.dot_general(a, b, CONTRACT_ROWS, preferred_element_type=F32)


def dot_cols(a, b):
    return lax.dot_general(a, b, CONTRACT_COLS, preferred_element_type=F32)


def sigmoid(v):
    return 1.0 / (1.0 + jnp.exp(-v))


def fetch(source, target, semaphore):
    copy = pltpu.make_async_copy(source, target, semaphore)
    copy.start()
    return copy


def tile_copy(source, target, semaphores, tile):
    index = (slice(None),) * (len(target.shape) - 1) + (lanes_of(tile),)
    return pltpu.make_async_copy(source.at[index], target.at[index], semaphores.at[tile])


def lanes_of(tile):
    return pl.ds(pl.multiple_of(tile * LANES, LANES), LANES)


def rows_of(j, count=CHUNKS):
    return pl.ds(pl.multiple_of(j * CHUNKS, CHUNKS), count)


def chunk_order(rows):
    row = lax.broadcasted_iota(jnp.int32, (rows, rows), 0)
    slot = lax.broadcasted_iota(jnp.int32, (rows, rows), 1)
    return slot == (row & (CHUNKS - 1)) * (rows // CHUNKS) + (row >> 3)


def image_ends(heights, widths):
    ends, total = [], 0
    for i in range(heights.shape[1]):
        total = total + heights[0, i] * widths[0, i]
        ends.append(total)
    return ends


def segment_of(places, ends):
    found = jnp.zeros_like(places)
    for end in ends:
        found = found + (places >= end).astype(jnp.int32)
    return found


def places_of(first, rows):
    row = lax.broadcasted_iota(jnp.int32, (rows, LANES), 0)
    return first + (row & (CHUNKS - 1)) * (rows // CHUNKS) + (row >> 3)


def edges_kernel(io, tokens, valid, to_core, to_chip):
    rows = tokens.shape[0]
    edge = to_core.shape[0]
    io.ready()
    row = lax.broadcasted_iota(jnp.int32, (edge, rows), 0)
    slot = lax.broadcasted_iota(jnp.int32, (edge, rows), 1)
    held = jnp.broadcast_to(valid[...].astype(F32), (edge, rows))
    first = jnp.where(slot == row, held, 0.0).astype(BF16)
    last = jnp.where(slot == rows - edge + row, held, 0.0).astype(BF16)
    first = dot(first, tokens[...]).astype(BF16)
    last = dot(last, tokens[...]).astype(BF16)
    even = (lax.axis_index("seq") & 1) == 0
    to_core[...] = jnp.where(even, last, first)
    to_chip[...] = jnp.where(even, first, last)


def spread(values, target):
    count = values.shape[1]
    high = values.astype(BF16)
    low = (values - high.astype(F32)).astype(BF16)
    both = jnp.concatenate([high, low], axis=1)
    wide = 2 * LANES
    column = lax.broadcasted_iota(jnp.int32, (2 * count, wide), 0)
    block = lax.broadcasted_iota(jnp.int32, (2 * count, wide), 1) // LANES
    for at in range(0, count * LANES, wide):
        place = block + at // LANES
        pick = ((column == place) | (column == place + count)).astype(BF16)
        target[:, at : at + wide] = dot(both, pick)


def windows(span, up, sublane):
    sign = 1 if up else -1

    def from_before(value, by, fill):
        moved = pltpu.roll(value, (sign * by) % CHUNKS, axis=0)
        kept = sublane >= by if up else sublane < CHUNKS - by
        return jnp.where(kept, moved, fill)

    two = span + from_before(span, 1, 0.0)
    four = two + from_before(two, 2, 0.0)
    eight = four + from_before(four, 4, 0.0)
    edge = [jnp.where(sublane >= by if up else sublane < CHUNKS - by, 0.0, BREAK) for by in (1, 2, 4)]
    return (span + edge[0], two + edge[1], four + edge[2]), from_before(eight, 1, 0.0)


def chain(rate, sums, tail, up, sublane):
    sign = 1 if up else -1
    for by, span in zip((1, 2, 4), sums):
        tail = jnp.exp2(rate * span) * pltpu.roll(tail, (sign * by) % CHUNKS, axis=0) + tail
    end = CHUNKS - 1 if up else 0
    kept = sublane >= 1 if up else sublane < CHUNKS - 1
    return jnp.where(kept, pltpu.roll(tail, sign % CHUNKS, axis=0), 0.0), tail[end : end + 1]


def middle_kernel(
    io, from_core, from_chip, heights, widths, valid, gain, conv_weight, conv_bias, xproj, dt_weight,
    dt_bias, a_log,
    tokens_far, cotangent_far, in_far, out_far,
    sum_out, sent_out, proj_out, nhalo_out, rate_out, before_out, after_out,
    normed_far, cotan_far, live_far, masks_far, zs_far, dgz_far, dy_far, s_far, dsilu_far,
    delta_far, gate_far, xext_far, tail_far, head_far,
    tokens, cotangent, in_weight, out_weight, normed, cotan, live, masks, zs_out, dgz_out, dy, s_out,
    dsilu_out, delta_out, gate_out, xext_out, tail_out, head_out,
    same_out, low_out, bc, tails, heads, spans, ins, outs,
    *, reach,
):
    rows, width = tokens.shape
    inner = out_weight.shape[0]
    steps = rows // CHUNKS
    state = a_log.shape[1]
    rank = dt_weight.shape[1]
    tiles = inner // LANES
    arriving = [
        fetch(source, target, ins.at[i])
        for i, (source, target) in enumerate(
            (
                (tokens_far, tokens), (in_far, in_weight), (cotangent_far, cotangent),
                (out_far, out_weight),
            )
        )
    ]
    io.ready()
    leaving = []

    def leave(source, target):
        leaving.append(fetch(source, target, outs.at[len(leaving)]))

    start = lax.axis_index("seq") * rows
    slots = lax.axis_size("seq") * rows
    even = (lax.axis_index("seq") & 1) == 0
    ends = image_ends(heights, widths)
    images = heights.shape[1]
    sublane = lax.broadcasted_iota(jnp.int32, (CHUNKS, LANES), 0)

    order = chunk_order(rows)
    order_low = order.astype(BF16)
    picked = jnp.where(order, jnp.broadcast_to(valid[...].astype(F32), order.shape), 0.0)
    alive = dot(picked.astype(BF16), jnp.ones((rows, LANES), BF16))
    places = places_of(start, rows)
    segment = segment_of(places, ends)
    live[...] = jnp.where(segment < images, alive, 0.0)
    leave(live, live_far)
    column = lax.broadcasted_iota(jnp.int32, (rows, LANES), 1)
    compact = jnp.zeros((rows, LANES), F32)
    for k in range(1, reach + 1):
        same = (segment_of(places - k, ends) == segment) & (places >= k)
        same = same.astype(F32)
        same_out[(k - 1) * rows : k * rows, :] = same
        compact = jnp.where(column == k - 1, same, compact)
        same = (segment_of(places + k, ends) == segment) & (places + k < slots)
        same = same.astype(F32)
        same_out[(reach + k - 1) * rows : (reach + k) * rows, :] = same
        compact = jnp.where(column == reach + k - 1, same, compact)
    masks[...] = compact
    leave(masks, masks_far)

    arriving[0].wait()
    inputs = dot(order_low, tokens[...])
    inv_rms = lax.rsqrt(jnp.mean(inputs * inputs, axis=-1, keepdims=True) + NORM_EPS)
    gains = gain[...].astype(F32).reshape(1, width)
    scaled = inputs * inv_rms * gains
    normed[0:rows, :] = scaled.astype(BF16)
    live_wide = jnp.concatenate([live[...]] * (width // LANES), axis=1)
    normed[rows : 2 * rows, :] = (scaled * live_wide).astype(BF16)
    leave(normed.at[0:rows, :], normed_far)
    before = jnp.where(even, from_chip[...], from_core[...])
    after = jnp.where(even, from_core[...], from_chip[...])
    htok = jnp.concatenate([before[CHUNKS:], after[:CHUNKS]], axis=0)
    hrow = lax.broadcasted_iota(jnp.int32, (2 * CHUNKS, LANES), 0)
    hplace = jnp.where(hrow < CHUNKS, start - CHUNKS + hrow, start + rows + hrow - CHUNKS)
    hlive = (segment_of(hplace, ends) < images).astype(F32)
    htok = htok.astype(F32) * jnp.concatenate([hlive] * (width // LANES), axis=1)
    hinv = lax.rsqrt(jnp.mean(htok * htok, axis=-1, keepdims=True) + NORM_EPS)
    scaled = htok * hinv
    nhalo = (scaled * gains).astype(BF16)
    nhalo_out[...] = jnp.concatenate([nhalo, scaled.astype(BF16)], axis=0)
    arriving[1].wait()
    step = 2 * LANES
    both = jnp.concatenate([normed[rows : 2 * rows, :], nhalo], axis=0)
    wide = lax.broadcasted_iota(jnp.int32, (CHUNKS, step), 0)
    for at in range(0, inner, step):
        lanes = slice(at, at + step)
        x = dot(both, in_weight[:, lanes]).astype(BF16).astype(F32)
        xext_out[reach * CHUNKS : (reach + steps) * CHUNKS, lanes] = x[:rows]
        for i in range(reach):
            to = steps - reach + i
            moved = pltpu.roll(x[to * CHUNKS : (to + 1) * CHUNKS, :], 1, axis=0)
            of = rows + CHUNKS - reach + i
            xext_out[i * CHUNKS : (i + 1) * CHUNKS, lanes] = jnp.where(
                wide == 0, x[of : of + 1], moved
            )
            moved = pltpu.roll(x[i * CHUNKS : (i + 1) * CHUNKS, :], CHUNKS - 1, axis=0)
            to = reach + steps + i
            of = rows + CHUNKS + i
            xext_out[to * CHUNKS : (to + 1) * CHUNKS, lanes] = jnp.where(
                wide == CHUNKS - 1, x[of : of + 1], moved
            )
    leave(xext_out, xext_far)

    arriving[2].wait()
    arriving[3].wait()
    cotan[...] = dot(order_low, cotangent[...]).astype(BF16)
    leave(cotan, cotan_far)
    block = 32
    for at in range(0, inner, step):
        lanes = slice(at, at + step)
        zs_out[:, lanes] = dot(normed[0:rows, :], in_weight[:, inner + at : inner + at + step])
        dgz_out[:, lanes] = dot_cols(cotan[...], out_weight[lanes, :])

    def gate_block(b, _):
        here = pl.ds(pl.multiple_of(b * block, block), block)
        alive = live[here, :]
        for tile in range(tiles):
            lanes = slice(tile * LANES, (tile + 1) * LANES)
            z = zs_out[here, lanes]
            grad = dgz_out[here, lanes] * alive
            gate = sigmoid(z)
            zs = z * gate * alive
            zs_out[here, lanes] = zs
            dy[here, lanes] = 0.5 * grad * zs
            dgz_out[here, lanes] = grad * (gate * (1.0 + z * (1.0 - gate)))
        return 0

    lax.fori_loop(0, rows // block, gate_block, 0)
    leave(zs_out, zs_far)
    leave(dgz_out, dgz_far)
    leave(dy, dy_far)

    taps = reach + 1
    conv_w = [conv_weight[d].astype(F32) for d in range(2)]
    conv_b = conv_bias[...].astype(F32)
    for tile in range(tiles):
        lanes = slice(tile * LANES, (tile + 1) * LANES)

        def conv_block(b, _, lanes=lanes):
            at = pl.multiple_of(b * block, block)
            for d in range(2):
                total = conv_b[d : d + 1, lanes] + conv_w[d][reach:taps, lanes] * (
                    xext_out[pl.ds(at + reach * CHUNKS, block), lanes]
                )
                for k in range(1, taps):
                    move = reach - k if d == 0 else reach + k
                    mask = same_out[pl.ds((d * reach + k - 1) * rows + at, block), :]
                    total = total + conv_w[d][reach - k : taps - k, lanes] * (
                        xext_out[pl.ds(at + move * CHUNKS, block), lanes] * mask
                    )
                gate = sigmoid(total)
                value = total * gate
                s_out[pl.ds(d * rows + at, block), lanes] = value
                low_out[pl.ds(d * rows + at, block), lanes] = value.astype(BF16)
                dsilu_out[pl.ds(d * rows + at, block), lanes] = gate * (1.0 + total * (1.0 - gate))
            return 0

        lax.fori_loop(0, rows // block, conv_block, 0)
    leave(s_out, s_far)
    leave(dsilu_out, dsilu_far)

    dt_b = dt_bias[...].astype(F32)
    for d in range(2):
        rate_out[d * state : (d + 1) * state, :] = jnp.minimum(
            -LOG2E * jnp.exp(a_log[d].astype(F32)), -1e-20
        )
        here = slice(d * rows, (d + 1) * rows)
        proj = dot_cols(low_out[here, :], xproj[d])
        proj_out[here, :] = proj
        dt_low = proj[:, :rank].astype(BF16)
        for at in range(0, inner, step):
            lanes = slice(at, at + step)
            delta_out[here, lanes] = dot(dt_low, dt_weight[d, :, lanes])
        spread(proj[:, rank:], bc)

        def delta_block(b, _, d=d):
            alive = live[pl.ds(pl.multiple_of(b * block, block), block), :]
            here = pl.ds(pl.multiple_of(d * rows + b * block, block), block)
            for tile in range(tiles):
                lanes = slice(tile * LANES, (tile + 1) * LANES)
                pre = delta_out[here, lanes] + dt_b[d : d + 1, lanes]
                small = jnp.exp(-jnp.abs(pre))
                log1p = jnp.where(small < 1e-4, small * (1.0 - 0.5 * small), jnp.log(1.0 + small))
                delta_out[here, lanes] = (jnp.maximum(pre, 0.0) + log1p) * alive
                gate_out[here, lanes] = jnp.where(pre >= 0.0, 1.0, small) / (1.0 + small) * alive
            return 0

        lax.fori_loop(0, rows // block, delta_block, 0)
        leave(delta_out.at[here, :], delta_far.at[here, :])
        leave(gate_out.at[here, :], gate_far.at[here, :])
        some = SUMMARY_STATES

        def scan_tile(tile, _, d=d):
            lanes = lanes_of(tile)
            for low in range(0, state, some):
                rates = [
                    jnp.broadcast_to(
                        rate_out[d * state + low + m : d * state + low + m + 1, lanes],
                        (CHUNKS, LANES),
                    )
                    for m in range(some)
                ]

                def scan_step(i, carried, d=d, low=low, rates=rates):
                    tail, lead, head, span = carried
                    j = i if d == 0 else steps - 1 - i
                    at = pl.multiple_of(j * CHUNKS, CHUNKS)
                    keep = same_out[pl.ds(d * reach * rows + at, CHUNKS), :]
                    delta = delta_out[pl.ds(d * rows + at, CHUNKS), lanes]
                    drive = delta * s_out[pl.ds(d * rows + at, CHUNKS), lanes]
                    back = dy[pl.ds(at, CHUNKS), lanes]
                    delta = jnp.where(keep > 0.0, delta, BREAK)
                    tail, lead, head = list(tail), list(lead), list(head)
                    for m in range(some):
                        b = bc[pl.ds(at, CHUNKS), (low + m) * LANES : (low + m + 1) * LANES]
                        n = state + low + m
                        c = bc[pl.ds(at, CHUNKS), n * LANES : (n + 1) * LANES]
                        decay = jnp.exp2(delta * rates[m])
                        tail[m] = decay * tail[m] + b * drive
                        lead[m] = lead[m] * decay
                        head[m] = head[m] + lead[m] * (c * back)
                    return tuple(tail), tuple(lead), tuple(head), span + delta

                zeros = tuple(jnp.zeros((CHUNKS, LANES), F32) for _ in range(some))
                ones = tuple(jnp.ones((CHUNKS, LANES), F32) for _ in range(some))
                tail, lead, head, span = lax.fori_loop(
                    0, steps, scan_step, (zeros, ones, zeros, zeros[0]), unroll=SUMMARY_UNROLL
                )
                for m in range(some):
                    tails[low + m, :, lanes] = tail[m]
                    heads[low + m, :, lanes] = head[m]
                spans[:, lanes] = span
            return 0

        lax.fori_loop(0, tiles, scan_tile, 0)

        tail_row = 0 if d == 0 else 2 * state
        head_row = 3 * state if d == 0 else state

        def chain_tile(tile, _, d=d, tail_row=tail_row, head_row=head_row):
            lanes = lanes_of(tile)
            span = spans[:, lanes]
            sums, before = windows(span, d == 0, sublane)
            sums_back, after = windows(span, d == 1, sublane)
            before_out[d * CHUNKS : (d + 1) * CHUNKS, lanes] = before
            after_out[d * CHUNKS : (d + 1) * CHUNKS, lanes] = after
            for n in range(state):
                rate = jnp.broadcast_to(
                    rate_out[d * state + n : d * state + n + 1, lanes], (CHUNKS, LANES)
                )
                carried, total = chain(rate, sums, tails[n, :, lanes], d == 0, sublane)
                tail_out[d * state + n, :, lanes] = carried
                sum_out[tail_row + n : tail_row + n + 1, lanes] = total
                carried, total = chain(rate, sums_back, heads[n, :, lanes], d == 1, sublane)
                head_out[d * state + n, :, lanes] = carried
                sum_out[head_row + n : head_row + n + 1, lanes] = total
            return 0

        lax.fori_loop(0, tiles, chain_tile, 0)
        mine = slice(d * state, (d + 1) * state)
        leave(tail_out.at[mine], tail_far.at[mine])
        leave(head_out.at[mine], head_far.at[mine])
        sum_out[4 * state + d : 4 * state + d + 1, :] = jnp.sum(spans[...], axis=0, keepdims=True)
    at = 4 * state + CHUNKS
    sum_out[4 * state + 2 : at, :] = jnp.zeros((CHUNKS - 2, inner), F32)
    sum_out[at:, :] = rate_out[...]
    sent_out[...] = packed(sum_out[0:at, :], state)
    io.done()
    for copy in leaving:
        copy.wait()


def packed(summary, state):
    rest = summary[4 * state :]
    high = rest.astype(BF16)
    low = (rest - high.astype(F32)).astype(BF16)
    return jnp.concatenate([summary[: 4 * state].astype(BF16), high, low], axis=0)


def leads(rate, spans, state, flip):
    parts = [jnp.exp2(rate[d * state : (d + 1) * state] * spans[d : d + 1]) for d in range(2)]
    return jnp.concatenate(parts[::-1] if flip else parts, axis=0)


def join_kernel(io, got, summary, entered, *outs, state, bit, final):
    half = 2 * state
    upper = ((lax.axis_index("seq") >> bit) & 1) == 1
    mine = summary[0 : 2 * half + CHUNKS, :]
    rates = summary[2 * half + CHUNKS :, :]
    entered_out, sent_out = outs[-2], outs[-1]
    values = got[...].astype(F32)
    spans = mine[4 * state : 4 * state + 2]
    other = values[4 * state : 4 * state + 2] + values[4 * state + CHUNKS : 4 * state + CHUNKS + 2]
    if entered is None:
        entered_up = jnp.where(upper, values[:half], 0.0)
        entered_down = jnp.where(upper, 0.0, values[half : 2 * half])
        span_up = jnp.where(upper, other, 0.0)
        span_down = jnp.where(upper, 0.0, other)
    else:
        held = entered[...]
        span_up, span_down = held[2 * half : 2 * half + 2], held[2 * half + 2 : 2 * half + 4]
        entered_up = held[:half] + jnp.where(
            upper, leads(rates, span_up, state, False) * values[:half], 0.0
        )
        entered_down = held[half : 2 * half] + jnp.where(
            upper, 0.0, leads(rates, span_down, state, True) * values[half : 2 * half]
        )
        span_up = span_up + jnp.where(upper, other, 0.0)
        span_down = span_down + jnp.where(upper, 0.0, other)
    entered_out[0:half, :] = entered_up
    entered_out[half : 2 * half, :] = entered_down
    entered_out[2 * half :, :] = jnp.concatenate(
        [span_up, span_down, jnp.zeros((CHUNKS - 4, mine.shape[1]), F32)], axis=0
    )
    low_up = jnp.where(upper, values[:half], mine[:half])
    high_up = jnp.where(upper, mine[:half], values[:half])
    low_down = jnp.where(upper, values[half : 2 * half], mine[half : 2 * half])
    high_down = jnp.where(upper, mine[half : 2 * half], values[half : 2 * half])
    low_span, high_span = jnp.where(upper, other, spans), jnp.where(upper, spans, other)
    up = leads(rates, high_span, state, False) * low_up + high_up
    down = leads(rates, low_span, state, True) * high_down + low_down
    if final:
        next_upper = ((lax.axis_index("seq") >> (bit + 1)) & 1) == 1
        sent_out[...] = jnp.where(next_upper, down, up).astype(BF16)
    else:
        total = jnp.concatenate(
            [up, down, spans + other, jnp.zeros((CHUNKS - 2, mine.shape[1]), F32)], axis=0
        )
        outs[0][0 : 2 * half + CHUNKS, :] = total
        outs[0][2 * half + CHUNKS :, :] = rates
        sent_out[...] = packed(total, state)


def first_join(io, got, summary, *outs, state, bit, final):
    join_kernel(io, got, summary, None, *outs, state=state, bit=bit, final=final)


def state_block(j, state):
    return pl.multiple_of(j * state * CHUNKS, CHUNKS)


def states_pass(d, steps, state, rates, begin, delta, s, keep, bc, y):
    def step(i, h):
        j = i if d == 0 else steps - 1 - i
        here = pl.ds(pl.multiple_of(j * CHUNKS, CHUNKS), CHUNKS)
        size = delta[here, :]
        drive = size * s[here, :]
        size = jnp.where(keep[here, :] > 0.0, size, BREAK)
        h = list(h)
        total = None if d == 0 else y[here, :]
        for n in range(state):
            b = bc[here, n * LANES : (n + 1) * LANES]
            c = bc[here, (state + n) * LANES : (state + n + 1) * LANES]
            h[n] = jnp.exp2(size * rates[n]) * h[n] + b * drive
            total = c * h[n] if total is None else total + c * h[n]
        y[here, :] = total
        return tuple(h)

    lax.fori_loop(0, steps, step, tuple(begin), unroll=STATES_UNROLL)


def held_pass(d, steps, state, rates, begin, delta, s, keep, bc, h_out, decay_out):
    start = state_block(0 if d == 0 else steps, state)
    for n in range(state):
        h_out[pl.ds(start + n * CHUNKS, CHUNKS), :] = begin[n]

    def step(i, h):
        j = i if d == 0 else steps - 1 - i
        here = pl.ds(pl.multiple_of(j * CHUNKS, CHUNKS), CHUNKS)
        to = state_block(j + 1 if d == 0 else j, state)
        at = state_block(j, state)
        size = delta[here, :]
        drive = size * s[here, :]
        size = jnp.where(keep[here, :] > 0.0, size, BREAK)
        h = list(h)
        for n in range(state):
            decay = jnp.exp2(size * rates[n])
            decay_out[pl.ds(at + n * CHUNKS, CHUNKS), :] = decay
            h[n] = decay * h[n] + bc[here, n * LANES : (n + 1) * LANES] * drive
            h_out[pl.ds(to + n * CHUNKS, CHUNKS), :] = h[n]
        return tuple(h)

    lax.fori_loop(0, steps, step, tuple(begin), unroll=STATES_UNROLL)


def adjoint_pass(
    d, steps, state, rates, back, delta, s, gate, dy, keep, skip, bc, h_in, decay_in, sums,
    dpre_out, ds_out, rows_out,
):
    some = ADJOINT_STATES
    edge = steps - 1
    skip = skip[...]
    zeros = jnp.zeros((CHUNKS, LANES), F32)
    grads = []
    for low in range(0, state, some):
        final = low + some == state

        def step(i, carried, low=low, final=final):
            g, acc, h, skip_acc, bias_acc = carried
            j = edge - i if d == 0 else i
            here = pl.ds(pl.multiple_of(j * CHUNKS, CHUNKS), CHUNKS)
            size = delta[here, :]
            value = s[here, :]
            grad = dy[here, :]
            drive = size * value
            masked = jnp.where(keep[here, :] > 0.0, size, BREAK)
            at = state_block(j, state)
            prev = at if d == 0 else state_block(j + 1, state)
            g, acc, h = list(g), list(acc), list(h)
            weighted = zeros if low == 0 else ds_out[here, :]
            rate_sum = zeros if low == 0 else dpre_out[here, :]
            for m in range(some):
                n = low + m
                b = bc[here, n * LANES : (n + 1) * LANES]
                c = bc[here, (state + n) * LANES : (state + n + 1) * LANES]
                adjoint = c * grad + g[m]
                before = h_in[pl.ds(prev + n * CHUNKS, CHUNKS), :]
                sums[here, n * LANES : (n + 1) * LANES] += adjoint * drive
                sums[here, (state + n) * LANES : (state + n + 1) * LANES] += grad * h[m]
                g[m] = adjoint * decay_in[pl.ds(at + n * CHUNKS, CHUNKS), :]
                held = g[m] * before
                weighted = weighted + adjoint * b
                rate_sum = rate_sum + held * rates[n]
                acc[m] = acc[m] + held * masked
                h[m] = before
            if final:
                ds_out[here, :] = skip * grad + size * weighted
                pre = ((LN2 * rate_sum + weighted * value) * gate[here, :]).astype(BF16).astype(F32)
                dpre_out[here, :] = pre
                bias_acc = bias_acc + pre
                skip_acc = skip_acc + grad * value
            else:
                dpre_out[here, :] = rate_sum
                ds_out[here, :] = weighted
            return tuple(g), tuple(acc), tuple(h), skip_acc, bias_acc

        last = state_block(steps if d == 0 else 0, state)
        h_last = tuple(h_in[pl.ds(last + (low + m) * CHUNKS, CHUNKS), :] for m in range(some))
        none = tuple(zeros for _ in range(some))
        _, acc, _, skip_acc, bias_acc = lax.fori_loop(
            0, steps, step, (tuple(back[low : low + some]), none, h_last, zeros, zeros),
            unroll=ADJOINT_UNROLL,
        )
        grads.extend(acc)
    for n in range(state):
        rows_out[n : n + 1, :] = jnp.sum(grads[n], axis=0, keepdims=True) * rates[n][0:1] * LN2
    rows_out[state : state + 1, :] = jnp.sum(bias_acc, axis=0, keepdims=True)
    rows_out[state + 1 : state + 2, :] = jnp.sum(skip_acc, axis=0, keepdims=True)


def lane_sums(sums, state):
    depth = 2 * state * LANES
    block = lax.broadcasted_iota(jnp.int32, (depth, LANES), 0) // LANES
    column = lax.broadcasted_iota(jnp.int32, (depth, LANES), 1)
    return dot(sums.astype(BF16), (block == column).astype(BF16))[:, : 2 * state]


def rate_tiles(rate, d, state, lanes):
    return [
        jnp.broadcast_to(rate[d * state + n : d * state + n + 1, lanes], (CHUNKS, LANES))
        for n in range(state)
    ]


def begin_tiles(rates, passed, maps, carry, at, base, d, state, lanes):
    passed = passed[d * CHUNKS : (d + 1) * CHUNKS, lanes]
    return [
        jnp.exp2(rates[n] * passed) * carry[at + n : at + n + 1, lanes] + maps[base + n, :, lanes]
        for n in range(state)
    ]


def slot_order(rows):
    row = lax.broadcasted_iota(jnp.int32, (rows, rows), 1)
    slot = lax.broadcasted_iota(jnp.int32, (rows, rows), 0)
    return (slot == (row & (CHUNKS - 1)) * (rows // CHUNKS) + (row >> 3)).astype(BF16)


def states_kernel(
    io, got, entered, before, rate, skip, proj, masks,
    delta_far, s_far, tail_far, zs_far, dgz_far, normed_far, cotan_far, tokens_far, out_far,
    kept, sent, carry_out, dz_far, output_far,
    bc0, bc1, keep, y, gated, dz, delta, s, tail, zs, dgz, normed, cotan, tokens, out_weight,
    output, tile_moves, ins, outs,
    *, reach, rank, bit,
):
    rows, inner = zs.shape
    width = tokens.shape[1]
    steps = rows // CHUNKS
    state = rate.shape[0] // 2
    half = 2 * state
    tiles = inner // LANES
    by_tiles = ((delta_far, delta), (s_far, s), (tail_far, tail))
    for tile in range(tiles):
        for i, (source, target) in enumerate(by_tiles):
            tile_copy(source, target, tile_moves.at[i], tile).start()
    later = [
        fetch(source, target, ins.at[i])
        for i, (source, target) in enumerate(
            (
                (zs_far, zs), (dgz_far, dgz), (normed_far, normed), (cotan_far, cotan),
                (tokens_far, tokens), (out_far, out_weight),
            )
        )
    ]
    io.ready()
    upper = ((lax.axis_index("seq") >> bit) & 1) == 1
    values = got[...].astype(F32)
    held = entered[...]
    rates = rate[...]
    carry_out[0:half, :] = held[:half] + jnp.where(
        upper, leads(rates, held[2 * half : 2 * half + 2], state, False) * values, 0.0
    )
    carry_out[half : 2 * half, :] = held[half : 2 * half] + jnp.where(
        upper, 0.0, leads(rates, held[2 * half + 2 : 2 * half + 4], state, True) * values
    )
    spread(proj[0:rows, rank:], bc0)
    spread(proj[rows : 2 * rows, rank:], bc1)
    spread(jnp.concatenate([masks[:, 0:1], masks[:, reach : reach + 1]], axis=1), keep)

    def scan_tile(tile, _):
        lanes = lanes_of(tile)
        for i, (source, target) in enumerate(by_tiles):
            tile_copy(source, target, tile_moves.at[i], tile).wait()
        for d, bc in enumerate((bc0, bc1)):
            rates = rate_tiles(rate, d, state, lanes)
            begin = begin_tiles(rates, before, tail, carry_out, d * half, d * state, d, state, lanes)
            mine = slice(d * rows, (d + 1) * rows)
            states_pass(
                d, steps, state, rates, begin, delta.at[mine, lanes], s.at[mine, lanes],
                keep.at[:, d * LANES : (d + 1) * LANES], bc, y.at[:, lanes],
            )
        return 0

    lax.fori_loop(0, tiles, scan_tile, 0)
    for copy in later:
        copy.wait()
    skips = skip[...].astype(F32)
    block = 32

    def gate_block(b, _):
        here = pl.ds(pl.multiple_of(b * block, block), block)
        there = pl.ds(pl.multiple_of(rows + b * block, block), block)
        for tile in range(tiles):
            lanes = slice(tile * LANES, (tile + 1) * LANES)
            total = 0.5 * (
                y[here, lanes] + skips[0:1, lanes] * s[here, lanes] + skips[1:2, lanes] * s[there, lanes]
            )
            gated[here, lanes] = (total * zs[here, lanes]).astype(BF16)
            dz[here, lanes] = (total * dgz[here, lanes]).astype(BF16)
        return 0

    lax.fori_loop(0, rows // block, gate_block, 0)
    leaving = [fetch(dz, dz_far, outs.at[0])]
    even = (lax.axis_index("seq") & 1) == 0
    out_grad = dot_rows(gated[...], cotan[...]).astype(BF16)
    z_grad = jnp.concatenate(
        [dot_rows(normed[...], dz[:, at : at + width]) for at in range(0, inner, width)], axis=0
    ).astype(BF16)
    sent[...] = jnp.where(even, z_grad, out_grad)
    kept[...] = jnp.where(even, out_grad, z_grad)
    ordered = dot(slot_order(rows), gated[...]).astype(BF16)
    output[...] = (tokens[...].astype(F32) + dot(ordered, out_weight[...])).astype(BF16)
    leaving.append(fetch(output, output_far, outs.at[1]))
    io.done()
    for copy in leaving:
        copy.wait()


def adjoint_kernel(
    io, before, after, carry, rate, skip, proj, masks, dt_weight, xproj, conv_weight,
    delta_far, s_far, gate_far, tail_far, head_far, dy_far, dsilu_far, xext_far, more,
    dc_rim, small_out,
    bc, same, sums, dpre, ds, rows_out, ext, dx_out, h, decays,
    delta, s, gate, tail, head, dy, dsilu, xext, tile_moves, ins,
    *, d, reach, rank, after_scan,
):
    rows, inner = dy.shape
    steps = rows // CHUNKS
    state = rate.shape[0] // 2
    half = 2 * state
    tiles = inner // LANES
    taps = reach + 1
    cols = proj.shape[1]
    mine = slice(d * rows, (d + 1) * rows)
    maps = slice(d * state, (d + 1) * state)
    by_tiles = (
        (delta_far.at[mine, :], delta), (s_far.at[mine, :], s), (tail_far.at[maps], tail),
        (head_far.at[maps], head), (dy_far, dy), (gate_far.at[mine, :], gate),
    )
    for tile in range(tiles):
        for i, (source, target) in enumerate(by_tiles):
            tile_copy(source, target, tile_moves.at[i], tile).start()
    later = [
        fetch(source, target, ins.at[i])
        for i, (source, target) in enumerate(
            ((dsilu_far.at[mine, :], dsilu), (xext_far, xext)) + tuple(more)
        )
    ]
    io.ready()
    spread(proj[mine, rank:], bc)
    spread(masks[:, 0 : 2 * reach], same)
    keep = same.at[:, d * reach * LANES : (d * reach + 1) * LANES]
    sums[...] = jnp.zeros_like(sums)
    skips = skip[...].astype(F32)[d : d + 1]
    rows_out[...] = jnp.zeros_like(rows_out)
    skip32 = ext.at[0:1, :]
    skip32[...] = skips
    state_at = 0 if d == 0 else half
    grad_at = (half if d == 0 else 0) + state

    def scan_tile(tile, _):
        lanes = lanes_of(tile)
        for i, (source, target) in enumerate(by_tiles):
            tile_copy(source, target, tile_moves.at[i], tile).wait()
        rates = rate_tiles(rate, d, state, lanes)
        begin = begin_tiles(rates, before, tail, carry, state_at, 0, d, state, lanes)
        held_pass(
            d, steps, state, rates, begin, delta.at[:, lanes], s.at[:, lanes], keep, bc, h, decays
        )
        back = begin_tiles(rates, after, head, carry, grad_at, 0, d, state, lanes)
        adjoint_pass(
            d, steps, state, rates, back, delta.at[:, lanes], s.at[:, lanes],
            gate.at[:, lanes], dy.at[:, lanes], keep, skip32.at[:, lanes], bc, h, decays, sums,
            dpre.at[:, lanes], ds.at[:, lanes], rows_out.at[:, lanes],
        )
        return 0

    lax.fori_loop(0, tiles, scan_tile, 0)
    dpre_low = dpre[...].astype(BF16)
    dt_grad = dot_rows(proj[mine, :rank].astype(BF16), dpre_low)
    dt_back = dot_cols(dpre_low, dt_weight[d])
    dproj = jnp.concatenate([dt_back, lane_sums(sums[...], state)], axis=1).astype(BF16)
    small_out[0:cols, :] = dot_rows(dproj, s[...].astype(BF16))
    small_out[cols : cols + rank, :] = dt_grad
    for copy in later:
        copy.wait()
    base = 0 if d == 0 else reach * CHUNKS
    step = 2 * LANES
    for lane in range(0, inner, step):
        lanes = slice(lane, lane + step)
        total = ds[:, lanes] + dot(dproj, xproj[d, :, lanes])
        ext[base : base + rows, lanes] = (total * dsilu[:, lanes]).astype(BF16).astype(F32)
    wide = lax.broadcasted_iota(jnp.int32, (CHUNKS, inner), 0)
    for i in range(reach):
        if d == 0:
            moved = pltpu.roll(ext[i * CHUNKS : (i + 1) * CHUNKS, :], CHUNKS - 1, axis=0)
            ext[rows + i * CHUNKS : rows + (i + 1) * CHUNKS, :] = jnp.where(
                wide == CHUNKS - 1, 0.0, moved
            )
        else:
            moved = pltpu.roll(ext[rows + i * CHUNKS : rows + (i + 1) * CHUNKS, :], 1, axis=0)
            ext[i * CHUNKS : (i + 1) * CHUNKS, :] = jnp.where(wide == 0, 0.0, moved)

    conv_w = conv_weight[d].astype(F32)
    block = 32
    zeros = jnp.zeros((CHUNKS, LANES), F32)

    def folded(values):
        return functools.reduce(
            lambda a, b: a + b, [values[i : i + CHUNKS] for i in range(0, block, CHUNKS)]
        )

    base_row = cols + rank
    for tile in range(tiles):
        lanes = slice(tile * LANES, (tile + 1) * LANES)
        weight = conv_w[:, lanes]

        def conv_block(b, totals, lanes=lanes, weight=weight):
            here = pl.multiple_of(b * block, block)
            totals = list(totals)
            mid = ext[pl.ds(here + base, block), lanes]
            total = weight[reach:taps] * mid
            totals[reach] = totals[reach] + folded(mid * xext[pl.ds(here + reach * CHUNKS, block), lanes])
            totals[taps] = totals[taps] + folded(mid)
            for k in range(1, taps):
                past = same[pl.ds(here, block), (k - 1) * LANES : k * LANES]
                ahead = same[pl.ds(here, block), (reach + k - 1) * LANES : (reach + k) * LANES]
                if d == 0:
                    given = ext[pl.ds(here + k * CHUNKS, block), lanes] * ahead
                    taken = xext[pl.ds(here + (reach - k) * CHUNKS, block), lanes] * past
                else:
                    given = ext[pl.ds(here + (reach - k) * CHUNKS, block), lanes] * past
                    taken = xext[pl.ds(here + (reach + k) * CHUNKS, block), lanes] * ahead
                total = total + weight[reach - k : taps - k] * given
                totals[reach - k] = totals[reach - k] + folded(mid * taken)
            if d == 1:
                total = total + dx_out[pl.ds(here, block), lanes]
            dx_out[pl.ds(here, block), lanes] = total
            return tuple(totals)

        totals = lax.fori_loop(0, rows // block, conv_block, (zeros,) * (taps + 1))
        for i in range(taps + 1):
            at = state + 2 + i
            rows_out[at : at + 1, lanes] = jnp.sum(totals[i], axis=0, keepdims=True)

    edge = []
    for i in range(CHUNKS):
        row = jnp.zeros((1, inner), F32)
        for k in range(1, taps):
            j = i - CHUNKS + k if d == 0 else steps + i - k
            if (d == 0 and j >= 0) or (d == 1 and j < steps):
                sub = 0 if d == 0 else CHUNKS - 1
                at = j * CHUNKS + sub
                column = (d * reach + k - 1) * LANES
                mask = jnp.concatenate([same[at : at + 1, column : column + LANES]] * tiles, axis=1)
                at = base + j * CHUNKS + sub
                row = row + conv_w[reach - k : taps - k] * ext[at : at + 1, :] * mask
        edge.append(row)
    dc_rim[...] = jnp.concatenate(edge, axis=0)
    small_out[base_row:, :] = rows_out[0 : small_out.shape[0] - base_row, :]
    after_scan()


def first_adjoint(io, *refs, **static):
    args, far, outs, rest = refs[:10], refs[10:18], refs[18:21], refs[21:]
    dc_rim, small_out, dx_far = outs
    dx_out = rest[7]
    moves = rest[-1]

    def hand_on():
        copy = fetch(dx_out, dx_far, moves.at[2])
        io.done()
        copy.wait()

    adjoint_kernel(
        io, *args, *far, (), dc_rim, small_out, *rest, after_scan=hand_on, **static
    )


def second_adjoint(io, *refs, count, **static):
    args, rim0, small0, nhalo = refs[:10], refs[10], refs[11], refs[12]
    far = refs[13:21]
    dx_far, normed_far, live_far, dz_far, in_far, tokens_far = refs[21:27]
    to_core, to_chip, kept, sent, dn_out = refs[27:32]
    rest = refs[32:52]
    normed, live, dz, in_weight, tokens, low, rim1, small1, grads = refs[52:]
    dx = rest[7]
    rows, width = tokens.shape
    more = (
        (dx_far, dx), (normed_far, normed), (live_far, live), (dz_far, dz), (in_far, in_weight),
        (tokens_far, tokens),
    )

    def input_grads():
        inner = dx.shape[1]
        folds = inner // width
        fold = grads.shape[0] // folds
        edges = 2 * CHUNKS
        for tile in range(inner // LANES):
            lanes = slice(tile * LANES, (tile + 1) * LANES)
            low[0:rows, lanes] = (dx[:, lanes] * live[...]).astype(BF16)
        low[rows : rows + edges, :] = jnp.concatenate([rim0[...], rim1[...]], axis=0).astype(BF16)
        both = jnp.concatenate([normed[0:rows, :], nhalo[0:edges, :]], axis=0)
        size = small0.shape[0]
        for i in range(folds):
            lanes = slice(i * width, (i + 1) * width)
            at = i * fold
            grads[at : at + width, :] = dot_rows(both, low[:, lanes])
            at += width
            grads[at : at + size, :] = small0[:, lanes]
            at += size
            grads[at : at + size, :] = small1[:, lanes]
            at += size
            grads[at : (i + 1) * fold, :] = jnp.zeros(((i + 1) * fold - at, width), F32)
        back = slot_order(rows)
        dn = dot_cols(dot(back, low[0:rows, :]).astype(BF16), in_weight[:, 0:inner]) + dot_cols(
            dot(back, dz[...]).astype(BF16), in_weight[:, inner : 2 * inner]
        )
        dn_out[...] = dn
        rim = dot_cols(low[rows : rows + edges, :], in_weight[:, 0:inner])
        even = (lax.axis_index("seq") & 1) == 0
        to_core[...] = jnp.where(even, rim[CHUNKS:], rim[:CHUNKS])
        to_chip[...] = jnp.where(even, rim[:CHUNKS], rim[CHUNKS:])
        inputs = tokens[...].astype(F32)
        inv_rms = lax.rsqrt(jnp.mean(inputs * inputs, axis=-1, keepdims=True) + NORM_EPS)
        at = width + 2 * size
        grads[at : at + 1, :] = jnp.sum(
            dn * (inputs * inv_rms), axis=0, keepdims=True
        ) + jnp.sum(rim * nhalo[edges : 2 * edges, :].astype(F32), axis=0, keepdims=True)
        left, right = grads[0:fold, :].astype(BF16), grads[fold : 2 * fold, :].astype(BF16)
        kept[...] = jnp.where(even, left, right)
        sent[...] = jnp.where(even, right, left)

    adjoint_kernel(io, *args, *far, more, rim1, small1, *rest, after_scan=input_grads, **static)


def finish_kernel(
    io, from_core, from_chip, heights, widths, dn, tokens, cotangent, valid, gain, input_grad
):
    rows, width = tokens.shape
    even = (lax.axis_index("seq") & 1) == 0
    start = lax.axis_index("seq") * rows
    io.ready()
    before = jnp.where(even, from_chip[...], from_core[...])
    after = jnp.where(even, from_core[...], from_chip[...])
    end = image_ends(heights, widths)[-1]
    row = lax.broadcasted_iota(jnp.int32, (CHUNKS, rows), 0)
    slot = lax.broadcasted_iota(jnp.int32, (CHUNKS, rows), 1)
    alive = jnp.broadcast_to(valid[...].astype(F32), (CHUNKS, rows))
    alive = jnp.where(start + slot < end, alive, 0.0)
    first = jnp.sum(jnp.where(slot == row, alive, 0.0), axis=1, keepdims=True)
    last = jnp.sum(jnp.where(slot == rows - CHUNKS + row, alive, 0.0), axis=1, keepdims=True)
    values = jnp.concatenate(
        [
            dn[0:CHUNKS, :] + first * before, dn[CHUNKS : rows - CHUNKS, :],
            dn[rows - CHUNKS : rows, :] + last * after,
        ],
        axis=0,
    )
    inputs = tokens[...].astype(F32)
    inv_rms = lax.rsqrt(jnp.mean(inputs * inputs, axis=-1, keepdims=True) + NORM_EPS)
    scaled = values * gain[...].astype(F32).reshape(1, width)
    mean = jnp.mean(scaled * inputs, axis=-1, keepdims=True)
    input_grad[...] = (
        cotangent[...].astype(F32) + inv_rms * scaled - inputs * (inv_rms * inv_rms * inv_rms) * mean
    )


def unpack_kernel(
    io, first_mine, first_other, second_mine, second_other,
    in_out, conv_w, conv_b, xproj, dt_w, dt_b, a_log, skip, out_w, gain,
    left, right,
    *, count, state, rank, cols, taps,
):
    blocks = first_mine.shape[0]
    width = out_w.shape[1]
    folds = out_w.shape[0] // width

    def ordered(mine, other, into_first, into_second):
        size = mine.shape[1]
        is_even = (lax.axis_index("seq") & 1) == 0
        plane = lax.axis_index("img")
        for k in range(blocks):
            source = plane ^ k
            a, b = mine[source].astype(F32), other[source].astype(F32)
            into_first(k * size, jnp.where(is_even, a, b))
            into_second(k * size, jnp.where(is_even, b, a))

    def put_out(at, values):
        out_w[at : at + values.shape[0], :] = values

    def put_z(at, values):
        size = values.shape[0]
        column = (folds + at // width) * width
        in_out[at % width : at % width + size, column : column + width] = values

    ordered(first_mine, first_other, put_out, put_z)

    def put_left(at, values):
        left[at : at + values.shape[0], :] = values

    def put_right(at, values):
        right[at : at + values.shape[0], :] = values

    ordered(second_mine, second_other, put_left, put_right)
    for i, half in enumerate((left, right)):
        lanes = slice(i * width, (i + 1) * width)
        in_out[:, lanes] = half[0:width, :]
        for d in range(2):
            at = width + d * count
            xproj[d, :, lanes] = half[at : at + cols, :]
            at += cols
            dt_w[d, :, lanes] = half[at : at + rank, :]
            at += rank
            a_log[d, :, lanes] = half[at : at + state, :]
            dt_b[d : d + 1, lanes] = half[at + state : at + state + 1, :]
            skip[d : d + 1, lanes] = half[at + state + 1 : at + state + 2, :]
            at += state + 2
            conv_w[d, :, lanes] = half[at : at + taps, :]
            conv_b[d : d + 1, lanes] = half[at + taps : at + taps + 1, :]
    gain[...] = left[width + 2 * count : width + 2 * count + 1, :].reshape(width)


IN_VMEM = pl.BlockSpec(memory_space=pltpu.VMEM)
IN_SMEM = pl.BlockSpec(memory_space=pltpu.SMEM)
FAR = pl.BlockSpec(memory_space=pltpu.HBM)


def shape(*dims, dtype=F32):
    return jax.ShapeDtypeStruct(dims, dtype)


def low(*dims):
    return jax.ShapeDtypeStruct(dims, BF16)


def near(*dims, dtype=F32):
    return pltpu.VMEM(dims, dtype)


def scratch(*dims, dtype=F32):
    return pltpu.VMEM(dims, dtype)


def like(*outs):
    return [pltpu.VMEM(out.shape, out.dtype) for out in outs]


def moves(*dims):
    return pltpu.SemaphoreType.DMA(dims)


class Moves:
    def __init__(self, arrive, leave):
        self.arrive, self.leave, self.left = arrive, leave, False
        for copy in arrive:
            copy.start()

    def ready(self):
        for copy in self.arrive:
            copy.wait()

    def done(self):
        self.left = True
        for copy in self.leave:
            copy.start()


def call(
    kernel, name, args, outs, scratches=(), far=(), far_outs=(), near_args=(), near_outs=(),
    scalars=(), us=4, limit=4,
):
    small = tuple(scalars) + tuple(args)
    small, far = (
        tuple(pltpu.with_memory_space_constraint(x, pltpu.HBM) for x in arrays)
        for arrays in (small, far)
    )
    n_near, n_small, n_far = len(near_args), len(small), len(far)
    n_near_outs, n_outs, n_far_outs = len(near_outs), len(outs), len(far_outs)

    def wrapped(*refs):
        refs = list(refs)

        def take(count):
            taken = refs[:count]
            del refs[:count]
            return taken

        near_in, small_in, far_in = take(n_near), take(n_small), take(n_far)
        near_out, out, far_out = take(n_near_outs), take(n_outs), take(n_far_outs)
        small_here, out_here = take(n_small), take(n_outs)
        in_moves, out_moves = take(2)
        io = Moves(
            [pltpu.make_async_copy(a, b, in_moves.at[i]) for i, (a, b) in enumerate(zip(small_in, small_here))],
            [pltpu.make_async_copy(a, b, out_moves.at[i]) for i, (a, b) in enumerate(zip(out_here, out))],
        )
        kernel(io, *near_in, *small_here, *far_in, *near_out, *out_here, *far_out, *refs)
        if not io.left:
            io.done()
        for copy in io.leave:
            copy.wait()

    return pl.pallas_call(
        wrapped,
        out_shape=list(near_outs) + [
            pltpu.HBM(out.shape, out.dtype) for out in tuple(outs) + tuple(far_outs)
        ],
        in_specs=[IN_VMEM] * n_near + [FAR] * (n_small + n_far),
        out_specs=[IN_VMEM] * n_near_outs + [FAR] * (n_outs + n_far_outs),
        scratch_shapes=(
            [pltpu.SMEM(a.shape, a.dtype) for a in scalars] + like(*args) + like(*outs)
            + [moves(max(n_small, 1)), moves(max(n_outs, 1))] + list(scratches)
        ),
        compiler_params=pltpu.CompilerParams(vmem_limit_bytes=limit * 2**20),
        cost_estimate=pl.CostEstimate(flops=us * 500000000, bytes_accessed=0, transcendentals=0),
        name=name,
    )(*near_args, *small, *far)


def call_edges(tokens, valid):
    edge = 2 * CHUNKS
    width = tokens.shape[1]
    outs = [near(edge, width, dtype=BF16), near(edge, width, dtype=BF16)]
    return call(edges_kernel, "edges", (tokens, valid), (), near_outs=outs, us=1, limit=2)


def call_middle(
    heights, widths, from_core, from_chip, valid, gain, conv_weight, conv_bias, xproj, dt_weight,
    dt_bias, a_log, tokens, cotangent, in_weight, out_weight,
):
    rows, width = tokens.shape
    inner = out_weight.shape[0]
    state, cols, reach = a_log.shape[1], xproj.shape[1], conv_weight.shape[1] - 1
    half = 2 * state
    ext = rows + 2 * reach * CHUNKS
    far_outs = [
        low(rows, width), low(rows, width), shape(rows, LANES), shape(rows, LANES),
        shape(rows, inner), shape(rows, inner), shape(rows, inner), shape(2 * rows, inner),
        shape(2 * rows, inner), shape(2 * rows, inner), shape(2 * rows, inner), shape(ext, inner),
        shape(half, CHUNKS, inner), shape(half, CHUNKS, inner),
    ]
    own = like(*far_outs)
    own[0] = scratch(2 * rows, width, dtype=BF16)
    return call(
        functools.partial(middle_kernel, reach=reach), "middle",
        (valid, gain, conv_weight, conv_bias, xproj, dt_weight, dt_bias, a_log),
        [
            shape(2 * rows, cols), low(4 * CHUNKS, width), shape(half, inner),
            shape(2 * CHUNKS, inner), shape(2 * CHUNKS, inner),
        ],
        like(tokens, cotangent, in_weight, out_weight) + own + [
            scratch(2 * reach * rows, LANES), scratch(2 * rows, inner, dtype=BF16),
            scratch(rows, half * LANES), scratch(state, CHUNKS, inner),
            scratch(state, CHUNKS, inner), scratch(CHUNKS, inner), moves(4), moves(20),
        ],
        (tokens, cotangent, in_weight, out_weight), far_outs, (from_core, from_chip),
        [near(2 * half + CHUNKS + half, inner), near(2 * half + 2 * CHUNKS, inner, dtype=BF16)],
        (heights, widths), us=20, limit=32,
    )


def call_join(got, summary, entered, state, bit, final):
    inner = summary.shape[1]
    half = 2 * state
    outs = [
        near(2 * half + CHUNKS, inner),
        near(half if final else 2 * half + 2 * CHUNKS, inner, dtype=BF16),
    ]
    if not final:
        outs = [near(2 * half + CHUNKS + half, inner)] + outs
    args = (got, summary) + (() if entered is None else (entered,))
    kernel = first_join if entered is None else join_kernel
    joined = call(
        functools.partial(kernel, state=state, bit=bit, final=final), "join", (), (),
        near_args=args, near_outs=outs, us=1, limit=4,
    )
    return joined if not final else [None] + list(joined)


def call_states(
    got, entered, before, rate, skip, proj, masks, delta, s, tail, zs, dgz, normed, cotan, tokens,
    out_weight, rank, reach, bit,
):
    rows, inner = zs.shape
    width = tokens.shape[1]
    half = rate.shape[0]
    tiles = inner // LANES
    grad = (inner, width)
    return call(
        functools.partial(states_kernel, reach=reach, rank=rank, bit=bit), "states",
        (before, rate, skip, proj, masks),
        [shape(2 * half, inner)],
        [
            scratch(rows, half * LANES), scratch(rows, half * LANES), scratch(rows, 2 * LANES),
            scratch(rows, inner), scratch(rows, inner, dtype=BF16),
            scratch(rows, inner, dtype=BF16),
        ] + like(delta, s, tail, zs, dgz, normed, cotan, tokens, out_weight) + like(
            low(rows, width)
        ) + [moves(3, tiles), moves(6), moves(2)],
        (delta, s, tail, zs, dgz, normed, cotan, tokens, out_weight),
        [low(rows, inner), low(rows, width)], (got, entered),
        [near(*grad, dtype=BF16), near(*grad, dtype=BF16)], us=12, limit=28,
    )


def adjoint_scratch(rows, inner, half, reach, small, cols, rank, xext):
    held = (rows // CHUNKS + 1) * (half // 2) * CHUNKS
    maps = scratch(half // 2, CHUNKS, inner)
    return [
        scratch(rows, half * LANES), scratch(rows, 2 * reach * LANES), scratch(rows, half * LANES),
        scratch(rows, inner), scratch(rows, inner), scratch(small - cols - rank, inner),
        scratch(rows + reach * CHUNKS, inner), scratch(rows, inner), scratch(held, LANES),
        scratch(held, LANES), scratch(rows, inner), scratch(rows, inner), scratch(rows, inner), maps,
        maps, scratch(rows, inner), scratch(rows, inner), scratch(*xext.shape),
        moves(6, inner // LANES), moves(8),
    ]


def call_adjoint(d, args, far, extra, small, reach, rank):
    before, after, carry, rate, skip, proj = args[:6]
    dy, xext = far[5], far[7]
    rows, inner = dy.shape
    half, cols = rate.shape[0], proj.shape[1]
    own = adjoint_scratch(rows, inner, half, reach, small, cols, rank, xext)
    if d == 0:
        return call(
            functools.partial(first_adjoint, d=0, reach=reach, rank=rank), "adjoint_up", args,
            [shape(CHUNKS, inner), shape(small, inner)], own, far, [shape(rows, inner)], us=14, limit=32,
        )
    near_args, far_args = extra
    dx, normed, live, dz, in_weight, tokens = far_args
    width = tokens.shape[1]
    folds = inner // width
    fold = -(-(width + 2 * small + CHUNKS) // 64) * 64
    return call(
        functools.partial(second_adjoint, d=1, reach=reach, rank=rank, count=small),
        "adjoint_down", args + near_args, [shape(rows, width)],
        own + like(normed, live, dz, in_weight, tokens) + [
            scratch(rows + 2 * CHUNKS, inner, dtype=BF16), scratch(CHUNKS, inner),
            scratch(small, inner), scratch(folds * fold, width),
        ],
        far + far_args, (), (),
        [
            near(CHUNKS, width), near(CHUNKS, width), near(fold, width, dtype=BF16),
            near(fold, width, dtype=BF16),
        ], us=16, limit=38,
    )


def partner(axis, bit):
    return [(i, i ^ (1 << bit)) for i in range(lax.axis_size(axis))]


def bits_of(axis):
    return (lax.axis_size(axis) - 1).bit_length()


def other_core(values):
    return lax.ppermute(values, "seq", partner("seq", 0))


def next_chip(values):
    count = lax.axis_size("seq")
    pairs = [(i, i + 1) for i in range(1, count - 1, 2)]
    return lax.ppermute(values, "seq", pairs + [(j, i) for i, j in pairs])


def core_sum(kept, sent):
    return kept.astype(F32) + other_core(sent).astype(F32)


def plane_pairs(k):
    return [(i, i ^ k) for i in range(lax.axis_size("img"))]


def plane_sum(values):
    count = lax.axis_size("img")
    here = lax.axis_index("img")
    blocks = values.reshape(count, values.shape[0] // count, values.shape[1])

    def block(k):
        return lax.dynamic_index_in_dim(blocks, here ^ k, 0, keepdims=False)

    total = block(0)
    for k in range(1, count):
        total = total + lax.ppermute(block(k).astype(BF16), "img", plane_pairs(k)).astype(F32)
    return total


def line_sum(values):
    bits = bits_of("seq")
    if bits > 3:
        for bit in range(1, bits):
            values = line_step(values, bit)
        return values
    low = values.astype(BF16)
    count = lax.axis_size("seq")
    for k in range(2, count, 2):
        values = values + lax.ppermute(low, "seq", [(i, i ^ k) for i in range(count)]).astype(F32)
    return values


def line_step(values, bit):
    return values + lax.ppermute(values.astype(BF16), "seq", partner("seq", bit)).astype(F32)


def plane_gather(low):
    count = lax.axis_size("img")
    return jnp.stack(
        [low] + [lax.ppermute(low, "img", plane_pairs(k)) for k in range(1, count)], axis=0
    )


def tied(first, second):
    return lax.optimization_barrier((first, second))


def body(
    tokens, cotangent, heights, widths, valid, norm_gain, in_weight, conv_weight, conv_bias,
    xproj_weight, dt_weight, dt_bias, a_log, skip, out_weight,
):
    rows, width = tokens.shape[1:]
    inner = out_weight.shape[0]
    state = a_log.shape[1]
    rank = dt_weight.shape[1]
    cols = xproj_weight.shape[2]
    taps = conv_weight.shape[1]
    reach = taps - 1
    count = bits_of("seq")
    tokens, cotangent = tokens[0], cotangent[0]
    xproj = xproj_weight.transpose(0, 2, 1)

    to_core, to_chip = call_edges(tokens, valid)
    from_core, from_chip = other_core(to_core), next_chip(to_chip)
    (
        summary, sent, proj, nhalo, rate, before, after, normed, cotan, live, masks, zs, dgz, dy, s,
        dsilu, delta, gate, xext, tail, head,
    ) = call_middle(
        heights, widths, from_core, from_chip, valid, norm_gain, conv_weight, conv_bias, xproj, dt_weight,
        dt_bias, a_log, tokens, cotangent, in_weight, out_weight,
    )
    entered = None
    for bit in range(count - 1):
        got = lax.ppermute(sent, "seq", partner("seq", bit))
        summary, entered, sent = call_join(got, summary, entered, state, bit, bit == count - 2)
    got = lax.ppermute(sent, "seq", partner("seq", count - 1))
    kept, sent, carry, dz, output = call_states(
        got, entered, before, rate, skip, proj, masks, delta, s, tail, zs, dgz, normed, cotan,
        tokens, out_weight, rank, reach, count - 1,
    )

    first_sum = core_sum(kept, sent)
    small = -(-(cols + rank + state + 2 + taps + 1) // CHUNKS) * CHUNKS
    args = (before, after, carry, rate, skip, proj, masks, dt_weight, xproj, conv_weight)
    far = (delta, s, gate, tail, head, dy, dsilu, xext)
    first_sum, far = tied(first_sum, far)
    first_sum = plane_sum(first_sum)
    rim0, small0, dx = call_adjoint(0, args, far, None, small, reach, rank)
    first_sum, dx = tied(first_sum, dx)
    first_sum = line_sum(first_sum)
    rim_core, rim_chip, kept, sent, dn = call_adjoint(
        1, args, far, ((rim0, small0, nhalo), (dx, normed, live, dz, in_weight, tokens)), small,
        reach, rank,
    )
    first_sum, kept, sent = lax.optimization_barrier((first_sum, kept, sent))
    second_sum = core_sum(kept, sent)
    first_mine = plane_gather(first_sum.astype(BF16))
    input_grad = call(
        finish_kernel, "finish", (dn, tokens, cotangent, valid, norm_gain), [shape(rows, width)],
        near_args=(other_core(rim_core), next_chip(rim_chip)), scalars=(heights, widths), us=1, limit=8,
    )[0]
    second_sum = plane_sum(second_sum)
    second_sum, first_mine, input_grad = lax.optimization_barrier((second_sum, first_mine, input_grad))
    first_other = other_core(first_mine)
    for bit in range(1, count):
        second_sum = line_step(second_sum, bit)
    second_sum, first_other = tied(second_sum, first_other)
    second_mine = plane_gather(second_sum.astype(BF16))
    second_other = other_core(second_mine)

    fold = kept.shape[0]
    (
        in_total, conv_total, bias_total, xproj_total, dtw_total, dtb_total, a_total, skip_total,
        out_total, gain_total,
    ) = call(
        functools.partial(
            unpack_kernel, count=small, state=state, rank=rank, cols=cols, taps=taps
        ),
        "unpack", (),
        [
            shape(width, 2 * inner), shape(2, taps, inner), shape(2, inner), shape(2, cols, inner),
            shape(2, rank, inner), shape(2, inner), shape(2, state, inner), shape(2, inner),
            shape(inner, width), shape(width),
        ],
        [scratch(fold, width), scratch(fold, width)],
        near_args=(first_mine, first_other, second_mine, second_other), us=2, limit=16,
    )
    return (
        output[None], input_grad[None], gain_total, in_total, conv_total, bias_total,
        xproj_total.transpose(0, 2, 1), dtw_total, dtb_total, a_total, skip_total, out_total,
    )


def solution(mesh):
    split = P("img", "seq", None)
    placed = (split, split, P("img", None), P("img", None), P("img", "seq")) + (P(),) * 10
    return jax.shard_map(
        body,
        mesh=mesh,
        in_specs=placed,
        out_specs=(split, split) + (P(),) * 10,
        check_vma=False,
    )
```

```python
import functools

import jax
import jax.numpy as jnp
from jax import lax
from jax.experimental import pallas as pl
from jax.experimental.pallas import tpu as pltpu
from jax.sharding import PartitionSpec as P

NORM_EPS = 1e-05
CONTRACT_ROWS = (((0,), (0,)), ((), ()))
CONTRACT_COLS = (((1,), (1,)), ((), ()))
LOG2E = 1.4426950408889634
LN2 = 0.6931471805599453
BREAK = 1e30
CHUNKS = 8
LANES = 128
SUMMARY_STATES = 8
SUMMARY_UNROLL = 8
STATES_UNROLL = 8
ADJOINT_STATES = 8
ADJOINT_UNROLL = 4
F32 = jnp.float32
BF16 = jnp.bfloat16


def dot(a, b):
    return jnp.dot(a, b, preferred_element_type=F32)


def dot_rows(a, b):
    return lax.dot_general(a, b, CONTRACT_ROWS, preferred_element_type=F32)


def dot_cols(a, b):
    return lax.dot_general(a, b, CONTRACT_COLS, preferred_element_type=F32)


def sigmoid(v):
    return 1.0 / (1.0 + jnp.exp(-v))


def fetch(source, target, semaphore):
    copy = pltpu.make_async_copy(source, target, semaphore)
    copy.start()
    return copy


def lanes_of(tile):
    return pl.ds(pl.multiple_of(tile * LANES, LANES), LANES)


def rows_of(j, count=CHUNKS):
    return pl.ds(pl.multiple_of(j * CHUNKS, CHUNKS), count)


def chunk_order(rows):
    row = lax.broadcasted_iota(jnp.int32, (rows, rows), 0)
    slot = lax.broadcasted_iota(jnp.int32, (rows, rows), 1)
    return slot == (row & (CHUNKS - 1)) * (rows // CHUNKS) + (row >> 3)


def image_ends(heights, widths):
    ends, total = [], 0
    for i in range(heights.shape[1]):
        total = total + heights[0, i] * widths[0, i]
        ends.append(total)
    return ends


def segment_of(places, ends):
    found = jnp.zeros_like(places)
    for end in ends:
        found = found + (places >= end).astype(jnp.int32)
    return found


def places_of(first, rows):
    row = lax.broadcasted_iota(jnp.int32, (rows, LANES), 0)
    return first + (row & (CHUNKS - 1)) * (rows // CHUNKS) + (row >> 3)


def edges_kernel(io, tokens, valid, to_core, to_chip):
    rows = tokens.shape[0]
    edge = to_core.shape[0]
    io.ready()
    row = lax.broadcasted_iota(jnp.int32, (edge, rows), 0)
    slot = lax.broadcasted_iota(jnp.int32, (edge, rows), 1)
    held = jnp.broadcast_to(valid[...].astype(F32), (edge, rows))
    first = jnp.where(slot == row, held, 0.0).astype(BF16)
    last = jnp.where(slot == rows - edge + row, held, 0.0).astype(BF16)
    first = dot(first, tokens[...]).astype(BF16)
    last = dot(last, tokens[...]).astype(BF16)
    even = (lax.axis_index("seq") & 1) == 0
    to_core[...] = jnp.where(even, last, first)
    to_chip[...] = jnp.where(even, first, last)


def spread(values, target):
    count = values.shape[1]
    high = values.astype(BF16)
    low = (values - high.astype(F32)).astype(BF16)
    both = jnp.concatenate([high, low], axis=1)
    wide = 2 * LANES
    column = lax.broadcasted_iota(jnp.int32, (2 * count, wide), 0)
    block = lax.broadcasted_iota(jnp.int32, (2 * count, wide), 1) // LANES
    for at in range(0, count * LANES, wide):
        place = block + at // LANES
        pick = ((column == place) | (column == place + count)).astype(BF16)
        target[:, at : at + wide] = dot(both, pick)


def windows(span, up, sublane):
    sign = 1 if up else -1

    def from_before(value, by, fill):
        moved = pltpu.roll(value, (sign * by) % CHUNKS, axis=0)
        kept = sublane >= by if up else sublane < CHUNKS - by
        return jnp.where(kept, moved, fill)

    two = span + from_before(span, 1, 0.0)
    four = two + from_before(two, 2, 0.0)
    eight = four + from_before(four, 4, 0.0)
    edge = [jnp.where(sublane >= by if up else sublane < CHUNKS - by, 0.0, BREAK) for by in (1, 2, 4)]
    return (span + edge[0], two + edge[1], four + edge[2]), from_before(eight, 1, 0.0)


def chain(rate, sums, tail, up, sublane):
    sign = 1 if up else -1
    for by, span in zip((1, 2, 4), sums):
        tail = jnp.exp2(rate * span) * pltpu.roll(tail, (sign * by) % CHUNKS, axis=0) + tail
    end = CHUNKS - 1 if up else 0
    kept = sublane >= 1 if up else sublane < CHUNKS - 1
    return jnp.where(kept, pltpu.roll(tail, sign % CHUNKS, axis=0), 0.0), tail[end : end + 1]


def middle_kernel(
    io, from_core, from_chip, heights, widths, valid, gain, conv_weight, conv_bias, xproj, dt_weight,
    dt_bias, a_log, skip,
    tokens_far, cotangent_far, in_far, out_far,
    sum_out, sent_out, delta_out, s_out, gate_out, dsilu_out, dy, tail_out, head_out, xext_out,
    proj_out, before_out, after_out, rate_out, masks, live, normed_out, nhalo_out, zs_out, dgz_out,
    cotan,
    tokens, cotangent, in_weight, out_weight, normed, same_out, low_out, bc, tails, heads, spans, ins,
    *, reach,
):
    rows, width = tokens.shape
    inner = out_weight.shape[0]
    steps = rows // CHUNKS
    state = a_log.shape[1]
    rank = dt_weight.shape[1]
    tiles = inner // LANES
    arriving = [
        fetch(source, target, ins.at[i])
        for i, (source, target) in enumerate(
            (
                (tokens_far, tokens), (in_far, in_weight), (cotangent_far, cotangent),
                (out_far, out_weight),
            )
        )
    ]
    io.ready()
    start = lax.axis_index("seq") * rows
    slots = lax.axis_size("seq") * rows
    even = (lax.axis_index("seq") & 1) == 0
    ends = image_ends(heights, widths)
    images = heights.shape[1]
    sublane = lax.broadcasted_iota(jnp.int32, (CHUNKS, LANES), 0)

    order = chunk_order(rows)
    order_low = order.astype(BF16)
    picked = jnp.where(order, jnp.broadcast_to(valid[...].astype(F32), order.shape), 0.0)
    alive = dot(picked.astype(BF16), jnp.ones((rows, LANES), BF16))
    places = places_of(start, rows)
    segment = segment_of(places, ends)
    live[...] = jnp.where(segment < images, alive, 0.0)
    column = lax.broadcasted_iota(jnp.int32, (rows, LANES), 1)
    compact = jnp.zeros((rows, LANES), F32)
    for k in range(1, reach + 1):
        same = (segment_of(places - k, ends) == segment) & (places >= k)
        same = same.astype(F32)
        same_out[(k - 1) * rows : k * rows, :] = same
        compact = jnp.where(column == k - 1, same, compact)
        same = (segment_of(places + k, ends) == segment) & (places + k < slots)
        same = same.astype(F32)
        same_out[(reach + k - 1) * rows : (reach + k) * rows, :] = same
        compact = jnp.where(column == reach + k - 1, same, compact)
    masks[...] = compact

    arriving[0].wait()
    inputs = dot(order_low, tokens[...])
    inv_rms = lax.rsqrt(jnp.mean(inputs * inputs, axis=-1, keepdims=True) + NORM_EPS)
    gains = gain[...].astype(F32).reshape(1, width)
    scaled = inputs * inv_rms * gains
    normed[0:rows, :] = scaled.astype(BF16)
    live_wide = jnp.concatenate([live[...]] * (width // LANES), axis=1)
    normed[rows : 2 * rows, :] = (scaled * live_wide).astype(BF16)
    normed_out[...] = normed[0:rows, :]
    before = jnp.where(even, from_chip[...], from_core[...])
    after = jnp.where(even, from_core[...], from_chip[...])
    htok = jnp.concatenate([before[CHUNKS:], after[:CHUNKS]], axis=0)
    hrow = lax.broadcasted_iota(jnp.int32, (2 * CHUNKS, LANES), 0)
    hplace = jnp.where(hrow < CHUNKS, start - CHUNKS + hrow, start + rows + hrow - CHUNKS)
    hlive = (segment_of(hplace, ends) < images).astype(F32)
    htok = htok.astype(F32) * jnp.concatenate([hlive] * (width // LANES), axis=1)
    hinv = lax.rsqrt(jnp.mean(htok * htok, axis=-1, keepdims=True) + NORM_EPS)
    scaled = htok * hinv
    nhalo = (scaled * gains).astype(BF16)
    nhalo_out[...] = jnp.concatenate([nhalo, scaled.astype(BF16)], axis=0)
    arriving[1].wait()
    step = 2 * LANES
    both = jnp.concatenate([normed[rows : 2 * rows, :], nhalo], axis=0)
    wide = lax.broadcasted_iota(jnp.int32, (CHUNKS, step), 0)
    for at in range(0, inner, step):
        lanes = slice(at, at + step)
        x = dot(both, in_weight[:, lanes]).astype(BF16).astype(F32)
        xext_out[reach * CHUNKS : (reach + steps) * CHUNKS, lanes] = x[:rows]
        for i in range(reach):
            to = steps - reach + i
            moved = pltpu.roll(x[to * CHUNKS : (to + 1) * CHUNKS, :], 1, axis=0)
            of = rows + CHUNKS - reach + i
            xext_out[i * CHUNKS : (i + 1) * CHUNKS, lanes] = jnp.where(
                wide == 0, x[of : of + 1], moved
            )
            moved = pltpu.roll(x[i * CHUNKS : (i + 1) * CHUNKS, :], CHUNKS - 1, axis=0)
            to = reach + steps + i
            of = rows + CHUNKS + i
            xext_out[to * CHUNKS : (to + 1) * CHUNKS, lanes] = jnp.where(
                wide == CHUNKS - 1, x[of : of + 1], moved
            )

    arriving[2].wait()
    arriving[3].wait()
    cotan[...] = dot(order_low, cotangent[...]).astype(BF16)
    block = 32
    for at in range(0, inner, step):
        lanes = slice(at, at + step)
        zs_out[:, lanes] = dot(normed[0:rows, :], in_weight[:, inner + at : inner + at + step])
        dgz_out[:, lanes] = dot_cols(cotan[...], out_weight[lanes, :])

    def gate_block(b, _):
        here = pl.ds(pl.multiple_of(b * block, block), block)
        alive = live[here, :]
        for tile in range(tiles):
            lanes = slice(tile * LANES, (tile + 1) * LANES)
            z = zs_out[here, lanes]
            grad = dgz_out[here, lanes] * alive
            gate = sigmoid(z)
            zs = z * gate * alive
            zs_out[here, lanes] = zs
            dy[here, lanes] = 0.5 * grad * zs
            dgz_out[here, lanes] = grad * (gate * (1.0 + z * (1.0 - gate)))
        return 0

    lax.fori_loop(0, rows // block, gate_block, 0)

    taps = reach + 1
    conv_w = [conv_weight[d].astype(F32) for d in range(2)]
    conv_b = conv_bias[...].astype(F32)
    for tile in range(tiles):
        lanes = slice(tile * LANES, (tile + 1) * LANES)

        def conv_block(b, _, lanes=lanes):
            at = pl.multiple_of(b * block, block)
            for d in range(2):
                total = conv_b[d : d + 1, lanes] + conv_w[d][reach:taps, lanes] * (
                    xext_out[pl.ds(at + reach * CHUNKS, block), lanes]
                )
                for k in range(1, taps):
                    move = reach - k if d == 0 else reach + k
                    mask = same_out[pl.ds((d * reach + k - 1) * rows + at, block), :]
                    total = total + conv_w[d][reach - k : taps - k, lanes] * (
                        xext_out[pl.ds(at + move * CHUNKS, block), lanes] * mask
                    )
                gate = sigmoid(total)
                value = total * gate
                s_out[pl.ds(d * rows + at, block), lanes] = value
                low_out[pl.ds(d * rows + at, block), lanes] = value.astype(BF16)
                dsilu_out[pl.ds(d * rows + at, block), lanes] = gate * (1.0 + total * (1.0 - gate))
            return 0

        lax.fori_loop(0, rows // block, conv_block, 0)

    dt_b = dt_bias[...].astype(F32)
    for d in range(2):
        rate_out[d * state : (d + 1) * state, :] = jnp.minimum(
            -LOG2E * jnp.exp(a_log[d].astype(F32)), -1e-20
        )
        here = slice(d * rows, (d + 1) * rows)
        proj = dot_cols(low_out[here, :], xproj[d])
        proj_out[here, :] = proj
        dt_low = proj[:, :rank].astype(BF16)
        for at in range(0, inner, step):
            lanes = slice(at, at + step)
            delta_out[here, lanes] = dot(dt_low, dt_weight[d, :, lanes])
        spread(proj[:, rank:], bc)

        def delta_block(b, _, d=d):
            alive = live[pl.ds(pl.multiple_of(b * block, block), block), :]
            here = pl.ds(pl.multiple_of(d * rows + b * block, block), block)
            for tile in range(tiles):
                lanes = slice(tile * LANES, (tile + 1) * LANES)
                pre = delta_out[here, lanes] + dt_b[d : d + 1, lanes]
                small = jnp.exp(-jnp.abs(pre))
                log1p = jnp.where(small < 1e-4, small * (1.0 - 0.5 * small), jnp.log(1.0 + small))
                delta_out[here, lanes] = (jnp.maximum(pre, 0.0) + log1p) * alive
                gate_out[here, lanes] = jnp.where(pre >= 0.0, 1.0, small) / (1.0 + small) * alive
            return 0

        lax.fori_loop(0, rows // block, delta_block, 0)
        some = SUMMARY_STATES

        def scan_tile(tile, _, d=d):
            lanes = lanes_of(tile)
            for low in range(0, state, some):
                rates = [
                    jnp.broadcast_to(
                        rate_out[d * state + low + m : d * state + low + m + 1, lanes],
                        (CHUNKS, LANES),
                    )
                    for m in range(some)
                ]

                def scan_step(i, carried, d=d, low=low, rates=rates):
                    tail, lead, head, span = carried
                    j = i if d == 0 else steps - 1 - i
                    at = pl.multiple_of(j * CHUNKS, CHUNKS)
                    keep = same_out[pl.ds(d * reach * rows + at, CHUNKS), :]
                    delta = delta_out[pl.ds(d * rows + at, CHUNKS), lanes]
                    drive = delta * s_out[pl.ds(d * rows + at, CHUNKS), lanes]
                    back = dy[pl.ds(at, CHUNKS), lanes]
                    delta = jnp.where(keep > 0.0, delta, BREAK)
                    tail, lead, head = list(tail), list(lead), list(head)
                    for m in range(some):
                        b = bc[pl.ds(at, CHUNKS), (low + m) * LANES : (low + m + 1) * LANES]
                        n = state + low + m
                        c = bc[pl.ds(at, CHUNKS), n * LANES : (n + 1) * LANES]
                        decay = jnp.exp2(delta * rates[m])
                        tail[m] = decay * tail[m] + b * drive
                        lead[m] = lead[m] * decay
                        head[m] = head[m] + lead[m] * (c * back)
                    return tuple(tail), tuple(lead), tuple(head), span + delta

                zeros = tuple(jnp.zeros((CHUNKS, LANES), F32) for _ in range(some))
                ones = tuple(jnp.ones((CHUNKS, LANES), F32) for _ in range(some))
                tail, lead, head, span = lax.fori_loop(
                    0, steps, scan_step, (zeros, ones, zeros, zeros[0]), unroll=SUMMARY_UNROLL
                )
                for m in range(some):
                    tails[low + m, :, lanes] = tail[m]
                    heads[low + m, :, lanes] = head[m]
                spans[:, lanes] = span
            return 0

        lax.fori_loop(0, tiles, scan_tile, 0)

        tail_row = 0 if d == 0 else 2 * state
        head_row = 3 * state if d == 0 else state

        def chain_tile(tile, _, d=d, tail_row=tail_row, head_row=head_row):
            lanes = lanes_of(tile)
            span = spans[:, lanes]
            sums, before = windows(span, d == 0, sublane)
            sums_back, after = windows(span, d == 1, sublane)
            before_out[d * CHUNKS : (d + 1) * CHUNKS, lanes] = before
            after_out[d * CHUNKS : (d + 1) * CHUNKS, lanes] = after
            for n in range(state):
                rate = jnp.broadcast_to(
                    rate_out[d * state + n : d * state + n + 1, lanes], (CHUNKS, LANES)
                )
                carried, total = chain(rate, sums, tails[n, :, lanes], d == 0, sublane)
                tail_out[d * state + n, :, lanes] = carried
                sum_out[tail_row + n : tail_row + n + 1, lanes] = total
                carried, total = chain(rate, sums_back, heads[n, :, lanes], d == 1, sublane)
                head_out[d * state + n, :, lanes] = carried
                sum_out[head_row + n : head_row + n + 1, lanes] = total
            return 0

        lax.fori_loop(0, tiles, chain_tile, 0)
        sum_out[4 * state + d : 4 * state + d + 1, :] = jnp.sum(spans[...], axis=0, keepdims=True)
    at = 4 * state + CHUNKS
    sum_out[4 * state + 2 : at, :] = jnp.zeros((CHUNKS - 2, inner), F32)
    sum_out[at:, :] = rate_out[0 : 2 * state, :]
    sent_out[...] = packed(sum_out[0:at, :], state)
    rate_out[2 * state : 2 * state + 2, :] = skip[...].astype(F32)


def packed(summary, state):
    rest = summary[4 * state :]
    high = rest.astype(BF16)
    low = (rest - high.astype(F32)).astype(BF16)
    return jnp.concatenate([summary[: 4 * state].astype(BF16), high, low], axis=0)


def leads(rate, spans, state, flip):
    parts = [jnp.exp2(rate[d * state : (d + 1) * state] * spans[d : d + 1]) for d in range(2)]
    return jnp.concatenate(parts[::-1] if flip else parts, axis=0)


def join_kernel(io, got, summary, entered, *outs, state, bit, final):
    half = 2 * state
    upper = ((lax.axis_index("seq") >> bit) & 1) == 1
    mine = summary[0 : 2 * half + CHUNKS, :]
    rates = summary[2 * half + CHUNKS :, :]
    entered_out, sent_out = outs[-2], outs[-1]
    values = got[...].astype(F32)
    spans = mine[4 * state : 4 * state + 2]
    other = values[4 * state : 4 * state + 2] + values[4 * state + CHUNKS : 4 * state + CHUNKS + 2]
    if entered is None:
        entered_up = jnp.where(upper, values[:half], 0.0)
        entered_down = jnp.where(upper, 0.0, values[half : 2 * half])
        span_up = jnp.where(upper, other, 0.0)
        span_down = jnp.where(upper, 0.0, other)
    else:
        held = entered[...]
        span_up, span_down = held[2 * half : 2 * half + 2], held[2 * half + 2 : 2 * half + 4]
        entered_up = held[:half] + jnp.where(
            upper, leads(rates, span_up, state, False) * values[:half], 0.0
        )
        entered_down = held[half : 2 * half] + jnp.where(
            upper, 0.0, leads(rates, span_down, state, True) * values[half : 2 * half]
        )
        span_up = span_up + jnp.where(upper, other, 0.0)
        span_down = span_down + jnp.where(upper, 0.0, other)
    entered_out[0:half, :] = entered_up
    entered_out[half : 2 * half, :] = entered_down
    entered_out[2 * half :, :] = jnp.concatenate(
        [span_up, span_down, jnp.zeros((CHUNKS - 4, mine.shape[1]), F32)], axis=0
    )
    low_up = jnp.where(upper, values[:half], mine[:half])
    high_up = jnp.where(upper, mine[:half], values[:half])
    low_down = jnp.where(upper, values[half : 2 * half], mine[half : 2 * half])
    high_down = jnp.where(upper, mine[half : 2 * half], values[half : 2 * half])
    low_span, high_span = jnp.where(upper, other, spans), jnp.where(upper, spans, other)
    up = leads(rates, high_span, state, False) * low_up + high_up
    down = leads(rates, low_span, state, True) * high_down + low_down
    if final:
        next_upper = ((lax.axis_index("seq") >> (bit + 1)) & 1) == 1
        sent_out[...] = jnp.where(next_upper, down, up).astype(BF16)
    else:
        total = jnp.concatenate(
            [up, down, spans + other, jnp.zeros((CHUNKS - 2, mine.shape[1]), F32)], axis=0
        )
        outs[0][0 : 2 * half + CHUNKS, :] = total
        outs[0][2 * half + CHUNKS :, :] = rates
        sent_out[...] = packed(total, state)


def first_join(io, got, summary, *outs, state, bit, final):
    join_kernel(io, got, summary, None, *outs, state=state, bit=bit, final=final)


def state_block(j, state):
    return pl.multiple_of(j * state * CHUNKS, CHUNKS)


def states_pass(d, steps, state, rates, begin, delta, s, keep, bc, y):
    def step(i, h):
        j = i if d == 0 else steps - 1 - i
        here = pl.ds(pl.multiple_of(j * CHUNKS, CHUNKS), CHUNKS)
        size = delta[here, :]
        drive = size * s[here, :]
        size = jnp.where(keep[here, :] > 0.0, size, BREAK)
        h = list(h)
        total = None if d == 0 else y[here, :]
        for n in range(state):
            b = bc[here, n * LANES : (n + 1) * LANES]
            c = bc[here, (state + n) * LANES : (state + n + 1) * LANES]
            h[n] = jnp.exp2(size * rates[n]) * h[n] + b * drive
            total = c * h[n] if total is None else total + c * h[n]
        y[here, :] = total
        return tuple(h)

    lax.fori_loop(0, steps, step, tuple(begin), unroll=STATES_UNROLL)


def held_pass(d, steps, state, rates, begin, delta, s, keep, bc, h_out, decay_out):
    start = state_block(0 if d == 0 else steps, state)
    for n in range(state):
        h_out[pl.ds(start + n * CHUNKS, CHUNKS), :] = begin[n]

    def step(i, h):
        j = i if d == 0 else steps - 1 - i
        here = pl.ds(pl.multiple_of(j * CHUNKS, CHUNKS), CHUNKS)
        to = state_block(j + 1 if d == 0 else j, state)
        at = state_block(j, state)
        size = delta[here, :]
        drive = size * s[here, :]
        size = jnp.where(keep[here, :] > 0.0, size, BREAK)
        h = list(h)
        for n in range(state):
            decay = jnp.exp2(size * rates[n])
            decay_out[pl.ds(at + n * CHUNKS, CHUNKS), :] = decay
            h[n] = decay * h[n] + bc[here, n * LANES : (n + 1) * LANES] * drive
            h_out[pl.ds(to + n * CHUNKS, CHUNKS), :] = h[n]
        return tuple(h)

    lax.fori_loop(0, steps, step, tuple(begin), unroll=STATES_UNROLL)


def adjoint_pass(
    d, steps, state, rates, back, delta, s, gate, dy, keep, skip, bc, h_in, decay_in, sums,
    dpre_out, ds_out, rows_out,
):
    some = ADJOINT_STATES
    edge = steps - 1
    skip = skip[...]
    zeros = jnp.zeros((CHUNKS, LANES), F32)
    grads = []
    for low in range(0, state, some):
        final = low + some == state

        def step(i, carried, low=low, final=final):
            g, acc, h, skip_acc, bias_acc = carried
            j = edge - i if d == 0 else i
            here = pl.ds(pl.multiple_of(j * CHUNKS, CHUNKS), CHUNKS)
            size = delta[here, :]
            value = s[here, :]
            grad = dy[here, :]
            drive = size * value
            masked = jnp.where(keep[here, :] > 0.0, size, BREAK)
            at = state_block(j, state)
            prev = at if d == 0 else state_block(j + 1, state)
            g, acc, h = list(g), list(acc), list(h)
            weighted = zeros if low == 0 else ds_out[here, :]
            rate_sum = zeros if low == 0 else dpre_out[here, :]
            for m in range(some):
                n = low + m
                b = bc[here, n * LANES : (n + 1) * LANES]
                c = bc[here, (state + n) * LANES : (state + n + 1) * LANES]
                adjoint = c * grad + g[m]
                before = h_in[pl.ds(prev + n * CHUNKS, CHUNKS), :]
                sums[here, n * LANES : (n + 1) * LANES] += adjoint * drive
                sums[here, (state + n) * LANES : (state + n + 1) * LANES] += grad * h[m]
                g[m] = adjoint * decay_in[pl.ds(at + n * CHUNKS, CHUNKS), :]
                held = g[m] * before
                weighted = weighted + adjoint * b
                rate_sum = rate_sum + held * rates[n]
                acc[m] = acc[m] + held * masked
                h[m] = before
            if final:
                ds_out[here, :] = skip * grad + size * weighted
                pre = ((LN2 * rate_sum + weighted * value) * gate[here, :]).astype(BF16).astype(F32)
                dpre_out[here, :] = pre
                bias_acc = bias_acc + pre
                skip_acc = skip_acc + grad * value
            else:
                dpre_out[here, :] = rate_sum
                ds_out[here, :] = weighted
            return tuple(g), tuple(acc), tuple(h), skip_acc, bias_acc

        last = state_block(steps if d == 0 else 0, state)
        h_last = tuple(h_in[pl.ds(last + (low + m) * CHUNKS, CHUNKS), :] for m in range(some))
        none = tuple(zeros for _ in range(some))
        _, acc, _, skip_acc, bias_acc = lax.fori_loop(
            0, steps, step, (tuple(back[low : low + some]), none, h_last, zeros, zeros),
            unroll=ADJOINT_UNROLL,
        )
        grads.extend(acc)
    for n in range(state):
        rows_out[n : n + 1, :] = jnp.sum(grads[n], axis=0, keepdims=True) * rates[n][0:1] * LN2
    rows_out[state : state + 1, :] = jnp.sum(bias_acc, axis=0, keepdims=True)
    rows_out[state + 1 : state + 2, :] = jnp.sum(skip_acc, axis=0, keepdims=True)


def lane_sums(sums, state):
    depth = 2 * state * LANES
    block = lax.broadcasted_iota(jnp.int32, (depth, LANES), 0) // LANES
    column = lax.broadcasted_iota(jnp.int32, (depth, LANES), 1)
    return dot(sums.astype(BF16), (block == column).astype(BF16))[:, : 2 * state]


def rate_tiles(rate, d, state, lanes):
    return [
        jnp.broadcast_to(rate[d * state + n : d * state + n + 1, lanes], (CHUNKS, LANES))
        for n in range(state)
    ]


def begin_tiles(rates, passed, maps, carry, at, d, state, lanes):
    passed = passed[d * CHUNKS : (d + 1) * CHUNKS, lanes]
    return [
        jnp.exp2(rates[n] * passed) * carry[at + n : at + n + 1, lanes]
        + maps[d * state + n, :, lanes]
        for n in range(state)
    ]


def slot_order(rows):
    row = lax.broadcasted_iota(jnp.int32, (rows, rows), 1)
    slot = lax.broadcasted_iota(jnp.int32, (rows, rows), 0)
    return (slot == (row & (CHUNKS - 1)) * (rows // CHUNKS) + (row >> 3)).astype(BF16)


def states_kernel(
    io, delta, s, tail, proj, before, rate, masks, normed, got, entered, zs, dgz, cotan,
    tokens_far, out_far,
    kept, sent, carry_out, dz, output_far,
    bc0, bc1, keep, y, gated, tokens, out_weight, output, moves,
    *, reach, rank, state, bit,
):
    rows, inner = zs.shape
    width = tokens.shape[1]
    steps = rows // CHUNKS
    half = 2 * state
    tiles = inner // LANES
    arriving = [fetch(tokens_far, tokens, moves.at[0]), fetch(out_far, out_weight, moves.at[1])]
    upper = ((lax.axis_index("seq") >> bit) & 1) == 1
    values = got[...].astype(F32)
    held = entered[...]
    rates = rate[0:half, :]
    carry_out[0:half, :] = held[:half] + jnp.where(
        upper, leads(rates, held[2 * half : 2 * half + 2], state, False) * values, 0.0
    )
    carry_out[half : 2 * half, :] = held[half : 2 * half] + jnp.where(
        upper, 0.0, leads(rates, held[2 * half + 2 : 2 * half + 4], state, True) * values
    )
    spread(proj[0:rows, rank:], bc0)
    spread(proj[rows : 2 * rows, rank:], bc1)
    spread(jnp.concatenate([masks[:, 0:1], masks[:, reach : reach + 1]], axis=1), keep)

    def scan_tile(tile, _):
        lanes = lanes_of(tile)
        for d, bc in enumerate((bc0, bc1)):
            rates = rate_tiles(rate, d, state, lanes)
            begin = begin_tiles(rates, before, tail, carry_out, d * half, d, state, lanes)
            mine = slice(d * rows, (d + 1) * rows)
            states_pass(
                d, steps, state, rates, begin, delta.at[mine, lanes], s.at[mine, lanes],
                keep.at[:, d * LANES : (d + 1) * LANES], bc, y.at[:, lanes],
            )
        return 0

    lax.fori_loop(0, tiles, scan_tile, 0)
    block = 32

    def gate_block(b, _):
        here = pl.ds(pl.multiple_of(b * block, block), block)
        there = pl.ds(pl.multiple_of(rows + b * block, block), block)
        for tile in range(tiles):
            lanes = slice(tile * LANES, (tile + 1) * LANES)
            total = 0.5 * (
                y[here, lanes] + rate[half : half + 1, lanes] * s[here, lanes]
                + rate[half + 1 : half + 2, lanes] * s[there, lanes]
            )
            gated[here, lanes] = (total * zs[here, lanes]).astype(BF16)
            dz[here, lanes] = (total * dgz[here, lanes]).astype(BF16)
        return 0

    lax.fori_loop(0, rows // block, gate_block, 0)
    for copy in arriving:
        copy.wait()
    ordered = dot(slot_order(rows), gated[...]).astype(BF16)
    output[...] = (tokens[...].astype(F32) + dot(ordered, out_weight[...])).astype(BF16)
    leaving = fetch(output, output_far, moves.at[2])
    even = (lax.axis_index("seq") & 1) == 0
    out_grad = dot_rows(gated[...], cotan[...]).astype(BF16)
    z_grad = jnp.concatenate(
        [dot_rows(normed[...], dz[:, at : at + width]) for at in range(0, inner, width)], axis=0
    ).astype(BF16)
    sent[...] = jnp.where(even, z_grad, out_grad)
    kept[...] = jnp.where(even, out_grad, z_grad)
    leaving.wait()


def adjoint_kernel(
    io, delta, s, gate, dsilu, dy, tail, head, xext, proj, before, after, rate, masks, carry, dx_in,
    dt_weight, xproj, conv_weight,
    dc_rim, small_out, dx_out,
    bc, same, sums, dpre, ds, rows_out, ext, h, decays,
    *, d, reach, rank, state,
):
    rows, inner = dy.shape
    steps = rows // CHUNKS
    half = 2 * state
    tiles = inner // LANES
    taps = reach + 1
    cols = proj.shape[1]
    mine = slice(d * rows, (d + 1) * rows)
    spread(proj[mine, rank:], bc)
    spread(masks[:, 0 : 2 * reach], same)
    keep = same.at[:, d * reach * LANES : (d * reach + 1) * LANES]
    sums[...] = jnp.zeros_like(sums)
    rows_out[...] = jnp.zeros_like(rows_out)
    state_at = 0 if d == 0 else half
    grad_at = (half if d == 0 else 0) + state

    def scan_tile(tile, _):
        lanes = lanes_of(tile)
        rates = rate_tiles(rate, d, state, lanes)
        begin = begin_tiles(rates, before, tail, carry, state_at, d, state, lanes)
        held_pass(
            d, steps, state, rates, begin, delta.at[mine, lanes], s.at[mine, lanes], keep, bc, h,
            decays,
        )
        back = begin_tiles(rates, after, head, carry, grad_at, d, state, lanes)
        adjoint_pass(
            d, steps, state, rates, back, delta.at[mine, lanes], s.at[mine, lanes],
            gate.at[mine, lanes], dy.at[:, lanes], keep, rate.at[half + d : half + d + 1, lanes], bc,
            h, decays, sums, dpre.at[:, lanes], ds.at[:, lanes], rows_out.at[:, lanes],
        )
        return 0

    lax.fori_loop(0, tiles, scan_tile, 0)
    io.ready()
    dpre_low = dpre[...].astype(BF16)
    dt_grad = dot_rows(proj[mine, :rank].astype(BF16), dpre_low)
    dt_back = dot_cols(dpre_low, dt_weight[d])
    dproj = jnp.concatenate([dt_back, lane_sums(sums[...], state)], axis=1).astype(BF16)
    small_out[0:cols, :] = dot_rows(dproj, s[mine, :].astype(BF16))
    small_out[cols : cols + rank, :] = dt_grad
    base = 0 if d == 0 else reach * CHUNKS
    step = 2 * LANES
    for lane in range(0, inner, step):
        lanes = slice(lane, lane + step)
        total = ds[:, lanes] + dot(dproj, xproj[d, :, lanes])
        ext[base : base + rows, lanes] = (total * dsilu[mine, lanes]).astype(BF16).astype(F32)
    wide = lax.broadcasted_iota(jnp.int32, (CHUNKS, inner), 0)
    for i in range(reach):
        if d == 0:
            moved = pltpu.roll(ext[i * CHUNKS : (i + 1) * CHUNKS, :], CHUNKS - 1, axis=0)
            ext[rows + i * CHUNKS : rows + (i + 1) * CHUNKS, :] = jnp.where(
                wide == CHUNKS - 1, 0.0, moved
            )
        else:
            moved = pltpu.roll(ext[rows + i * CHUNKS : rows + (i + 1) * CHUNKS, :], 1, axis=0)
            ext[i * CHUNKS : (i + 1) * CHUNKS, :] = jnp.where(wide == 0, 0.0, moved)

    conv_w = conv_weight[d].astype(F32)
    block = 32
    zeros = jnp.zeros((CHUNKS, LANES), F32)

    def folded(values):
        return functools.reduce(
            lambda a, b: a + b, [values[i : i + CHUNKS] for i in range(0, block, CHUNKS)]
        )

    base_row = cols + rank
    for tile in range(tiles):
        lanes = slice(tile * LANES, (tile + 1) * LANES)
        weight = conv_w[:, lanes]

        def conv_block(b, totals, lanes=lanes, weight=weight):
            here = pl.multiple_of(b * block, block)
            totals = list(totals)
            mid = ext[pl.ds(here + base, block), lanes]
            total = weight[reach:taps] * mid
            totals[reach] = totals[reach] + folded(mid * xext[pl.ds(here + reach * CHUNKS, block), lanes])
            totals[taps] = totals[taps] + folded(mid)
            for k in range(1, taps):
                past = same[pl.ds(here, block), (k - 1) * LANES : k * LANES]
                ahead = same[pl.ds(here, block), (reach + k - 1) * LANES : (reach + k) * LANES]
                if d == 0:
                    given = ext[pl.ds(here + k * CHUNKS, block), lanes] * ahead
                    taken = xext[pl.ds(here + (reach - k) * CHUNKS, block), lanes] * past
                else:
                    given = ext[pl.ds(here + (reach - k) * CHUNKS, block), lanes] * past
                    taken = xext[pl.ds(here + (reach + k) * CHUNKS, block), lanes] * ahead
                total = total + weight[reach - k : taps - k] * given
                totals[reach - k] = totals[reach - k] + folded(mid * taken)
            if dx_in is not None:
                total = total + dx_in[pl.ds(here, block), lanes]
            dx_out[pl.ds(here, block), lanes] = total
            return tuple(totals)

        totals = lax.fori_loop(0, rows // block, conv_block, (zeros,) * (taps + 1))
        for i in range(taps + 1):
            at = state + 2 + i
            rows_out[at : at + 1, lanes] = jnp.sum(totals[i], axis=0, keepdims=True)

    edge = []
    for i in range(CHUNKS):
        row = jnp.zeros((1, inner), F32)
        for k in range(1, taps):
            j = i - CHUNKS + k if d == 0 else steps + i - k
            if (d == 0 and j >= 0) or (d == 1 and j < steps):
                sub = 0 if d == 0 else CHUNKS - 1
                at = j * CHUNKS + sub
                column = (d * reach + k - 1) * LANES
                mask = jnp.concatenate([same[at : at + 1, column : column + LANES]] * tiles, axis=1)
                at = base + j * CHUNKS + sub
                row = row + conv_w[reach - k : taps - k] * ext[at : at + 1, :] * mask
        edge.append(row)
    dc_rim[...] = jnp.concatenate(edge, axis=0)
    small_out[base_row:, :] = rows_out[0 : small_out.shape[0] - base_row, :]


def first_adjoint(io, *refs, **static):
    adjoint_kernel(io, *refs[:14], None, *refs[14:], **static)


def second_adjoint(io, *refs, count, **static):
    live, normed, nhalo, dz, rim0, small0 = refs[15:21]
    in_far, tokens_far = refs[24:26]
    to_core, to_chip, kept, sent, dn_out = refs[26:31]
    in_weight, tokens, low, rim1, small1, dx, grads, moves = refs[31:39]
    arriving = [fetch(in_far, in_weight, moves.at[0]), fetch(tokens_far, tokens, moves.at[1])]
    adjoint_kernel(io, *refs[:15], *refs[21:24], rim1, small1, dx, *refs[39:], **static)
    for copy in arriving:
        copy.wait()
    rows, width = tokens.shape

    inner = dx.shape[1]
    folds = inner // width
    fold = grads.shape[0] // folds
    edges = 2 * CHUNKS
    for tile in range(inner // LANES):
        lanes = slice(tile * LANES, (tile + 1) * LANES)
        low[0:rows, lanes] = (dx[:, lanes] * live[...]).astype(BF16)
    low[rows : rows + edges, :] = jnp.concatenate([rim0[...], rim1[...]], axis=0).astype(BF16)
    both = jnp.concatenate([normed[0:rows, :], nhalo[0:edges, :]], axis=0)
    size = small0.shape[0]
    for i in range(folds):
        lanes = slice(i * width, (i + 1) * width)
        at = i * fold
        grads[at : at + width, :] = dot_rows(both, low[:, lanes])
        at += width
        grads[at : at + size, :] = small0[:, lanes]
        at += size
        grads[at : at + size, :] = small1[:, lanes]
        at += size
        grads[at : (i + 1) * fold, :] = jnp.zeros(((i + 1) * fold - at, width), F32)
    back = slot_order(rows)
    dn = dot_cols(dot(back, low[0:rows, :]).astype(BF16), in_weight[:, 0:inner]) + dot_cols(
        dot(back, dz[...]).astype(BF16), in_weight[:, inner : 2 * inner]
    )
    dn_out[...] = dn
    rim = dot_cols(low[rows : rows + edges, :], in_weight[:, 0:inner])
    even = (lax.axis_index("seq") & 1) == 0
    to_core[...] = jnp.where(even, rim[CHUNKS:], rim[:CHUNKS])
    to_chip[...] = jnp.where(even, rim[:CHUNKS], rim[CHUNKS:])
    inputs = tokens[...].astype(F32)
    inv_rms = lax.rsqrt(jnp.mean(inputs * inputs, axis=-1, keepdims=True) + NORM_EPS)
    at = width + 2 * size
    grads[at : at + 1, :] = jnp.sum(
        dn * (inputs * inv_rms), axis=0, keepdims=True
    ) + jnp.sum(rim * nhalo[edges : 2 * edges, :].astype(F32), axis=0, keepdims=True)
    left, right = grads[0:fold, :].astype(BF16), grads[fold : 2 * fold, :].astype(BF16)
    kept[...] = jnp.where(even, left, right)
    sent[...] = jnp.where(even, right, left)


def finish_kernel(
    io, from_core, from_chip, dn, heights, widths, tokens, cotangent, valid, gain, input_grad
):
    rows, width = tokens.shape
    even = (lax.axis_index("seq") & 1) == 0
    start = lax.axis_index("seq") * rows
    io.ready()
    before = jnp.where(even, from_chip[...], from_core[...])
    after = jnp.where(even, from_core[...], from_chip[...])
    end = image_ends(heights, widths)[-1]
    row = lax.broadcasted_iota(jnp.int32, (CHUNKS, rows), 0)
    slot = lax.broadcasted_iota(jnp.int32, (CHUNKS, rows), 1)
    alive = jnp.broadcast_to(valid[...].astype(F32), (CHUNKS, rows))
    alive = jnp.where(start + slot < end, alive, 0.0)
    first = jnp.sum(jnp.where(slot == row, alive, 0.0), axis=1, keepdims=True)
    last = jnp.sum(jnp.where(slot == rows - CHUNKS + row, alive, 0.0), axis=1, keepdims=True)
    values = jnp.concatenate(
        [
            dn[0:CHUNKS, :] + first * before, dn[CHUNKS : rows - CHUNKS, :],
            dn[rows - CHUNKS : rows, :] + last * after,
        ],
        axis=0,
    )
    inputs = tokens[...].astype(F32)
    inv_rms = lax.rsqrt(jnp.mean(inputs * inputs, axis=-1, keepdims=True) + NORM_EPS)
    scaled = values * gain[...].astype(F32).reshape(1, width)
    mean = jnp.mean(scaled * inputs, axis=-1, keepdims=True)
    input_grad[...] = (
        cotangent[...].astype(F32) + inv_rms * scaled - inputs * (inv_rms * inv_rms * inv_rms) * mean
    )


def unpack_kernel(
    io, first_mine, first_other, second_mine, second_other,
    in_out, conv_w, conv_b, xproj, dt_w, dt_b, a_log, skip, out_w, gain,
    left, right,
    *, count, state, rank, cols, taps,
):
    blocks = first_mine.shape[0]
    width = out_w.shape[1]
    folds = out_w.shape[0] // width

    def ordered(mine, other, into_first, into_second):
        size = mine.shape[1]
        is_even = (lax.axis_index("seq") & 1) == 0
        plane = lax.axis_index("img")
        for k in range(blocks):
            source = plane ^ k
            a, b = mine[source].astype(F32), other[source].astype(F32)
            into_first(k * size, jnp.where(is_even, a, b))
            into_second(k * size, jnp.where(is_even, b, a))

    def put_out(at, values):
        out_w[at : at + values.shape[0], :] = values

    def put_z(at, values):
        size = values.shape[0]
        column = (folds + at // width) * width
        in_out[at % width : at % width + size, column : column + width] = values

    ordered(first_mine, first_other, put_out, put_z)

    def put_left(at, values):
        left[at : at + values.shape[0], :] = values

    def put_right(at, values):
        right[at : at + values.shape[0], :] = values

    ordered(second_mine, second_other, put_left, put_right)
    for i, half in enumerate((left, right)):
        lanes = slice(i * width, (i + 1) * width)
        in_out[:, lanes] = half[0:width, :]
        for d in range(2):
            at = width + d * count
            xproj[d, :, lanes] = half[at : at + cols, :]
            at += cols
            dt_w[d, :, lanes] = half[at : at + rank, :]
            at += rank
            a_log[d, :, lanes] = half[at : at + state, :]
            dt_b[d : d + 1, lanes] = half[at + state : at + state + 1, :]
            skip[d : d + 1, lanes] = half[at + state + 1 : at + state + 2, :]
            at += state + 2
            conv_w[d, :, lanes] = half[at : at + taps, :]
            conv_b[d : d + 1, lanes] = half[at + taps : at + taps + 1, :]
    gain[...] = left[width + 2 * count : width + 2 * count + 1, :].reshape(width)


IN_VMEM = pl.BlockSpec(memory_space=pltpu.VMEM)
IN_SMEM = pl.BlockSpec(memory_space=pltpu.SMEM)
FAR = pl.BlockSpec(memory_space=pltpu.HBM)


def shape(*dims, dtype=F32):
    return jax.ShapeDtypeStruct(dims, dtype)


def low(*dims):
    return jax.ShapeDtypeStruct(dims, BF16)


def near(*dims, dtype=F32):
    return pltpu.VMEM(dims, dtype)


def scratch(*dims, dtype=F32):
    return pltpu.VMEM(dims, dtype)


def like(*outs):
    return [pltpu.VMEM(out.shape, out.dtype) for out in outs]


def moves(*dims):
    return pltpu.SemaphoreType.DMA(dims)


class Moves:
    def __init__(self, arrive, leave):
        self.arrive, self.leave, self.left = arrive, leave, False
        for copy in arrive:
            copy.start()

    def ready(self):
        for copy in self.arrive:
            copy.wait()

    def done(self):
        self.left = True
        for copy in self.leave:
            copy.start()


def call(
    kernel, name, args, outs, scratches=(), far=(), far_outs=(), near_args=(), near_outs=(),
    scalars=(), handed=(), us=4, limit=4,
):
    small = tuple(scalars) + tuple(args)
    small, far = (
        tuple(pltpu.with_memory_space_constraint(x, pltpu.HBM) for x in arrays)
        for arrays in (small, far)
    )
    n_hand = len(handed)
    near_args = tuple(handed) + tuple(near_args)
    n_near, n_small, n_far = len(near_args), len(small), len(far)
    n_near_outs, n_outs, n_far_outs = len(near_outs), len(outs), len(far_outs)

    def wrapped(*refs):
        refs = list(refs)

        def take(count):
            taken = refs[:count]
            del refs[:count]
            return taken

        near_in, small_in, far_in = take(n_near), take(n_small), take(n_far)
        near_out, out, far_out = take(n_near_outs), take(n_outs), take(n_far_outs)
        take(n_hand)
        small_here, out_here = take(n_small), take(n_outs)
        in_moves, out_moves = take(2)
        io = Moves(
            [pltpu.make_async_copy(a, b, in_moves.at[i]) for i, (a, b) in enumerate(zip(small_in, small_here))],
            [pltpu.make_async_copy(a, b, out_moves.at[i]) for i, (a, b) in enumerate(zip(out_here, out))],
        )
        kernel(io, *near_in, *small_here, *far_in, *near_out, *out_here, *far_out, *refs)
        if not io.left:
            io.done()
        for copy in io.leave:
            copy.wait()

    return pl.pallas_call(
        wrapped,
        out_shape=list(near_outs) + [
            pltpu.HBM(out.shape, out.dtype) for out in tuple(outs) + tuple(far_outs)
        ] + [pltpu.VMEM(x.shape, x.dtype) for x in handed],
        in_specs=[IN_VMEM] * n_near + [FAR] * (n_small + n_far),
        out_specs=[IN_VMEM] * n_near_outs + [FAR] * (n_outs + n_far_outs) + [IN_VMEM] * n_hand,
        input_output_aliases={i: n_near_outs + n_outs + n_far_outs + i for i in range(n_hand)},
        scratch_shapes=(
            [pltpu.SMEM(a.shape, a.dtype) for a in scalars] + like(*args) + like(*outs)
            + [moves(max(n_small, 1)), moves(max(n_outs, 1))] + list(scratches)
        ),
        compiler_params=pltpu.CompilerParams(vmem_limit_bytes=limit * 2**20),
        cost_estimate=pl.CostEstimate(flops=us * 500000000, bytes_accessed=0, transcendentals=0),
        name=name,
    )(*near_args, *small, *far)


def call_edges(tokens, valid):
    edge = 2 * CHUNKS
    width = tokens.shape[1]
    outs = [near(edge, width, dtype=BF16), near(edge, width, dtype=BF16)]
    return call(edges_kernel, "edges", (tokens, valid), (), near_outs=outs, us=1, limit=2)


def call_middle(
    heights, widths, from_core, from_chip, valid, gain, conv_weight, conv_bias, xproj, dt_weight,
    dt_bias, a_log, skip, tokens, cotangent, in_weight, out_weight,
):
    rows, width = tokens.shape
    inner = out_weight.shape[0]
    state, cols, reach = a_log.shape[1], xproj.shape[1], conv_weight.shape[1] - 1
    half = 2 * state
    both = near(2 * rows, inner)
    one = near(rows, inner)
    maps = near(half, CHUNKS, inner)
    ends = near(2 * CHUNKS, inner)
    return call(
        functools.partial(middle_kernel, reach=reach), "middle",
        (valid, gain, conv_weight, conv_bias, xproj, dt_weight, dt_bias, a_log, skip), (),
        like(tokens, cotangent, in_weight, out_weight) + [
            scratch(2 * rows, width, dtype=BF16), scratch(2 * reach * rows, LANES),
            scratch(2 * rows, inner, dtype=BF16), scratch(rows, half * LANES),
            scratch(state, CHUNKS, inner), scratch(state, CHUNKS, inner), scratch(CHUNKS, inner),
            moves(4),
        ],
        (tokens, cotangent, in_weight, out_weight), (), (from_core, from_chip),
        [
            near(2 * half + CHUNKS + half, inner), near(2 * half + 2 * CHUNKS, inner, dtype=BF16),
            both, both, both, both, one, maps, maps, near(rows + 2 * reach * CHUNKS, inner),
            near(2 * rows, cols), ends, ends, near(half + CHUNKS, inner), near(rows, LANES),
            near(rows, LANES), near(rows, width, dtype=BF16), near(4 * CHUNKS, width, dtype=BF16),
            one, one, near(rows, width, dtype=BF16),
        ],
        (heights, widths), us=20, limit=16,
    )


def call_join(got, summary, entered, state, bit, final):
    inner = summary.shape[1]
    half = 2 * state
    outs = [
        near(2 * half + CHUNKS, inner),
        near(half if final else 2 * half + 2 * CHUNKS, inner, dtype=BF16),
    ]
    if not final:
        outs = [near(2 * half + CHUNKS + half, inner)] + outs
    args = (got, summary) + (() if entered is None else (entered,))
    kernel = first_join if entered is None else join_kernel
    joined = call(
        functools.partial(kernel, state=state, bit=bit, final=final), "join", (), (),
        near_args=args, near_outs=outs, us=1, limit=4,
    )
    return joined if not final else [None] + list(joined)


def call_states(handed, used, got, entered, zs, dgz, cotan, tokens, out_weight, rank, reach, state, bit):
    rows, inner = zs.shape
    width = tokens.shape[1]
    half = 2 * state
    n_hand = len(handed)

    def kernel(io, *refs):
        states_kernel(
            io, *(refs[i] for i in used), *refs[n_hand:], reach=reach, rank=rank, state=state, bit=bit
        )

    grad = near(inner, width, dtype=BF16)
    return call(
        kernel, "states", (), (),
        [
            scratch(rows, half * LANES), scratch(rows, half * LANES), scratch(rows, 2 * LANES),
            scratch(rows, inner), scratch(rows, inner, dtype=BF16),
        ] + like(tokens, out_weight, low(rows, width)) + [moves(3)],
        (tokens, out_weight), [low(rows, width)], (got, entered, zs, dgz, cotan),
        [grad, grad, near(2 * half, inner), near(rows, inner, dtype=BF16)], handed=handed, us=12,
        limit=16,
    )


def adjoint_scratch(rows, inner, half, reach, small, cols, rank):
    held = (rows // CHUNKS + 1) * (half // 2) * CHUNKS
    return [
        scratch(rows, half * LANES), scratch(rows, 2 * reach * LANES), scratch(rows, half * LANES),
        scratch(rows, inner), scratch(rows, inner), scratch(small - cols - rank, inner),
        scratch(rows + reach * CHUNKS, inner), scratch(held, LANES), scratch(held, LANES),
    ]


def call_first_adjoint(handed, used, weights, small, reach, rank, state):
    rows, inner = handed[used[4]].shape
    cols = handed[used[8]].shape[1]
    n_hand = len(handed)

    def kernel(io, *refs):
        first_adjoint(
            io, *(refs[i] for i in used), *refs[n_hand:], d=0, reach=reach, rank=rank, state=state
        )

    return call(
        kernel, "adjoint_up", weights, (),
        adjoint_scratch(rows, inner, 2 * state, reach, small, cols, rank), near_outs=[
            near(CHUNKS, inner), near(small, inner), near(rows, inner),
        ], handed=handed, us=14, limit=20,
    )


def call_second_adjoint(arrays, weights, in_weight, tokens, small, reach, rank, state):
    rows, inner = arrays[4].shape
    cols = arrays[8].shape[1]
    width = tokens.shape[1]
    folds = inner // width
    fold = -(-(width + 2 * small + CHUNKS) // 64) * 64
    return call(
        functools.partial(second_adjoint, d=1, reach=reach, rank=rank, state=state, count=small),
        "adjoint_down", weights, (),
        like(in_weight, tokens) + [
            scratch(rows + 2 * CHUNKS, inner, dtype=BF16), scratch(CHUNKS, inner),
            scratch(small, inner), scratch(rows, inner), scratch(folds * fold, width), moves(2),
        ] + adjoint_scratch(rows, inner, 2 * state, reach, small, cols, rank),
        (in_weight, tokens), (), arrays,
        [
            near(CHUNKS, width), near(CHUNKS, width), near(fold, width, dtype=BF16),
            near(fold, width, dtype=BF16), near(rows, width),
        ], us=16, limit=24,
    )


def partner(axis, bit):
    return [(i, i ^ (1 << bit)) for i in range(lax.axis_size(axis))]


def bits_of(axis):
    return (lax.axis_size(axis) - 1).bit_length()


def other_core(values):
    return lax.ppermute(values, "seq", partner("seq", 0))


def next_chip(values):
    count = lax.axis_size("seq")
    pairs = [(i, i + 1) for i in range(1, count - 1, 2)]
    return lax.ppermute(values, "seq", pairs + [(j, i) for i, j in pairs])


def split_kernel(io, kept, got, own, *sent):
    count = len(sent) + 1
    rows = own.shape[0]
    here = lax.axis_index("img")
    for k in range(count):
        at = pl.ds(pl.multiple_of((here ^ k) * rows, rows), rows)
        total = kept[at, :].astype(F32) + got[at, :].astype(F32)
        if k == 0:
            own[...] = total
        else:
            sent[k - 1][...] = total.astype(BF16)


def add_kernel(io, *refs, outs):
    total = refs[0][...].astype(F32)
    for ref in refs[1 : len(refs) - outs]:
        total = total + ref[...].astype(F32)
    for ref in refs[len(refs) - outs :]:
        ref[...] = total.astype(ref.dtype)


def add(values, whole=True):
    rows, width = values[0].shape
    outs = [near(rows, width)] * whole + [near(rows, width, dtype=BF16)]
    sums = call(
        functools.partial(add_kernel, outs=len(outs)), "add", (), (), near_args=values,
        near_outs=outs, us=1, limit=2,
    )
    return sums if whole else sums[0]


def stack_kernel(io, *refs):
    for k, ref in enumerate(refs[:-1]):
        refs[-1][k] = ref[...]


def plane_pairs(k):
    return [(i, i ^ k) for i in range(lax.axis_size("img"))]


def chips_sum(kept, sent):
    count = lax.axis_size("img")
    rows, width = kept.shape
    block = (rows // count, width)
    own, *parts = call(
        split_kernel, "split", (), (), near_args=(kept, other_core(sent)),
        near_outs=[near(*block)] + [near(*block, dtype=BF16)] * (count - 1), us=1, limit=2,
    )
    got = [lax.ppermute(part, "img", plane_pairs(k + 1)) for k, part in enumerate(parts)]
    return add([own] + got)


def line_sum(total, low):
    bits = bits_of("seq")
    if bits > 3:
        return line_steps(total, low)
    count = lax.axis_size("seq")
    got = [
        lax.ppermute(low, "seq", [(i, i ^ k) for i in range(count)]) for k in range(2, count, 2)
    ]
    return add([total] + got, whole=False)


def line_steps(total, low):
    bits = bits_of("seq")
    for bit in range(1, bits):
        got = lax.ppermute(low, "seq", partner("seq", bit))
        if bit < bits - 1:
            total, low = add([total, got])
        else:
            low = add([total, got], whole=False)
    return low


def plane_gather(low):
    count = lax.axis_size("img")
    blocks = [low] + [lax.ppermute(low, "img", plane_pairs(k)) for k in range(1, count)]
    return call(
        stack_kernel, "stack", (), (), near_args=blocks,
        near_outs=[near(count, *low.shape, dtype=BF16)], us=1, limit=2,
    )[0]


def tied(first, second):
    return lax.optimization_barrier((first, second))


def body(
    tokens, cotangent, heights, widths, valid, norm_gain, in_weight, conv_weight, conv_bias,
    xproj_weight, dt_weight, dt_bias, a_log, skip, out_weight,
):
    rows, width = tokens.shape[1:]
    inner = out_weight.shape[0]
    state = a_log.shape[1]
    rank = dt_weight.shape[1]
    cols = xproj_weight.shape[2]
    taps = conv_weight.shape[1]
    reach = taps - 1
    count = bits_of("seq")
    tokens, cotangent = tokens[0], cotangent[0]
    xproj = xproj_weight.transpose(0, 2, 1)

    to_core, to_chip = call_edges(tokens, valid)
    from_core, from_chip = other_core(to_core), next_chip(to_chip)
    (
        summary, sent, delta, s, gate, dsilu, dy, tail, head, xext, proj, before, after, rate, masks,
        live, normed, nhalo, zs, dgz, cotan,
    ) = call_middle(
        heights, widths, from_core, from_chip, valid, norm_gain, conv_weight, conv_bias, xproj,
        dt_weight, dt_bias, a_log, skip, tokens, cotangent, in_weight, out_weight,
    )
    entered = None
    for bit in range(count - 1):
        got = lax.ppermute(sent, "seq", partner("seq", bit))
        summary, entered, sent = call_join(got, summary, entered, state, bit, bit == count - 2)
    got = lax.ppermute(sent, "seq", partner("seq", count - 1))
    handed = (
        delta, s, gate, dsilu, dy, tail, head, xext, proj, before, after, rate, masks, live, normed,
        nhalo,
    )
    kept, sent, carry, dz, output, *handed = call_states(
        handed, (0, 1, 5, 8, 9, 11, 12, 14), got, entered, zs, dgz, cotan, tokens, out_weight, rank,
        reach, state, count - 1,
    )

    first_sum, first_low = chips_sum(kept, sent)
    small = -(-(cols + rank + state + 2 + taps + 1) // CHUNKS) * CHUNKS
    weights = (dt_weight, xproj, conv_weight)
    handed = tuple(handed[:13]) + (carry,) + tuple(handed[13:]) + (dz,)
    rim0, small0, dx, *handed = call_first_adjoint(
        handed, tuple(range(14)), weights, small, reach, rank, state
    )
    first_sum, first_low, dx = lax.optimization_barrier((first_sum, first_low, dx))
    first_low = line_sum(first_sum, first_low)
    rim_core, rim_chip, kept, sent, dn = call_second_adjoint(
        tuple(handed[:14]) + (dx,) + tuple(handed[14:]) + (rim0, small0), weights, in_weight, tokens,
        small, reach, rank, state,
    )
    first_low, kept, sent = lax.optimization_barrier((first_low, kept, sent))
    second_sum, second_low = chips_sum(kept, sent)
    first_mine = plane_gather(first_low)
    input_grad = call(
        finish_kernel, "finish", (tokens, cotangent, valid, norm_gain), [shape(rows, width)],
        near_args=(other_core(rim_core), next_chip(rim_chip), dn), scalars=(heights, widths), us=1,
        limit=8,
    )[0]
    second_low, first_mine = tied(second_low, first_mine)
    first_other = other_core(first_mine)
    second_low = line_steps(second_sum, second_low)
    second_low, first_other, input_grad = lax.optimization_barrier((second_low, first_other, input_grad))
    second_mine = plane_gather(second_low)
    second_other = other_core(second_mine)

    fold = kept.shape[0]
    (
        in_total, conv_total, bias_total, xproj_total, dtw_total, dtb_total, a_total, skip_total,
        out_total, gain_total,
    ) = call(
        functools.partial(
            unpack_kernel, count=small, state=state, rank=rank, cols=cols, taps=taps
        ),
        "unpack", (),
        [
            shape(width, 2 * inner), shape(2, taps, inner), shape(2, inner), shape(2, cols, inner),
            shape(2, rank, inner), shape(2, inner), shape(2, state, inner), shape(2, inner),
            shape(inner, width), shape(width),
        ],
        [scratch(fold, width), scratch(fold, width)],
        near_args=(first_mine, first_other, second_mine, second_other), us=2, limit=16,
    )
    return (
        output[None], input_grad[None], gain_total, in_total, conv_total, bias_total,
        xproj_total.transpose(0, 2, 1), dtw_total, dtb_total, a_total, skip_total, out_total,
    )


def solution(mesh):
    split = P("img", "seq", None)
    placed = (split, split, P("img", None), P("img", None), P("img", "seq")) + (P(),) * 10
    return jax.shard_map(
        body,
        mesh=mesh,
        in_specs=placed,
        out_specs=(split, split) + (P(),) * 10,
        check_vma=False,
    )
```

```python
import functools

import jax
import jax.numpy as jnp
from jax import lax
from jax.experimental import pallas as pl
from jax.experimental.pallas import tpu as pltpu
from jax.sharding import PartitionSpec as P

NORM_EPS = 1e-05
CONTRACT_ROWS = (((0,), (0,)), ((), ()))
CONTRACT_COLS = (((1,), (1,)), ((), ()))
LOG2E = 1.4426950408889634
LN2 = 0.6931471805599453
BREAK = 1e30
CHUNKS = 8
LANES = 128
SUMMARY_STATES = 8
SUMMARY_UNROLL = 8
STATES_UNROLL = 8
ADJOINT_STATES = 8
ADJOINT_UNROLL = 4
F32 = jnp.float32
BF16 = jnp.bfloat16


def dot(a, b):
    return jnp.dot(a, b, preferred_element_type=F32)


def dot_rows(a, b):
    return lax.dot_general(a, b, CONTRACT_ROWS, preferred_element_type=F32)


def dot_cols(a, b):
    return lax.dot_general(a, b, CONTRACT_COLS, preferred_element_type=F32)


def sigmoid(v):
    return 1.0 / (1.0 + jnp.exp(-v))


def fetch(source, target, semaphore):
    copy = pltpu.make_async_copy(source, target, semaphore)
    copy.start()
    return copy


def lanes_of(tile):
    return pl.ds(pl.multiple_of(tile * LANES, LANES), LANES)


def rows_of(j, count=CHUNKS):
    return pl.ds(pl.multiple_of(j * CHUNKS, CHUNKS), count)


def chunk_order(rows):
    row = lax.broadcasted_iota(jnp.int32, (rows, rows), 0)
    slot = lax.broadcasted_iota(jnp.int32, (rows, rows), 1)
    return slot == (row & (CHUNKS - 1)) * (rows // CHUNKS) + (row >> 3)


def image_ends(heights, widths):
    ends, total = [], 0
    for i in range(heights.shape[1]):
        total = total + heights[0, i] * widths[0, i]
        ends.append(total)
    return ends


def segment_of(places, ends):
    found = jnp.zeros_like(places)
    for end in ends:
        found = found + (places >= end).astype(jnp.int32)
    return found


def places_of(first, rows):
    row = lax.broadcasted_iota(jnp.int32, (rows, LANES), 0)
    return first + (row & (CHUNKS - 1)) * (rows // CHUNKS) + (row >> 3)


def edges_kernel(io, tokens, valid, to_core, to_chip):
    rows = tokens.shape[0]
    edge = to_core.shape[0]
    io.ready()
    row = lax.broadcasted_iota(jnp.int32, (edge, rows), 0)
    slot = lax.broadcasted_iota(jnp.int32, (edge, rows), 1)
    held = jnp.broadcast_to(valid[...].astype(F32), (edge, rows))
    first = jnp.where(slot == row, held, 0.0).astype(BF16)
    last = jnp.where(slot == rows - edge + row, held, 0.0).astype(BF16)
    first = dot(first, tokens[...]).astype(BF16)
    last = dot(last, tokens[...]).astype(BF16)
    even = (lax.axis_index("seq") & 1) == 0
    to_core[...] = jnp.where(even, last, first)
    to_chip[...] = jnp.where(even, first, last)


def spread(values, target):
    count = values.shape[1]
    high = values.astype(BF16)
    low = (values - high.astype(F32)).astype(BF16)
    both = jnp.concatenate([high, low], axis=1)
    wide = 2 * LANES
    column = lax.broadcasted_iota(jnp.int32, (2 * count, wide), 0)
    block = lax.broadcasted_iota(jnp.int32, (2 * count, wide), 1) // LANES
    for at in range(0, count * LANES, wide):
        place = block + at // LANES
        pick = ((column == place) | (column == place + count)).astype(BF16)
        target[:, at : at + wide] = dot(both, pick)


def windows(span, up, sublane):
    sign = 1 if up else -1

    def from_before(value, by, fill):
        moved = pltpu.roll(value, (sign * by) % CHUNKS, axis=0)
        kept = sublane >= by if up else sublane < CHUNKS - by
        return jnp.where(kept, moved, fill)

    two = span + from_before(span, 1, 0.0)
    four = two + from_before(two, 2, 0.0)
    eight = four + from_before(four, 4, 0.0)
    edge = [jnp.where(sublane >= by if up else sublane < CHUNKS - by, 0.0, BREAK) for by in (1, 2, 4)]
    return (span + edge[0], two + edge[1], four + edge[2]), from_before(eight, 1, 0.0)


def chain(rate, sums, tail, up, sublane):
    sign = 1 if up else -1
    for by, span in zip((1, 2, 4), sums):
        tail = jnp.exp2(rate * span) * pltpu.roll(tail, (sign * by) % CHUNKS, axis=0) + tail
    end = CHUNKS - 1 if up else 0
    kept = sublane >= 1 if up else sublane < CHUNKS - 1
    return jnp.where(kept, pltpu.roll(tail, sign % CHUNKS, axis=0), 0.0), tail[end : end + 1]


def middle_kernel(
    io, from_core, from_chip, heights, widths, valid, gain, conv_weight, conv_bias, xproj, dt_weight,
    dt_bias, a_log, skip,
    tokens_far, cotangent_far, in_far, out_far,
    sum_out, sent_out, delta_out, s_out, dsilu_out, dy, tail_out, head_out, xext_out,
    proj_out, before_out, after_out, rate_out, masks, live, normed_out, nhalo_out, zs_out, dgz_out,
    cotan,
    tokens, cotangent, in_weight, out_weight, normed, same_out, low_out, bc, tails, heads, spans, ins,
    *, reach,
):
    rows, width = tokens.shape
    inner = out_weight.shape[0]
    steps = rows // CHUNKS
    state = a_log.shape[1]
    rank = dt_weight.shape[1]
    tiles = inner // LANES
    arriving = [
        fetch(source, target, ins.at[i])
        for i, (source, target) in enumerate(
            (
                (tokens_far, tokens), (in_far, in_weight), (cotangent_far, cotangent),
                (out_far, out_weight),
            )
        )
    ]
    io.ready()
    start = lax.axis_index("seq") * rows
    slots = lax.axis_size("seq") * rows
    even = (lax.axis_index("seq") & 1) == 0
    ends = image_ends(heights, widths)
    images = heights.shape[1]
    sublane = lax.broadcasted_iota(jnp.int32, (CHUNKS, LANES), 0)

    order = chunk_order(rows)
    order_low = order.astype(BF16)
    picked = jnp.where(order, jnp.broadcast_to(valid[...].astype(F32), order.shape), 0.0)
    alive = dot(picked.astype(BF16), jnp.ones((rows, LANES), BF16))
    places = places_of(start, rows)
    segment = segment_of(places, ends)
    live[...] = jnp.where(segment < images, alive, 0.0)
    column = lax.broadcasted_iota(jnp.int32, (rows, LANES), 1)
    compact = jnp.zeros((rows, LANES), F32)
    for k in range(1, reach + 1):
        same = (segment_of(places - k, ends) == segment) & (places >= k)
        same = same.astype(F32)
        same_out[(k - 1) * rows : k * rows, :] = same
        compact = jnp.where(column == k - 1, same, compact)
        same = (segment_of(places + k, ends) == segment) & (places + k < slots)
        same = same.astype(F32)
        same_out[(reach + k - 1) * rows : (reach + k) * rows, :] = same
        compact = jnp.where(column == reach + k - 1, same, compact)
    masks[...] = compact

    arriving[0].wait()
    inputs = dot(order_low, tokens[...])
    inv_rms = lax.rsqrt(jnp.mean(inputs * inputs, axis=-1, keepdims=True) + NORM_EPS)
    gains = gain[...].astype(F32).reshape(1, width)
    scaled = inputs * inv_rms * gains
    normed[0:rows, :] = scaled.astype(BF16)
    live_wide = jnp.concatenate([live[...]] * (width // LANES), axis=1)
    normed[rows : 2 * rows, :] = (scaled * live_wide).astype(BF16)
    normed_out[...] = normed[0:rows, :]
    before = jnp.where(even, from_chip[...], from_core[...])
    after = jnp.where(even, from_core[...], from_chip[...])
    htok = jnp.concatenate([before[CHUNKS:], after[:CHUNKS]], axis=0)
    hrow = lax.broadcasted_iota(jnp.int32, (2 * CHUNKS, LANES), 0)
    hplace = jnp.where(hrow < CHUNKS, start - CHUNKS + hrow, start + rows + hrow - CHUNKS)
    hlive = (segment_of(hplace, ends) < images).astype(F32)
    htok = htok.astype(F32) * jnp.concatenate([hlive] * (width // LANES), axis=1)
    hinv = lax.rsqrt(jnp.mean(htok * htok, axis=-1, keepdims=True) + NORM_EPS)
    scaled = htok * hinv
    nhalo = (scaled * gains).astype(BF16)
    nhalo_out[...] = jnp.concatenate([nhalo, scaled.astype(BF16)], axis=0)
    arriving[1].wait()
    step = 2 * LANES
    both = jnp.concatenate([normed[rows : 2 * rows, :], nhalo], axis=0)
    wide = lax.broadcasted_iota(jnp.int32, (CHUNKS, step), 0)
    for at in range(0, inner, step):
        lanes = slice(at, at + step)
        x = dot(both, in_weight[:, lanes]).astype(BF16).astype(F32)
        xext_out[reach * CHUNKS : (reach + steps) * CHUNKS, lanes] = x[:rows]
        for i in range(reach):
            to = steps - reach + i
            moved = pltpu.roll(x[to * CHUNKS : (to + 1) * CHUNKS, :], 1, axis=0)
            of = rows + CHUNKS - reach + i
            xext_out[i * CHUNKS : (i + 1) * CHUNKS, lanes] = jnp.where(
                wide == 0, x[of : of + 1], moved
            )
            moved = pltpu.roll(x[i * CHUNKS : (i + 1) * CHUNKS, :], CHUNKS - 1, axis=0)
            to = reach + steps + i
            of = rows + CHUNKS + i
            xext_out[to * CHUNKS : (to + 1) * CHUNKS, lanes] = jnp.where(
                wide == CHUNKS - 1, x[of : of + 1], moved
            )

    arriving[2].wait()
    arriving[3].wait()
    cotan[...] = dot(order_low, cotangent[...]).astype(BF16)
    block = 32
    for at in range(0, inner, step):
        lanes = slice(at, at + step)
        zs_out[:, lanes] = dot(normed[0:rows, :], in_weight[:, inner + at : inner + at + step])
        dgz_out[:, lanes] = dot_cols(cotan[...], out_weight[lanes, :])

    def gate_block(b, _):
        here = pl.ds(pl.multiple_of(b * block, block), block)
        alive = live[here, :]
        for tile in range(tiles):
            lanes = slice(tile * LANES, (tile + 1) * LANES)
            z = zs_out[here, lanes]
            grad = dgz_out[here, lanes] * alive
            gate = sigmoid(z)
            zs = z * gate * alive
            zs_out[here, lanes] = zs
            dy[here, lanes] = 0.5 * grad * zs
            dgz_out[here, lanes] = grad * (gate * (1.0 + z * (1.0 - gate)))
        return 0

    lax.fori_loop(0, rows // block, gate_block, 0)

    taps = reach + 1
    conv_w = [conv_weight[d].astype(F32) for d in range(2)]
    conv_b = conv_bias[...].astype(F32)
    for tile in range(tiles):
        lanes = slice(tile * LANES, (tile + 1) * LANES)

        def conv_block(b, _, lanes=lanes):
            at = pl.multiple_of(b * block, block)
            for d in range(2):
                total = conv_b[d : d + 1, lanes] + conv_w[d][reach:taps, lanes] * (
                    xext_out[pl.ds(at + reach * CHUNKS, block), lanes]
                )
                for k in range(1, taps):
                    move = reach - k if d == 0 else reach + k
                    mask = same_out[pl.ds((d * reach + k - 1) * rows + at, block), :]
                    total = total + conv_w[d][reach - k : taps - k, lanes] * (
                        xext_out[pl.ds(at + move * CHUNKS, block), lanes] * mask
                    )
                gate = sigmoid(total)
                value = total * gate
                s_out[pl.ds(d * rows + at, block), lanes] = value
                low_out[pl.ds(d * rows + at, block), lanes] = value.astype(BF16)
                dsilu_out[pl.ds(d * rows + at, block), lanes] = gate * (1.0 + total * (1.0 - gate))
            return 0

        lax.fori_loop(0, rows // block, conv_block, 0)

    dt_b = dt_bias[...].astype(F32)
    for d in range(2):
        rate_out[d * state : (d + 1) * state, :] = jnp.minimum(
            -LOG2E * jnp.exp(a_log[d].astype(F32)), -1e-20
        )
        here = slice(d * rows, (d + 1) * rows)
        proj = dot_cols(low_out[here, :], xproj[d])
        proj_out[here, :] = proj
        dt_low = proj[:, :rank].astype(BF16)
        for at in range(0, inner, step):
            lanes = slice(at, at + step)
            delta_out[here, lanes] = dot(dt_low, dt_weight[d, :, lanes])
        spread(proj[:, rank:], bc)

        def delta_block(b, _, d=d):
            alive = live[pl.ds(pl.multiple_of(b * block, block), block), :]
            here = pl.ds(pl.multiple_of(d * rows + b * block, block), block)
            for tile in range(tiles):
                lanes = slice(tile * LANES, (tile + 1) * LANES)
                pre = delta_out[here, lanes] + dt_b[d : d + 1, lanes]
                small = jnp.exp(-jnp.abs(pre))
                log1p = jnp.where(small < 1e-4, small * (1.0 - 0.5 * small), jnp.log(1.0 + small))
                delta_out[here, lanes] = (jnp.maximum(pre, 0.0) + log1p) * alive
            return 0

        lax.fori_loop(0, rows // block, delta_block, 0)
        some = SUMMARY_STATES

        def scan_tile(tile, _, d=d):
            lanes = lanes_of(tile)
            for low in range(0, state, some):
                rates = [
                    jnp.broadcast_to(
                        rate_out[d * state + low + m : d * state + low + m + 1, lanes],
                        (CHUNKS, LANES),
                    )
                    for m in range(some)
                ]

                def scan_step(i, carried, d=d, low=low, rates=rates):
                    tail, lead, head, span = carried
                    j = i if d == 0 else steps - 1 - i
                    at = pl.multiple_of(j * CHUNKS, CHUNKS)
                    keep = same_out[pl.ds(d * reach * rows + at, CHUNKS), :]
                    delta = delta_out[pl.ds(d * rows + at, CHUNKS), lanes]
                    drive = delta * s_out[pl.ds(d * rows + at, CHUNKS), lanes]
                    back = dy[pl.ds(at, CHUNKS), lanes]
                    delta = jnp.where(keep > 0.0, delta, BREAK)
                    tail, lead, head = list(tail), list(lead), list(head)
                    for m in range(some):
                        b = bc[pl.ds(at, CHUNKS), (low + m) * LANES : (low + m + 1) * LANES]
                        n = state + low + m
                        c = bc[pl.ds(at, CHUNKS), n * LANES : (n + 1) * LANES]
                        decay = jnp.exp2(delta * rates[m])
                        tail[m] = decay * tail[m] + b * drive
                        lead[m] = lead[m] * decay
                        head[m] = head[m] + lead[m] * (c * back)
                    return tuple(tail), tuple(lead), tuple(head), span + delta

                zeros = tuple(jnp.zeros((CHUNKS, LANES), F32) for _ in range(some))
                ones = tuple(jnp.ones((CHUNKS, LANES), F32) for _ in range(some))
                tail, lead, head, span = lax.fori_loop(
                    0, steps, scan_step, (zeros, ones, zeros, zeros[0]), unroll=SUMMARY_UNROLL
                )
                for m in range(some):
                    tails[low + m, :, lanes] = tail[m]
                    heads[low + m, :, lanes] = head[m]
                spans[:, lanes] = span
            return 0

        lax.fori_loop(0, tiles, scan_tile, 0)

        tail_row = 0 if d == 0 else 2 * state
        head_row = 3 * state if d == 0 else state

        def chain_tile(tile, _, d=d, tail_row=tail_row, head_row=head_row):
            lanes = lanes_of(tile)
            span = spans[:, lanes]
            sums, before = windows(span, d == 0, sublane)
            sums_back, after = windows(span, d == 1, sublane)
            before_out[d * CHUNKS : (d + 1) * CHUNKS, lanes] = before
            after_out[d * CHUNKS : (d + 1) * CHUNKS, lanes] = after
            for n in range(state):
                rate = jnp.broadcast_to(
                    rate_out[d * state + n : d * state + n + 1, lanes], (CHUNKS, LANES)
                )
                carried, total = chain(rate, sums, tails[n, :, lanes], d == 0, sublane)
                tail_out[d * state + n, :, lanes] = carried
                sum_out[tail_row + n : tail_row + n + 1, lanes] = total
                carried, total = chain(rate, sums_back, heads[n, :, lanes], d == 1, sublane)
                head_out[d * state + n, :, lanes] = carried
                sum_out[head_row + n : head_row + n + 1, lanes] = total
            return 0

        lax.fori_loop(0, tiles, chain_tile, 0)
        sum_out[4 * state + d : 4 * state + d + 1, :] = jnp.sum(spans[...], axis=0, keepdims=True)
    at = 4 * state + CHUNKS
    sum_out[4 * state + 2 : at, :] = jnp.zeros((CHUNKS - 2, inner), F32)
    sum_out[at:, :] = rate_out[0 : 2 * state, :]
    sent_out[...] = packed(sum_out[0:at, :], state)
    rate_out[2 * state : 2 * state + 2, :] = skip[...].astype(F32)


def packed(summary, state):
    rest = summary[4 * state :]
    high = rest.astype(BF16)
    low = (rest - high.astype(F32)).astype(BF16)
    return jnp.concatenate([summary[: 4 * state].astype(BF16), high, low], axis=0)


def leads(rate, spans, state, flip):
    parts = [jnp.exp2(rate[d * state : (d + 1) * state] * spans[d : d + 1]) for d in range(2)]
    return jnp.concatenate(parts[::-1] if flip else parts, axis=0)


def join_kernel(io, got, summary, entered, *outs, state, bit, final):
    half = 2 * state
    upper = ((lax.axis_index("seq") >> bit) & 1) == 1
    mine = summary[0 : 2 * half + CHUNKS, :]
    rates = summary[2 * half + CHUNKS :, :]
    entered_out, sent_out = outs[-2], outs[-1]
    values = got[...].astype(F32)
    spans = mine[4 * state : 4 * state + 2]
    other = values[4 * state : 4 * state + 2] + values[4 * state + CHUNKS : 4 * state + CHUNKS + 2]
    if entered is None:
        entered_up = jnp.where(upper, values[:half], 0.0)
        entered_down = jnp.where(upper, 0.0, values[half : 2 * half])
        span_up = jnp.where(upper, other, 0.0)
        span_down = jnp.where(upper, 0.0, other)
    else:
        held = entered[...]
        span_up, span_down = held[2 * half : 2 * half + 2], held[2 * half + 2 : 2 * half + 4]
        entered_up = held[:half] + jnp.where(
            upper, leads(rates, span_up, state, False) * values[:half], 0.0
        )
        entered_down = held[half : 2 * half] + jnp.where(
            upper, 0.0, leads(rates, span_down, state, True) * values[half : 2 * half]
        )
        span_up = span_up + jnp.where(upper, other, 0.0)
        span_down = span_down + jnp.where(upper, 0.0, other)
    entered_out[0:half, :] = entered_up
    entered_out[half : 2 * half, :] = entered_down
    entered_out[2 * half :, :] = jnp.concatenate(
        [span_up, span_down, jnp.zeros((CHUNKS - 4, mine.shape[1]), F32)], axis=0
    )
    low_up = jnp.where(upper, values[:half], mine[:half])
    high_up = jnp.where(upper, mine[:half], values[:half])
    low_down = jnp.where(upper, values[half : 2 * half], mine[half : 2 * half])
    high_down = jnp.where(upper, mine[half : 2 * half], values[half : 2 * half])
    low_span, high_span = jnp.where(upper, other, spans), jnp.where(upper, spans, other)
    up = leads(rates, high_span, state, False) * low_up + high_up
    down = leads(rates, low_span, state, True) * high_down + low_down
    if final:
        next_upper = ((lax.axis_index("seq") >> (bit + 1)) & 1) == 1
        sent_out[...] = jnp.where(next_upper, down, up).astype(BF16)
    else:
        total = jnp.concatenate(
            [up, down, spans + other, jnp.zeros((CHUNKS - 2, mine.shape[1]), F32)], axis=0
        )
        outs[0][0 : 2 * half + CHUNKS, :] = total
        outs[0][2 * half + CHUNKS :, :] = rates
        sent_out[...] = packed(total, state)


def first_join(io, got, summary, *outs, state, bit, final):
    join_kernel(io, got, summary, None, *outs, state=state, bit=bit, final=final)


def state_block(j, state):
    return pl.multiple_of(j * state * CHUNKS, CHUNKS)


def states_pass(d, steps, state, rates, begin, delta, s, keep, bc, h_out, y):
    start = state_block(0 if d == 0 else steps, state)
    for n in range(state):
        h_out[pl.ds(start + n * CHUNKS, CHUNKS), :] = begin[n]

    def step(i, h):
        j = i if d == 0 else steps - 1 - i
        here = pl.ds(pl.multiple_of(j * CHUNKS, CHUNKS), CHUNKS)
        to = state_block(j + 1 if d == 0 else j, state)
        size = delta[here, :]
        drive = size * s[here, :]
        size = jnp.where(keep[here, :] > 0.0, size, BREAK)
        h = list(h)
        total = None if d == 0 else y[here, :]
        for n in range(state):
            b = bc[here, n * LANES : (n + 1) * LANES]
            c = bc[here, (state + n) * LANES : (state + n + 1) * LANES]
            h[n] = jnp.exp2(size * rates[n]) * h[n] + b * drive
            h_out[pl.ds(to + n * CHUNKS, CHUNKS), :] = h[n]
            total = c * h[n] if total is None else total + c * h[n]
        y[here, :] = total
        return tuple(h)

    lax.fori_loop(0, steps, step, tuple(begin), unroll=STATES_UNROLL)


def adjoint_pass(
    d, steps, state, rates, back, delta, s, dy, keep, skip, bc, h_in, sums,
    dpre_out, ds_out, rows_out,
):
    some = ADJOINT_STATES
    edge = steps - 1
    skip = skip[...]
    zeros = jnp.zeros((CHUNKS, LANES), F32)
    grads = []
    for low in range(0, state, some):
        final = low + some == state

        def step(i, carried, low=low, final=final):
            g, acc, h, skip_acc, bias_acc = carried
            j = edge - i if d == 0 else i
            here = pl.ds(pl.multiple_of(j * CHUNKS, CHUNKS), CHUNKS)
            size = delta[here, :]
            value = s[here, :]
            grad = dy[here, :]
            drive = size * value
            masked = jnp.where(keep[here, :] > 0.0, size, BREAK)
            prev = state_block(j if d == 0 else j + 1, state)
            g, acc, h = list(g), list(acc), list(h)
            weighted = zeros if low == 0 else ds_out[here, :]
            rate_sum = zeros if low == 0 else dpre_out[here, :]
            for m in range(some):
                n = low + m
                b = bc[here, n * LANES : (n + 1) * LANES]
                c = bc[here, (state + n) * LANES : (state + n + 1) * LANES]
                adjoint = c * grad + g[m]
                before = h_in[pl.ds(prev + n * CHUNKS, CHUNKS), :]
                sums[here, n * LANES : (n + 1) * LANES] += adjoint * drive
                sums[here, (state + n) * LANES : (state + n + 1) * LANES] += grad * h[m]
                g[m] = adjoint * jnp.exp2(masked * rates[n])
                held = g[m] * before
                weighted = weighted + adjoint * b
                rate_sum = rate_sum + held * rates[n]
                acc[m] = acc[m] + held * masked
                h[m] = before
            if final:
                ds_out[here, :] = skip * grad + size * weighted
                gate = jnp.where(
                    size < 0.01, size * (1.0 - size * (0.5 - size * (1.0 / 6.0))), 1.0 - jnp.exp(-size)
                )
                pre = ((LN2 * rate_sum + weighted * value) * gate).astype(BF16).astype(F32)
                dpre_out[here, :] = pre
                bias_acc = bias_acc + pre
                skip_acc = skip_acc + grad * value
            else:
                dpre_out[here, :] = rate_sum
                ds_out[here, :] = weighted
            return tuple(g), tuple(acc), tuple(h), skip_acc, bias_acc

        last = state_block(steps if d == 0 else 0, state)
        h_last = tuple(h_in[pl.ds(last + (low + m) * CHUNKS, CHUNKS), :] for m in range(some))
        none = tuple(zeros for _ in range(some))
        _, acc, _, skip_acc, bias_acc = lax.fori_loop(
            0, steps, step, (tuple(back[low : low + some]), none, h_last, zeros, zeros),
            unroll=ADJOINT_UNROLL,
        )
        grads.extend(acc)
    for n in range(state):
        rows_out[n : n + 1, :] = jnp.sum(grads[n], axis=0, keepdims=True) * rates[n][0:1] * LN2
    rows_out[state : state + 1, :] = jnp.sum(bias_acc, axis=0, keepdims=True)
    rows_out[state + 1 : state + 2, :] = jnp.sum(skip_acc, axis=0, keepdims=True)


def lane_sums(sums, state):
    depth = 2 * state * LANES
    block = lax.broadcasted_iota(jnp.int32, (depth, LANES), 0) // LANES
    column = lax.broadcasted_iota(jnp.int32, (depth, LANES), 1)
    return dot(sums.astype(BF16), (block == column).astype(BF16))[:, : 2 * state]


def rate_tiles(rate, d, state, lanes):
    return [
        jnp.broadcast_to(rate[d * state + n : d * state + n + 1, lanes], (CHUNKS, LANES))
        for n in range(state)
    ]


def begin_tiles(rates, passed, maps, carry, at, d, state, lanes):
    passed = passed[d * CHUNKS : (d + 1) * CHUNKS, lanes]
    return [
        jnp.exp2(rates[n] * passed) * carry[at + n : at + n + 1, lanes]
        + maps[d * state + n, :, lanes]
        for n in range(state)
    ]


def slot_order(rows):
    row = lax.broadcasted_iota(jnp.int32, (rows, rows), 1)
    slot = lax.broadcasted_iota(jnp.int32, (rows, rows), 0)
    return (slot == (row & (CHUNKS - 1)) * (rows // CHUNKS) + (row >> 3)).astype(BF16)


def states_kernel(
    io, delta, s, proj, rate, masks, normed, before, tail, got, entered, zs, dgz, cotan,
    kept, sent, carry_out, dz, h0, h1, gated,
    bc, keep, y,
    *, reach, rank, state, bit,
):
    rows, inner = zs.shape
    width = cotan.shape[1]
    steps = rows // CHUNKS
    half = 2 * state
    tiles = inner // LANES
    upper = ((lax.axis_index("seq") >> bit) & 1) == 1
    values = got[...].astype(F32)
    held = entered[...]
    rates = rate[0:half, :]
    carry_out[0:half, :] = held[:half] + jnp.where(
        upper, leads(rates, held[2 * half : 2 * half + 2], state, False) * values, 0.0
    )
    carry_out[half : 2 * half, :] = held[half : 2 * half] + jnp.where(
        upper, 0.0, leads(rates, held[2 * half + 2 : 2 * half + 4], state, True) * values
    )
    spread(jnp.concatenate([masks[:, 0:1], masks[:, reach : reach + 1]], axis=1), keep)
    for d, h in enumerate((h0, h1)):
        mine = slice(d * rows, (d + 1) * rows)
        spread(proj[mine, rank:], bc)

        def scan_tile(tile, _, d=d, h=h, mine=mine):
            lanes = lanes_of(tile)
            rates = rate_tiles(rate, d, state, lanes)
            begin = begin_tiles(rates, before, tail, carry_out, d * half, d, state, lanes)
            states_pass(
                d, steps, state, rates, begin, delta.at[mine, lanes], s.at[mine, lanes],
                keep.at[:, d * LANES : (d + 1) * LANES], bc, h.at[tile], y.at[:, lanes],
            )
            return 0

        lax.fori_loop(0, tiles, scan_tile, 0)
    block = 32

    def gate_block(b, _):
        here = pl.ds(pl.multiple_of(b * block, block), block)
        there = pl.ds(pl.multiple_of(rows + b * block, block), block)
        for tile in range(tiles):
            lanes = slice(tile * LANES, (tile + 1) * LANES)
            total = 0.5 * (
                y[here, lanes] + rate[half : half + 1, lanes] * s[here, lanes]
                + rate[half + 1 : half + 2, lanes] * s[there, lanes]
            )
            gated[here, lanes] = (total * zs[here, lanes]).astype(BF16)
            dz[here, lanes] = (total * dgz[here, lanes]).astype(BF16)
        return 0

    lax.fori_loop(0, rows // block, gate_block, 0)
    even = (lax.axis_index("seq") & 1) == 0
    out_grad = dot_rows(gated[...], cotan[...]).astype(BF16)
    z_grad = jnp.concatenate(
        [dot_rows(normed[...], dz[:, at : at + width]) for at in range(0, inner, width)], axis=0
    ).astype(BF16)
    sent[...] = jnp.where(even, z_grad, out_grad)
    kept[...] = jnp.where(even, out_grad, z_grad)


def output_kernel(io, gated, tokens, out_weight, output):
    ordered = dot(slot_order(gated.shape[0]), gated[...]).astype(BF16)
    io.ready()
    output[...] = (tokens[...].astype(F32) + dot(ordered, out_weight[...])).astype(BF16)


def adjoint_kernel(
    io, delta, s, dsilu, dy, head, xext, proj, after, rate, masks, carry, h, dx_in,
    dt_weight, xproj, conv_weight,
    dc_rim, small_out, dx_out,
    bc, same, sums, dpre, ds, rows_out, ext,
    *, d, reach, rank, state,
):
    rows, inner = dy.shape
    steps = rows // CHUNKS
    half = 2 * state
    tiles = inner // LANES
    taps = reach + 1
    cols = proj.shape[1]
    mine = slice(d * rows, (d + 1) * rows)
    spread(proj[mine, rank:], bc)
    spread(masks[:, 0 : 2 * reach], same)
    keep = same.at[:, d * reach * LANES : (d * reach + 1) * LANES]
    sums[...] = jnp.zeros_like(sums)
    rows_out[...] = jnp.zeros_like(rows_out)
    grad_at = (half if d == 0 else 0) + state

    def scan_tile(tile, _):
        lanes = lanes_of(tile)
        rates = rate_tiles(rate, d, state, lanes)
        back = begin_tiles(rates, after, head, carry, grad_at, d, state, lanes)
        adjoint_pass(
            d, steps, state, rates, back, delta.at[mine, lanes], s.at[mine, lanes],
            dy.at[:, lanes], keep, rate.at[half + d : half + d + 1, lanes], bc,
            h.at[tile], sums, dpre.at[:, lanes], ds.at[:, lanes], rows_out.at[:, lanes],
        )
        return 0

    lax.fori_loop(0, tiles, scan_tile, 0)
    io.ready()
    dpre_low = dpre[...].astype(BF16)
    dt_grad = dot_rows(proj[mine, :rank].astype(BF16), dpre_low)
    dt_back = dot_cols(dpre_low, dt_weight[d])
    dproj = jnp.concatenate([dt_back, lane_sums(sums[...], state)], axis=1).astype(BF16)
    small_out[0:cols, :] = dot_rows(dproj, s[mine, :].astype(BF16))
    small_out[cols : cols + rank, :] = dt_grad
    base = 0 if d == 0 else reach * CHUNKS
    step = 2 * LANES
    for lane in range(0, inner, step):
        lanes = slice(lane, lane + step)
        total = ds[:, lanes] + dot(dproj, xproj[d, :, lanes])
        ext[base : base + rows, lanes] = (total * dsilu[mine, lanes]).astype(BF16).astype(F32)
    wide = lax.broadcasted_iota(jnp.int32, (CHUNKS, inner), 0)
    for i in range(reach):
        if d == 0:
            moved = pltpu.roll(ext[i * CHUNKS : (i + 1) * CHUNKS, :], CHUNKS - 1, axis=0)
            ext[rows + i * CHUNKS : rows + (i + 1) * CHUNKS, :] = jnp.where(
                wide == CHUNKS - 1, 0.0, moved
            )
        else:
            moved = pltpu.roll(ext[rows + i * CHUNKS : rows + (i + 1) * CHUNKS, :], 1, axis=0)
            ext[i * CHUNKS : (i + 1) * CHUNKS, :] = jnp.where(wide == 0, 0.0, moved)

    conv_w = conv_weight[d].astype(F32)
    block = 32
    zeros = jnp.zeros((CHUNKS, LANES), F32)

    def folded(values):
        return functools.reduce(
            lambda a, b: a + b, [values[i : i + CHUNKS] for i in range(0, block, CHUNKS)]
        )

    base_row = cols + rank
    for tile in range(tiles):
        lanes = slice(tile * LANES, (tile + 1) * LANES)
        weight = conv_w[:, lanes]

        def conv_block(b, totals, lanes=lanes, weight=weight):
            here = pl.multiple_of(b * block, block)
            totals = list(totals)
            mid = ext[pl.ds(here + base, block), lanes]
            total = weight[reach:taps] * mid
            totals[reach] = totals[reach] + folded(mid * xext[pl.ds(here + reach * CHUNKS, block), lanes])
            totals[taps] = totals[taps] + folded(mid)
            for k in range(1, taps):
                past = same[pl.ds(here, block), (k - 1) * LANES : k * LANES]
                ahead = same[pl.ds(here, block), (reach + k - 1) * LANES : (reach + k) * LANES]
                if d == 0:
                    given = ext[pl.ds(here + k * CHUNKS, block), lanes] * ahead
                    taken = xext[pl.ds(here + (reach - k) * CHUNKS, block), lanes] * past
                else:
                    given = ext[pl.ds(here + (reach - k) * CHUNKS, block), lanes] * past
                    taken = xext[pl.ds(here + (reach + k) * CHUNKS, block), lanes] * ahead
                total = total + weight[reach - k : taps - k] * given
                totals[reach - k] = totals[reach - k] + folded(mid * taken)
            if dx_in is not None:
                total = total + dx_in[pl.ds(here, block), lanes]
            dx_out[pl.ds(here, block), lanes] = total
            return tuple(totals)

        totals = lax.fori_loop(0, rows // block, conv_block, (zeros,) * (taps + 1))
        for i in range(taps + 1):
            at = state + 2 + i
            rows_out[at : at + 1, lanes] = jnp.sum(totals[i], axis=0, keepdims=True)

    edge = []
    for i in range(CHUNKS):
        row = jnp.zeros((1, inner), F32)
        for k in range(1, taps):
            j = i - CHUNKS + k if d == 0 else steps + i - k
            if (d == 0 and j >= 0) or (d == 1 and j < steps):
                sub = 0 if d == 0 else CHUNKS - 1
                at = j * CHUNKS + sub
                column = (d * reach + k - 1) * LANES
                mask = jnp.concatenate([same[at : at + 1, column : column + LANES]] * tiles, axis=1)
                at = base + j * CHUNKS + sub
                row = row + conv_w[reach - k : taps - k] * ext[at : at + 1, :] * mask
        edge.append(row)
    dc_rim[...] = jnp.concatenate(edge, axis=0)
    small_out[base_row:, :] = rows_out[0 : small_out.shape[0] - base_row, :]


def first_adjoint(io, *refs, **static):
    adjoint_kernel(io, *refs[:12], None, *refs[12:], **static)


def second_adjoint(io, *refs, **static):
    in_far, in_near, moves = refs[16], refs[20], refs[21]
    copy = fetch(in_far, in_near, moves.at[0])
    adjoint_kernel(io, *refs[:16], *refs[17:20], *refs[22:], **static)
    copy.wait()


def last_kernel(
    io, dx, rim0, rim1, small0, small1, normed, nhalo, live, in_weight,
    kept, sent, low,
    lines, grads,
):
    rows, inner = dx.shape
    width = normed.shape[1]
    folds = inner // width
    fold = kept.shape[0]
    edges = 2 * CHUNKS
    for tile in range(inner // LANES):
        lanes = slice(tile * LANES, (tile + 1) * LANES)
        lines[0:rows, lanes] = (dx[:, lanes] * live[...]).astype(BF16)
    low[...] = lines[0:rows, :]
    lines[rows : rows + edges, :] = jnp.concatenate([rim0[...], rim1[...]], axis=0).astype(BF16)
    both = jnp.concatenate([normed[...], nhalo[0:edges, :]], axis=0)
    size = small0.shape[0]
    for i in range(folds):
        lanes = slice(i * width, (i + 1) * width)
        at = i * fold
        grads[at : at + width, :] = dot_rows(both, lines[:, lanes]).astype(BF16)
        at += width
        grads[at : at + 2 * size, :] = jnp.concatenate(
            [small0[:, lanes], small1[:, lanes]], axis=0
        ).astype(BF16)
        at += 2 * size
        grads[at : (i + 1) * fold, :] = jnp.zeros(((i + 1) * fold - at, width), BF16)
    rim = dot_cols(lines[rows : rows + edges, :], in_weight[:, 0:inner])
    even = (lax.axis_index("seq") & 1) == 0
    turned = jnp.concatenate([rim[CHUNKS:], rim[:CHUNKS]], axis=0)
    left, right = grads[0:fold, :], grads[fold : 2 * fold, :]
    kept[...] = jnp.where(even, left, right)
    sent[...] = jnp.where(even, right, left)
    at = width + 2 * size
    sent[at : at + edges, :] = jnp.where(even, turned, rim).astype(BF16)


def finish_kernel(
    io, low, dz, in_weight, rims, chip_rim, heights, widths, tokens, cotangent, valid, gain,
    input_grad,
):
    rows, width = tokens.shape
    inner = low.shape[1]
    even = (lax.axis_index("seq") & 1) == 0
    start = lax.axis_index("seq") * rows
    back = slot_order(rows)
    dn = dot_cols(dot(back, low[...]).astype(BF16), in_weight[:, 0:inner]) + dot_cols(
        dot(back, dz[...]).astype(BF16), in_weight[:, inner : 2 * inner]
    )
    io.ready()
    from_core = rims[0:CHUNKS, :].astype(F32)
    from_chip = chip_rim[CHUNKS : 2 * CHUNKS, :].astype(F32)
    before = jnp.where(even, from_chip, from_core)
    after = jnp.where(even, from_core, from_chip)
    end = image_ends(heights, widths)[-1]
    row = lax.broadcasted_iota(jnp.int32, (CHUNKS, rows), 0)
    slot = lax.broadcasted_iota(jnp.int32, (CHUNKS, rows), 1)
    alive = jnp.broadcast_to(valid[...].astype(F32), (CHUNKS, rows))
    alive = jnp.where(start + slot < end, alive, 0.0)
    first = jnp.sum(jnp.where(slot == row, alive, 0.0), axis=1, keepdims=True)
    last = jnp.sum(jnp.where(slot == rows - CHUNKS + row, alive, 0.0), axis=1, keepdims=True)
    values = jnp.concatenate(
        [
            dn[0:CHUNKS, :] + first * before, dn[CHUNKS : rows - CHUNKS, :],
            dn[rows - CHUNKS : rows, :] + last * after,
        ],
        axis=0,
    )
    inputs = tokens[...].astype(F32)
    inv_rms = lax.rsqrt(jnp.mean(inputs * inputs, axis=-1, keepdims=True) + NORM_EPS)
    scaled = values * gain[...].astype(F32).reshape(1, width)
    mean = jnp.mean(scaled * inputs, axis=-1, keepdims=True)
    input_grad[...] = (
        cotangent[...].astype(F32) + inv_rms * scaled - inputs * (inv_rms * inv_rms * inv_rms) * mean
    )


def blocks_in_order(mine, other, into_first, into_second):
    size = mine.shape[1]
    is_even = (lax.axis_index("seq") & 1) == 0
    here = lax.axis_index("img")
    for k in range(mine.shape[0]):
        a, b = mine[here ^ k].astype(F32), other[here ^ k].astype(F32)
        into_first(k * size, jnp.where(is_even, a, b))
        into_second(k * size, jnp.where(is_even, b, a))


def weighted_rows(values, weights):
    total = None
    for at in range(0, values.shape[1], LANES):
        part = values[:, at : at + LANES] * weights[:, at : at + LANES].astype(F32)
        total = part if total is None else total + part
    return total


def first_unpack(io, mine, other, in_weight, parts, in_far, out_far, out_w, z_half, moves):
    width = out_w.shape[1]
    inner = out_w.shape[0]

    def put_out(at, values):
        out_w[at : at + values.shape[0], :] = values

    def put_z(at, values):
        size = values.shape[0]
        column = at // width * width
        z_half[at % width : at % width + size, column : column + width] = values

    blocks_in_order(mine, other, put_out, put_z)
    leaving = [
        fetch(out_w, out_far, moves.at[0]),
        fetch(z_half, in_far.at[:, inner : 2 * inner], moves.at[1]),
    ]
    parts[...] = weighted_rows(z_half[...], in_weight[:, inner : 2 * inner])
    for copy in leaving:
        copy.wait()


def second_unpack(
    io, mine, other, in_weight, parts, gain_in, in_before,
    conv_w, conv_b, xproj, dt_w, dt_b, a_log, skip, gain, in_far,
    left, right, x_half, moves,
    *, count, state, rank, cols, taps,
):
    width = left.shape[1]
    inner = x_half.shape[1]

    def put_left(at, values):
        left[at : at + values.shape[0], :] = values

    def put_right(at, values):
        right[at : at + values.shape[0], :] = values

    blocks_in_order(mine, other, put_left, put_right)
    for i, half in enumerate((left, right)):
        x_half[:, i * width : (i + 1) * width] = half[0:width, :]
    leaving = fetch(x_half, in_far.at[:, 0:inner], moves.at[0])
    for i, half in enumerate((left, right)):
        lanes = slice(i * width, (i + 1) * width)
        for d in range(2):
            at = width + d * count
            xproj[d, :, lanes] = half[at : at + cols, :]
            at += cols
            dt_w[d, :, lanes] = half[at : at + rank, :]
            at += rank
            a_log[d, :, lanes] = half[at : at + state, :]
            dt_b[d : d + 1, lanes] = half[at + state : at + state + 1, :]
            skip[d : d + 1, lanes] = half[at + state + 1 : at + state + 2, :]
            at += state + 2
            conv_w[d, :, lanes] = half[at : at + taps, :]
            conv_b[d : d + 1, lanes] = half[at + taps : at + taps + 1, :]
    total = parts[...] + weighted_rows(x_half[...], in_weight[:, 0:inner])
    high = total.astype(BF16)
    rest = (total - high.astype(F32)).astype(BF16)
    ones = jnp.ones((2 * CHUNKS, LANES), BF16)
    sums = (dot_cols(ones, high) + dot_cols(ones, rest))[0:1]
    io.ready()
    gain[...] = (sums / gain_in[...].astype(F32).reshape(1, width)).reshape(width)
    io.done()
    leaving.wait()


IN_VMEM = pl.BlockSpec(memory_space=pltpu.VMEM)
IN_SMEM = pl.BlockSpec(memory_space=pltpu.SMEM)
FAR = pl.BlockSpec(memory_space=pltpu.HBM)


def shape(*dims, dtype=F32):
    return jax.ShapeDtypeStruct(dims, dtype)


def low(*dims):
    return jax.ShapeDtypeStruct(dims, BF16)


def near(*dims, dtype=F32):
    return pltpu.VMEM(dims, dtype)


def scratch(*dims, dtype=F32):
    return pltpu.VMEM(dims, dtype)


def like(*outs):
    return [pltpu.VMEM(out.shape, out.dtype) for out in outs]


def moves(*dims):
    return pltpu.SemaphoreType.DMA(dims)


class Moves:
    def __init__(self, arrive, leave):
        self.arrive, self.leave, self.left = arrive, leave, False
        for copy in arrive:
            copy.start()

    def ready(self):
        for copy in self.arrive:
            copy.wait()

    def done(self):
        self.left = True
        for copy in self.leave:
            copy.start()


def call(
    kernel, name, args, outs, scratches=(), far=(), far_outs=(), near_args=(), near_outs=(),
    scalars=(), handed=(), aliases=(), us=4, limit=4,
):
    small = tuple(scalars) + tuple(args)
    small, far = (
        tuple(pltpu.with_memory_space_constraint(x, pltpu.HBM) for x in arrays)
        for arrays in (small, far)
    )
    n_hand = len(handed)
    near_args = tuple(handed) + tuple(near_args)
    n_near, n_small, n_far = len(near_args), len(small), len(far)
    n_near_outs, n_outs, n_far_outs = len(near_outs), len(outs), len(far_outs)

    def wrapped(*refs):
        refs = list(refs)

        def take(count):
            taken = refs[:count]
            del refs[:count]
            return taken

        near_in, small_in, far_in = take(n_near), take(n_small), take(n_far)
        near_out, out, far_out = take(n_near_outs), take(n_outs), take(n_far_outs)
        take(n_hand)
        small_here, out_here = take(n_small), take(n_outs)
        in_moves, out_moves = take(2)
        io = Moves(
            [pltpu.make_async_copy(a, b, in_moves.at[i]) for i, (a, b) in enumerate(zip(small_in, small_here))],
            [pltpu.make_async_copy(a, b, out_moves.at[i]) for i, (a, b) in enumerate(zip(out_here, out))],
        )
        kernel(io, *near_in, *small_here, *far_in, *near_out, *out_here, *far_out, *refs)
        if not io.left:
            io.done()
        for copy in io.leave:
            copy.wait()

    return pl.pallas_call(
        wrapped,
        out_shape=list(near_outs) + [
            pltpu.HBM(out.shape, out.dtype) for out in tuple(outs) + tuple(far_outs)
        ] + [pltpu.VMEM(x.shape, x.dtype) for x in handed],
        in_specs=[IN_VMEM] * n_near + [FAR] * (n_small + n_far),
        out_specs=[IN_VMEM] * n_near_outs + [FAR] * (n_outs + n_far_outs) + [IN_VMEM] * n_hand,
        input_output_aliases={
            **{i: n_near_outs + n_outs + n_far_outs + i for i in range(n_hand)},
            **{n_near + n_small + i: n_near_outs + n_outs + o for i, o in aliases},
        },
        scratch_shapes=(
            [pltpu.SMEM(a.shape, a.dtype) for a in scalars] + like(*args) + like(*outs)
            + [moves(max(n_small, 1)), moves(max(n_outs, 1))] + list(scratches)
        ),
        compiler_params=pltpu.CompilerParams(vmem_limit_bytes=limit * 2**20),
        cost_estimate=pl.CostEstimate(flops=us * 500000000, bytes_accessed=0, transcendentals=0),
        name=name,
    )(*near_args, *small, *far)


def call_edges(tokens, valid):
    edge = 2 * CHUNKS
    width = tokens.shape[1]
    outs = [near(edge, width, dtype=BF16), near(edge, width, dtype=BF16)]
    return call(edges_kernel, "edges", (tokens, valid), (), near_outs=outs, us=1, limit=2)


def call_middle(
    heights, widths, from_core, from_chip, valid, gain, conv_weight, conv_bias, xproj, dt_weight,
    dt_bias, a_log, skip, tokens, cotangent, in_weight, out_weight,
):
    rows, width = tokens.shape
    inner = out_weight.shape[0]
    state, cols, reach = a_log.shape[1], xproj.shape[1], conv_weight.shape[1] - 1
    half = 2 * state
    both = near(2 * rows, inner)
    one = near(rows, inner)
    maps = near(half, CHUNKS, inner)
    ends = near(2 * CHUNKS, inner)
    return call(
        functools.partial(middle_kernel, reach=reach), "middle",
        (valid, gain, conv_weight, conv_bias, xproj, dt_weight, dt_bias, a_log, skip), (),
        like(tokens, cotangent, in_weight, out_weight) + [
            scratch(2 * rows, width, dtype=BF16), scratch(2 * reach * rows, LANES),
            scratch(2 * rows, inner, dtype=BF16), scratch(rows, half * LANES),
            scratch(state, CHUNKS, inner), scratch(state, CHUNKS, inner), scratch(CHUNKS, inner),
            moves(4),
        ],
        (tokens, cotangent, in_weight, out_weight), (), (from_core, from_chip),
        [
            near(2 * half + CHUNKS + half, inner), near(2 * half + 2 * CHUNKS, inner, dtype=BF16),
            both, both, both, one, maps, maps, near(rows + 2 * reach * CHUNKS, inner),
            near(2 * rows, cols), ends, ends, near(half + CHUNKS, inner), near(rows, LANES),
            near(rows, LANES), near(rows, width, dtype=BF16), near(4 * CHUNKS, width, dtype=BF16),
            one, one, near(rows, width, dtype=BF16),
        ],
        (heights, widths), us=20, limit=16,
    )


def call_join(got, summary, entered, state, bit, final):
    inner = summary.shape[1]
    half = 2 * state
    outs = [
        near(2 * half + CHUNKS, inner),
        near(half if final else 2 * half + 2 * CHUNKS, inner, dtype=BF16),
    ]
    if not final:
        outs = [near(2 * half + CHUNKS + half, inner)] + outs
    args = (got, summary) + (() if entered is None else (entered,))
    kernel = first_join if entered is None else join_kernel
    joined = call(
        functools.partial(kernel, state=state, bit=bit, final=final), "join", (), (),
        near_args=args, near_outs=outs, us=1, limit=4,
    )
    return joined if not final else [None] + list(joined)


def call_states(handed, used, before, tail, got, entered, zs, dgz, cotan, rank, reach, state, bit):
    rows, inner = zs.shape
    width = cotan.shape[1]
    half = 2 * state
    n_hand = len(handed)

    def kernel(io, *refs):
        states_kernel(
            io, *(refs[i] for i in used), *refs[n_hand:], reach=reach, rank=rank, state=state, bit=bit
        )

    grad = near(inner, width, dtype=BF16)
    one = near(rows, inner, dtype=BF16)
    held = near(inner // LANES, (rows // CHUNKS + 1) * state * CHUNKS, LANES)
    return call(
        kernel, "states", (), (),
        [scratch(rows, half * LANES), scratch(rows, 2 * LANES), scratch(rows, inner)],
        near_args=(before, tail, got, entered, zs, dgz, cotan),
        near_outs=[grad, grad, near(2 * half, inner), one, held, held, one], handed=handed, us=12,
        limit=9,
    )


def adjoint_scratch(rows, inner, half, reach, small, cols, rank):
    return [
        scratch(rows, half * LANES), scratch(rows, 2 * reach * LANES), scratch(rows, half * LANES),
        scratch(rows, inner), scratch(rows, inner), scratch(small - cols - rank, inner),
        scratch(rows + reach * CHUNKS, inner),
    ]


def call_first_adjoint(handed, used, h, weights, small, reach, rank, state):
    rows, inner = handed[used[3]].shape
    cols = handed[used[6]].shape[1]
    n_hand = len(handed)

    def kernel(io, *refs):
        first_adjoint(
            io, *(refs[i] for i in used), *refs[n_hand:], d=0, reach=reach, rank=rank, state=state
        )

    return call(
        kernel, "adjoint_up", weights, (),
        adjoint_scratch(rows, inner, 2 * state, reach, small, cols, rank), near_outs=[
            near(CHUNKS, inner), near(small, inner), near(rows, inner),
        ], near_args=(h,), handed=handed, us=14, limit=14,
    )


def call_second_adjoint(handed, arrays, weights, in_weight, small, reach, rank, state):
    rows, inner = arrays[3].shape
    cols = arrays[6].shape[1]
    n_hand = len(handed)

    def kernel(io, *refs):
        second_adjoint(io, *refs[n_hand:], d=1, reach=reach, rank=rank, state=state)

    return call(
        kernel, "adjoint_down", weights, (),
        [moves(1)] + adjoint_scratch(rows, inner, 2 * state, reach, small, cols, rank),
        (in_weight,), (), arrays,
        [near(CHUNKS, inner), near(small, inner), near(rows, inner), near(*in_weight.shape, dtype=BF16)],
        handed=handed, us=14, limit=14,
    )


def call_last(handed, dx, rim0, rim1, small0, small1, normed, nhalo, live, in_weight):
    rows, inner = dx.shape
    width = normed.shape[1]
    small = small0.shape[0]
    folds = inner // width
    edges = 2 * CHUNKS
    fold = -(-(width + 2 * small + edges) // 64) * 64
    n_hand = len(handed)

    def kernel(io, *refs):
        last_kernel(io, *refs[n_hand:])

    return call(
        kernel, "last", (), (),
        [
            scratch(rows + edges, inner, dtype=BF16), scratch(folds * fold, width, dtype=BF16),
        ],
        near_args=(dx, rim0, rim1, small0, small1, normed, nhalo, live, in_weight),
        near_outs=[
            near(fold, width, dtype=BF16), near(fold, width, dtype=BF16),
            near(rows, inner, dtype=BF16),
        ],
        handed=handed, us=3, limit=8,
    )


def partner(axis, bit):
    return [(i, i ^ (1 << bit)) for i in range(lax.axis_size(axis))]


def bits_of(axis):
    return (lax.axis_size(axis) - 1).bit_length()


def other_core(values):
    return lax.ppermute(values, "seq", partner("seq", 0))


def next_chip(values):
    count = lax.axis_size("seq")
    pairs = [(i, i + 1) for i in range(1, count - 1, 2)]
    return lax.ppermute(values, "seq", pairs + [(j, i) for i, j in pairs])


def split_kernel(io, kept, got, own, *sent, edges):
    if edges:
        at = got.shape[0] - edges[1]
        sent[-1][...] = got[at : at + edges[0], :]
        sent = sent[:-1]
    count = len(sent) + 1
    rows = own.shape[0]
    here = lax.axis_index("img")
    for k in range(count):
        at = pl.ds(pl.multiple_of((here ^ k) * rows, rows), rows)
        total = kept[at, :].astype(F32) + got[at, :].astype(F32)
        if k == 0:
            own[...] = total
        else:
            sent[k - 1][...] = total.astype(BF16)


def add_kernel(io, *refs, outs):
    total = refs[0][...].astype(F32)
    for ref in refs[1 : len(refs) - outs]:
        total = total + ref[...].astype(F32)
    for ref in refs[len(refs) - outs :]:
        ref[...] = total.astype(ref.dtype)


def add(values, whole=True):
    rows, width = values[0].shape
    outs = [near(rows, width)] * whole + [near(rows, width, dtype=BF16)]
    sums = call(
        functools.partial(add_kernel, outs=len(outs)), "add", (), (), near_args=values,
        near_outs=outs, us=1, limit=2,
    )
    return sums if whole else sums[0]


def add_rim_kernel(io, *refs, count, bit):
    values, moving, stay = refs[:count], refs[count], refs[count + 1]
    total_out, low_out, stay_out = refs[-3:]
    rows = total_out.shape[0]
    total = values[0][...]
    for ref in values[1:]:
        total = total + ref[0:rows, :].astype(F32)
    total_out[...] = total
    low_out[0:rows, :] = total.astype(BF16)
    if bit is None:
        low_out[rows:, :] = moving[...]
        stay_out[...] = jnp.zeros_like(stay_out)
        return
    came = values[-1][rows:, :]
    if low_out.shape[0] > rows:
        low_out[rows:, :] = came
    position = lax.axis_index("seq")
    chip = position >> 1
    chip = jnp.where((position & 1) == 0, chip, lax.axis_size("seq") // 2 - 1 - chip)
    lowest = chip & ((2 << bit) - 1)
    stay_out[...] = jnp.where(lowest == (1 << bit), came, stay[...])


def add_rim(values, moving, stay, bit, final=False):
    rows, width = values[0].shape
    edge = moving.shape[0]
    sent = rows if final else rows + edge
    return call(
        functools.partial(add_rim_kernel, count=len(values), bit=bit), "add", (), (),
        near_args=tuple(values) + (moving, stay),
        near_outs=[near(rows, width), near(sent, width, dtype=BF16), near(edge, width, dtype=BF16)],
        us=1, limit=2,
    )


def stack_kernel(io, *refs):
    for k, ref in enumerate(refs[:-1]):
        refs[-1][k] = ref[...]


def plane_pairs(k):
    return [(i, i ^ k) for i in range(lax.axis_size("img"))]


def chips_sum(kept, sent, edges=()):
    count = lax.axis_size("img")
    rows, width = kept.shape
    block = (rows // count, width)
    got = other_core(sent)
    own, *parts = call(
        functools.partial(split_kernel, edges=edges), "split", (), (), near_args=(kept, got),
        near_outs=[near(*block)] + [near(*block, dtype=BF16)] * (count - 1)
        + [near(rim_rows, width, dtype=BF16) for rim_rows in edges[:1]],
        us=1, limit=2,
    )
    rim = parts.pop() if edges else None
    blocks = [own] + [
        lax.ppermute(part, "img", plane_pairs(k + 1)) for k, part in enumerate(parts)
    ]
    return blocks, rim


def line_steps(total, low):
    bits = bits_of("seq")
    for bit in range(1, bits):
        got = lax.ppermute(low, "seq", partner("seq", bit))
        if bit < bits - 1:
            total, low = add([total, got])
        else:
            low = add([total, got], whole=False)
    return low


def line_steps_with_rims(blocks, rim, first_low, beside):
    stay = rim
    total, low, stay = add_rim(blocks, rim, stay, None)
    low, first_low = tied(low, first_low)
    bits = bits_of("seq")
    for bit in range(1, bits):
        got = lax.ppermute(low, "seq", partner("seq", bit))
        if bit == 1:
            got, beside = tied(got, beside)
        if bit == bits - 1:
            first_mine = stacked(plane_blocks(first_low))
            got, first_mine = tied(got, first_mine)
        total, low, stay = add_rim([total, got], rim, stay, bit - 1, bit == bits - 1)
        if bit == bits - 2:
            low, first_low = tied(low, first_low)
    return low, stay, first_mine, beside


def plane_blocks(low):
    count = lax.axis_size("img")
    return [low] + [lax.ppermute(low, "img", plane_pairs(k)) for k in range(1, count)]


def stacked(blocks):
    low, count = blocks[0], len(blocks)
    return call(
        stack_kernel, "stack", (), (), near_args=blocks,
        near_outs=[near(count, *low.shape, dtype=BF16)], us=1, limit=2,
    )[0]


def tied(first, second):
    return lax.optimization_barrier((first, second))


def body(
    tokens, cotangent, heights, widths, valid, norm_gain, in_weight, conv_weight, conv_bias,
    xproj_weight, dt_weight, dt_bias, a_log, skip, out_weight,
):
    rows, width = tokens.shape[1:]
    inner = out_weight.shape[0]
    state = a_log.shape[1]
    rank = dt_weight.shape[1]
    cols = xproj_weight.shape[2]
    taps = conv_weight.shape[1]
    reach = taps - 1
    count = bits_of("seq")
    tokens, cotangent = tokens[0], cotangent[0]
    xproj = xproj_weight.transpose(0, 2, 1)

    to_core, to_chip = call_edges(tokens, valid)
    from_core, from_chip = other_core(to_core), next_chip(to_chip)
    (
        summary, sent, delta, s, dsilu, dy, tail, head, xext, proj, before, after, rate, masks,
        live, normed, nhalo, zs, dgz, cotan,
    ) = call_middle(
        heights, widths, from_core, from_chip, valid, norm_gain, conv_weight, conv_bias, xproj,
        dt_weight, dt_bias, a_log, skip, tokens, cotangent, in_weight, out_weight,
    )
    entered = None
    for bit in range(count - 1):
        got = lax.ppermute(sent, "seq", partner("seq", bit))
        summary, entered, sent = call_join(got, summary, entered, state, bit, bit == count - 2)
    got = lax.ppermute(sent, "seq", partner("seq", count - 1))
    handed = (delta, s, dsilu, dy, head, xext, proj, after, rate, masks, live, normed, nhalo)
    kept, sent, carry, dz, h0, h1, gated, *handed = call_states(
        handed, (0, 1, 6, 8, 9, 11), before, tail, got, entered, zs, dgz, cotan, rank, reach, state,
        count - 1,
    )

    blocks, _ = chips_sum(kept, sent)
    small = -(-(cols + rank + state + 2 + taps + 1) // CHUNKS) * CHUNKS
    weights = (dt_weight, xproj, conv_weight)
    handed = tuple(handed[:10]) + (carry,) + tuple(handed[10:]) + (dz, gated, h1)
    rim0, small0, dx, *handed = call_first_adjoint(
        handed, tuple(range(11)), h0, weights, small, reach, rank, state
    )
    *blocks, dx = lax.optimization_barrier((*blocks, dx))
    first_sum, first_low = add(blocks)
    first_sum, first_low, dx = lax.optimization_barrier((first_sum, first_low, dx))
    arrays, passed, h1 = tuple(handed[:11]), tuple(handed[11:-1]), handed[-1]
    if bits_of("seq") > 3:
        first_low = line_steps(first_sum, first_low)
    else:
        devices = lax.axis_size("seq")
        blocks = [first_sum] + [
            lax.ppermute(first_low, "seq", [(i, i ^ k) for i in range(devices)])
            for k in range(2, devices, 2)
        ]
    rim1, small1, dx, in_near, *passed = call_second_adjoint(
        passed, arrays + (h1, dx), weights, in_weight, small, reach, rank, state
    )
    live, normed, nhalo, dz, gated = passed
    if bits_of("seq") <= 3:
        *blocks, dx = lax.optimization_barrier((*blocks, dx))
        first_low = add(blocks, whole=False)
    kept, sent, dx_low, dz, gated, in_near = call_last(
        (dz, gated, in_near), dx, rim0, rim1, small0, small1, normed, nhalo, live, in_near
    )

    edges = (2 * CHUNKS, kept.shape[0] - width - 2 * small)
    blocks, rim = chips_sum(kept, sent, edges)


    output = call(
        output_kernel, "output", (tokens, out_weight), [low(rows, width)], near_args=(gated,), us=2,
        limit=6,
    )[0]
    second_low, chip_rim, first_mine, output = line_steps_with_rims(blocks, rim, first_low, output)
    first_other = other_core(first_mine)
    blocks = plane_blocks(second_low)
    parts, in_total, out_total = call(
        first_unpack, "unpack_first", (), (),
        [scratch(inner, width), scratch(width, inner), moves(2)],
        far_outs=[shape(width, 2 * inner), shape(inner, width)],
        near_args=(first_mine, first_other, in_near), near_outs=[near(width, LANES)], us=2, limit=8,
    )
    input_grad = call(
        finish_kernel, "finish", (tokens, cotangent, valid, norm_gain), [shape(rows, width)],
        near_args=(dx_low, dz, in_near, rim, chip_rim), scalars=(heights, widths), us=3, limit=8,
    )[0]
    blocks, input_grad, parts = lax.optimization_barrier((blocks, input_grad, parts))
    second_mine = stacked(blocks)
    second_other = other_core(second_mine)
    fold = kept.shape[0]
    (
        conv_total, bias_total, xproj_total, dtw_total, dtb_total, a_total, skip_total, gain_total,
        in_total,
    ) = call(
        functools.partial(
            second_unpack, count=small, state=state, rank=rank, cols=cols, taps=taps
        ),
        "unpack_second", (norm_gain,),
        [
            shape(2, taps, inner), shape(2, inner), shape(2, cols, inner), shape(2, rank, inner),
            shape(2, inner), shape(2, state, inner), shape(2, inner), shape(width),
        ],
        [scratch(fold, width), scratch(fold, width), scratch(width, inner), moves(1)],
        (in_total,), [shape(width, 2 * inner)], (second_mine, second_other, in_near, parts),
        aliases=((0, 0),), us=2, limit=10,
    )
    return (
        output[None], input_grad[None], gain_total, in_total, conv_total, bias_total,
        xproj_total.transpose(0, 2, 1), dtw_total, dtb_total, a_total, skip_total, out_total,
    )


def solution(mesh):
    split = P("img", "seq", None)
    placed = (split, split, P("img", None), P("img", None), P("img", "seq")) + (P(),) * 10
    return jax.shard_map(
        body,
        mesh=mesh,
        in_specs=placed,
        out_specs=(split, split) + (P(),) * 10,
        check_vma=False,
    )
```

```python
import functools

import jax
import jax.numpy as jnp
from jax import lax
from jax.experimental import pallas as pl
from jax.experimental.pallas import tpu as pltpu
from jax.sharding import PartitionSpec as P

NORM_EPS = 1e-05
CONTRACT_ROWS = (((0,), (0,)), ((), ()))
CONTRACT_COLS = (((1,), (1,)), ((), ()))
LOG2E = 1.4426950408889634
LN2 = 0.6931471805599453
BREAK = 1e30
CHUNKS = 8
LANES = 128
SUMMARY_STATES = 8
SUMMARY_UNROLL = 16
STATES_UNROLL = 8
ADJOINT_STATES = 8
ADJOINT_UNROLL = 8
F32 = jnp.float32
BF16 = jnp.bfloat16


def dot(a, b):
    return jnp.dot(a, b, preferred_element_type=F32)


def dot_rows(a, b):
    return lax.dot_general(a, b, CONTRACT_ROWS, preferred_element_type=F32)


def dot_cols(a, b):
    return lax.dot_general(a, b, CONTRACT_COLS, preferred_element_type=F32)


def sigmoid(v):
    return 1.0 / (1.0 + jnp.exp(-v))


def fetch(source, target, semaphore):
    copy = pltpu.make_async_copy(source, target, semaphore)
    copy.start()
    return copy


def lanes_of(tile):
    return pl.ds(pl.multiple_of(tile * LANES, LANES), LANES)


def rows_of(j, count=CHUNKS):
    return pl.ds(pl.multiple_of(j * CHUNKS, CHUNKS), count)


def chunk_order(rows):
    row = lax.broadcasted_iota(jnp.int32, (rows, rows), 0)
    slot = lax.broadcasted_iota(jnp.int32, (rows, rows), 1)
    return slot == (row & (CHUNKS - 1)) * (rows // CHUNKS) + (row >> 3)


def image_ends(heights, widths):
    ends, total = [], 0
    for i in range(heights.shape[1]):
        total = total + heights[0, i] * widths[0, i]
        ends.append(total)
    return ends


def segment_of(places, ends):
    found = jnp.zeros_like(places)
    for end in ends:
        found = found + (places >= end).astype(jnp.int32)
    return found


def places_of(first, rows):
    row = lax.broadcasted_iota(jnp.int32, (rows, LANES), 0)
    return first + (row & (CHUNKS - 1)) * (rows // CHUNKS) + (row >> 3)


def edges_kernel(io, tokens, valid, to_core, to_chip):
    rows = tokens.shape[0]
    edge = to_core.shape[0]
    io.ready()
    row = lax.broadcasted_iota(jnp.int32, (edge, rows), 0)
    slot = lax.broadcasted_iota(jnp.int32, (edge, rows), 1)
    held = jnp.broadcast_to(valid[...].astype(F32), (edge, rows))
    first = jnp.where(slot == row, held, 0.0).astype(BF16)
    last = jnp.where(slot == rows - edge + row, held, 0.0).astype(BF16)
    first = dot(first, tokens[...]).astype(BF16)
    last = dot(last, tokens[...]).astype(BF16)
    even = (lax.axis_index("seq") & 1) == 0
    to_core[...] = jnp.where(even, last, first)
    to_chip[...] = jnp.where(even, first, last)


def spread(values, target):
    count = values.shape[1]
    high = values.astype(BF16)
    low = (values - high.astype(F32)).astype(BF16)
    both = jnp.concatenate([high, low], axis=1)
    wide = 2 * LANES
    column = lax.broadcasted_iota(jnp.int32, (2 * count, wide), 0)
    block = lax.broadcasted_iota(jnp.int32, (2 * count, wide), 1) // LANES
    for at in range(0, count * LANES, wide):
        place = block + at // LANES
        pick = ((column == place) | (column == place + count)).astype(BF16)
        target[:, at : at + wide] = dot(both, pick)


def windows(span, up, sublane):
    sign = 1 if up else -1

    def from_before(value, by, fill):
        moved = pltpu.roll(value, (sign * by) % CHUNKS, axis=0)
        kept = sublane >= by if up else sublane < CHUNKS - by
        return jnp.where(kept, moved, fill)

    two = span + from_before(span, 1, 0.0)
    four = two + from_before(two, 2, 0.0)
    eight = four + from_before(four, 4, 0.0)
    edge = [jnp.where(sublane >= by if up else sublane < CHUNKS - by, 0.0, BREAK) for by in (1, 2, 4)]
    return (span + edge[0], two + edge[1], four + edge[2]), from_before(eight, 1, 0.0)


def chain(rate, sums, tail, up, sublane):
    sign = 1 if up else -1
    for by, span in zip((1, 2, 4), sums):
        tail = jnp.exp2(rate * span) * pltpu.roll(tail, (sign * by) % CHUNKS, axis=0) + tail
    end = CHUNKS - 1 if up else 0
    kept = sublane >= 1 if up else sublane < CHUNKS - 1
    return jnp.where(kept, pltpu.roll(tail, sign % CHUNKS, axis=0), 0.0), tail[end : end + 1]


def front_kernel(
    io, heights, widths, valid, gain,
    tokens_far, cotangent_far, in_far, out_far, *refs,
    reach, weights,
):
    (
        normed_out, x_out, zs_out, dgz_out, dy, live, same_out, cotan, in_x,
    ) = refs[weights : weights + 9]
    near_weights = refs[weights + 9 : 2 * weights + 9]
    tokens, cotangent, in_z, out_weight, ins = refs[2 * weights + 9 :]
    rows, width = tokens.shape
    inner = out_weight.shape[0]
    tiles = inner // LANES
    arriving = [
        fetch(source, target, ins.at[i])
        for i, (source, target) in enumerate(
            (
                (tokens_far, tokens), (in_far.at[:, 0:inner], in_x),
                (cotangent_far, cotangent), (in_far.at[:, inner : 2 * inner], in_z),
                (out_far, out_weight),
            )
            + tuple(zip(refs[:weights], near_weights))
        )
    ]
    io.ready()
    start = lax.axis_index("seq") * rows
    slots = lax.axis_size("seq") * rows
    ends = image_ends(heights, widths)
    images = heights.shape[1]

    order = chunk_order(rows)
    order_low = order.astype(BF16)
    picked = jnp.where(order, jnp.broadcast_to(valid[...].astype(F32), order.shape), 0.0)
    alive = dot(picked.astype(BF16), jnp.ones((rows, LANES), BF16))
    places = places_of(start, rows)
    segment = segment_of(places, ends)
    live[...] = jnp.where(segment < images, alive, 0.0)
    for k in range(1, reach + 1):
        same = (segment_of(places - k, ends) == segment) & (places >= k)
        same_out[(k - 1) * rows : k * rows, :] = same.astype(F32)
        same = (segment_of(places + k, ends) == segment) & (places + k < slots)
        same_out[(reach + k - 1) * rows : (reach + k) * rows, :] = same.astype(F32)

    arriving[0].wait()
    inputs = dot(order_low, tokens[...])
    inv_rms = lax.rsqrt(jnp.mean(inputs * inputs, axis=-1, keepdims=True) + NORM_EPS)
    scaled = inputs * inv_rms * gain[...].astype(F32).reshape(1, width)
    normed = scaled.astype(BF16)
    normed_out[...] = normed
    live_wide = jnp.concatenate([live[...]] * (width // LANES), axis=1)
    normed_live = (scaled * live_wide).astype(BF16)
    step = 2 * LANES
    arriving[1].wait()
    for at in range(0, inner, step):
        lanes = slice(at, at + step)
        x_out[:, lanes] = dot(normed_live, in_x[:, lanes]).astype(BF16).astype(F32)
    for copy in arriving[2:]:
        copy.wait()
    cotan[...] = dot(order_low, cotangent[...]).astype(BF16)
    block = 32
    for at in range(0, inner, step):
        lanes = slice(at, at + step)
        zs_out[:, lanes] = dot(normed, in_z[:, lanes])
        dgz_out[:, lanes] = dot_cols(cotan[...], out_weight[lanes, :])

    def gate_block(b, _):
        here = pl.ds(pl.multiple_of(b * block, block), block)
        alive = live[here, :]
        for tile in range(tiles):
            lanes = slice(tile * LANES, (tile + 1) * LANES)
            z = zs_out[here, lanes]
            grad = dgz_out[here, lanes] * alive
            gate = sigmoid(z)
            zs = z * gate * alive
            zs_out[here, lanes] = zs
            dy[here, lanes] = 0.5 * grad * zs
            dgz_out[here, lanes] = grad * (gate * (1.0 + z * (1.0 - gate)))
        return 0

    lax.fori_loop(0, rows // block, gate_block, 0)


def middle_kernel(
    io, dy, live, same_out, from_core, from_chip, x, in_x, conv_weight, conv_bias, xproj, dt_weight,
    dt_bias, a_log, skip, heights, widths, gain,
    sum_out, sent_out, delta_out, s_out, dsilu_out, tail_out, head_out, xext_out, proj_out,
    before_out, after_out, rate_out, nhalo_out,
    low_out, bc, tails, heads, spans,
    *, reach,
):
    rows, inner = x.shape
    width = in_x.shape[0]
    steps = rows // CHUNKS
    state = a_log.shape[1]
    rank = dt_weight.shape[1]
    tiles = inner // LANES
    start = lax.axis_index("seq") * rows
    even = (lax.axis_index("seq") & 1) == 0
    sublane = lax.broadcasted_iota(jnp.int32, (CHUNKS, LANES), 0)
    wide = lax.broadcasted_iota(jnp.int32, (CHUNKS, inner), 0)
    xext_out[reach * CHUNKS : (reach + steps) * CHUNKS, :] = x[...]

    io.ready()
    ends = image_ends(heights, widths)
    before = jnp.where(even, from_chip[...], from_core[...])
    after = jnp.where(even, from_core[...], from_chip[...])
    htok = jnp.concatenate([before[CHUNKS:], after[:CHUNKS]], axis=0)
    hrow = lax.broadcasted_iota(jnp.int32, (2 * CHUNKS, LANES), 0)
    hplace = jnp.where(hrow < CHUNKS, start - CHUNKS + hrow, start + rows + hrow - CHUNKS)
    hlive = (segment_of(hplace, ends) < heights.shape[1]).astype(F32)
    htok = htok.astype(F32) * jnp.concatenate([hlive] * (width // LANES), axis=1)
    hinv = lax.rsqrt(jnp.mean(htok * htok, axis=-1, keepdims=True) + NORM_EPS)
    scaled = htok * hinv
    nhalo = (scaled * gain[...].astype(F32).reshape(1, width)).astype(BF16)
    nhalo_out[...] = jnp.concatenate([nhalo, scaled.astype(BF16)], axis=0)
    hx = dot(nhalo, in_x[...]).astype(BF16).astype(F32)
    for i in range(reach):
        to = steps - reach + i
        moved = pltpu.roll(x[to * CHUNKS : (to + 1) * CHUNKS, :], 1, axis=0)
        of = CHUNKS - reach + i
        xext_out[i * CHUNKS : (i + 1) * CHUNKS, :] = jnp.where(wide == 0, hx[of : of + 1], moved)
        moved = pltpu.roll(x[i * CHUNKS : (i + 1) * CHUNKS, :], CHUNKS - 1, axis=0)
        to = reach + steps + i
        of = CHUNKS + i
        xext_out[to * CHUNKS : (to + 1) * CHUNKS, :] = jnp.where(
            wide == CHUNKS - 1, hx[of : of + 1], moved
        )

    block = 32
    step = 2 * LANES
    taps = reach + 1
    conv_w = [conv_weight[d].astype(F32) for d in range(2)]
    conv_b = conv_bias[...].astype(F32)
    for tile in range(tiles):
        lanes = slice(tile * LANES, (tile + 1) * LANES)

        def conv_block(b, _, lanes=lanes):
            at = pl.multiple_of(b * block, block)
            for d in range(2):
                total = conv_b[d : d + 1, lanes] + conv_w[d][reach:taps, lanes] * (
                    xext_out[pl.ds(at + reach * CHUNKS, block), lanes]
                )
                for k in range(1, taps):
                    move = reach - k if d == 0 else reach + k
                    mask = same_out[pl.ds((d * reach + k - 1) * rows + at, block), :]
                    total = total + conv_w[d][reach - k : taps - k, lanes] * (
                        xext_out[pl.ds(at + move * CHUNKS, block), lanes] * mask
                    )
                gate = sigmoid(total)
                value = total * gate
                s_out[pl.ds(d * rows + at, block), lanes] = value
                low_out[pl.ds(d * rows + at, block), lanes] = value.astype(BF16)
                dsilu_out[pl.ds(d * rows + at, block), lanes] = gate * (1.0 + total * (1.0 - gate))
            return 0

        lax.fori_loop(0, rows // block, conv_block, 0, unroll=2)

    dt_b = dt_bias[...].astype(F32)
    for d in range(2):
        rate_out[d * state : (d + 1) * state, :] = jnp.minimum(
            -LOG2E * jnp.exp(a_log[d].astype(F32)), -1e-20
        )
        here = slice(d * rows, (d + 1) * rows)
        proj = dot_cols(low_out[here, :], xproj[d])
        proj_out[here, :] = proj
        dt_low = proj[:, :rank].astype(BF16)
        for at in range(0, inner, step):
            lanes = slice(at, at + step)
            delta_out[here, lanes] = dot(dt_low, dt_weight[d, :, lanes])
        spread(proj[:, rank:], bc)

        def delta_block(b, _, d=d):
            alive = live[pl.ds(pl.multiple_of(b * block, block), block), :]
            here = pl.ds(pl.multiple_of(d * rows + b * block, block), block)
            for tile in range(tiles):
                lanes = slice(tile * LANES, (tile + 1) * LANES)
                pre = delta_out[here, lanes] + dt_b[d : d + 1, lanes]
                small = jnp.exp(-jnp.abs(pre))
                log1p = jnp.where(small < 1e-4, small * (1.0 - 0.5 * small), jnp.log(1.0 + small))
                delta_out[here, lanes] = (jnp.maximum(pre, 0.0) + log1p) * alive
            return 0

        lax.fori_loop(0, rows // block, delta_block, 0, unroll=2)
        some = SUMMARY_STATES

        def scan_tile(tile, _, d=d):
            lanes = lanes_of(tile)
            for low in range(0, state, some):
                rates = [
                    jnp.broadcast_to(
                        rate_out[d * state + low + m : d * state + low + m + 1, lanes],
                        (CHUNKS, LANES),
                    )
                    for m in range(some)
                ]

                def scan_step(i, carried, d=d, low=low, rates=rates):
                    tail, lead, head, span = carried
                    j = i if d == 0 else steps - 1 - i
                    at = pl.multiple_of(j * CHUNKS, CHUNKS)
                    keep = same_out[pl.ds(d * reach * rows + at, CHUNKS), :]
                    delta = delta_out[pl.ds(d * rows + at, CHUNKS), lanes]
                    drive = delta * s_out[pl.ds(d * rows + at, CHUNKS), lanes]
                    back = dy[pl.ds(at, CHUNKS), lanes]
                    delta = jnp.where(keep > 0.0, delta, BREAK)
                    tail, lead, head = list(tail), list(lead), list(head)
                    for m in range(some):
                        b = bc[pl.ds(at, CHUNKS), (low + m) * LANES : (low + m + 1) * LANES]
                        n = state + low + m
                        c = bc[pl.ds(at, CHUNKS), n * LANES : (n + 1) * LANES]
                        decay = jnp.exp2(delta * rates[m])
                        tail[m] = decay * tail[m] + b * drive
                        lead[m] = lead[m] * decay
                        head[m] = head[m] + lead[m] * (c * back)
                    return tuple(tail), tuple(lead), tuple(head), span + delta

                zeros = tuple(jnp.zeros((CHUNKS, LANES), F32) for _ in range(some))
                ones = tuple(jnp.ones((CHUNKS, LANES), F32) for _ in range(some))
                tail, lead, head, span = lax.fori_loop(
                    0, steps, scan_step, (zeros, ones, zeros, zeros[0]), unroll=SUMMARY_UNROLL
                )
                for m in range(some):
                    tails[low + m, :, lanes] = tail[m]
                    heads[low + m, :, lanes] = head[m]
                spans[:, lanes] = span
            return 0

        lax.fori_loop(0, tiles, scan_tile, 0)

        tail_row = 0 if d == 0 else 2 * state
        head_row = 3 * state if d == 0 else state

        def chain_tile(tile, _, d=d, tail_row=tail_row, head_row=head_row):
            lanes = lanes_of(tile)
            span = spans[:, lanes]
            sums, before = windows(span, d == 0, sublane)
            sums_back, after = windows(span, d == 1, sublane)
            before_out[d * CHUNKS : (d + 1) * CHUNKS, lanes] = before
            after_out[d * CHUNKS : (d + 1) * CHUNKS, lanes] = after
            for n in range(state):
                rate = jnp.broadcast_to(
                    rate_out[d * state + n : d * state + n + 1, lanes], (CHUNKS, LANES)
                )
                carried, total = chain(rate, sums, tails[n, :, lanes], d == 0, sublane)
                tail_out[d * state + n, :, lanes] = carried
                sum_out[tail_row + n : tail_row + n + 1, lanes] = total
                carried, total = chain(rate, sums_back, heads[n, :, lanes], d == 1, sublane)
                head_out[d * state + n, :, lanes] = carried
                sum_out[head_row + n : head_row + n + 1, lanes] = total
            return 0

        lax.fori_loop(0, tiles, chain_tile, 0)
        sum_out[4 * state + d : 4 * state + d + 1, :] = jnp.sum(spans[...], axis=0, keepdims=True)
    at = 4 * state + CHUNKS
    sum_out[4 * state + 2 : at, :] = jnp.zeros((CHUNKS - 2, inner), F32)
    sum_out[at:, :] = rate_out[0 : 2 * state, :]
    sent_out[...] = packed(sum_out[0:at, :], state)
    rate_out[2 * state : 2 * state + 2, :] = skip[...].astype(F32)


def packed(summary, state):
    rest = summary[4 * state :]
    high = rest.astype(BF16)
    low = (rest - high.astype(F32)).astype(BF16)
    return jnp.concatenate([summary[: 4 * state].astype(BF16), high, low], axis=0)


def leads(rate, spans, state, flip):
    parts = [jnp.exp2(rate[d * state : (d + 1) * state] * spans[d : d + 1]) for d in range(2)]
    return jnp.concatenate(parts[::-1] if flip else parts, axis=0)


def join_kernel(io, got, summary, entered, *outs, state, bit, final):
    half = 2 * state
    upper = ((lax.axis_index("seq") >> bit) & 1) == 1
    mine = summary[0 : 2 * half + CHUNKS, :]
    rates = summary[2 * half + CHUNKS :, :]
    entered_out, sent_out = outs[-2], outs[-1]
    values = got[...].astype(F32)
    spans = mine[4 * state : 4 * state + 2]
    other = values[4 * state : 4 * state + 2] + values[4 * state + CHUNKS : 4 * state + CHUNKS + 2]
    if entered is None:
        entered_up = jnp.where(upper, values[:half], 0.0)
        entered_down = jnp.where(upper, 0.0, values[half : 2 * half])
        span_up = jnp.where(upper, other, 0.0)
        span_down = jnp.where(upper, 0.0, other)
    else:
        held = entered[...]
        span_up, span_down = held[2 * half : 2 * half + 2], held[2 * half + 2 : 2 * half + 4]
        entered_up = held[:half] + jnp.where(
            upper, leads(rates, span_up, state, False) * values[:half], 0.0
        )
        entered_down = held[half : 2 * half] + jnp.where(
            upper, 0.0, leads(rates, span_down, state, True) * values[half : 2 * half]
        )
        span_up = span_up + jnp.where(upper, other, 0.0)
        span_down = span_down + jnp.where(upper, 0.0, other)
    entered_out[0:half, :] = entered_up
    entered_out[half : 2 * half, :] = entered_down
    entered_out[2 * half :, :] = jnp.concatenate(
        [span_up, span_down, jnp.zeros((CHUNKS - 4, mine.shape[1]), F32)], axis=0
    )
    low_up = jnp.where(upper, values[:half], mine[:half])
    high_up = jnp.where(upper, mine[:half], values[:half])
    low_down = jnp.where(upper, values[half : 2 * half], mine[half : 2 * half])
    high_down = jnp.where(upper, mine[half : 2 * half], values[half : 2 * half])
    low_span, high_span = jnp.where(upper, other, spans), jnp.where(upper, spans, other)
    up = leads(rates, high_span, state, False) * low_up + high_up
    down = leads(rates, low_span, state, True) * high_down + low_down
    if final:
        next_upper = ((lax.axis_index("seq") >> (bit + 1)) & 1) == 1
        sent_out[...] = jnp.where(next_upper, down, up).astype(BF16)
    else:
        total = jnp.concatenate(
            [up, down, spans + other, jnp.zeros((CHUNKS - 2, mine.shape[1]), F32)], axis=0
        )
        outs[0][0 : 2 * half + CHUNKS, :] = total
        outs[0][2 * half + CHUNKS :, :] = rates
        sent_out[...] = packed(total, state)


def first_join(io, got, summary, *outs, state, bit, final):
    join_kernel(io, got, summary, None, *outs, state=state, bit=bit, final=final)


def state_block(j, state):
    return pl.multiple_of(j * state * CHUNKS, CHUNKS)


def states_pass(d, steps, state, rates, begin, delta, s, keep, bc, h_out, y):
    start = state_block(0 if d == 0 else steps, state)
    for n in range(state):
        h_out[pl.ds(start + n * CHUNKS, CHUNKS), :] = begin[n]

    def step(i, h):
        j = i if d == 0 else steps - 1 - i
        here = pl.ds(pl.multiple_of(j * CHUNKS, CHUNKS), CHUNKS)
        to = state_block(j + 1 if d == 0 else j, state)
        size = delta[here, :]
        drive = size * s[here, :]
        size = jnp.where(keep[here, :] > 0.0, size, BREAK)
        h = list(h)
        parts = [None if d == 0 else y[here, :], None]
        for n in range(state):
            b = bc[here, n * LANES : (n + 1) * LANES]
            c = bc[here, (state + n) * LANES : (state + n + 1) * LANES]
            h[n] = jnp.exp2(size * rates[n]) * h[n] + b * drive
            h_out[pl.ds(to + n * CHUNKS, CHUNKS), :] = h[n]
            part = parts[n % 2]
            parts[n % 2] = c * h[n] if part is None else part + c * h[n]
        y[here, :] = parts[0] + parts[1]
        return tuple(h)

    lax.fori_loop(0, steps, step, tuple(begin), unroll=STATES_UNROLL)


def adjoint_pass(
    d, steps, state, rates, back, delta, s, dy, keep, skip, bc, h_in, sums,
    dpre_out, ds_out, rows_out,
):
    some = ADJOINT_STATES
    edge = steps - 1
    skip = skip[...]
    zeros = jnp.zeros((CHUNKS, LANES), F32)
    grads = []
    for low in range(0, state, some):
        final = low + some == state

        def step(i, carried, low=low, final=final):
            g, acc, h, skip_acc, bias_acc = carried
            j = edge - i if d == 0 else i
            here = pl.ds(pl.multiple_of(j * CHUNKS, CHUNKS), CHUNKS)
            size = delta[here, :]
            value = s[here, :]
            grad = dy[here, :]
            drive = size * value
            masked = jnp.where(keep[here, :] > 0.0, size, BREAK)
            prev = state_block(j if d == 0 else j + 1, state)
            g, acc, h = list(g), list(acc), list(h)
            weighted = zeros if low == 0 else ds_out[here, :]
            rate_sum = zeros if low == 0 else dpre_out[here, :]
            for m in range(some):
                n = low + m
                b = bc[here, n * LANES : (n + 1) * LANES]
                c = bc[here, (state + n) * LANES : (state + n + 1) * LANES]
                adjoint = c * grad + g[m]
                before = h_in[pl.ds(prev + n * CHUNKS, CHUNKS), :]
                sums[here, n * LANES : (n + 1) * LANES] += adjoint * drive
                sums[here, (state + n) * LANES : (state + n + 1) * LANES] += grad * h[m]
                g[m] = adjoint * jnp.exp2(masked * rates[n])
                held = g[m] * before
                weighted = weighted + adjoint * b
                rate_sum = rate_sum + held * rates[n]
                acc[m] = acc[m] + held * masked
                h[m] = before
            if final:
                ds_out[here, :] = skip * grad + size * weighted
                gate = jnp.where(
                    size < 0.01, size * (1.0 - size * (0.5 - size * (1.0 / 6.0))), 1.0 - jnp.exp(-size)
                )
                pre = ((LN2 * rate_sum + weighted * value) * gate).astype(BF16).astype(F32)
                dpre_out[here, :] = pre
                bias_acc = bias_acc + pre
                skip_acc = skip_acc + grad * value
            else:
                dpre_out[here, :] = rate_sum
                ds_out[here, :] = weighted
            return tuple(g), tuple(acc), tuple(h), skip_acc, bias_acc

        last = state_block(steps if d == 0 else 0, state)
        h_last = tuple(h_in[pl.ds(last + (low + m) * CHUNKS, CHUNKS), :] for m in range(some))
        none = tuple(zeros for _ in range(some))
        _, acc, _, skip_acc, bias_acc = lax.fori_loop(
            0, steps, step, (tuple(back[low : low + some]), none, h_last, zeros, zeros),
            unroll=ADJOINT_UNROLL,
        )
        grads.extend(acc)
    for n in range(state):
        rows_out[n : n + 1, :] = jnp.sum(grads[n], axis=0, keepdims=True) * rates[n][0:1] * LN2
    rows_out[state : state + 1, :] = jnp.sum(bias_acc, axis=0, keepdims=True)
    rows_out[state + 1 : state + 2, :] = jnp.sum(skip_acc, axis=0, keepdims=True)


def lane_sums(sums, state):
    depth = 2 * state * LANES
    block = lax.broadcasted_iota(jnp.int32, (depth, LANES), 0) // LANES
    column = lax.broadcasted_iota(jnp.int32, (depth, LANES), 1)
    return dot(sums.astype(BF16), (block == column).astype(BF16))[:, : 2 * state]


def rate_tiles(rate, d, state, lanes):
    return [
        jnp.broadcast_to(rate[d * state + n : d * state + n + 1, lanes], (CHUNKS, LANES))
        for n in range(state)
    ]


def begin_tiles(rates, passed, maps, carry, at, d, state, lanes):
    passed = passed[d * CHUNKS : (d + 1) * CHUNKS, lanes]
    return [
        jnp.exp2(rates[n] * passed) * carry[at + n : at + n + 1, lanes]
        + maps[d * state + n, :, lanes]
        for n in range(state)
    ]


def slot_order(rows):
    row = lax.broadcasted_iota(jnp.int32, (rows, rows), 1)
    slot = lax.broadcasted_iota(jnp.int32, (rows, rows), 0)
    return (slot == (row & (CHUNKS - 1)) * (rows // CHUNKS) + (row >> 3)).astype(BF16)


def states_kernel(
    io, delta, s, proj, rate, same, normed, before, tail, got, entered, zs, dgz, cotan,
    kept, sent, carry_out, dz, h0, h1, gated,
    bc, y,
    *, reach, rank, state, bit,
):
    rows, inner = zs.shape
    width = cotan.shape[1]
    steps = rows // CHUNKS
    half = 2 * state
    tiles = inner // LANES
    upper = ((lax.axis_index("seq") >> bit) & 1) == 1
    values = got[...].astype(F32)
    held = entered[...]
    rates = rate[0:half, :]
    carry_out[0:half, :] = held[:half] + jnp.where(
        upper, leads(rates, held[2 * half : 2 * half + 2], state, False) * values, 0.0
    )
    carry_out[half : 2 * half, :] = held[half : 2 * half] + jnp.where(
        upper, 0.0, leads(rates, held[2 * half + 2 : 2 * half + 4], state, True) * values
    )
    for d, h in enumerate((h0, h1)):
        mine = slice(d * rows, (d + 1) * rows)
        spread(proj[mine, rank:], bc)
        keep = same.at[d * reach * rows : (d * reach + 1) * rows, :]

        def scan_tile(tile, _, d=d, h=h, mine=mine, keep=keep):
            lanes = lanes_of(tile)
            rates = rate_tiles(rate, d, state, lanes)
            begin = begin_tiles(rates, before, tail, carry_out, d * half, d, state, lanes)
            states_pass(
                d, steps, state, rates, begin, delta.at[mine, lanes], s.at[mine, lanes],
                keep, bc, h.at[tile], y.at[:, lanes],
            )
            return 0

        lax.fori_loop(0, tiles, scan_tile, 0)
    block = 32

    def gate_block(b, _):
        here = pl.ds(pl.multiple_of(b * block, block), block)
        there = pl.ds(pl.multiple_of(rows + b * block, block), block)
        for tile in range(tiles):
            lanes = slice(tile * LANES, (tile + 1) * LANES)
            total = 0.5 * (
                y[here, lanes] + rate[half : half + 1, lanes] * s[here, lanes]
                + rate[half + 1 : half + 2, lanes] * s[there, lanes]
            )
            gated[here, lanes] = (total * zs[here, lanes]).astype(BF16)
            dz[here, lanes] = (total * dgz[here, lanes]).astype(BF16)
        return 0

    lax.fori_loop(0, rows // block, gate_block, 0)
    even = (lax.axis_index("seq") & 1) == 0
    out_grad = dot_rows(gated[...], cotan[...]).astype(BF16)
    z_grad = jnp.concatenate(
        [dot_rows(normed[...], dz[:, at : at + width]) for at in range(0, inner, width)], axis=0
    ).astype(BF16)
    sent[...] = jnp.where(even, z_grad, out_grad)
    kept[...] = jnp.where(even, out_grad, z_grad)


def output_kernel(io, gated, tokens, out_weight, output):
    ordered = dot(slot_order(gated.shape[0]), gated[...]).astype(BF16)
    io.ready()
    output[...] = (tokens[...].astype(F32) + dot(ordered, out_weight[...])).astype(BF16)


def adjoint_kernel(
    io, delta, s, dsilu, dy, head, xext, proj, after, rate, same, carry, h, dx_in,
    dt_weight, xproj, conv_weight,
    dc_rim, small_out, dx_out,
    bc, sums, dpre, ds, rows_out, ext,
    *, d, reach, rank, state,
):
    rows, inner = dy.shape
    steps = rows // CHUNKS
    half = 2 * state
    tiles = inner // LANES
    taps = reach + 1
    cols = proj.shape[1]
    mine = slice(d * rows, (d + 1) * rows)
    keep = same.at[d * reach * rows : (d * reach + 1) * rows, :]
    spread(proj[mine, rank:], bc)
    sums[...] = jnp.zeros_like(sums)
    rows_out[...] = jnp.zeros_like(rows_out)
    grad_at = (half if d == 0 else 0) + state

    def scan_tile(tile, _):
        lanes = lanes_of(tile)
        rates = rate_tiles(rate, d, state, lanes)
        back = begin_tiles(rates, after, head, carry, grad_at, d, state, lanes)
        adjoint_pass(
            d, steps, state, rates, back, delta.at[mine, lanes], s.at[mine, lanes],
            dy.at[:, lanes], keep, rate.at[half + d : half + d + 1, lanes], bc,
            h.at[tile], sums, dpre.at[:, lanes], ds.at[:, lanes], rows_out.at[:, lanes],
        )
        return 0

    lax.fori_loop(0, tiles, scan_tile, 0)
    io.ready()
    dpre_low = dpre[...].astype(BF16)
    dt_grad = dot_rows(proj[mine, :rank].astype(BF16), dpre_low)
    dt_back = dot_cols(dpre_low, dt_weight[d])
    dproj = jnp.concatenate([dt_back, lane_sums(sums[...], state)], axis=1).astype(BF16)
    small_out[0:cols, :] = dot_rows(dproj, s[mine, :].astype(BF16))
    small_out[cols : cols + rank, :] = dt_grad
    base = 0 if d == 0 else reach * CHUNKS
    step = 2 * LANES
    for lane in range(0, inner, step):
        lanes = slice(lane, lane + step)
        total = ds[:, lanes] + dot(dproj, xproj[d, :, lanes])
        ext[base : base + rows, lanes] = (total * dsilu[mine, lanes]).astype(BF16).astype(F32)
    wide = lax.broadcasted_iota(jnp.int32, (CHUNKS, inner), 0)
    for i in range(reach):
        if d == 0:
            moved = pltpu.roll(ext[i * CHUNKS : (i + 1) * CHUNKS, :], CHUNKS - 1, axis=0)
            ext[rows + i * CHUNKS : rows + (i + 1) * CHUNKS, :] = jnp.where(
                wide == CHUNKS - 1, 0.0, moved
            )
        else:
            moved = pltpu.roll(ext[rows + i * CHUNKS : rows + (i + 1) * CHUNKS, :], 1, axis=0)
            ext[i * CHUNKS : (i + 1) * CHUNKS, :] = jnp.where(wide == 0, 0.0, moved)

    conv_w = conv_weight[d].astype(F32)
    block = 32
    zeros = jnp.zeros((CHUNKS, LANES), F32)

    def folded(values):
        return functools.reduce(
            lambda a, b: a + b, [values[i : i + CHUNKS] for i in range(0, block, CHUNKS)]
        )

    base_row = cols + rank
    for tile in range(tiles):
        lanes = slice(tile * LANES, (tile + 1) * LANES)
        weight = conv_w[:, lanes]

        def conv_block(b, totals, lanes=lanes, weight=weight):
            here = pl.multiple_of(b * block, block)
            totals = list(totals)
            mid = ext[pl.ds(here + base, block), lanes]
            total = weight[reach:taps] * mid
            totals[reach] = totals[reach] + folded(mid * xext[pl.ds(here + reach * CHUNKS, block), lanes])
            totals[taps] = totals[taps] + folded(mid)
            for k in range(1, taps):
                past = same[pl.ds((k - 1) * rows + here, block), :]
                ahead = same[pl.ds((reach + k - 1) * rows + here, block), :]
                if d == 0:
                    given = ext[pl.ds(here + k * CHUNKS, block), lanes] * ahead
                    taken = xext[pl.ds(here + (reach - k) * CHUNKS, block), lanes] * past
                else:
                    given = ext[pl.ds(here + (reach - k) * CHUNKS, block), lanes] * past
                    taken = xext[pl.ds(here + (reach + k) * CHUNKS, block), lanes] * ahead
                total = total + weight[reach - k : taps - k] * given
                totals[reach - k] = totals[reach - k] + folded(mid * taken)
            if dx_in is not None:
                total = total + dx_in[pl.ds(here, block), lanes]
            dx_out[pl.ds(here, block), lanes] = total
            return tuple(totals)

        totals = lax.fori_loop(0, rows // block, conv_block, (zeros,) * (taps + 1), unroll=2)
        for i in range(taps + 1):
            at = state + 2 + i
            rows_out[at : at + 1, lanes] = jnp.sum(totals[i], axis=0, keepdims=True)

    edge = []
    for i in range(CHUNKS):
        row = jnp.zeros((1, inner), F32)
        for k in range(1, taps):
            j = i - CHUNKS + k if d == 0 else steps + i - k
            if (d == 0 and j >= 0) or (d == 1 and j < steps):
                sub = 0 if d == 0 else CHUNKS - 1
                at = (d * reach + k - 1) * rows + j * CHUNKS + sub
                mask = jnp.concatenate([same[at : at + 1, :]] * tiles, axis=1)
                at = base + j * CHUNKS + sub
                row = row + conv_w[reach - k : taps - k] * ext[at : at + 1, :] * mask
        edge.append(row)
    dc_rim[...] = jnp.concatenate(edge, axis=0)
    small_out[base_row:, :] = rows_out[0 : small_out.shape[0] - base_row, :]


def first_adjoint(io, *refs, **static):
    adjoint_kernel(io, *refs[:12], None, *refs[12:], **static)


def second_adjoint(io, *refs, **static):
    in_far, in_near, moves = refs[16], refs[20], refs[21]
    copy = fetch(in_far, in_near, moves.at[0])
    adjoint_kernel(io, *refs[:16], *refs[17:20], *refs[22:], **static)
    copy.wait()


def last_kernel(
    io, dx, rim0, rim1, small0, small1, normed, nhalo, live, in_weight,
    kept, sent, low,
    lines, grads,
):
    rows, inner = dx.shape
    width = normed.shape[1]
    folds = inner // width
    fold = kept.shape[0]
    edges = 2 * CHUNKS
    for tile in range(inner // LANES):
        lanes = slice(tile * LANES, (tile + 1) * LANES)
        lines[0:rows, lanes] = (dx[:, lanes] * live[...]).astype(BF16)
    low[...] = lines[0:rows, :]
    lines[rows : rows + edges, :] = jnp.concatenate([rim0[...], rim1[...]], axis=0).astype(BF16)
    both = jnp.concatenate([normed[...], nhalo[0:edges, :]], axis=0)
    size = small0.shape[0]
    for i in range(folds):
        lanes = slice(i * width, (i + 1) * width)
        at = i * fold
        grads[at : at + width, :] = dot_rows(both, lines[:, lanes]).astype(BF16)
        at += width
        grads[at : at + 2 * size, :] = jnp.concatenate(
            [small0[:, lanes], small1[:, lanes]], axis=0
        ).astype(BF16)
        at += 2 * size
        grads[at : (i + 1) * fold, :] = jnp.zeros(((i + 1) * fold - at, width), BF16)
    rim = dot_cols(lines[rows : rows + edges, :], in_weight[:, 0:inner])
    even = (lax.axis_index("seq") & 1) == 0
    turned = jnp.concatenate([rim[CHUNKS:], rim[:CHUNKS]], axis=0)
    left, right = grads[0:fold, :], grads[fold : 2 * fold, :]
    kept[...] = jnp.where(even, left, right)
    sent[...] = jnp.where(even, right, left)
    at = width + 2 * size
    sent[at : at + edges, :] = jnp.where(even, turned, rim).astype(BF16)


def finish_kernel(
    io, low, dz, in_weight, rims, chip_rim, heights, widths, tokens, cotangent, valid, gain,
    input_grad,
):
    rows, width = tokens.shape
    inner = low.shape[1]
    even = (lax.axis_index("seq") & 1) == 0
    start = lax.axis_index("seq") * rows
    back = slot_order(rows)
    dn = dot_cols(dot(back, low[...]).astype(BF16), in_weight[:, 0:inner]) + dot_cols(
        dot(back, dz[...]).astype(BF16), in_weight[:, inner : 2 * inner]
    )
    io.ready()
    from_core = rims[0:CHUNKS, :].astype(F32)
    from_chip = chip_rim[CHUNKS : 2 * CHUNKS, :].astype(F32)
    before = jnp.where(even, from_chip, from_core)
    after = jnp.where(even, from_core, from_chip)
    end = image_ends(heights, widths)[-1]
    row = lax.broadcasted_iota(jnp.int32, (CHUNKS, rows), 0)
    slot = lax.broadcasted_iota(jnp.int32, (CHUNKS, rows), 1)
    alive = jnp.broadcast_to(valid[...].astype(F32), (CHUNKS, rows))
    alive = jnp.where(start + slot < end, alive, 0.0)
    first = jnp.sum(jnp.where(slot == row, alive, 0.0), axis=1, keepdims=True)
    last = jnp.sum(jnp.where(slot == rows - CHUNKS + row, alive, 0.0), axis=1, keepdims=True)
    values = jnp.concatenate(
        [
            dn[0:CHUNKS, :] + first * before, dn[CHUNKS : rows - CHUNKS, :],
            dn[rows - CHUNKS : rows, :] + last * after,
        ],
        axis=0,
    )
    inputs = tokens[...].astype(F32)
    inv_rms = lax.rsqrt(jnp.mean(inputs * inputs, axis=-1, keepdims=True) + NORM_EPS)
    scaled = values * gain[...].astype(F32).reshape(1, width)
    mean = jnp.mean(scaled * inputs, axis=-1, keepdims=True)
    input_grad[...] = (
        cotangent[...].astype(F32) + inv_rms * scaled - inputs * (inv_rms * inv_rms * inv_rms) * mean
    )


def blocks_in_order(mine, other, into_first, into_second):
    size = mine.shape[1]
    is_even = (lax.axis_index("seq") & 1) == 0
    here = lax.axis_index("img")
    for k in range(mine.shape[0]):
        a, b = mine[here ^ k].astype(F32), other[here ^ k].astype(F32)
        into_first(k * size, jnp.where(is_even, a, b))
        into_second(k * size, jnp.where(is_even, b, a))


def weighted_rows(values, weights):
    total = None
    for at in range(0, values.shape[1], LANES):
        part = values[:, at : at + LANES] * weights[:, at : at + LANES].astype(F32)
        total = part if total is None else total + part
    return total


def first_unpack(io, mine, other, in_weight, parts, in_far, out_far, out_w, z_half, moves):
    width = out_w.shape[1]
    inner = out_w.shape[0]

    def put_out(at, values):
        out_w[at : at + values.shape[0], :] = values

    def put_z(at, values):
        size = values.shape[0]
        column = at // width * width
        z_half[at % width : at % width + size, column : column + width] = values

    blocks_in_order(mine, other, put_out, put_z)
    leaving = [
        fetch(out_w, out_far, moves.at[0]),
        fetch(z_half, in_far.at[:, inner : 2 * inner], moves.at[1]),
    ]
    parts[...] = weighted_rows(z_half[...], in_weight[:, inner : 2 * inner])
    for copy in leaving:
        copy.wait()


def second_unpack(
    io, mine, other, in_weight, parts, gain_in, in_before,
    conv_w, conv_b, xproj, dt_w, dt_b, a_log, skip, gain, in_far,
    left, right, x_half, moves,
    *, count, state, rank, cols, taps,
):
    width = left.shape[1]
    inner = x_half.shape[1]

    def put_left(at, values):
        left[at : at + values.shape[0], :] = values

    def put_right(at, values):
        right[at : at + values.shape[0], :] = values

    blocks_in_order(mine, other, put_left, put_right)
    for i, half in enumerate((left, right)):
        x_half[:, i * width : (i + 1) * width] = half[0:width, :]
    leaving = fetch(x_half, in_far.at[:, 0:inner], moves.at[0])
    for i, half in enumerate((left, right)):
        lanes = slice(i * width, (i + 1) * width)
        for d in range(2):
            at = width + d * count
            xproj[d, :, lanes] = half[at : at + cols, :]
            at += cols
            dt_w[d, :, lanes] = half[at : at + rank, :]
            at += rank
            a_log[d, :, lanes] = half[at : at + state, :]
            dt_b[d : d + 1, lanes] = half[at + state : at + state + 1, :]
            skip[d : d + 1, lanes] = half[at + state + 1 : at + state + 2, :]
            at += state + 2
            conv_w[d, :, lanes] = half[at : at + taps, :]
            conv_b[d : d + 1, lanes] = half[at + taps : at + taps + 1, :]
    total = parts[...] + weighted_rows(x_half[...], in_weight[:, 0:inner])
    high = total.astype(BF16)
    rest = (total - high.astype(F32)).astype(BF16)
    ones = jnp.ones((2 * CHUNKS, LANES), BF16)
    sums = (dot_cols(ones, high) + dot_cols(ones, rest))[0:1]
    io.ready()
    gain[...] = (sums / gain_in[...].astype(F32).reshape(1, width)).reshape(width)
    io.done()
    leaving.wait()


IN_VMEM = pl.BlockSpec(memory_space=pltpu.VMEM)
IN_SMEM = pl.BlockSpec(memory_space=pltpu.SMEM)
FAR = pl.BlockSpec(memory_space=pltpu.HBM)


def shape(*dims, dtype=F32):
    return jax.ShapeDtypeStruct(dims, dtype)


def low(*dims):
    return jax.ShapeDtypeStruct(dims, BF16)


def near(*dims, dtype=F32):
    return pltpu.VMEM(dims, dtype)


def scratch(*dims, dtype=F32):
    return pltpu.VMEM(dims, dtype)


def like(*outs):
    return [pltpu.VMEM(out.shape, out.dtype) for out in outs]


def moves(*dims):
    return pltpu.SemaphoreType.DMA(dims)


class Moves:
    def __init__(self, arrive, leave):
        self.arrive, self.leave, self.left = arrive, leave, False
        for copy in arrive:
            copy.start()

    def ready(self):
        for copy in self.arrive:
            copy.wait()

    def done(self):
        self.left = True
        for copy in self.leave:
            copy.start()


def call(
    kernel, name, args, outs, scratches=(), far=(), far_outs=(), near_args=(), near_outs=(),
    scalars=(), handed=(), aliases=(), us=4, limit=4,
):
    small = tuple(scalars) + tuple(args)
    small, far = (
        tuple(pltpu.with_memory_space_constraint(x, pltpu.HBM) for x in arrays)
        for arrays in (small, far)
    )
    n_hand = len(handed)
    near_args = tuple(handed) + tuple(near_args)
    n_near, n_small, n_far = len(near_args), len(small), len(far)
    n_near_outs, n_outs, n_far_outs = len(near_outs), len(outs), len(far_outs)

    def wrapped(*refs):
        refs = list(refs)

        def take(count):
            taken = refs[:count]
            del refs[:count]
            return taken

        near_in, small_in, far_in = take(n_near), take(n_small), take(n_far)
        near_out, out, far_out = take(n_near_outs), take(n_outs), take(n_far_outs)
        take(n_hand)
        small_here, out_here = take(n_small), take(n_outs)
        in_moves, out_moves = take(2)
        io = Moves(
            [pltpu.make_async_copy(a, b, in_moves.at[i]) for i, (a, b) in enumerate(zip(small_in, small_here))],
            [pltpu.make_async_copy(a, b, out_moves.at[i]) for i, (a, b) in enumerate(zip(out_here, out))],
        )
        kernel(io, *near_in, *small_here, *far_in, *near_out, *out_here, *far_out, *refs)
        if not io.left:
            io.done()
        for copy in io.leave:
            copy.wait()

    return pl.pallas_call(
        wrapped,
        out_shape=list(near_outs) + [
            pltpu.HBM(out.shape, out.dtype) for out in tuple(outs) + tuple(far_outs)
        ] + [pltpu.VMEM(x.shape, x.dtype) for x in handed],
        in_specs=[IN_VMEM] * n_near + [FAR] * (n_small + n_far),
        out_specs=[IN_VMEM] * n_near_outs + [FAR] * (n_outs + n_far_outs) + [IN_VMEM] * n_hand,
        input_output_aliases={
            **{i: n_near_outs + n_outs + n_far_outs + i for i in range(n_hand)},
            **{n_near + n_small + i: n_near_outs + n_outs + o for i, o in aliases},
        },
        scratch_shapes=(
            [pltpu.SMEM(a.shape, a.dtype) for a in scalars] + like(*args) + like(*outs)
            + [moves(max(n_small, 1)), moves(max(n_outs, 1))] + list(scratches)
        ),
        compiler_params=pltpu.CompilerParams(vmem_limit_bytes=limit * 2**20),
        cost_estimate=pl.CostEstimate(flops=us * 2000000000, bytes_accessed=0, transcendentals=0),
        name=name,
    )(*near_args, *small, *far)


def call_edges(tokens, valid):
    edge = 2 * CHUNKS
    width = tokens.shape[1]
    outs = [near(edge, width, dtype=BF16), near(edge, width, dtype=BF16)]
    return call(edges_kernel, "edges", (tokens, valid), (), near_outs=outs, us=1, limit=2)


def call_front(
    heights, widths, valid, gain, tokens, cotangent, in_weight, out_weight, weights, reach,
):
    rows, width = tokens.shape
    inner = out_weight.shape[0]
    one = near(rows, inner)
    row = near(rows, width, dtype=BF16)
    return call(
        functools.partial(front_kernel, reach=reach, weights=len(weights)), "front", (valid, gain), (),
        like(tokens, cotangent, low(width, inner), out_weight) + [moves(5 + len(weights))],
        (tokens, cotangent, in_weight, out_weight) + weights, (), (),
        [
            row, one, one, one, one, near(rows, LANES), near(2 * reach * rows, LANES), row,
            near(width, inner, dtype=BF16),
        ] + like(*weights),
        (heights, widths), us=4, limit=12,
    )


def call_middle(handed, used, from_core, from_chip, arrays, scalars, gain, reach, cols):
    x, a_log = arrays[0], arrays[-2]
    rows, inner = x.shape
    state, width = a_log.shape[1], gain.shape[0]
    half = 2 * state
    both = near(2 * rows, inner)
    maps = near(half, CHUNKS, inner)
    ends = near(2 * CHUNKS, inner)
    n_hand = len(handed)

    def kernel(io, *refs):
        middle_kernel(io, *(refs[i] for i in used), *refs[n_hand:], reach=reach)

    return call(
        kernel, "middle", (gain,), (),
        [
            scratch(2 * rows, inner, dtype=BF16), scratch(rows, half * LANES),
            scratch(state, CHUNKS, inner), scratch(state, CHUNKS, inner), scratch(CHUNKS, inner),
        ],
        near_args=(from_core, from_chip) + arrays,
        near_outs=[
            near(2 * half + CHUNKS + half, inner), near(2 * half + 2 * CHUNKS, inner, dtype=BF16),
            both, both, both, maps, maps, near(rows + 2 * reach * CHUNKS, inner),
            near(2 * rows, cols), ends, ends, near(half + CHUNKS, inner),
            near(4 * CHUNKS, width, dtype=BF16),
        ],
        scalars=scalars, handed=handed, us=20, limit=9,
    )


def call_join(got, summary, entered, state, bit, final):
    inner = summary.shape[1]
    half = 2 * state
    outs = [
        near(2 * half + CHUNKS, inner),
        near(half if final else 2 * half + 2 * CHUNKS, inner, dtype=BF16),
    ]
    if not final:
        outs = [near(2 * half + CHUNKS + half, inner)] + outs
    args = (got, summary) + (() if entered is None else (entered,))
    kernel = first_join if entered is None else join_kernel
    joined = call(
        functools.partial(kernel, state=state, bit=bit, final=final), "join", (), (),
        near_args=args, near_outs=outs, us=1, limit=4,
    )
    return joined if not final else [None] + list(joined)


def call_states(handed, used, before, tail, got, entered, zs, dgz, cotan, rank, reach, state, bit):
    rows, inner = zs.shape
    width = cotan.shape[1]
    half = 2 * state
    n_hand = len(handed)

    def kernel(io, *refs):
        states_kernel(
            io, *(refs[i] for i in used), *refs[n_hand:], reach=reach, rank=rank, state=state, bit=bit
        )

    grad = near(inner, width, dtype=BF16)
    one = near(rows, inner, dtype=BF16)
    held = near(inner // LANES, (rows // CHUNKS + 1) * state * CHUNKS, LANES)
    return call(
        kernel, "states", (), (),
        [scratch(rows, half * LANES), scratch(rows, inner)],
        near_args=(before, tail, got, entered, zs, dgz, cotan),
        near_outs=[grad, grad, near(2 * half, inner), one, held, held, one], handed=handed, us=12,
        limit=9,
    )


def adjoint_scratch(rows, inner, half, reach, small, cols, rank):
    return [
        scratch(rows, half * LANES), scratch(rows, half * LANES), scratch(rows, inner), scratch(rows, inner), scratch(small - cols - rank, inner),
        scratch(rows + reach * CHUNKS, inner),
    ]


def call_first_adjoint(handed, used, h, weights, small, reach, rank, state):
    rows, inner = handed[used[3]].shape
    cols = handed[used[6]].shape[1]
    n_hand = len(handed)

    def kernel(io, *refs):
        first_adjoint(
            io, *(refs[i] for i in used), *refs[n_hand:], d=0, reach=reach, rank=rank, state=state
        )

    return call(
        kernel, "adjoint_up", weights, (),
        adjoint_scratch(rows, inner, 2 * state, reach, small, cols, rank), near_outs=[
            near(CHUNKS, inner), near(small, inner), near(rows, inner),
        ], near_args=(h,), handed=handed, us=14, limit=13,
    )


def call_second_adjoint(handed, arrays, weights, in_weight, small, reach, rank, state):
    rows, inner = arrays[3].shape
    cols = arrays[6].shape[1]
    n_hand = len(handed)

    def kernel(io, *refs):
        second_adjoint(io, *refs[n_hand:], d=1, reach=reach, rank=rank, state=state)

    return call(
        kernel, "adjoint_down", weights, (),
        [moves(1)] + adjoint_scratch(rows, inner, 2 * state, reach, small, cols, rank),
        (in_weight,), (), arrays,
        [near(CHUNKS, inner), near(small, inner), near(rows, inner), near(*in_weight.shape, dtype=BF16)],
        handed=handed, us=14, limit=13,
    )


def call_last(handed, dx, rim0, rim1, small0, small1, normed, nhalo, live):
    rows, inner = dx.shape
    width = normed.shape[1]
    small = small0.shape[0]
    folds = inner // width
    edges = 2 * CHUNKS
    fold = -(-(width + 2 * small + edges) // 64) * 64
    n_hand = len(handed)

    def kernel(io, *refs):
        last_kernel(io, *refs[n_hand : n_hand + 8], refs[n_hand - 1], *refs[n_hand + 8 :])

    return call(
        kernel, "last", (), (),
        [
            scratch(rows + edges, inner, dtype=BF16), scratch(folds * fold, width, dtype=BF16),
        ],
        near_args=(dx, rim0, rim1, small0, small1, normed, nhalo, live),
        near_outs=[
            near(fold, width, dtype=BF16), near(fold, width, dtype=BF16),
            near(rows, inner, dtype=BF16),
        ],
        handed=handed, us=3, limit=8,
    )


def partner(axis, bit):
    return [(i, i ^ (1 << bit)) for i in range(lax.axis_size(axis))]


def bits_of(axis):
    return (lax.axis_size(axis) - 1).bit_length()


def other_core(values):
    return lax.ppermute(values, "seq", partner("seq", 0))


def next_chip(values):
    count = lax.axis_size("seq")
    pairs = [(i, i + 1) for i in range(1, count - 1, 2)]
    return lax.ppermute(values, "seq", pairs + [(j, i) for i, j in pairs])


def split_kernel(io, kept, got, own, *sent, edges):
    if edges:
        at = got.shape[0] - edges[1]
        sent[-1][...] = got[at : at + edges[0], :]
        sent = sent[:-1]
    count = len(sent) + 1
    rows = own.shape[0]
    here = lax.axis_index("img")
    for k in range(count):
        at = pl.ds(pl.multiple_of((here ^ k) * rows, rows), rows)
        total = kept[at, :].astype(F32) + got[at, :].astype(F32)
        if k == 0:
            own[...] = total
        else:
            sent[k - 1][...] = total.astype(BF16)


def add_kernel(io, *refs, outs):
    total = refs[0][...].astype(F32)
    for ref in refs[1 : len(refs) - outs]:
        total = total + ref[...].astype(F32)
    for ref in refs[len(refs) - outs :]:
        ref[...] = total.astype(ref.dtype)


def add(values, whole=True):
    rows, width = values[0].shape
    outs = [near(rows, width)] * whole + [near(rows, width, dtype=BF16)]
    sums = call(
        functools.partial(add_kernel, outs=len(outs)), "add", (), (), near_args=values,
        near_outs=outs, us=1, limit=2,
    )
    return sums if whole else sums[0]


def add_rim_kernel(io, *refs, count, bit):
    values, moving, stay = refs[:count], refs[count], refs[count + 1]
    low_out, stay_out = refs[-2:]
    rows = values[0].shape[0]
    total = values[0][...]
    for ref in values[1:]:
        total = total + ref[0:rows, :].astype(F32)
    if len(refs) > count + 4:
        refs[-3][...] = total
    low_out[0:rows, :] = total.astype(BF16)
    if bit is None:
        low_out[rows:, :] = moving[...]
        stay_out[...] = jnp.zeros_like(stay_out)
        return
    came = values[-1][rows:, :]
    if low_out.shape[0] > rows:
        low_out[rows:, :] = came
    position = lax.axis_index("seq")
    chip = position >> 1
    chip = jnp.where((position & 1) == 0, chip, lax.axis_size("seq") // 2 - 1 - chip)
    lowest = chip & ((2 << bit) - 1)
    stay_out[...] = jnp.where(lowest == (1 << bit), came, stay[...])


def add_rim(values, moving, stay, bit, final=False):
    rows, width = values[0].shape
    edge = moving.shape[0]
    sent = rows if final else rows + edge
    outs = [near(rows, width)] * (not final)
    outs += [near(sent, width, dtype=BF16), near(edge, width, dtype=BF16)]
    sums = call(
        functools.partial(add_rim_kernel, count=len(values), bit=bit), "add", (), (),
        near_args=tuple(values) + (moving, stay), near_outs=outs, us=1, limit=2,
    )
    return [None] * final + list(sums)


def stack_kernel(io, *refs):
    for k, ref in enumerate(refs[:-1]):
        refs[-1][k] = ref[...]


def plane_pairs(k):
    return [(i, i ^ k) for i in range(lax.axis_size("img"))]


def chips_sum(kept, sent, edges=()):
    count = lax.axis_size("img")
    rows, width = kept.shape
    block = (rows // count, width)
    got = other_core(sent)
    own, *parts = call(
        functools.partial(split_kernel, edges=edges), "split", (), (), near_args=(kept, got),
        near_outs=[near(*block)] + [near(*block, dtype=BF16)] * (count - 1)
        + [near(rim_rows, width, dtype=BF16) for rim_rows in edges[:1]],
        us=1, limit=2,
    )
    rim = parts.pop() if edges else None
    blocks = [own] + [
        lax.ppermute(part, "img", plane_pairs(k + 1)) for k, part in enumerate(parts)
    ]
    return blocks, rim


def line_steps(total, low):
    bits = bits_of("seq")
    for bit in range(1, bits):
        got = lax.ppermute(low, "seq", partner("seq", bit))
        if bit < bits - 1:
            total, low = add([total, got])
        else:
            low = add([total, got], whole=False)
    return low


def line_steps_with_rims(blocks, rim, first_low, beside):
    stay = rim
    total, low, stay = add_rim(blocks, rim, stay, None)
    low, first_low = tied(low, first_low)
    bits = bits_of("seq")
    for bit in range(1, bits):
        got = lax.ppermute(low, "seq", partner("seq", bit))
        if bit == 1:
            got, beside = tied(got, beside)
        if bit == bits - 1:
            first_blocks = plane_blocks(first_low)
        total, low, stay = add_rim([total, got], rim, stay, bit - 1, bit == bits - 1)
        if bit == bits - 2:
            low, first_low = tied(low, first_low)
    return low, stay, first_blocks, beside


def plane_blocks(low):
    count = lax.axis_size("img")
    return [low] + [lax.ppermute(low, "img", plane_pairs(k)) for k in range(1, count)]


def stacked(blocks):
    low, count = blocks[0], len(blocks)
    return call(
        stack_kernel, "stack", (), (), near_args=blocks,
        near_outs=[near(count, *low.shape, dtype=BF16)], us=1, limit=2,
    )[0]


def tied(first, second):
    return lax.optimization_barrier((first, second))


def body(
    tokens, cotangent, heights, widths, valid, norm_gain, in_weight, conv_weight, conv_bias,
    xproj_weight, dt_weight, dt_bias, a_log, skip, out_weight,
):
    rows, width = tokens.shape[1:]
    inner = out_weight.shape[0]
    state = a_log.shape[1]
    rank = dt_weight.shape[1]
    cols = xproj_weight.shape[2]
    taps = conv_weight.shape[1]
    reach = taps - 1
    count = bits_of("seq")
    tokens, cotangent = tokens[0], cotangent[0]
    xproj = xproj_weight.transpose(0, 2, 1)

    to_core, to_chip = call_edges(tokens, valid)
    from_core, from_chip = other_core(to_core), next_chip(to_chip)
    weights = (conv_weight, conv_bias, xproj, dt_weight, dt_bias, a_log, skip)
    normed, x, zs, dgz, dy, live, same, cotan, in_x, *near_weights = call_front(
        heights, widths, valid, norm_gain, tokens, cotangent, in_weight, out_weight, weights, reach
    )
    (
        summary, sent, delta, s, dsilu, tail, head, xext, proj, before, after, rate, nhalo,
        dy, live, same, normed, zs, dgz, cotan,
    ) = call_middle(
        (dy, live, same, normed, zs, dgz, cotan), (0, 1, 2), from_core, from_chip,
        (x, in_x) + tuple(near_weights), (heights, widths), norm_gain, reach, cols,
    )
    entered = None
    for bit in range(count - 1):
        got = lax.ppermute(sent, "seq", partner("seq", bit))
        summary, entered, sent = call_join(got, summary, entered, state, bit, bit == count - 2)
    got = lax.ppermute(sent, "seq", partner("seq", count - 1))
    handed = (
        delta, s, dsilu, dy, head, xext, proj, after, rate, same, live, normed, nhalo,
    )
    kept, sent, carry, dz, h0, h1, gated, *handed = call_states(
        handed, (0, 1, 6, 8, 9, 11), before, tail, got, entered, zs, dgz, cotan, rank, reach, state,
        count - 1,
    )

    blocks, _ = chips_sum(kept, sent)
    small = -(-(cols + rank + state + 2 + taps + 1) // CHUNKS) * CHUNKS
    weights = (dt_weight, xproj, conv_weight)
    handed = tuple(handed[:10]) + (carry,) + tuple(handed[10:]) + (dz, gated, h1)
    rim0, small0, dx, *handed = call_first_adjoint(
        handed, tuple(range(11)), h0, weights, small, reach, rank, state
    )
    *blocks, dx = lax.optimization_barrier((*blocks, dx))
    first_sum, first_low = add(blocks)
    first_sum, first_low, dx = lax.optimization_barrier((first_sum, first_low, dx))
    arrays, passed, h1 = tuple(handed[:11]), tuple(handed[11:-1]), handed[-1]
    if bits_of("seq") > 3:
        first_low = line_steps(first_sum, first_low)
    else:
        devices = lax.axis_size("seq")
        blocks = [first_sum] + [
            lax.ppermute(first_low, "seq", [(i, i ^ k) for i in range(devices)])
            for k in range(2, devices, 2)
        ]
    rim1, small1, dx, in_near, *passed = call_second_adjoint(
        passed, arrays + (h1, dx), weights, in_weight, small, reach, rank, state
    )
    live, normed, nhalo, dz, gated = passed
    if bits_of("seq") <= 3:
        *blocks, dx = lax.optimization_barrier((*blocks, dx))
        first_low = add(blocks, whole=False)
    kept, sent, dx_low, dz, gated, in_near = call_last(
        (dz, gated, in_near), dx, rim0, rim1, small0, small1, normed, nhalo, live
    )

    edges = (2 * CHUNKS, kept.shape[0] - width - 2 * small)
    blocks, rim = chips_sum(kept, sent, edges)


    output = call(
        output_kernel, "output", (tokens, out_weight), [low(rows, width)], near_args=(gated,), us=2,
        limit=6,
    )[0]
    second_low, chip_rim, first_blocks, output = line_steps_with_rims(blocks, rim, first_low, output)
    blocks = plane_blocks(second_low)
    _, *first_blocks = lax.optimization_barrier((blocks[1], *first_blocks))
    first_mine = stacked(first_blocks)
    first_other = other_core(first_mine)
    input_grad = call(
        finish_kernel, "finish", (tokens, cotangent, valid, norm_gain), [shape(rows, width)],
        near_args=(dx_low, dz, in_near, rim, chip_rim), scalars=(heights, widths), us=3, limit=8,
    )[0]
    blocks, input_grad = lax.optimization_barrier((blocks, input_grad))
    second_mine = stacked(blocks)
    second_other = other_core(second_mine)
    parts, in_total, out_total = call(
        first_unpack, "unpack_first", (), (),
        [scratch(inner, width), scratch(width, inner), moves(2)],
        far_outs=[shape(width, 2 * inner), shape(inner, width)],
        near_args=(first_mine, first_other, in_near), near_outs=[near(width, LANES)], us=2, limit=8,
    )
    second_other, parts = tied(second_other, parts)
    fold = kept.shape[0]
    (
        conv_total, bias_total, xproj_total, dtw_total, dtb_total, a_total, skip_total, gain_total,
        in_total,
    ) = call(
        functools.partial(
            second_unpack, count=small, state=state, rank=rank, cols=cols, taps=taps
        ),
        "unpack_second", (norm_gain,),
        [
            shape(2, taps, inner), shape(2, inner), shape(2, cols, inner), shape(2, rank, inner),
            shape(2, inner), shape(2, state, inner), shape(2, inner), shape(width),
        ],
        [scratch(fold, width), scratch(fold, width), scratch(width, inner), moves(1)],
        (in_total,), [shape(width, 2 * inner)], (second_mine, second_other, in_near, parts),
        aliases=((0, 0),), us=2, limit=10,
    )
    return (
        output[None], input_grad[None], gain_total, in_total, conv_total, bias_total,
        xproj_total.transpose(0, 2, 1), dtw_total, dtb_total, a_total, skip_total, out_total,
    )


def solution(mesh):
    split = P("img", "seq", None)
    placed = (split, split, P("img", None), P("img", None), P("img", "seq")) + (P(),) * 10
    return jax.shard_map(
        body,
        mesh=mesh,
        in_specs=placed,
        out_specs=(split, split) + (P(),) * 10,
        check_vma=False,
    )
```

```python
import functools

import jax
import jax.numpy as jnp
from jax import lax
from jax.experimental import pallas as pl
from jax.experimental.pallas import tpu as pltpu
from jax.sharding import PartitionSpec as P

NORM_EPS = 1e-05
CONTRACT_ROWS = (((0,), (0,)), ((), ()))
CONTRACT_COLS = (((1,), (1,)), ((), ()))
LOG2E = 1.4426950408889634
LN2 = 0.6931471805599453
BREAK = 1e30
CHUNKS = 8
LANES = 128
SUMMARY_STATES = 8
SUMMARY_UNROLL = 16
STATES_UNROLL = 32
ADJOINT_STATES = 8
ADJOINT_UNROLL = 16
F32 = jnp.float32
BF16 = jnp.bfloat16


def dot(a, b):
    return jnp.dot(a, b, preferred_element_type=F32)


def dot_rows(a, b):
    return lax.dot_general(a, b, CONTRACT_ROWS, preferred_element_type=F32)


def dot_cols(a, b):
    return lax.dot_general(a, b, CONTRACT_COLS, preferred_element_type=F32)


def sigmoid(v):
    return 1.0 / (1.0 + jnp.exp(-v))


def fetch(source, target, semaphore):
    copy = pltpu.make_async_copy(source, target, semaphore)
    copy.start()
    return copy


def lanes_of(tile):
    return pl.ds(pl.multiple_of(tile * LANES, LANES), LANES)


def rows_of(j, count=CHUNKS):
    return pl.ds(pl.multiple_of(j * CHUNKS, CHUNKS), count)


def chunk_order(rows):
    row = lax.broadcasted_iota(jnp.int32, (rows, rows), 0)
    slot = lax.broadcasted_iota(jnp.int32, (rows, rows), 1)
    return slot == (row & (CHUNKS - 1)) * (rows // CHUNKS) + (row >> 3)


def image_ends(heights, widths):
    ends, total = [], 0
    for i in range(heights.shape[1]):
        total = total + heights[0, i] * widths[0, i]
        ends.append(total)
    return ends


def segment_of(places, ends):
    found = jnp.zeros_like(places)
    for end in ends:
        found = found + (places >= end).astype(jnp.int32)
    return found


def places_of(first, rows):
    row = lax.broadcasted_iota(jnp.int32, (rows, LANES), 0)
    return first + (row & (CHUNKS - 1)) * (rows // CHUNKS) + (row >> 3)


def edges_kernel(io, tokens, valid, to_core, to_chip):
    rows = tokens.shape[0]
    edge = to_core.shape[0]
    io.ready()
    row = lax.broadcasted_iota(jnp.int32, (edge, rows), 0)
    slot = lax.broadcasted_iota(jnp.int32, (edge, rows), 1)
    held = jnp.broadcast_to(valid[...].astype(F32), (edge, rows))
    first = jnp.where(slot == row, held, 0.0).astype(BF16)
    last = jnp.where(slot == rows - edge + row, held, 0.0).astype(BF16)
    first = dot(first, tokens[...]).astype(BF16)
    last = dot(last, tokens[...]).astype(BF16)
    even = (lax.axis_index("seq") & 1) == 0
    to_core[...] = jnp.where(even, last, first)
    to_chip[...] = jnp.where(even, first, last)


def spread(values, target):
    count = values.shape[1]
    high = values.astype(BF16)
    low = (values - high.astype(F32)).astype(BF16)
    both = jnp.concatenate([high, low], axis=1)
    row = lax.broadcasted_iota(jnp.int32, (2 * count, LANES), 0)
    row = jnp.where(row < count, row, row - count)
    for at in range(0, count, 2):
        pick = jnp.concatenate([(row == at).astype(BF16), (row == at + 1).astype(BF16)], axis=1)
        target[:, at * LANES : (at + 2) * LANES] = dot(both, pick)


def windows(span, up, sublane):
    sign = 1 if up else -1

    def from_before(value, by, fill):
        moved = pltpu.roll(value, (sign * by) % CHUNKS, axis=0)
        kept = sublane >= by if up else sublane < CHUNKS - by
        return jnp.where(kept, moved, fill)

    two = span + from_before(span, 1, 0.0)
    four = two + from_before(two, 2, 0.0)
    eight = four + from_before(four, 4, 0.0)
    edge = [jnp.where(sublane >= by if up else sublane < CHUNKS - by, 0.0, BREAK) for by in (1, 2, 4)]
    return (span + edge[0], two + edge[1], four + edge[2]), from_before(eight, 1, 0.0)


def chain(rate, sums, tail, up, sublane):
    sign = 1 if up else -1
    for by, span in zip((1, 2, 4), sums):
        tail = jnp.exp2(rate * span) * pltpu.roll(tail, (sign * by) % CHUNKS, axis=0) + tail
    end = CHUNKS - 1 if up else 0
    kept = sublane >= 1 if up else sublane < CHUNKS - 1
    return jnp.where(kept, pltpu.roll(tail, sign % CHUNKS, axis=0), 0.0), tail[end : end + 1]


def front_kernel(
    io, tokens, cotangent, in_weight, out_weight, heights, widths, valid, gain, *refs, reach, weights,
):
    (
        normed_out, x_out, zs_out, dgz_out, dy, live, same_out, cotan, in_x, halo_live, gains_out,
    ) = refs[weights : weights + 11]
    near_weights = refs[weights + 11 : 2 * weights + 11]
    ins = refs[2 * weights + 11]
    rows, width = tokens.shape
    inner = out_weight.shape[0]
    tiles = inner // LANES
    arriving = [
        fetch(source, target, ins.at[i])
        for i, (source, target) in enumerate(zip(refs[:weights], near_weights))
    ]
    order = chunk_order(rows)
    order_low = order.astype(BF16)
    inputs = dot(order_low, tokens[...])
    inv_rms = lax.rsqrt(jnp.mean(inputs * inputs, axis=-1, keepdims=True) + NORM_EPS)
    cotan[...] = dot(order_low, cotangent[...]).astype(BF16)
    step = 2 * LANES
    for at in range(0, inner, step):
        lanes = slice(at, at + step)
        dgz_out[:, lanes] = dot_cols(cotan[...], out_weight[lanes, :])
    in_x[...] = in_weight[:, 0:inner]

    io.ready()
    start = lax.axis_index("seq") * rows
    slots = lax.axis_size("seq") * rows
    ends = image_ends(heights, widths)
    images = heights.shape[1]
    picked = jnp.where(order, jnp.broadcast_to(valid[...].astype(F32), order.shape), 0.0)
    alive = dot(picked.astype(BF16), jnp.ones((rows, LANES), BF16))
    places = places_of(start, rows)
    segment = segment_of(places, ends)
    live[...] = jnp.where(segment < images, alive, 0.0)
    for k in range(1, reach + 1):
        same = (segment_of(places - k, ends) == segment) & (places >= k)
        same_out[(k - 1) * rows : k * rows, :] = same.astype(F32)
        same = (segment_of(places + k, ends) == segment) & (places + k < slots)
        same_out[(reach + k - 1) * rows : (reach + k) * rows, :] = same.astype(F32)
    near_row = lax.broadcasted_iota(jnp.int32, (2 * CHUNKS, LANES), 0)
    near_place = jnp.where(
        near_row < CHUNKS, start - CHUNKS + near_row, start + rows + near_row - CHUNKS
    )
    halo_live[...] = (segment_of(near_place, ends) < images).astype(F32)

    gains = gain[...].astype(F32).reshape(1, width)
    gains_out[...] = jnp.broadcast_to(gains, gains_out.shape)
    scaled = inputs * inv_rms * gains
    normed = scaled.astype(BF16)
    normed_out[...] = normed
    live_wide = jnp.concatenate([live[...]] * (width // LANES), axis=1)
    normed_live = (scaled * live_wide).astype(BF16)
    for at in range(0, inner, step):
        lanes = slice(at, at + step)
        x_out[:, lanes] = dot(normed_live, in_x[:, lanes]).astype(BF16).astype(F32)
        zs_out[:, lanes] = dot(normed, in_weight[:, inner + at : inner + at + step])
    block = 32

    def gate_block(b, _):
        here = pl.ds(pl.multiple_of(b * block, block), block)
        alive = live[here, :]
        for tile in range(tiles):
            lanes = slice(tile * LANES, (tile + 1) * LANES)
            z = zs_out[here, lanes]
            grad = dgz_out[here, lanes] * alive
            gate = sigmoid(z)
            zs = z * gate * alive
            zs_out[here, lanes] = zs
            dy[here, lanes] = 0.5 * grad * zs
            dgz_out[here, lanes] = grad * (gate * (1.0 + z * (1.0 - gate)))
        return 0

    lax.fori_loop(0, rows // block, gate_block, 0, unroll=4)
    for copy in arriving:
        copy.wait()


def middle_kernel(
    io, dy, live, same_out, from_core, from_chip, x, in_x, halo_live, gains, conv_weight, conv_bias,
    xproj, dt_weight, dt_bias, a_log, skip,
    sum_out, sent_out, delta_out, s_out, dsilu_out, tail_out, head_out, xext_out, proj_out,
    before_out, after_out, rate_out, nhalo_out,
    low_out, bc, tails, heads, spans,
    *, reach,
):
    rows, inner = x.shape
    width = in_x.shape[0]
    steps = rows // CHUNKS
    state = a_log.shape[1]
    rank = dt_weight.shape[1]
    tiles = inner // LANES
    even = (lax.axis_index("seq") & 1) == 0
    sublane = lax.broadcasted_iota(jnp.int32, (CHUNKS, LANES), 0)
    wide = lax.broadcasted_iota(jnp.int32, (CHUNKS, inner), 0)
    xext_out[reach * CHUNKS : (reach + steps) * CHUNKS, :] = x[...]

    before = jnp.where(even, from_chip[...], from_core[...])
    after = jnp.where(even, from_core[...], from_chip[...])
    htok = jnp.concatenate([before[CHUNKS:], after[:CHUNKS]], axis=0)
    htok = htok.astype(F32) * jnp.concatenate([halo_live[...]] * (width // LANES), axis=1)
    hinv = lax.rsqrt(jnp.mean(htok * htok, axis=-1, keepdims=True) + NORM_EPS)
    scaled = htok * hinv
    nhalo = (scaled * gains[0:1, :]).astype(BF16)
    nhalo_out[...] = jnp.concatenate([nhalo, scaled.astype(BF16)], axis=0)
    hx = dot(nhalo, in_x[...]).astype(BF16).astype(F32)
    for i in range(reach):
        to = steps - reach + i
        moved = pltpu.roll(x[to * CHUNKS : (to + 1) * CHUNKS, :], 1, axis=0)
        of = CHUNKS - reach + i
        xext_out[i * CHUNKS : (i + 1) * CHUNKS, :] = jnp.where(wide == 0, hx[of : of + 1], moved)
        moved = pltpu.roll(x[i * CHUNKS : (i + 1) * CHUNKS, :], CHUNKS - 1, axis=0)
        to = reach + steps + i
        of = CHUNKS + i
        xext_out[to * CHUNKS : (to + 1) * CHUNKS, :] = jnp.where(
            wide == CHUNKS - 1, hx[of : of + 1], moved
        )

    block = 64
    step = 2 * LANES
    taps = reach + 1
    conv_w = [conv_weight[d].astype(F32) for d in range(2)]
    conv_b = conv_bias[...].astype(F32)
    for tile in range(tiles):
        lanes = slice(tile * LANES, (tile + 1) * LANES)

        def conv_block(b, _, lanes=lanes):
            at = pl.multiple_of(b * block, block)
            for d in range(2):
                total = conv_b[d : d + 1, lanes] + conv_w[d][reach:taps, lanes] * (
                    xext_out[pl.ds(at + reach * CHUNKS, block), lanes]
                )
                for k in range(1, taps):
                    move = reach - k if d == 0 else reach + k
                    mask = same_out[pl.ds((d * reach + k - 1) * rows + at, block), :]
                    total = total + conv_w[d][reach - k : taps - k, lanes] * (
                        xext_out[pl.ds(at + move * CHUNKS, block), lanes] * mask
                    )
                gate = sigmoid(total)
                value = total * gate
                s_out[pl.ds(d * rows + at, block), lanes] = value
                low_out[pl.ds(d * rows + at, block), lanes] = value.astype(BF16)
                dsilu_out[pl.ds(d * rows + at, block), lanes] = gate * (1.0 + total * (1.0 - gate))
            return 0

        lax.fori_loop(0, rows // block, conv_block, 0, unroll=4)

    dt_b = dt_bias[...].astype(F32)
    for d in range(2):
        rate_out[d * state : (d + 1) * state, :] = jnp.minimum(
            -LOG2E * jnp.exp(a_log[d].astype(F32)), -1e-20
        )
        here = slice(d * rows, (d + 1) * rows)
        proj = dot_cols(low_out[here, :], xproj[d])
        proj_out[here, :] = proj
        dt_low = proj[:, :rank].astype(BF16)
        for at in range(0, inner, step):
            lanes = slice(at, at + step)
            delta_out[here, lanes] = dot(dt_low, dt_weight[d, :, lanes])
        spread(proj[:, rank:], bc)

        def delta_block(b, _, d=d):
            alive = live[pl.ds(pl.multiple_of(b * block, block), block), :]
            here = pl.ds(pl.multiple_of(d * rows + b * block, block), block)
            for tile in range(tiles):
                lanes = slice(tile * LANES, (tile + 1) * LANES)
                pre = delta_out[here, lanes] + dt_b[d : d + 1, lanes]
                small = jnp.exp(-jnp.abs(pre))
                log1p = jnp.where(small < 1e-4, small * (1.0 - 0.5 * small), jnp.log(1.0 + small))
                delta_out[here, lanes] = (jnp.maximum(pre, 0.0) + log1p) * alive
            return 0

        lax.fori_loop(0, rows // block, delta_block, 0, unroll=4)
        some = SUMMARY_STATES

        def scan_tile(tile, _, d=d):
            lanes = lanes_of(tile)
            for low in range(0, state, some):
                rates = [
                    jnp.broadcast_to(
                        rate_out[d * state + low + m : d * state + low + m + 1, lanes],
                        (CHUNKS, LANES),
                    )
                    for m in range(some)
                ]

                def scan_step(i, carried, d=d, low=low, rates=rates):
                    tail, lead, head, span = carried
                    j = i if d == 0 else steps - 1 - i
                    at = pl.multiple_of(j * CHUNKS, CHUNKS)
                    keep = same_out[pl.ds(d * reach * rows + at, CHUNKS), :]
                    delta = delta_out[pl.ds(d * rows + at, CHUNKS), lanes]
                    drive = delta * s_out[pl.ds(d * rows + at, CHUNKS), lanes]
                    back = dy[pl.ds(at, CHUNKS), lanes]
                    delta = jnp.maximum(delta, BREAK - keep * BREAK)
                    tail, lead, head = list(tail), list(lead), list(head)
                    for m in range(some):
                        b = bc[pl.ds(at, CHUNKS), (low + m) * LANES : (low + m + 1) * LANES]
                        n = state + low + m
                        c = bc[pl.ds(at, CHUNKS), n * LANES : (n + 1) * LANES]
                        decay = jnp.exp2(delta * rates[m])
                        tail[m] = decay * tail[m] + b * drive
                        lead[m] = lead[m] * decay
                        head[m] = head[m] + lead[m] * (c * back)
                    return tuple(tail), tuple(lead), tuple(head), span + delta

                zeros = tuple(jnp.zeros((CHUNKS, LANES), F32) for _ in range(some))
                ones = tuple(jnp.ones((CHUNKS, LANES), F32) for _ in range(some))
                tail, lead, head, span = lax.fori_loop(
                    0, steps, scan_step, (zeros, ones, zeros, zeros[0]), unroll=SUMMARY_UNROLL
                )
                for m in range(some):
                    tails[low + m, :, lanes] = tail[m]
                    heads[low + m, :, lanes] = head[m]
                spans[:, lanes] = span
            return 0

        lax.fori_loop(0, tiles, scan_tile, 0)

        tail_row = 0 if d == 0 else 2 * state
        head_row = 3 * state if d == 0 else state

        def chain_tile(tile, _, d=d, tail_row=tail_row, head_row=head_row):
            lanes = lanes_of(tile)
            span = spans[:, lanes]
            sums, before = windows(span, d == 0, sublane)
            sums_back, after = windows(span, d == 1, sublane)
            before_out[d * CHUNKS : (d + 1) * CHUNKS, lanes] = before
            after_out[d * CHUNKS : (d + 1) * CHUNKS, lanes] = after
            for n in range(state):
                rate = jnp.broadcast_to(
                    rate_out[d * state + n : d * state + n + 1, lanes], (CHUNKS, LANES)
                )
                carried, total = chain(rate, sums, tails[n, :, lanes], d == 0, sublane)
                tail_out[d * state + n, :, lanes] = carried
                sum_out[tail_row + n : tail_row + n + 1, lanes] = total
                carried, total = chain(rate, sums_back, heads[n, :, lanes], d == 1, sublane)
                head_out[d * state + n, :, lanes] = carried
                sum_out[head_row + n : head_row + n + 1, lanes] = total
            return 0

        lax.fori_loop(0, tiles, chain_tile, 0)
        sum_out[4 * state + d : 4 * state + d + 1, :] = jnp.sum(spans[...], axis=0, keepdims=True)
    at = 4 * state + CHUNKS
    sum_out[4 * state + 2 : at, :] = jnp.zeros((CHUNKS - 2, inner), F32)
    sum_out[at:, :] = rate_out[0 : 2 * state, :]
    sent_out[...] = packed(sum_out[0:at, :], state)
    rate_out[2 * state : 2 * state + 2, :] = skip[...].astype(F32)


def packed(summary, state):
    rest = summary[4 * state :]
    high = rest.astype(BF16)
    low = (rest - high.astype(F32)).astype(BF16)
    return jnp.concatenate([summary[: 4 * state].astype(BF16), high, low], axis=0)


def leads(rate, spans, state, flip):
    parts = [jnp.exp2(rate[d * state : (d + 1) * state] * spans[d : d + 1]) for d in range(2)]
    return jnp.concatenate(parts[::-1] if flip else parts, axis=0)


def join_kernel(io, got, summary, entered, *outs, state, bit, final):
    half = 2 * state
    upper = ((lax.axis_index("seq") >> bit) & 1) == 1
    mine = summary[0 : 2 * half + CHUNKS, :]
    rates = summary[2 * half + CHUNKS :, :]
    entered_out, sent_out = outs[-2], outs[-1]
    values = got[...].astype(F32)
    spans = mine[4 * state : 4 * state + 2]
    other = values[4 * state : 4 * state + 2] + values[4 * state + CHUNKS : 4 * state + CHUNKS + 2]
    if entered is None:
        entered_up = jnp.where(upper, values[:half], 0.0)
        entered_down = jnp.where(upper, 0.0, values[half : 2 * half])
        span_up = jnp.where(upper, other, 0.0)
        span_down = jnp.where(upper, 0.0, other)
    else:
        held = entered[...]
        span_up, span_down = held[2 * half : 2 * half + 2], held[2 * half + 2 : 2 * half + 4]
        entered_up = held[:half] + jnp.where(
            upper, leads(rates, span_up, state, False) * values[:half], 0.0
        )
        entered_down = held[half : 2 * half] + jnp.where(
            upper, 0.0, leads(rates, span_down, state, True) * values[half : 2 * half]
        )
        span_up = span_up + jnp.where(upper, other, 0.0)
        span_down = span_down + jnp.where(upper, 0.0, other)
    entered_out[0:half, :] = entered_up
    entered_out[half : 2 * half, :] = entered_down
    entered_out[2 * half :, :] = jnp.concatenate(
        [span_up, span_down, jnp.zeros((CHUNKS - 4, mine.shape[1]), F32)], axis=0
    )
    low_up = jnp.where(upper, values[:half], mine[:half])
    high_up = jnp.where(upper, mine[:half], values[:half])
    low_down = jnp.where(upper, values[half : 2 * half], mine[half : 2 * half])
    high_down = jnp.where(upper, mine[half : 2 * half], values[half : 2 * half])
    low_span, high_span = jnp.where(upper, other, spans), jnp.where(upper, spans, other)
    up = leads(rates, high_span, state, False) * low_up + high_up
    down = leads(rates, low_span, state, True) * high_down + low_down
    if final:
        next_upper = ((lax.axis_index("seq") >> (bit + 1)) & 1) == 1
        sent_out[...] = jnp.where(next_upper, down, up).astype(BF16)
    else:
        total = jnp.concatenate(
            [up, down, spans + other, jnp.zeros((CHUNKS - 2, mine.shape[1]), F32)], axis=0
        )
        outs[0][0 : 2 * half + CHUNKS, :] = total
        outs[0][2 * half + CHUNKS :, :] = rates
        sent_out[...] = packed(total, state)


def first_join(io, got, summary, *outs, state, bit, final):
    join_kernel(io, got, summary, None, *outs, state=state, bit=bit, final=final)


def state_block(j, state):
    return pl.multiple_of(j * state * CHUNKS, CHUNKS)


def states_pass(d, steps, state, rates, begin, delta, s, keep, bc, h_out, y):
    start = state_block(0 if d == 0 else steps, state)
    for n in range(state):
        h_out[pl.ds(start + n * CHUNKS, CHUNKS), :] = begin[n]

    def step(i, h):
        j = i if d == 0 else steps - 1 - i
        here = pl.ds(pl.multiple_of(j * CHUNKS, CHUNKS), CHUNKS)
        to = state_block(j + 1 if d == 0 else j, state)
        size = delta[here, :]
        drive = size * s[here, :]
        size = jnp.maximum(size, BREAK - keep[here, :] * BREAK)
        h = list(h)
        parts = [None if d == 0 else y[here, :], None]
        for n in range(state):
            b = bc[here, n * LANES : (n + 1) * LANES]
            c = bc[here, (state + n) * LANES : (state + n + 1) * LANES]
            h[n] = jnp.exp2(size * rates[n]) * h[n] + b * drive
            h_out[pl.ds(to + n * CHUNKS, CHUNKS), :] = h[n]
            part = parts[n % 2]
            parts[n % 2] = c * h[n] if part is None else part + c * h[n]
        y[here, :] = parts[0] + parts[1]
        return tuple(h)

    lax.fori_loop(0, steps, step, tuple(begin), unroll=STATES_UNROLL)


def adjoint_pass(
    d, steps, state, rates, back, delta, s, dy, keep, skip, bc, h_in, sums,
    dpre_out, ds_out, rows_out,
):
    some = ADJOINT_STATES
    edge = steps - 1
    skip = skip[...]
    zeros = jnp.zeros((CHUNKS, LANES), F32)
    grads = []
    for low in range(0, state, some):
        final = low + some == state

        def step(i, carried, low=low, final=final):
            g, acc, h, skip_acc, bias_acc = carried
            j = edge - i if d == 0 else i
            here = pl.ds(pl.multiple_of(j * CHUNKS, CHUNKS), CHUNKS)
            size = delta[here, :]
            value = s[here, :]
            grad = dy[here, :]
            drive = size * value
            masked = jnp.maximum(size, BREAK - keep[here, :] * BREAK)
            prev = state_block(j if d == 0 else j + 1, state)
            g, acc, h = list(g), list(acc), list(h)
            weighted = zeros if low == 0 else ds_out[here, :]
            rate_sum = zeros if low == 0 else dpre_out[here, :]
            for m in range(some):
                n = low + m
                b = bc[here, n * LANES : (n + 1) * LANES]
                c = bc[here, (state + n) * LANES : (state + n + 1) * LANES]
                adjoint = c * grad + g[m]
                before = h_in[pl.ds(prev + n * CHUNKS, CHUNKS), :]
                sums[here, n * LANES : (n + 1) * LANES] += adjoint * drive
                sums[here, (state + n) * LANES : (state + n + 1) * LANES] += grad * h[m]
                g[m] = adjoint * jnp.exp2(masked * rates[n])
                held = g[m] * before
                weighted = weighted + adjoint * b
                rate_sum = rate_sum + held * rates[n]
                acc[m] = acc[m] + held * masked
                h[m] = before
            if final:
                ds_out[here, :] = skip * grad + size * weighted
                gate = jnp.where(
                    size < 0.01, size * (1.0 - size * (0.5 - size * (1.0 / 6.0))), 1.0 - jnp.exp(-size)
                )
                pre = ((LN2 * rate_sum + weighted * value) * gate).astype(BF16).astype(F32)
                dpre_out[here, :] = pre
                bias_acc = bias_acc + pre
                skip_acc = skip_acc + grad * value
            else:
                dpre_out[here, :] = rate_sum
                ds_out[here, :] = weighted
            return tuple(g), tuple(acc), tuple(h), skip_acc, bias_acc

        last = state_block(steps if d == 0 else 0, state)
        h_last = tuple(h_in[pl.ds(last + (low + m) * CHUNKS, CHUNKS), :] for m in range(some))
        none = tuple(zeros for _ in range(some))
        _, acc, _, skip_acc, bias_acc = lax.fori_loop(
            0, steps, step, (tuple(back[low : low + some]), none, h_last, zeros, zeros),
            unroll=ADJOINT_UNROLL,
        )
        grads.extend(acc)
    for n in range(state):
        rows_out[n : n + 1, :] = jnp.sum(grads[n], axis=0, keepdims=True) * rates[n][0:1] * LN2
    rows_out[state : state + 1, :] = jnp.sum(bias_acc, axis=0, keepdims=True)
    rows_out[state + 1 : state + 2, :] = jnp.sum(skip_acc, axis=0, keepdims=True)


def lane_sums(sums, state):
    column = lax.broadcasted_iota(jnp.int32, (2 * CHUNKS, LANES), 1)
    picks = [(column == n).astype(BF16) for n in range(2 * state)]
    pick = jnp.concatenate([p for p in picks for _ in range(LANES // (2 * CHUNKS))], axis=0)
    return dot(sums.astype(BF16), pick)[:, : 2 * state]


def rate_tiles(rate, d, state, lanes):
    return [
        jnp.broadcast_to(rate[d * state + n : d * state + n + 1, lanes], (CHUNKS, LANES))
        for n in range(state)
    ]


def begin_tiles(rates, passed, maps, carry, at, d, state, lanes):
    passed = passed[d * CHUNKS : (d + 1) * CHUNKS, lanes]
    return [
        jnp.exp2(rates[n] * passed) * carry[at + n : at + n + 1, lanes]
        + maps[d * state + n, :, lanes]
        for n in range(state)
    ]


def slot_order(rows):
    row = lax.broadcasted_iota(jnp.int32, (rows, rows), 1)
    slot = lax.broadcasted_iota(jnp.int32, (rows, rows), 0)
    return (slot == (row & (CHUNKS - 1)) * (rows // CHUNKS) + (row >> 3)).astype(BF16)


def states_kernel(
    io, delta, s, proj, rate, same, normed, before, tail, got, entered, zs, dgz, cotan,
    kept, sent, carry_out, dz, h0, h1, gated,
    bc, y,
    *, reach, rank, state, bit,
):
    rows, inner = zs.shape
    width = cotan.shape[1]
    steps = rows // CHUNKS
    half = 2 * state
    tiles = inner // LANES
    upper = ((lax.axis_index("seq") >> bit) & 1) == 1
    values = got[...].astype(F32)
    held = entered[...]
    rates = rate[0:half, :]
    carry_out[0:half, :] = held[:half] + jnp.where(
        upper, leads(rates, held[2 * half : 2 * half + 2], state, False) * values, 0.0
    )
    carry_out[half : 2 * half, :] = held[half : 2 * half] + jnp.where(
        upper, 0.0, leads(rates, held[2 * half + 2 : 2 * half + 4], state, True) * values
    )
    for d, h in enumerate((h0, h1)):
        mine = slice(d * rows, (d + 1) * rows)
        spread(proj[mine, rank:], bc)
        keep = same.at[d * reach * rows : (d * reach + 1) * rows, :]

        def scan_tile(tile, _, d=d, h=h, mine=mine, keep=keep):
            lanes = lanes_of(tile)
            rates = rate_tiles(rate, d, state, lanes)
            begin = begin_tiles(rates, before, tail, carry_out, d * half, d, state, lanes)
            states_pass(
                d, steps, state, rates, begin, delta.at[mine, lanes], s.at[mine, lanes],
                keep, bc, h.at[tile], y.at[:, lanes],
            )
            return 0

        lax.fori_loop(0, tiles, scan_tile, 0)
    block = 32

    def gate_block(b, _):
        here = pl.ds(pl.multiple_of(b * block, block), block)
        there = pl.ds(pl.multiple_of(rows + b * block, block), block)
        for tile in range(tiles):
            lanes = slice(tile * LANES, (tile + 1) * LANES)
            total = 0.5 * (
                y[here, lanes] + rate[half : half + 1, lanes] * s[here, lanes]
                + rate[half + 1 : half + 2, lanes] * s[there, lanes]
            )
            gated[here, lanes] = (total * zs[here, lanes]).astype(BF16)
            dz[here, lanes] = (total * dgz[here, lanes]).astype(BF16)
        return 0

    lax.fori_loop(0, rows // block, gate_block, 0, unroll=4)
    even = (lax.axis_index("seq") & 1) == 0
    out_grad = dot_rows(gated[...], cotan[...]).astype(BF16)
    z_grad = jnp.concatenate(
        [dot_rows(normed[...], dz[:, at : at + width]) for at in range(0, inner, width)], axis=0
    ).astype(BF16)
    sent[...] = jnp.where(even, z_grad, out_grad)
    kept[...] = jnp.where(even, out_grad, z_grad)


def output_kernel(io, gated, tokens, out_weight, output):
    ordered = dot(slot_order(gated.shape[0]), gated[...]).astype(BF16)
    io.ready()
    output[...] = (tokens[...].astype(F32) + dot(ordered, out_weight[...])).astype(BF16)


def adjoint_kernel(
    io, delta, s, dsilu, dy, head, xext, proj, after, rate, same, carry, h, dx_in,
    dt_weight, xproj, conv_weight,
    dc_rim, small_out, dx_out,
    bc, sums, dpre, ds, rows_out, ext,
    *, d, reach, rank, state,
):
    rows, inner = dy.shape
    steps = rows // CHUNKS
    half = 2 * state
    tiles = inner // LANES
    taps = reach + 1
    cols = proj.shape[1]
    mine = slice(d * rows, (d + 1) * rows)
    keep = same.at[d * reach * rows : (d * reach + 1) * rows, :]
    spread(proj[mine, rank:], bc)
    sums[...] = jnp.zeros_like(sums)
    rows_out[...] = jnp.zeros_like(rows_out)
    grad_at = (half if d == 0 else 0) + state

    def scan_tile(tile, _):
        lanes = lanes_of(tile)
        rates = rate_tiles(rate, d, state, lanes)
        back = begin_tiles(rates, after, head, carry, grad_at, d, state, lanes)
        adjoint_pass(
            d, steps, state, rates, back, delta.at[mine, lanes], s.at[mine, lanes],
            dy.at[:, lanes], keep, rate.at[half + d : half + d + 1, lanes], bc,
            h.at[tile], sums, dpre.at[:, lanes], ds.at[:, lanes], rows_out.at[:, lanes],
        )
        return 0

    lax.fori_loop(0, tiles, scan_tile, 0)
    io.ready()
    dpre_low = dpre[...].astype(BF16)
    dt_grad = dot_rows(proj[mine, :rank].astype(BF16), dpre_low)
    dt_back = dot_cols(dpre_low, dt_weight[d])
    dproj = jnp.concatenate([dt_back, lane_sums(sums[...], state)], axis=1).astype(BF16)
    small_out[0:cols, :] = dot_rows(dproj, s[mine, :].astype(BF16))
    small_out[cols : cols + rank, :] = dt_grad
    base = 0 if d == 0 else reach * CHUNKS
    step = 2 * LANES
    for lane in range(0, inner, step):
        lanes = slice(lane, lane + step)
        total = ds[:, lanes] + dot(dproj, xproj[d, :, lanes])
        ext[base : base + rows, lanes] = (total * dsilu[mine, lanes]).astype(BF16).astype(F32)
    wide = lax.broadcasted_iota(jnp.int32, (CHUNKS, inner), 0)
    for i in range(reach):
        if d == 0:
            moved = pltpu.roll(ext[i * CHUNKS : (i + 1) * CHUNKS, :], CHUNKS - 1, axis=0)
            ext[rows + i * CHUNKS : rows + (i + 1) * CHUNKS, :] = jnp.where(
                wide == CHUNKS - 1, 0.0, moved
            )
        else:
            moved = pltpu.roll(ext[rows + i * CHUNKS : rows + (i + 1) * CHUNKS, :], 1, axis=0)
            ext[i * CHUNKS : (i + 1) * CHUNKS, :] = jnp.where(wide == 0, 0.0, moved)

    conv_w = conv_weight[d].astype(F32)
    block = 64
    zeros = jnp.zeros((CHUNKS, LANES), F32)

    def folded(values):
        return functools.reduce(
            lambda a, b: a + b, [values[i : i + CHUNKS] for i in range(0, block, CHUNKS)]
        )

    base_row = cols + rank
    for tile in range(tiles):
        lanes = slice(tile * LANES, (tile + 1) * LANES)
        weight = conv_w[:, lanes]

        def conv_block(b, totals, lanes=lanes, weight=weight):
            here = pl.multiple_of(b * block, block)
            totals = list(totals)
            mid = ext[pl.ds(here + base, block), lanes]
            total = weight[reach:taps] * mid
            totals[reach] = totals[reach] + folded(mid * xext[pl.ds(here + reach * CHUNKS, block), lanes])
            totals[taps] = totals[taps] + folded(mid)
            for k in range(1, taps):
                past = same[pl.ds((k - 1) * rows + here, block), :]
                ahead = same[pl.ds((reach + k - 1) * rows + here, block), :]
                if d == 0:
                    given = ext[pl.ds(here + k * CHUNKS, block), lanes] * ahead
                    taken = xext[pl.ds(here + (reach - k) * CHUNKS, block), lanes] * past
                else:
                    given = ext[pl.ds(here + (reach - k) * CHUNKS, block), lanes] * past
                    taken = xext[pl.ds(here + (reach + k) * CHUNKS, block), lanes] * ahead
                total = total + weight[reach - k : taps - k] * given
                totals[reach - k] = totals[reach - k] + folded(mid * taken)
            if dx_in is not None:
                total = total + dx_in[pl.ds(here, block), lanes]
            dx_out[pl.ds(here, block), lanes] = total
            return tuple(totals)

        totals = lax.fori_loop(0, rows // block, conv_block, (zeros,) * (taps + 1), unroll=4)
        for i in range(taps + 1):
            at = state + 2 + i
            rows_out[at : at + 1, lanes] = jnp.sum(totals[i], axis=0, keepdims=True)

    edge = []
    for i in range(CHUNKS):
        row = jnp.zeros((1, inner), F32)
        for k in range(1, taps):
            j = i - CHUNKS + k if d == 0 else steps + i - k
            if (d == 0 and j >= 0) or (d == 1 and j < steps):
                sub = 0 if d == 0 else CHUNKS - 1
                at = (d * reach + k - 1) * rows + j * CHUNKS + sub
                mask = jnp.concatenate([same[at : at + 1, :]] * tiles, axis=1)
                at = base + j * CHUNKS + sub
                row = row + conv_w[reach - k : taps - k] * ext[at : at + 1, :] * mask
        edge.append(row)
    dc_rim[...] = jnp.concatenate(edge, axis=0)
    small_out[base_row:, :] = rows_out[0 : small_out.shape[0] - base_row, :]


def first_adjoint(io, *refs, **static):
    adjoint_kernel(io, *refs[:12], None, *refs[12:], **static)


def second_adjoint(io, *refs, **static):
    in_far, in_near, moves = refs[16], refs[20], refs[21]
    copy = fetch(in_far, in_near, moves.at[0])
    adjoint_kernel(io, *refs[:16], *refs[17:20], *refs[22:], **static)
    copy.wait()


def last_kernel(
    io, dx, rim0, rim1, small0, small1, normed, nhalo, live, in_weight,
    kept, sent, low,
    lines, grads,
):
    rows, inner = dx.shape
    width = normed.shape[1]
    folds = inner // width
    fold = kept.shape[0]
    edges = 2 * CHUNKS
    for tile in range(inner // LANES):
        lanes = slice(tile * LANES, (tile + 1) * LANES)
        lines[0:rows, lanes] = (dx[:, lanes] * live[...]).astype(BF16)
    low[...] = lines[0:rows, :]
    lines[rows : rows + edges, :] = jnp.concatenate([rim0[...], rim1[...]], axis=0).astype(BF16)
    both = jnp.concatenate([normed[...], nhalo[0:edges, :]], axis=0)
    size = small0.shape[0]
    for i in range(folds):
        lanes = slice(i * width, (i + 1) * width)
        at = i * fold
        grads[at : at + width, :] = dot_rows(both, lines[:, lanes]).astype(BF16)
        at += width
        grads[at : at + 2 * size, :] = jnp.concatenate(
            [small0[:, lanes], small1[:, lanes]], axis=0
        ).astype(BF16)
        at += 2 * size
        grads[at : (i + 1) * fold, :] = jnp.zeros(((i + 1) * fold - at, width), BF16)
    rim = dot_cols(lines[rows : rows + edges, :], in_weight[:, 0:inner])
    even = (lax.axis_index("seq") & 1) == 0
    turned = jnp.concatenate([rim[CHUNKS:], rim[:CHUNKS]], axis=0)
    left, right = grads[0:fold, :], grads[fold : 2 * fold, :]
    kept[...] = jnp.where(even, left, right)
    sent[...] = jnp.where(even, right, left)
    at = width + 2 * size
    sent[at : at + edges, :] = jnp.where(even, turned, rim).astype(BF16)


def finish_kernel(
    io, low, dz, in_weight, rims, chip_rim, heights, widths, tokens, cotangent, valid, gain,
    input_grad,
):
    rows, width = tokens.shape
    inner = low.shape[1]
    even = (lax.axis_index("seq") & 1) == 0
    start = lax.axis_index("seq") * rows
    back = slot_order(rows)
    dn = dot_cols(dot(back, low[...]).astype(BF16), in_weight[:, 0:inner]) + dot_cols(
        dot(back, dz[...]).astype(BF16), in_weight[:, inner : 2 * inner]
    )
    io.ready()
    from_core = rims[0:CHUNKS, :].astype(F32)
    from_chip = chip_rim[CHUNKS : 2 * CHUNKS, :].astype(F32)
    before = jnp.where(even, from_chip, from_core)
    after = jnp.where(even, from_core, from_chip)
    end = image_ends(heights, widths)[-1]
    row = lax.broadcasted_iota(jnp.int32, (CHUNKS, rows), 0)
    slot = lax.broadcasted_iota(jnp.int32, (CHUNKS, rows), 1)
    alive = jnp.broadcast_to(valid[...].astype(F32), (CHUNKS, rows))
    alive = jnp.where(start + slot < end, alive, 0.0)
    first = jnp.sum(jnp.where(slot == row, alive, 0.0), axis=1, keepdims=True)
    last = jnp.sum(jnp.where(slot == rows - CHUNKS + row, alive, 0.0), axis=1, keepdims=True)
    values = jnp.concatenate(
        [
            dn[0:CHUNKS, :] + first * before, dn[CHUNKS : rows - CHUNKS, :],
            dn[rows - CHUNKS : rows, :] + last * after,
        ],
        axis=0,
    )
    inputs = tokens[...].astype(F32)
    inv_rms = lax.rsqrt(jnp.mean(inputs * inputs, axis=-1, keepdims=True) + NORM_EPS)
    scaled = values * gain[...].astype(F32).reshape(1, width)
    mean = jnp.mean(scaled * inputs, axis=-1, keepdims=True)
    input_grad[...] = (
        cotangent[...].astype(F32) + inv_rms * scaled - inputs * (inv_rms * inv_rms * inv_rms) * mean
    )


def blocks_in_order(mine, other, into_first, into_second):
    size = mine.shape[1]
    is_even = (lax.axis_index("seq") & 1) == 0
    here = lax.axis_index("img")
    for k in range(mine.shape[0]):
        a, b = mine[here ^ k].astype(F32), other[here ^ k].astype(F32)
        into_first(k * size, jnp.where(is_even, a, b))
        into_second(k * size, jnp.where(is_even, b, a))


def weighted_rows(values, weights):
    total = None
    for at in range(0, values.shape[1], LANES):
        part = values[:, at : at + LANES] * weights[:, at : at + LANES].astype(F32)
        total = part if total is None else total + part
    return total


def first_unpack(io, mine, other, in_weight, parts, in_far, out_far, out_w, z_half, moves):
    width = out_w.shape[1]
    inner = out_w.shape[0]

    def put_out(at, values):
        out_w[at : at + values.shape[0], :] = values

    def put_z(at, values):
        size = values.shape[0]
        column = at // width * width
        z_half[at % width : at % width + size, column : column + width] = values

    blocks_in_order(mine, other, put_out, put_z)
    leaving = [
        fetch(out_w, out_far, moves.at[0]),
        fetch(z_half, in_far.at[:, inner : 2 * inner], moves.at[1]),
    ]
    parts[...] = weighted_rows(z_half[...], in_weight[:, inner : 2 * inner])
    for copy in leaving:
        copy.wait()


def second_unpack(
    io, mine, other, in_weight, parts, gain_in, in_before,
    conv_w, conv_b, xproj, dt_w, dt_b, a_log, skip, gain, in_far,
    left, right, x_half, moves,
    *, count, state, rank, cols, taps,
):
    width = left.shape[1]
    inner = x_half.shape[1]

    def put_left(at, values):
        left[at : at + values.shape[0], :] = values

    def put_right(at, values):
        right[at : at + values.shape[0], :] = values

    blocks_in_order(mine, other, put_left, put_right)
    for i, half in enumerate((left, right)):
        x_half[:, i * width : (i + 1) * width] = half[0:width, :]
    leaving = fetch(x_half, in_far.at[:, 0:inner], moves.at[0])
    for i, half in enumerate((left, right)):
        lanes = slice(i * width, (i + 1) * width)
        for d in range(2):
            at = width + d * count
            xproj[d, :, lanes] = half[at : at + cols, :]
            at += cols
            dt_w[d, :, lanes] = half[at : at + rank, :]
            at += rank
            a_log[d, :, lanes] = half[at : at + state, :]
            dt_b[d : d + 1, lanes] = half[at + state : at + state + 1, :]
            skip[d : d + 1, lanes] = half[at + state + 1 : at + state + 2, :]
            at += state + 2
            conv_w[d, :, lanes] = half[at : at + taps, :]
            conv_b[d : d + 1, lanes] = half[at + taps : at + taps + 1, :]
    total = parts[...] + weighted_rows(x_half[...], in_weight[:, 0:inner])
    high = total.astype(BF16)
    rest = (total - high.astype(F32)).astype(BF16)
    ones = jnp.ones((2 * CHUNKS, LANES), BF16)
    sums = (dot_cols(ones, high) + dot_cols(ones, rest))[0:1]
    io.ready()
    gain[...] = (sums / gain_in[...].astype(F32).reshape(1, width)).reshape(width)
    io.done()
    leaving.wait()


IN_VMEM = pl.BlockSpec(memory_space=pltpu.VMEM)
IN_SMEM = pl.BlockSpec(memory_space=pltpu.SMEM)
FAR = pl.BlockSpec(memory_space=pltpu.HBM)


def shape(*dims, dtype=F32):
    return jax.ShapeDtypeStruct(dims, dtype)


def low(*dims):
    return jax.ShapeDtypeStruct(dims, BF16)


def near(*dims, dtype=F32):
    return pltpu.VMEM(dims, dtype)


def scratch(*dims, dtype=F32):
    return pltpu.VMEM(dims, dtype)


def like(*outs):
    return [pltpu.VMEM(out.shape, out.dtype) for out in outs]


def moves(*dims):
    return pltpu.SemaphoreType.DMA(dims)


class Moves:
    def __init__(self, arrive, leave):
        self.arrive, self.leave, self.left = arrive, leave, False
        for copy in arrive:
            copy.start()

    def ready(self):
        for copy in self.arrive:
            copy.wait()

    def done(self):
        self.left = True
        for copy in self.leave:
            copy.start()


def call(
    kernel, name, args, outs, scratches=(), far=(), far_outs=(), near_args=(), near_outs=(),
    scalars=(), handed=(), aliases=(), us=4, limit=4,
):
    small = tuple(scalars) + tuple(args)
    small, far = (
        tuple(pltpu.with_memory_space_constraint(x, pltpu.HBM) for x in arrays)
        for arrays in (small, far)
    )
    n_hand = len(handed)
    near_args = tuple(handed) + tuple(near_args)
    n_near, n_small, n_far = len(near_args), len(small), len(far)
    n_near_outs, n_outs, n_far_outs = len(near_outs), len(outs), len(far_outs)

    def wrapped(*refs):
        refs = list(refs)

        def take(count):
            taken = refs[:count]
            del refs[:count]
            return taken

        near_in, small_in, far_in = take(n_near), take(n_small), take(n_far)
        near_out, out, far_out = take(n_near_outs), take(n_outs), take(n_far_outs)
        take(n_hand)
        small_here, out_here = take(n_small), take(n_outs)
        in_moves, out_moves = take(2)
        io = Moves(
            [pltpu.make_async_copy(a, b, in_moves.at[i]) for i, (a, b) in enumerate(zip(small_in, small_here))],
            [pltpu.make_async_copy(a, b, out_moves.at[i]) for i, (a, b) in enumerate(zip(out_here, out))],
        )
        kernel(io, *near_in, *small_here, *far_in, *near_out, *out_here, *far_out, *refs)
        if not io.left:
            io.done()
        for copy in io.leave:
            copy.wait()

    return pl.pallas_call(
        wrapped,
        out_shape=list(near_outs) + [
            pltpu.HBM(out.shape, out.dtype) for out in tuple(outs) + tuple(far_outs)
        ] + [pltpu.VMEM(x.shape, x.dtype) for x in handed],
        in_specs=[IN_VMEM] * n_near + [FAR] * (n_small + n_far),
        out_specs=[IN_VMEM] * n_near_outs + [FAR] * (n_outs + n_far_outs) + [IN_VMEM] * n_hand,
        input_output_aliases={
            **{i: n_near_outs + n_outs + n_far_outs + i for i in range(n_hand)},
            **{n_near + n_small + i: n_near_outs + n_outs + o for i, o in aliases},
        },
        scratch_shapes=(
            [pltpu.SMEM(a.shape, a.dtype) for a in scalars] + like(*args) + like(*outs)
            + [moves(max(n_small, 1)), moves(max(n_outs, 1))] + list(scratches)
        ),
        compiler_params=pltpu.CompilerParams(vmem_limit_bytes=limit * 2**20),
        cost_estimate=pl.CostEstimate(flops=us * 2000000000, bytes_accessed=0, transcendentals=0),
        name=name,
    )(*near_args, *small, *far)


def call_edges(tokens, valid):
    edge = 2 * CHUNKS
    width = tokens.shape[1]
    outs = [near(edge, width, dtype=BF16), near(edge, width, dtype=BF16)]
    return call(edges_kernel, "edges", (tokens, valid), (), near_outs=outs, us=1, limit=2)


def call_front(
    heights, widths, valid, gain, tokens, cotangent, in_weight, out_weight, weights, reach,
):
    rows, width = tokens.shape
    inner = out_weight.shape[0]
    one = near(rows, inner)
    row = near(rows, width, dtype=BF16)
    return call(
        functools.partial(front_kernel, reach=reach, weights=len(weights)), "front", (valid, gain), (),
        [moves(len(weights))], weights, (),
        tuple(
            pltpu.with_memory_space_constraint(x, pltpu.VMEM)
            for x in (tokens, cotangent, in_weight, out_weight)
        ),
        [
            row, one, one, one, one, near(rows, LANES), near(2 * reach * rows, LANES), row,
            near(width, inner, dtype=BF16), near(2 * CHUNKS, LANES), near(CHUNKS, width),
        ] + like(*weights),
        (heights, widths), us=4, limit=12,
    )


def call_middle(handed, used, from_core, from_chip, arrays, reach, cols):
    x, a_log = arrays[0], arrays[-2]
    rows, inner = x.shape
    state, width = a_log.shape[1], from_core.shape[1]
    half = 2 * state
    both = near(2 * rows, inner)
    maps = near(half, CHUNKS, inner)
    ends = near(2 * CHUNKS, inner)
    n_hand = len(handed)

    def kernel(io, *refs):
        middle_kernel(io, *(refs[i] for i in used), *refs[n_hand:], reach=reach)

    return call(
        kernel, "middle", (), (),
        [
            scratch(2 * rows, inner, dtype=BF16), scratch(rows, half * LANES),
            scratch(state, CHUNKS, inner), scratch(state, CHUNKS, inner), scratch(CHUNKS, inner),
        ],
        near_args=(from_core, from_chip) + arrays,
        near_outs=[
            near(2 * half + CHUNKS + half, inner), near(2 * half + 2 * CHUNKS, inner, dtype=BF16),
            both, both, both, maps, maps, near(rows + 2 * reach * CHUNKS, inner),
            near(2 * rows, cols), ends, ends, near(half + CHUNKS, inner),
            near(4 * CHUNKS, width, dtype=BF16),
        ],
        handed=handed, us=20, limit=9,
    )


def call_join(got, summary, entered, state, bit, final):
    inner = summary.shape[1]
    half = 2 * state
    outs = [
        near(2 * half + CHUNKS, inner),
        near(half if final else 2 * half + 2 * CHUNKS, inner, dtype=BF16),
    ]
    if not final:
        outs = [near(2 * half + CHUNKS + half, inner)] + outs
    args = (got, summary) + (() if entered is None else (entered,))
    kernel = first_join if entered is None else join_kernel
    joined = call(
        functools.partial(kernel, state=state, bit=bit, final=final), "join", (), (),
        near_args=args, near_outs=outs, us=1, limit=4,
    )
    return joined if not final else [None] + list(joined)


def call_states(handed, used, before, tail, got, entered, zs, dgz, cotan, rank, reach, state, bit):
    rows, inner = zs.shape
    width = cotan.shape[1]
    half = 2 * state
    n_hand = len(handed)

    def kernel(io, *refs):
        states_kernel(
            io, *(refs[i] for i in used), *refs[n_hand:], reach=reach, rank=rank, state=state, bit=bit
        )

    grad = near(inner, width, dtype=BF16)
    one = near(rows, inner, dtype=BF16)
    held = near(inner // LANES, (rows // CHUNKS + 1) * state * CHUNKS, LANES)
    return call(
        kernel, "states", (), (),
        [scratch(rows, half * LANES), scratch(rows, inner)],
        near_args=(before, tail, got, entered, zs, dgz, cotan),
        near_outs=[grad, grad, near(2 * half, inner), one, held, held, one], handed=handed, us=12,
        limit=9,
    )


def adjoint_scratch(rows, inner, half, reach, small, cols, rank):
    return [
        scratch(rows, half * LANES), scratch(rows, half * LANES), scratch(rows, inner), scratch(rows, inner), scratch(small - cols - rank, inner),
        scratch(rows + reach * CHUNKS, inner),
    ]


def call_first_adjoint(handed, used, h, weights, small, reach, rank, state):
    rows, inner = handed[used[3]].shape
    cols = handed[used[6]].shape[1]
    n_hand = len(handed)

    def kernel(io, *refs):
        first_adjoint(
            io, *(refs[i] for i in used), *refs[n_hand:], d=0, reach=reach, rank=rank, state=state
        )

    return call(
        kernel, "adjoint_up", weights, (),
        adjoint_scratch(rows, inner, 2 * state, reach, small, cols, rank), near_outs=[
            near(CHUNKS, inner), near(small, inner), near(rows, inner),
        ], near_args=(h,), handed=handed, us=14, limit=13,
    )


def call_second_adjoint(handed, arrays, weights, in_weight, small, reach, rank, state):
    rows, inner = arrays[3].shape
    cols = arrays[6].shape[1]
    n_hand = len(handed)

    def kernel(io, *refs):
        second_adjoint(io, *refs[n_hand:], d=1, reach=reach, rank=rank, state=state)

    return call(
        kernel, "adjoint_down", weights, (),
        [moves(1)] + adjoint_scratch(rows, inner, 2 * state, reach, small, cols, rank),
        (in_weight,), (), arrays,
        [near(CHUNKS, inner), near(small, inner), near(rows, inner), near(*in_weight.shape, dtype=BF16)],
        handed=handed, us=14, limit=13,
    )


def call_last(handed, dx, rim0, rim1, small0, small1, normed, nhalo, live):
    rows, inner = dx.shape
    width = normed.shape[1]
    small = small0.shape[0]
    folds = inner // width
    edges = 2 * CHUNKS
    fold = -(-(width + 2 * small + edges) // 64) * 64
    n_hand = len(handed)

    def kernel(io, *refs):
        last_kernel(io, *refs[n_hand : n_hand + 8], refs[n_hand - 1], *refs[n_hand + 8 :])

    return call(
        kernel, "last", (), (),
        [
            scratch(rows + edges, inner, dtype=BF16), scratch(folds * fold, width, dtype=BF16),
        ],
        near_args=(dx, rim0, rim1, small0, small1, normed, nhalo, live),
        near_outs=[
            near(fold, width, dtype=BF16), near(fold, width, dtype=BF16),
            near(rows, inner, dtype=BF16),
        ],
        handed=handed, us=3, limit=8,
    )


def partner(axis, bit):
    return [(i, i ^ (1 << bit)) for i in range(lax.axis_size(axis))]


def bits_of(axis):
    return (lax.axis_size(axis) - 1).bit_length()


def other_core(values):
    return lax.ppermute(values, "seq", partner("seq", 0))


def next_chip(values):
    count = lax.axis_size("seq")
    pairs = [(i, i + 1) for i in range(1, count - 1, 2)]
    return lax.ppermute(values, "seq", pairs + [(j, i) for i, j in pairs])


def split_kernel(io, kept, got, own, *sent, edges):
    if edges:
        at = got.shape[0] - edges[1]
        sent[-1][...] = got[at : at + edges[0], :]
        sent = sent[:-1]
    count = len(sent) + 1
    rows = own.shape[0]
    here = lax.axis_index("img")
    for k in range(count):
        at = pl.ds(pl.multiple_of((here ^ k) * rows, rows), rows)
        total = kept[at, :].astype(F32) + got[at, :].astype(F32)
        if k == 0:
            own[...] = total
        else:
            sent[k - 1][...] = total.astype(BF16)


def add_kernel(io, *refs, outs):
    total = refs[0][...].astype(F32)
    for ref in refs[1 : len(refs) - outs]:
        total = total + ref[...].astype(F32)
    for ref in refs[len(refs) - outs :]:
        ref[...] = total.astype(ref.dtype)


def add(values, whole=True):
    rows, width = values[0].shape
    outs = [near(rows, width)] * whole + [near(rows, width, dtype=BF16)]
    sums = call(
        functools.partial(add_kernel, outs=len(outs)), "add", (), (), near_args=values,
        near_outs=outs, us=1, limit=2,
    )
    return sums if whole else sums[0]


def add_rim_kernel(io, *refs, count, bit):
    values, moving, stay = refs[:count], refs[count], refs[count + 1]
    low_out, stay_out = refs[-2:]
    rows = values[0].shape[0]
    total = values[0][...]
    for ref in values[1:]:
        total = total + ref[0:rows, :].astype(F32)
    if len(refs) > count + 4:
        refs[-3][...] = total
    low_out[0:rows, :] = total.astype(BF16)
    if bit is None:
        low_out[rows:, :] = moving[...]
        stay_out[...] = jnp.zeros_like(stay_out)
        return
    came = values[-1][rows:, :]
    if low_out.shape[0] > rows:
        low_out[rows:, :] = came
    position = lax.axis_index("seq")
    chip = position >> 1
    chip = jnp.where((position & 1) == 0, chip, lax.axis_size("seq") // 2 - 1 - chip)
    lowest = chip & ((2 << bit) - 1)
    stay_out[...] = jnp.where(lowest == (1 << bit), came, stay[...])


def add_rim(values, moving, stay, bit, final=False):
    rows, width = values[0].shape
    edge = moving.shape[0]
    sent = rows if final else rows + edge
    outs = [near(rows, width)] * (not final)
    outs += [near(sent, width, dtype=BF16), near(edge, width, dtype=BF16)]
    sums = call(
        functools.partial(add_rim_kernel, count=len(values), bit=bit), "add", (), (),
        near_args=tuple(values) + (moving, stay), near_outs=outs, us=1, limit=2,
    )
    return [None] * final + list(sums)


def stack_kernel(io, *refs):
    for k, ref in enumerate(refs[:-1]):
        refs[-1][k] = ref[...]


def plane_pairs(k):
    return [(i, i ^ k) for i in range(lax.axis_size("img"))]


def chips_sum(kept, sent, edges=()):
    count = lax.axis_size("img")
    rows, width = kept.shape
    block = (rows // count, width)
    got = other_core(sent)
    own, *parts = call(
        functools.partial(split_kernel, edges=edges), "split", (), (), near_args=(kept, got),
        near_outs=[near(*block)] + [near(*block, dtype=BF16)] * (count - 1)
        + [near(rim_rows, width, dtype=BF16) for rim_rows in edges[:1]],
        us=1, limit=2,
    )
    rim = parts.pop() if edges else None
    blocks = [own] + [
        lax.ppermute(part, "img", plane_pairs(k + 1)) for k, part in enumerate(parts)
    ]
    return blocks, rim


def line_steps(total, low):
    bits = bits_of("seq")
    for bit in range(1, bits):
        got = lax.ppermute(low, "seq", partner("seq", bit))
        if bit < bits - 1:
            total, low = add([total, got])
        else:
            low = add([total, got], whole=False)
    return low


def line_steps_with_rims(blocks, rim, first_low, beside):
    stay = rim
    total, low, stay = add_rim(blocks, rim, stay, None)
    low, first_low = tied(low, first_low)
    bits = bits_of("seq")
    for bit in range(1, bits):
        got = lax.ppermute(low, "seq", partner("seq", bit))
        if bit == 1:
            first_blocks = plane_blocks(first_low)
        if bit == bits - 1:
            got, beside, *first_blocks = lax.optimization_barrier((got, beside, *first_blocks))
        total, low, stay = add_rim([total, got], rim, stay, bit - 1, bit == bits - 1)
    return low, stay, first_blocks, beside


def plane_blocks(low):
    count = lax.axis_size("img")
    return [low] + [lax.ppermute(low, "img", plane_pairs(k)) for k in range(1, count)]


def stacked(blocks):
    low, count = blocks[0], len(blocks)
    return call(
        stack_kernel, "stack", (), (), near_args=blocks,
        near_outs=[near(count, *low.shape, dtype=BF16)], us=1, limit=2,
    )[0]


def tied(first, second):
    return lax.optimization_barrier((first, second))


def body(
    tokens, cotangent, heights, widths, valid, norm_gain, in_weight, conv_weight, conv_bias,
    xproj_weight, dt_weight, dt_bias, a_log, skip, out_weight,
):
    rows, width = tokens.shape[1:]
    inner = out_weight.shape[0]
    state = a_log.shape[1]
    rank = dt_weight.shape[1]
    cols = xproj_weight.shape[2]
    taps = conv_weight.shape[1]
    reach = taps - 1
    count = bits_of("seq")
    tokens, cotangent = tokens[0], cotangent[0]
    xproj = xproj_weight.transpose(0, 2, 1)

    to_core, to_chip = call_edges(tokens, valid)
    from_core, from_chip = other_core(to_core), next_chip(to_chip)
    weights = (conv_weight, conv_bias, xproj, dt_weight, dt_bias, a_log, skip)
    normed, x, zs, dgz, dy, live, same, cotan, in_x, halo_live, gains, *near_weights = call_front(
        heights, widths, valid, norm_gain, tokens, cotangent, in_weight, out_weight, weights, reach
    )
    (
        summary, sent, delta, s, dsilu, tail, head, xext, proj, before, after, rate, nhalo,
        dy, live, same, normed, zs, dgz, cotan,
    ) = call_middle(
        (dy, live, same, normed, zs, dgz, cotan), (0, 1, 2), from_core, from_chip,
        (x, in_x, halo_live, gains) + tuple(near_weights), reach, cols,
    )
    entered = None
    for bit in range(count - 1):
        got = lax.ppermute(sent, "seq", partner("seq", bit))
        summary, entered, sent = call_join(got, summary, entered, state, bit, bit == count - 2)
    got = lax.ppermute(sent, "seq", partner("seq", count - 1))
    handed = (
        delta, s, dsilu, dy, head, xext, proj, after, rate, same, live, normed, nhalo,
    )
    kept, sent, carry, dz, h0, h1, gated, *handed = call_states(
        handed, (0, 1, 6, 8, 9, 11), before, tail, got, entered, zs, dgz, cotan, rank, reach, state,
        count - 1,
    )

    blocks, _ = chips_sum(kept, sent)
    small = -(-(cols + rank + state + 2 + taps + 1) // CHUNKS) * CHUNKS
    weights = (dt_weight, xproj, conv_weight)
    handed = tuple(handed[:10]) + (carry,) + tuple(handed[10:]) + (dz, gated, h1)
    rim0, small0, dx, *handed = call_first_adjoint(
        handed, tuple(range(11)), h0, weights, small, reach, rank, state
    )
    *blocks, dx = lax.optimization_barrier((*blocks, dx))
    first_sum, first_low = add(blocks)
    first_sum, first_low, dx = lax.optimization_barrier((first_sum, first_low, dx))
    arrays, passed, h1 = tuple(handed[:11]), tuple(handed[11:-1]), handed[-1]
    if bits_of("seq") > 3:
        first_low = line_steps(first_sum, first_low)
    else:
        devices = lax.axis_size("seq")
        blocks = [first_sum] + [
            lax.ppermute(first_low, "seq", [(i, i ^ k) for i in range(devices)])
            for k in range(2, devices, 2)
        ]
    rim1, small1, dx, in_near, *passed = call_second_adjoint(
        passed, arrays + (h1, dx), weights, in_weight, small, reach, rank, state
    )
    live, normed, nhalo, dz, gated = passed
    if bits_of("seq") <= 3:
        *blocks, dx = lax.optimization_barrier((*blocks, dx))
        first_low = add(blocks, whole=False)
    kept, sent, dx_low, dz, gated, in_near = call_last(
        (dz, gated, in_near), dx, rim0, rim1, small0, small1, normed, nhalo, live
    )

    edges = (2 * CHUNKS, kept.shape[0] - width - 2 * small)
    blocks, rim = chips_sum(kept, sent, edges)


    output = call(
        output_kernel, "output", (tokens, out_weight), [low(rows, width)], near_args=(gated,), us=2,
        limit=6,
    )[0]
    second_low, chip_rim, first_blocks, output = line_steps_with_rims(blocks, rim, first_low, output)
    blocks = plane_blocks(second_low)
    _, *first_blocks = lax.optimization_barrier((blocks[1], *first_blocks))
    first_mine = stacked(first_blocks)
    first_other = other_core(first_mine)
    input_grad = call(
        finish_kernel, "finish", (tokens, cotangent, valid, norm_gain), [shape(rows, width)],
        near_args=(dx_low, dz, in_near, rim, chip_rim), scalars=(heights, widths), us=3, limit=8,
    )[0]
    blocks, input_grad = lax.optimization_barrier((blocks, input_grad))
    second_mine = stacked(blocks)
    second_other = other_core(second_mine)
    parts, in_total, out_total = call(
        first_unpack, "unpack_first", (), (),
        [scratch(inner, width), scratch(width, inner), moves(2)],
        far_outs=[shape(width, 2 * inner), shape(inner, width)],
        near_args=(first_mine, first_other, in_near), near_outs=[near(width, LANES)], us=2, limit=8,
    )
    second_other, parts = tied(second_other, parts)
    fold = kept.shape[0]
    (
        conv_total, bias_total, xproj_total, dtw_total, dtb_total, a_total, skip_total, gain_total,
        in_total,
    ) = call(
        functools.partial(
            second_unpack, count=small, state=state, rank=rank, cols=cols, taps=taps
        ),
        "unpack_second", (norm_gain,),
        [
            shape(2, taps, inner), shape(2, inner), shape(2, cols, inner), shape(2, rank, inner),
            shape(2, inner), shape(2, state, inner), shape(2, inner), shape(width),
        ],
        [scratch(fold, width), scratch(fold, width), scratch(width, inner), moves(1)],
        (in_total,), [shape(width, 2 * inner)], (second_mine, second_other, in_near, parts),
        aliases=((0, 0),), us=2, limit=10,
    )
    return (
        output[None], input_grad[None], gain_total, in_total, conv_total, bias_total,
        xproj_total.transpose(0, 2, 1), dtw_total, dtb_total, a_total, skip_total, out_total,
    )


def solution(mesh):
    split = P("img", "seq", None)
    placed = (split, split, P("img", None), P("img", None), P("img", "seq")) + (P(),) * 10
    return jax.shard_map(
        body,
        mesh=mesh,
        in_specs=placed,
        out_specs=(split, split) + (P(),) * 10,
        check_vma=False,
    )
```

```python
import functools

import jax
import jax.numpy as jnp
from jax import lax
from jax.experimental import pallas as pl
from jax.experimental.pallas import tpu as pltpu
from jax.sharding import PartitionSpec as P

NORM_EPS = 1e-05
CONTRACT_ROWS = (((0,), (0,)), ((), ()))
CONTRACT_COLS = (((1,), (1,)), ((), ()))
LOG2E = 1.4426950408889634
LN2 = 0.6931471805599453
BREAK = 1e30
CHUNKS = 8
LANES = 128
SUMMARY_STATES = 8
SUMMARY_UNROLL = 16
STATES_UNROLL = 32
ADJOINT_STATES = 8
ADJOINT_UNROLL = 16
F32 = jnp.float32
BF16 = jnp.bfloat16


def dot(a, b):
    return jnp.dot(a, b, preferred_element_type=F32)


def dot_rows(a, b):
    return lax.dot_general(a, b, CONTRACT_ROWS, preferred_element_type=F32)


def dot_cols(a, b):
    return lax.dot_general(a, b, CONTRACT_COLS, preferred_element_type=F32)


def sigmoid(v):
    return 1.0 / (1.0 + jnp.exp(-v))


def fetch(source, target, semaphore):
    copy = pltpu.make_async_copy(source, target, semaphore)
    copy.start()
    return copy


def lanes_of(tile):
    return pl.ds(pl.multiple_of(tile * LANES, LANES), LANES)


def rows_of(j, count=CHUNKS):
    return pl.ds(pl.multiple_of(j * CHUNKS, CHUNKS), count)


def chunk_order(rows):
    row = lax.broadcasted_iota(jnp.int32, (rows, rows), 0)
    slot = lax.broadcasted_iota(jnp.int32, (rows, rows), 1)
    return slot == (row & (CHUNKS - 1)) * (rows // CHUNKS) + (row >> 3)


def image_ends(heights, widths):
    ends, total = [], 0
    for i in range(heights.shape[1]):
        total = total + heights[0, i] * widths[0, i]
        ends.append(total)
    return ends


def segment_of(places, ends):
    found = jnp.zeros_like(places)
    for end in ends:
        found = found + (places >= end).astype(jnp.int32)
    return found


def places_of(first, rows):
    row = lax.broadcasted_iota(jnp.int32, (rows, LANES), 0)
    return first + (row & (CHUNKS - 1)) * (rows // CHUNKS) + (row >> 3)


def edges_kernel(io, tokens, valid, to_core, to_chip):
    rows = tokens.shape[0]
    edge = to_core.shape[0]
    io.ready()
    row = lax.broadcasted_iota(jnp.int32, (edge, rows), 0)
    slot = lax.broadcasted_iota(jnp.int32, (edge, rows), 1)
    held = jnp.broadcast_to(valid[...].astype(F32), (edge, rows))
    first = jnp.where(slot == row, held, 0.0).astype(BF16)
    last = jnp.where(slot == rows - edge + row, held, 0.0).astype(BF16)
    first = dot(first, tokens[...]).astype(BF16)
    last = dot(last, tokens[...]).astype(BF16)
    even = (lax.axis_index("seq") & 1) == 0
    to_core[...] = jnp.where(even, last, first)
    to_chip[...] = jnp.where(even, first, last)


def spread(values, target):
    count = values.shape[1]
    high = values.astype(BF16)
    low = (values - high.astype(F32)).astype(BF16)
    both = jnp.concatenate([high, low], axis=1)
    row = lax.broadcasted_iota(jnp.int32, (2 * count, LANES), 0)
    row = jnp.where(row < count, row, row - count)
    for at in range(0, count, 2):
        pick = jnp.concatenate([(row == at).astype(BF16), (row == at + 1).astype(BF16)], axis=1)
        target[:, at * LANES : (at + 2) * LANES] = dot(both, pick)


def windows(span, up, sublane):
    sign = 1 if up else -1

    def from_before(value, by, fill):
        moved = pltpu.roll(value, (sign * by) % CHUNKS, axis=0)
        kept = sublane >= by if up else sublane < CHUNKS - by
        return jnp.where(kept, moved, fill)

    two = span + from_before(span, 1, 0.0)
    four = two + from_before(two, 2, 0.0)
    eight = four + from_before(four, 4, 0.0)
    edge = [jnp.where(sublane >= by if up else sublane < CHUNKS - by, 0.0, BREAK) for by in (1, 2, 4)]
    return (span + edge[0], two + edge[1], four + edge[2]), from_before(eight, 1, 0.0)


def chain(rate, sums, tail, up, sublane):
    sign = 1 if up else -1
    for by, span in zip((1, 2, 4), sums):
        tail = jnp.exp2(rate * span) * pltpu.roll(tail, (sign * by) % CHUNKS, axis=0) + tail
    end = CHUNKS - 1 if up else 0
    kept = sublane >= 1 if up else sublane < CHUNKS - 1
    return jnp.where(kept, pltpu.roll(tail, sign % CHUNKS, axis=0), 0.0), tail[end : end + 1]


def front_kernel(
    io, tokens, cotangent, in_weight, out_weight, heights, widths, valid, gain, *refs, reach, weights,
):
    (
        normed_out, x_out, zs_out, dgz_out, dy, live, same_out, cotan, in_x, halo_live, gains_out,
    ) = refs[weights : weights + 11]
    near_weights = refs[weights + 11 : 2 * weights + 11]
    ins = refs[2 * weights + 11]
    rows, width = tokens.shape
    inner = out_weight.shape[0]
    tiles = inner // LANES
    arriving = [
        fetch(source, target, ins.at[i])
        for i, (source, target) in enumerate(zip(refs[:weights], near_weights))
    ]
    order = chunk_order(rows)
    order_low = order.astype(BF16)
    inputs = dot(order_low, tokens[...])
    inv_rms = lax.rsqrt(jnp.mean(inputs * inputs, axis=-1, keepdims=True) + NORM_EPS)
    cotan[...] = dot(order_low, cotangent[...]).astype(BF16)
    step = 2 * LANES
    for at in range(0, inner, step):
        lanes = slice(at, at + step)
        dgz_out[:, lanes] = dot_cols(cotan[...], out_weight[lanes, :])
    in_x[...] = in_weight[:, 0:inner]

    io.ready()
    start = lax.axis_index("seq") * rows
    slots = lax.axis_size("seq") * rows
    ends = image_ends(heights, widths)
    images = heights.shape[1]
    picked = jnp.where(order, jnp.broadcast_to(valid[...].astype(F32), order.shape), 0.0)
    alive = dot(picked.astype(BF16), jnp.ones((rows, LANES), BF16))
    places = places_of(start, rows)
    segment = segment_of(places, ends)
    live[...] = jnp.where(segment < images, alive, 0.0)
    for k in range(1, reach + 1):
        same = (segment_of(places - k, ends) == segment) & (places >= k)
        same_out[(k - 1) * rows : k * rows, :] = same.astype(F32)
        same = (segment_of(places + k, ends) == segment) & (places + k < slots)
        same_out[(reach + k - 1) * rows : (reach + k) * rows, :] = same.astype(F32)
    near_row = lax.broadcasted_iota(jnp.int32, (2 * CHUNKS, LANES), 0)
    near_place = jnp.where(
        near_row < CHUNKS, start - CHUNKS + near_row, start + rows + near_row - CHUNKS
    )
    halo_live[...] = (segment_of(near_place, ends) < images).astype(F32)

    gains = gain[...].astype(F32).reshape(1, width)
    gains_out[...] = jnp.broadcast_to(gains, gains_out.shape)
    scaled = inputs * inv_rms * gains
    normed = scaled.astype(BF16)
    normed_out[...] = normed
    live_wide = jnp.concatenate([live[...]] * (width // LANES), axis=1)
    normed_live = (scaled * live_wide).astype(BF16)
    for at in range(0, inner, step):
        lanes = slice(at, at + step)
        x_out[:, lanes] = dot(normed_live, in_x[:, lanes]).astype(BF16).astype(F32)
        zs_out[:, lanes] = dot(normed, in_weight[:, inner + at : inner + at + step])
    block = 32

    def gate_block(b, _):
        here = pl.ds(pl.multiple_of(b * block, block), block)
        alive = live[here, :]
        for tile in range(tiles):
            lanes = slice(tile * LANES, (tile + 1) * LANES)
            z = zs_out[here, lanes]
            grad = dgz_out[here, lanes] * alive
            gate = sigmoid(z)
            zs = z * gate * alive
            zs_out[here, lanes] = zs
            dy[here, lanes] = 0.5 * grad * zs
            dgz_out[here, lanes] = grad * (gate * (1.0 + z * (1.0 - gate)))
        return 0

    lax.fori_loop(0, rows // block, gate_block, 0, unroll=4)
    for copy in arriving:
        copy.wait()


def middle_kernel(
    io, dy, live, same_out, from_core, from_chip, x, in_x, halo_live, gains, conv_weight, conv_bias,
    xproj, dt_weight, dt_bias, a_log, skip,
    sum_out, sent_out, delta_out, s_out, dsilu_out, tail_out, head_out, xext_out, proj_out,
    before_out, after_out, rate_out, nhalo_out,
    low_out, bc, tails, heads, spans,
    *, reach,
):
    rows, inner = x.shape
    width = in_x.shape[0]
    steps = rows // CHUNKS
    state = a_log.shape[1]
    rank = dt_weight.shape[1]
    tiles = inner // LANES
    even = (lax.axis_index("seq") & 1) == 0
    sublane = lax.broadcasted_iota(jnp.int32, (CHUNKS, LANES), 0)
    wide = lax.broadcasted_iota(jnp.int32, (CHUNKS, inner), 0)
    xext_out[reach * CHUNKS : (reach + steps) * CHUNKS, :] = x[...]

    core, chip = from_core[...].astype(F32), from_chip[...].astype(F32)
    before = jnp.where(even, chip, core)
    after = jnp.where(even, core, chip)
    htok = jnp.concatenate([before[CHUNKS:], after[:CHUNKS]], axis=0)
    htok = htok * jnp.concatenate([halo_live[...]] * (width // LANES), axis=1)
    hinv = lax.rsqrt(jnp.mean(htok * htok, axis=-1, keepdims=True) + NORM_EPS)
    scaled = htok * hinv
    nhalo = (scaled * gains[0:1, :]).astype(BF16)
    nhalo_out[...] = jnp.concatenate([nhalo, scaled.astype(BF16)], axis=0)
    hx = dot(nhalo, in_x[...]).astype(BF16).astype(F32)
    for i in range(reach):
        to = steps - reach + i
        moved = pltpu.roll(x[to * CHUNKS : (to + 1) * CHUNKS, :], 1, axis=0)
        of = CHUNKS - reach + i
        xext_out[i * CHUNKS : (i + 1) * CHUNKS, :] = jnp.where(wide == 0, hx[of : of + 1], moved)
        moved = pltpu.roll(x[i * CHUNKS : (i + 1) * CHUNKS, :], CHUNKS - 1, axis=0)
        to = reach + steps + i
        of = CHUNKS + i
        xext_out[to * CHUNKS : (to + 1) * CHUNKS, :] = jnp.where(
            wide == CHUNKS - 1, hx[of : of + 1], moved
        )

    block = 64
    step = 2 * LANES
    taps = reach + 1
    conv_w = [conv_weight[d].astype(F32) for d in range(2)]
    conv_b = conv_bias[...].astype(F32)
    for tile in range(tiles):
        lanes = slice(tile * LANES, (tile + 1) * LANES)

        def conv_block(b, _, lanes=lanes):
            at = pl.multiple_of(b * block, block)
            for d in range(2):
                total = conv_b[d : d + 1, lanes] + conv_w[d][reach:taps, lanes] * (
                    xext_out[pl.ds(at + reach * CHUNKS, block), lanes]
                )
                for k in range(1, taps):
                    move = reach - k if d == 0 else reach + k
                    mask = same_out[pl.ds((d * reach + k - 1) * rows + at, block), :]
                    total = total + conv_w[d][reach - k : taps - k, lanes] * (
                        xext_out[pl.ds(at + move * CHUNKS, block), lanes] * mask
                    )
                gate = sigmoid(total)
                value = total * gate
                s_out[pl.ds(d * rows + at, block), lanes] = value
                low_out[pl.ds(d * rows + at, block), lanes] = value.astype(BF16)
                dsilu_out[pl.ds(d * rows + at, block), lanes] = gate * (1.0 + total * (1.0 - gate))
            return 0

        lax.fori_loop(0, rows // block, conv_block, 0, unroll=4)

    dt_b = dt_bias[...].astype(F32)
    for d in range(2):
        rate_out[d * state : (d + 1) * state, :] = jnp.minimum(
            -LOG2E * jnp.exp(a_log[d].astype(F32)), -1e-20
        )
        here = slice(d * rows, (d + 1) * rows)
        proj = dot_cols(low_out[here, :], xproj[d])
        proj_out[here, :] = proj
        dt_low = proj[:, :rank].astype(BF16)
        for at in range(0, inner, step):
            lanes = slice(at, at + step)
            delta_out[here, lanes] = dot(dt_low, dt_weight[d, :, lanes])
        spread(proj[:, rank:], bc)

        def delta_block(b, _, d=d):
            alive = live[pl.ds(pl.multiple_of(b * block, block), block), :]
            here = pl.ds(pl.multiple_of(d * rows + b * block, block), block)
            for tile in range(tiles):
                lanes = slice(tile * LANES, (tile + 1) * LANES)
                pre = delta_out[here, lanes] + dt_b[d : d + 1, lanes]
                small = jnp.exp(-jnp.abs(pre))
                log1p = jnp.where(small < 1e-4, small * (1.0 - 0.5 * small), jnp.log(1.0 + small))
                delta_out[here, lanes] = (jnp.maximum(pre, 0.0) + log1p) * alive
            return 0

        lax.fori_loop(0, rows // block, delta_block, 0, unroll=4)
        some = SUMMARY_STATES

        def scan_tile(tile, _, d=d):
            lanes = lanes_of(tile)
            for low in range(0, state, some):
                rates = [
                    jnp.broadcast_to(
                        rate_out[d * state + low + m : d * state + low + m + 1, lanes],
                        (CHUNKS, LANES),
                    )
                    for m in range(some)
                ]

                def scan_step(i, carried, d=d, low=low, rates=rates):
                    tail, lead, head, span = carried
                    j = i if d == 0 else steps - 1 - i
                    at = pl.multiple_of(j * CHUNKS, CHUNKS)
                    keep = same_out[pl.ds(d * reach * rows + at, CHUNKS), :]
                    delta = delta_out[pl.ds(d * rows + at, CHUNKS), lanes]
                    drive = delta * s_out[pl.ds(d * rows + at, CHUNKS), lanes]
                    back = dy[pl.ds(at, CHUNKS), lanes]
                    delta = jnp.maximum(delta, BREAK - keep * BREAK)
                    tail, lead, head = list(tail), list(lead), list(head)
                    for m in range(some):
                        b = bc[pl.ds(at, CHUNKS), (low + m) * LANES : (low + m + 1) * LANES]
                        n = state + low + m
                        c = bc[pl.ds(at, CHUNKS), n * LANES : (n + 1) * LANES]
                        decay = jnp.exp2(delta * rates[m])
                        tail[m] = decay * tail[m] + b * drive
                        lead[m] = lead[m] * decay
                        head[m] = head[m] + lead[m] * (c * back)
                    return tuple(tail), tuple(lead), tuple(head), span + delta

                zeros = tuple(jnp.zeros((CHUNKS, LANES), F32) for _ in range(some))
                ones = tuple(jnp.ones((CHUNKS, LANES), F32) for _ in range(some))
                tail, lead, head, span = lax.fori_loop(
                    0, steps, scan_step, (zeros, ones, zeros, zeros[0]), unroll=SUMMARY_UNROLL
                )
                for m in range(some):
                    tails[low + m, :, lanes] = tail[m]
                    heads[low + m, :, lanes] = head[m]
                spans[:, lanes] = span
            return 0

        lax.fori_loop(0, tiles, scan_tile, 0)

        tail_row = 0 if d == 0 else 2 * state
        head_row = 3 * state if d == 0 else state

        def chain_tile(tile, _, d=d, tail_row=tail_row, head_row=head_row):
            lanes = lanes_of(tile)
            span = spans[:, lanes]
            sums, before = windows(span, d == 0, sublane)
            sums_back, after = windows(span, d == 1, sublane)
            before_out[d * CHUNKS : (d + 1) * CHUNKS, lanes] = before
            after_out[d * CHUNKS : (d + 1) * CHUNKS, lanes] = after
            for n in range(state):
                rate = jnp.broadcast_to(
                    rate_out[d * state + n : d * state + n + 1, lanes], (CHUNKS, LANES)
                )
                carried, total = chain(rate, sums, tails[n, :, lanes], d == 0, sublane)
                tail_out[d * state + n, :, lanes] = carried
                sum_out[tail_row + n : tail_row + n + 1, lanes] = total
                carried, total = chain(rate, sums_back, heads[n, :, lanes], d == 1, sublane)
                head_out[d * state + n, :, lanes] = carried
                sum_out[head_row + n : head_row + n + 1, lanes] = total
            return 0

        lax.fori_loop(0, tiles, chain_tile, 0)
        sum_out[4 * state + d : 4 * state + d + 1, :] = jnp.sum(spans[...], axis=0, keepdims=True)
    at = 4 * state + CHUNKS
    sum_out[4 * state + 2 : at, :] = jnp.zeros((CHUNKS - 2, inner), F32)
    sum_out[at:, :] = rate_out[0 : 2 * state, :]
    sent_out[...] = packed(sum_out[0:at, :], state)
    rate_out[2 * state : 2 * state + 2, :] = skip[...].astype(F32)


def packed(summary, state):
    rest = summary[4 * state :]
    high = rest.astype(BF16).astype(F32)
    return jnp.concatenate([summary[: 4 * state], high, rest - high], axis=0).astype(BF16)


def leads(rate, spans, state, flip):
    parts = [jnp.exp2(rate[d * state : (d + 1) * state] * spans[d : d + 1]) for d in range(2)]
    return jnp.concatenate(parts[::-1] if flip else parts, axis=0)


def join_kernel(io, got, summary, entered, *outs, state, bit, final):
    half = 2 * state
    upper = ((lax.axis_index("seq") >> bit) & 1) == 1
    mine = summary[0 : 2 * half + CHUNKS, :]
    rates = summary[2 * half + CHUNKS :, :]
    entered_out, sent_out = outs[-2], outs[-1]
    values = got[...].astype(F32)
    spans = mine[4 * state : 4 * state + 2]
    other = values[4 * state : 4 * state + 2] + values[4 * state + CHUNKS : 4 * state + CHUNKS + 2]
    if entered is None:
        entered_up = jnp.where(upper, values[:half], 0.0)
        entered_down = jnp.where(upper, 0.0, values[half : 2 * half])
        span_up = jnp.where(upper, other, 0.0)
        span_down = jnp.where(upper, 0.0, other)
    else:
        held = entered[...]
        span_up, span_down = held[2 * half : 2 * half + 2], held[2 * half + 2 : 2 * half + 4]
        entered_up = held[:half] + jnp.where(
            upper, leads(rates, span_up, state, False) * values[:half], 0.0
        )
        entered_down = held[half : 2 * half] + jnp.where(
            upper, 0.0, leads(rates, span_down, state, True) * values[half : 2 * half]
        )
        span_up = span_up + jnp.where(upper, other, 0.0)
        span_down = span_down + jnp.where(upper, 0.0, other)
    entered_out[0:half, :] = entered_up
    entered_out[half : 2 * half, :] = entered_down
    entered_out[2 * half :, :] = jnp.concatenate(
        [span_up, span_down, jnp.zeros((CHUNKS - 4, mine.shape[1]), F32)], axis=0
    )
    low_up = jnp.where(upper, values[:half], mine[:half])
    high_up = jnp.where(upper, mine[:half], values[:half])
    low_down = jnp.where(upper, values[half : 2 * half], mine[half : 2 * half])
    high_down = jnp.where(upper, mine[half : 2 * half], values[half : 2 * half])
    low_span, high_span = jnp.where(upper, other, spans), jnp.where(upper, spans, other)
    up = leads(rates, high_span, state, False) * low_up + high_up
    down = leads(rates, low_span, state, True) * high_down + low_down
    if final:
        next_upper = ((lax.axis_index("seq") >> (bit + 1)) & 1) == 1
        sent_out[...] = jnp.where(next_upper, down, up).astype(BF16)
    else:
        total = jnp.concatenate(
            [up, down, spans + other, jnp.zeros((CHUNKS - 2, mine.shape[1]), F32)], axis=0
        )
        outs[0][0 : 2 * half + CHUNKS, :] = total
        outs[0][2 * half + CHUNKS :, :] = rates
        sent_out[...] = packed(total, state)


def first_join(io, got, summary, *outs, state, bit, final):
    join_kernel(io, got, summary, None, *outs, state=state, bit=bit, final=final)


def state_block(j, state):
    return pl.multiple_of(j * state * CHUNKS, CHUNKS)


def states_pass(d, steps, state, rates, begin, delta, s, keep, bc, h_out, y):
    start = state_block(0 if d == 0 else steps, state)
    for n in range(state):
        h_out[pl.ds(start + n * CHUNKS, CHUNKS), :] = begin[n]

    def step(i, h):
        j = i if d == 0 else steps - 1 - i
        here = pl.ds(pl.multiple_of(j * CHUNKS, CHUNKS), CHUNKS)
        to = state_block(j + 1 if d == 0 else j, state)
        size = delta[here, :]
        drive = size * s[here, :]
        size = jnp.maximum(size, BREAK - keep[here, :] * BREAK)
        h = list(h)
        parts = [None if d == 0 else y[here, :], None]
        for n in range(state):
            b = bc[here, n * LANES : (n + 1) * LANES]
            c = bc[here, (state + n) * LANES : (state + n + 1) * LANES]
            h[n] = jnp.exp2(size * rates[n]) * h[n] + b * drive
            h_out[pl.ds(to + n * CHUNKS, CHUNKS), :] = h[n]
            part = parts[n % 2]
            parts[n % 2] = c * h[n] if part is None else part + c * h[n]
        y[here, :] = parts[0] + parts[1]
        return tuple(h)

    lax.fori_loop(0, steps, step, tuple(begin), unroll=STATES_UNROLL)


def adjoint_pass(
    d, steps, state, rates, back, delta, s, dy, keep, skip, bc, h_in, sums,
    dpre_out, ds_out, rows_out,
):
    some = ADJOINT_STATES
    edge = steps - 1
    skip = skip[...]
    zeros = jnp.zeros((CHUNKS, LANES), F32)
    grads = []
    for low in range(0, state, some):
        final = low + some == state

        def step(i, carried, low=low, final=final):
            g, acc, h, skip_acc, bias_acc = carried
            j = edge - i if d == 0 else i
            here = pl.ds(pl.multiple_of(j * CHUNKS, CHUNKS), CHUNKS)
            size = delta[here, :]
            value = s[here, :]
            grad = dy[here, :]
            drive = size * value
            masked = jnp.maximum(size, BREAK - keep[here, :] * BREAK)
            prev = state_block(j if d == 0 else j + 1, state)
            g, acc, h = list(g), list(acc), list(h)
            weighted = zeros if low == 0 else ds_out[here, :]
            rate_sum = zeros if low == 0 else dpre_out[here, :]
            for m in range(some):
                n = low + m
                b = bc[here, n * LANES : (n + 1) * LANES]
                c = bc[here, (state + n) * LANES : (state + n + 1) * LANES]
                adjoint = c * grad + g[m]
                before = h_in[pl.ds(prev + n * CHUNKS, CHUNKS), :]
                sums[here, n * LANES : (n + 1) * LANES] += adjoint * drive
                sums[here, (state + n) * LANES : (state + n + 1) * LANES] += grad * h[m]
                g[m] = adjoint * jnp.exp2(masked * rates[n])
                held = g[m] * before
                weighted = weighted + adjoint * b
                rate_sum = rate_sum + held * rates[n]
                acc[m] = acc[m] + held * masked
                h[m] = before
            if final:
                ds_out[here, :] = skip * grad + size * weighted
                gate = jnp.where(
                    size < 0.01, size * (1.0 - size * (0.5 - size * (1.0 / 6.0))), 1.0 - jnp.exp(-size)
                )
                pre = ((LN2 * rate_sum + weighted * value) * gate).astype(BF16).astype(F32)
                dpre_out[here, :] = pre
                bias_acc = bias_acc + pre
                skip_acc = skip_acc + grad * value
            else:
                dpre_out[here, :] = rate_sum
                ds_out[here, :] = weighted
            return tuple(g), tuple(acc), tuple(h), skip_acc, bias_acc

        last = state_block(steps if d == 0 else 0, state)
        h_last = tuple(h_in[pl.ds(last + (low + m) * CHUNKS, CHUNKS), :] for m in range(some))
        none = tuple(zeros for _ in range(some))
        _, acc, _, skip_acc, bias_acc = lax.fori_loop(
            0, steps, step, (tuple(back[low : low + some]), none, h_last, zeros, zeros),
            unroll=ADJOINT_UNROLL,
        )
        grads.extend(acc)
    for n in range(state):
        rows_out[n : n + 1, :] = jnp.sum(grads[n], axis=0, keepdims=True) * rates[n][0:1] * LN2
    rows_out[state : state + 1, :] = jnp.sum(bias_acc, axis=0, keepdims=True)
    rows_out[state + 1 : state + 2, :] = jnp.sum(skip_acc, axis=0, keepdims=True)


def lane_sums(sums, state):
    column = lax.broadcasted_iota(jnp.int32, (2 * CHUNKS, LANES), 1)
    picks = [(column == n).astype(BF16) for n in range(2 * state)]
    pick = jnp.concatenate([p for p in picks for _ in range(LANES // (2 * CHUNKS))], axis=0)
    return dot(sums.astype(BF16), pick)[:, : 2 * state]


def rate_tiles(rate, d, state, lanes):
    return [
        jnp.broadcast_to(rate[d * state + n : d * state + n + 1, lanes], (CHUNKS, LANES))
        for n in range(state)
    ]


def begin_tiles(rates, passed, maps, carry, at, d, state, lanes):
    passed = passed[d * CHUNKS : (d + 1) * CHUNKS, lanes]
    return [
        jnp.exp2(rates[n] * passed) * carry[at + n : at + n + 1, lanes]
        + maps[d * state + n, :, lanes]
        for n in range(state)
    ]


def slot_order(rows):
    row = lax.broadcasted_iota(jnp.int32, (rows, rows), 1)
    slot = lax.broadcasted_iota(jnp.int32, (rows, rows), 0)
    return (slot == (row & (CHUNKS - 1)) * (rows // CHUNKS) + (row >> 3)).astype(BF16)


def states_kernel(
    io, delta, s, proj, rate, same, normed, before, tail, got, entered, zs, dgz, cotan,
    kept, sent, carry_out, dz, h0, h1, gated,
    bc, y,
    *, reach, rank, state, bit,
):
    rows, inner = zs.shape
    width = cotan.shape[1]
    steps = rows // CHUNKS
    half = 2 * state
    tiles = inner // LANES
    upper = ((lax.axis_index("seq") >> bit) & 1) == 1
    values = got[...].astype(F32)
    held = entered[...]
    rates = rate[0:half, :]
    carry_out[0:half, :] = held[:half] + jnp.where(
        upper, leads(rates, held[2 * half : 2 * half + 2], state, False) * values, 0.0
    )
    carry_out[half : 2 * half, :] = held[half : 2 * half] + jnp.where(
        upper, 0.0, leads(rates, held[2 * half + 2 : 2 * half + 4], state, True) * values
    )
    for d, h in enumerate((h0, h1)):
        mine = slice(d * rows, (d + 1) * rows)
        spread(proj[mine, rank:], bc)
        keep = same.at[d * reach * rows : (d * reach + 1) * rows, :]

        def scan_tile(tile, _, d=d, h=h, mine=mine, keep=keep):
            lanes = lanes_of(tile)
            rates = rate_tiles(rate, d, state, lanes)
            begin = begin_tiles(rates, before, tail, carry_out, d * half, d, state, lanes)
            states_pass(
                d, steps, state, rates, begin, delta.at[mine, lanes], s.at[mine, lanes],
                keep, bc, h.at[tile], y.at[:, lanes],
            )
            return 0

        lax.fori_loop(0, tiles, scan_tile, 0)
    block = 32

    def gate_block(b, _):
        here = pl.ds(pl.multiple_of(b * block, block), block)
        there = pl.ds(pl.multiple_of(rows + b * block, block), block)
        for tile in range(tiles):
            lanes = slice(tile * LANES, (tile + 1) * LANES)
            total = 0.5 * (
                y[here, lanes] + rate[half : half + 1, lanes] * s[here, lanes]
                + rate[half + 1 : half + 2, lanes] * s[there, lanes]
            )
            gated[here, lanes] = (total * zs[here, lanes]).astype(BF16)
            dz[here, lanes] = (total * dgz[here, lanes]).astype(BF16)
        return 0

    lax.fori_loop(0, rows // block, gate_block, 0, unroll=4)
    even = (lax.axis_index("seq") & 1) == 0
    out_grad = dot_rows(gated[...], cotan[...]).astype(BF16)
    z_grad = jnp.concatenate(
        [dot_rows(normed[...], dz[:, at : at + width]) for at in range(0, inner, width)], axis=0
    ).astype(BF16)
    sent[...] = jnp.where(even, z_grad, out_grad)
    kept[...] = jnp.where(even, out_grad, z_grad)


def output_kernel(io, gated, tokens, out_weight, output):
    ordered = dot(slot_order(gated.shape[0]), gated[...]).astype(BF16)
    io.ready()
    output[...] = (tokens[...].astype(F32) + dot(ordered, out_weight[...])).astype(BF16)


def adjoint_kernel(
    io, delta, s, dsilu, dy, head, xext, proj, after, rate, same, carry, h, dx_in,
    dt_weight, xproj, conv_weight,
    dc_rim, small_out, dx_out,
    bc, sums, dpre, ds, rows_out, ext,
    *, d, reach, rank, state,
):
    rows, inner = dy.shape
    steps = rows // CHUNKS
    half = 2 * state
    tiles = inner // LANES
    taps = reach + 1
    cols = proj.shape[1]
    mine = slice(d * rows, (d + 1) * rows)
    keep = same.at[d * reach * rows : (d * reach + 1) * rows, :]
    spread(proj[mine, rank:], bc)
    sums[...] = jnp.zeros_like(sums)
    rows_out[...] = jnp.zeros_like(rows_out)
    grad_at = (half if d == 0 else 0) + state

    def scan_tile(tile, _):
        lanes = lanes_of(tile)
        rates = rate_tiles(rate, d, state, lanes)
        back = begin_tiles(rates, after, head, carry, grad_at, d, state, lanes)
        adjoint_pass(
            d, steps, state, rates, back, delta.at[mine, lanes], s.at[mine, lanes],
            dy.at[:, lanes], keep, rate.at[half + d : half + d + 1, lanes], bc,
            h.at[tile], sums, dpre.at[:, lanes], ds.at[:, lanes], rows_out.at[:, lanes],
        )
        return 0

    lax.fori_loop(0, tiles, scan_tile, 0)
    io.ready()
    dpre_low = dpre[...].astype(BF16)
    dt_grad = dot_rows(proj[mine, :rank].astype(BF16), dpre_low)
    dt_back = dot_cols(dpre_low, dt_weight[d])
    dproj = jnp.concatenate([dt_back, lane_sums(sums[...], state)], axis=1).astype(BF16)
    small_out[0:cols, :] = dot_rows(dproj, s[mine, :].astype(BF16))
    small_out[cols : cols + rank, :] = dt_grad
    base = 0 if d == 0 else reach * CHUNKS
    step = 2 * LANES
    for lane in range(0, inner, step):
        lanes = slice(lane, lane + step)
        total = ds[:, lanes] + dot(dproj, xproj[d, :, lanes])
        ext[base : base + rows, lanes] = (total * dsilu[mine, lanes]).astype(BF16).astype(F32)
    wide = lax.broadcasted_iota(jnp.int32, (CHUNKS, inner), 0)
    for i in range(reach):
        if d == 0:
            moved = pltpu.roll(ext[i * CHUNKS : (i + 1) * CHUNKS, :], CHUNKS - 1, axis=0)
            ext[rows + i * CHUNKS : rows + (i + 1) * CHUNKS, :] = jnp.where(
                wide == CHUNKS - 1, 0.0, moved
            )
        else:
            moved = pltpu.roll(ext[rows + i * CHUNKS : rows + (i + 1) * CHUNKS, :], 1, axis=0)
            ext[i * CHUNKS : (i + 1) * CHUNKS, :] = jnp.where(wide == 0, 0.0, moved)

    conv_w = conv_weight[d].astype(F32)
    block = 64
    zeros = jnp.zeros((CHUNKS, LANES), F32)

    def folded(values):
        return functools.reduce(
            lambda a, b: a + b, [values[i : i + CHUNKS] for i in range(0, block, CHUNKS)]
        )

    base_row = cols + rank
    for tile in range(tiles):
        lanes = slice(tile * LANES, (tile + 1) * LANES)
        weight = conv_w[:, lanes]

        def conv_block(b, totals, lanes=lanes, weight=weight):
            here = pl.multiple_of(b * block, block)
            totals = list(totals)
            mid = ext[pl.ds(here + base, block), lanes]
            total = weight[reach:taps] * mid
            totals[reach] = totals[reach] + folded(mid * xext[pl.ds(here + reach * CHUNKS, block), lanes])
            totals[taps] = totals[taps] + folded(mid)
            for k in range(1, taps):
                past = same[pl.ds((k - 1) * rows + here, block), :]
                ahead = same[pl.ds((reach + k - 1) * rows + here, block), :]
                if d == 0:
                    given = ext[pl.ds(here + k * CHUNKS, block), lanes] * ahead
                    taken = xext[pl.ds(here + (reach - k) * CHUNKS, block), lanes] * past
                else:
                    given = ext[pl.ds(here + (reach - k) * CHUNKS, block), lanes] * past
                    taken = xext[pl.ds(here + (reach + k) * CHUNKS, block), lanes] * ahead
                total = total + weight[reach - k : taps - k] * given
                totals[reach - k] = totals[reach - k] + folded(mid * taken)
            if dx_in is not None:
                total = total + dx_in[pl.ds(here, block), lanes]
            dx_out[pl.ds(here, block), lanes] = total
            return tuple(totals)

        totals = lax.fori_loop(0, rows // block, conv_block, (zeros,) * (taps + 1), unroll=4)
        for i in range(taps + 1):
            at = state + 2 + i
            rows_out[at : at + 1, lanes] = jnp.sum(totals[i], axis=0, keepdims=True)

    edge = []
    for i in range(CHUNKS):
        row = jnp.zeros((1, inner), F32)
        for k in range(1, taps):
            j = i - CHUNKS + k if d == 0 else steps + i - k
            if (d == 0 and j >= 0) or (d == 1 and j < steps):
                sub = 0 if d == 0 else CHUNKS - 1
                at = (d * reach + k - 1) * rows + j * CHUNKS + sub
                mask = jnp.concatenate([same[at : at + 1, :]] * tiles, axis=1)
                at = base + j * CHUNKS + sub
                row = row + conv_w[reach - k : taps - k] * ext[at : at + 1, :] * mask
        edge.append(row)
    dc_rim[...] = jnp.concatenate(edge, axis=0)
    small_out[base_row:, :] = rows_out[0 : small_out.shape[0] - base_row, :]


def first_adjoint(io, *refs, **static):
    adjoint_kernel(io, *refs[:12], None, *refs[12:], **static)


def second_adjoint(io, *refs, **static):
    in_far, in_near, moves = refs[16], refs[20], refs[21]
    copy = fetch(in_far, in_near, moves.at[0])
    adjoint_kernel(io, *refs[:16], *refs[17:20], *refs[22:], **static)
    copy.wait()


def last_kernel(
    io, dx, rim0, rim1, small0, small1, normed, nhalo, live, in_weight,
    kept, sent, low,
    lines, grads,
):
    rows, inner = dx.shape
    width = normed.shape[1]
    folds = inner // width
    fold = kept.shape[0]
    edges = 2 * CHUNKS
    for tile in range(inner // LANES):
        lanes = slice(tile * LANES, (tile + 1) * LANES)
        lines[0:rows, lanes] = (dx[:, lanes] * live[...]).astype(BF16)
    low[...] = lines[0:rows, :]
    lines[rows : rows + edges, :] = jnp.concatenate([rim0[...], rim1[...]], axis=0).astype(BF16)
    both = jnp.concatenate([normed[...], nhalo[0:edges, :]], axis=0)
    size = small0.shape[0]
    for i in range(folds):
        lanes = slice(i * width, (i + 1) * width)
        at = i * fold
        grads[at : at + width, :] = dot_rows(both, lines[:, lanes]).astype(BF16)
        at += width
        grads[at : at + 2 * size, :] = jnp.concatenate(
            [small0[:, lanes], small1[:, lanes]], axis=0
        ).astype(BF16)
        at += 2 * size
        grads[at : (i + 1) * fold, :] = jnp.zeros(((i + 1) * fold - at, width), BF16)
    rim = dot_cols(lines[rows : rows + edges, :], in_weight[:, 0:inner])
    even = (lax.axis_index("seq") & 1) == 0
    turned = jnp.concatenate([rim[CHUNKS:], rim[:CHUNKS]], axis=0)
    left, right = grads[0:fold, :], grads[fold : 2 * fold, :]
    kept[...] = jnp.where(even, left, right)
    sent[...] = jnp.where(even, right, left)
    at = width + 2 * size
    sent[at : at + edges, :] = jnp.where(even, turned, rim).astype(BF16)


def finish_kernel(
    io, low, dz, in_weight, rims, chip_rim, heights, widths, tokens, cotangent, valid, gain,
    input_grad,
):
    rows, width = tokens.shape
    inner = low.shape[1]
    even = (lax.axis_index("seq") & 1) == 0
    start = lax.axis_index("seq") * rows
    back = slot_order(rows)
    dn = dot_cols(dot(back, low[...]).astype(BF16), in_weight[:, 0:inner]) + dot_cols(
        dot(back, dz[...]).astype(BF16), in_weight[:, inner : 2 * inner]
    )
    io.ready()
    from_core = rims[...].astype(F32)[:CHUNKS]
    from_chip = chip_rim[...].astype(F32)[CHUNKS:]
    before = jnp.where(even, from_chip, from_core)
    after = jnp.where(even, from_core, from_chip)
    end = image_ends(heights, widths)[-1]
    row = lax.broadcasted_iota(jnp.int32, (CHUNKS, rows), 0)
    slot = lax.broadcasted_iota(jnp.int32, (CHUNKS, rows), 1)
    alive = jnp.broadcast_to(valid[...].astype(F32), (CHUNKS, rows))
    alive = jnp.where(start + slot < end, alive, 0.0)
    first = jnp.sum(jnp.where(slot == row, alive, 0.0), axis=1, keepdims=True)
    last = jnp.sum(jnp.where(slot == rows - CHUNKS + row, alive, 0.0), axis=1, keepdims=True)
    values = jnp.concatenate(
        [
            dn[0:CHUNKS, :] + first * before, dn[CHUNKS : rows - CHUNKS, :],
            dn[rows - CHUNKS : rows, :] + last * after,
        ],
        axis=0,
    )
    inputs = tokens[...].astype(F32)
    inv_rms = lax.rsqrt(jnp.mean(inputs * inputs, axis=-1, keepdims=True) + NORM_EPS)
    scaled = values * gain[...].astype(F32).reshape(1, width)
    mean = jnp.mean(scaled * inputs, axis=-1, keepdims=True)
    input_grad[...] = (
        cotangent[...].astype(F32) + inv_rms * scaled - inputs * (inv_rms * inv_rms * inv_rms) * mean
    )


def blocks_in_order(mine, other, into_first, into_second):
    size = mine.shape[1]
    is_even = (lax.axis_index("seq") & 1) == 0
    here = lax.axis_index("img")
    for k in range(mine.shape[0]):
        a, b = mine[here ^ k].astype(F32), other[here ^ k].astype(F32)
        into_first(k * size, jnp.where(is_even, a, b))
        into_second(k * size, jnp.where(is_even, b, a))


def weighted_rows(values, weights):
    total = None
    for at in range(0, values.shape[1], LANES):
        part = values[:, at : at + LANES] * weights[:, at : at + LANES].astype(F32)
        total = part if total is None else total + part
    return total


def first_unpack(io, mine, other, in_weight, parts, in_far, out_far, out_w, z_half, moves):
    width = out_w.shape[1]
    inner = out_w.shape[0]

    def put_out(at, values):
        out_w[at : at + values.shape[0], :] = values

    def put_z(at, values):
        size = values.shape[0]
        column = at // width * width
        z_half[at % width : at % width + size, column : column + width] = values

    blocks_in_order(mine, other, put_out, put_z)
    leaving = [
        fetch(out_w, out_far, moves.at[0]),
        fetch(z_half, in_far.at[:, inner : 2 * inner], moves.at[1]),
    ]
    parts[...] = weighted_rows(z_half[...], in_weight[:, inner : 2 * inner])
    for copy in leaving:
        copy.wait()


def second_unpack(
    io, mine, other, in_weight, parts, gain_in, in_before,
    conv_w, conv_b, xproj, dt_w, dt_b, a_log, skip, in_far, gain_far,
    left, right, x_half, gain, moves,
    *, count, state, rank, cols, taps,
):
    width = left.shape[1]
    inner = x_half.shape[1]

    def put(target, lane):
        def at_rows(at, values):
            size = values.shape[0]
            target[at : at + size, :] = values
            top = min(width - at, size)
            if top > 0:
                x_half[at : at + top, lane : lane + width] = values[:top]

        return at_rows

    blocks_in_order(mine, other, put(left, 0), put(right, width))
    leaving = fetch(x_half, in_far.at[:, 0:inner], moves.at[0])
    for i, half in enumerate((left, right)):
        lanes = slice(i * width, (i + 1) * width)
        for d in range(2):
            at = width + d * count
            xproj[d, :, lanes] = half[at : at + cols, :]
            at += cols
            dt_w[d, :, lanes] = half[at : at + rank, :]
            at += rank
            a_log[d, :, lanes] = half[at : at + state, :]
            dt_b[d : d + 1, lanes] = half[at + state : at + state + 1, :]
            skip[d : d + 1, lanes] = half[at + state + 1 : at + state + 2, :]
            at += state + 2
            conv_w[d, :, lanes] = half[at : at + taps, :]
            conv_b[d : d + 1, lanes] = half[at + taps : at + taps + 1, :]
    io.ready()
    io.done()
    total = parts[...] + weighted_rows(x_half[...], in_weight[:, 0:inner])
    high = total.astype(BF16)
    rest = (total - high.astype(F32)).astype(BF16)
    ones = jnp.ones((2 * CHUNKS, LANES), BF16)
    sums = (dot_cols(ones, high) + dot_cols(ones, rest))[0:1]
    gain[...] = (sums / gain_in[...].astype(F32).reshape(1, width)).reshape(width)
    last = fetch(gain, gain_far, moves.at[1])
    leaving.wait()
    last.wait()


IN_VMEM = pl.BlockSpec(memory_space=pltpu.VMEM)
IN_SMEM = pl.BlockSpec(memory_space=pltpu.SMEM)
FAR = pl.BlockSpec(memory_space=pltpu.HBM)


def shape(*dims, dtype=F32):
    return jax.ShapeDtypeStruct(dims, dtype)


def low(*dims):
    return jax.ShapeDtypeStruct(dims, BF16)


def near(*dims, dtype=F32):
    return pltpu.VMEM(dims, dtype)


def scratch(*dims, dtype=F32):
    return pltpu.VMEM(dims, dtype)


def like(*outs):
    return [pltpu.VMEM(out.shape, out.dtype) for out in outs]


def moves(*dims):
    return pltpu.SemaphoreType.DMA(dims)


class Moves:
    def __init__(self, arrive, leave):
        self.arrive, self.leave, self.left = arrive, leave, False
        for copy in arrive:
            copy.start()

    def ready(self):
        for copy in self.arrive:
            copy.wait()

    def done(self):
        self.left = True
        for copy in self.leave:
            copy.start()


def call(
    kernel, name, args, outs, scratches=(), far=(), far_outs=(), near_args=(), near_outs=(),
    scalars=(), handed=(), aliases=(), us=4, limit=4,
):
    small = tuple(scalars) + tuple(args)
    small, far = (
        tuple(pltpu.with_memory_space_constraint(x, pltpu.HBM) for x in arrays)
        for arrays in (small, far)
    )
    n_hand = len(handed)
    near_args = tuple(handed) + tuple(near_args)
    n_near, n_small, n_far = len(near_args), len(small), len(far)
    n_near_outs, n_outs, n_far_outs = len(near_outs), len(outs), len(far_outs)

    def wrapped(*refs):
        refs = list(refs)

        def take(count):
            taken = refs[:count]
            del refs[:count]
            return taken

        near_in, small_in, far_in = take(n_near), take(n_small), take(n_far)
        near_out, out, far_out = take(n_near_outs), take(n_outs), take(n_far_outs)
        take(n_hand)
        small_here, out_here = take(n_small), take(n_outs)
        in_moves, out_moves = take(2)
        io = Moves(
            [pltpu.make_async_copy(a, b, in_moves.at[i]) for i, (a, b) in enumerate(zip(small_in, small_here))],
            [pltpu.make_async_copy(a, b, out_moves.at[i]) for i, (a, b) in enumerate(zip(out_here, out))],
        )
        kernel(io, *near_in, *small_here, *far_in, *near_out, *out_here, *far_out, *refs)
        if not io.left:
            io.done()
        for copy in io.leave:
            copy.wait()

    return pl.pallas_call(
        wrapped,
        out_shape=list(near_outs) + [
            pltpu.HBM(out.shape, out.dtype) for out in tuple(outs) + tuple(far_outs)
        ] + [pltpu.VMEM(x.shape, x.dtype) for x in handed],
        in_specs=[IN_VMEM] * n_near + [FAR] * (n_small + n_far),
        out_specs=[IN_VMEM] * n_near_outs + [FAR] * (n_outs + n_far_outs) + [IN_VMEM] * n_hand,
        input_output_aliases={
            **{i: n_near_outs + n_outs + n_far_outs + i for i in range(n_hand)},
            **{n_near + n_small + i: n_near_outs + n_outs + o for i, o in aliases},
        },
        scratch_shapes=(
            [pltpu.SMEM(a.shape, a.dtype) for a in scalars] + like(*args) + like(*outs)
            + [moves(max(n_small, 1)), moves(max(n_outs, 1))] + list(scratches)
        ),
        compiler_params=pltpu.CompilerParams(vmem_limit_bytes=limit * 2**20),
        cost_estimate=pl.CostEstimate(flops=us * 2000000000, bytes_accessed=0, transcendentals=0),
        name=name,
    )(*near_args, *small, *far)


def call_edges(tokens, valid):
    edge = 2 * CHUNKS
    width = tokens.shape[1]
    outs = [near(edge, width, dtype=BF16), near(edge, width, dtype=BF16)]
    return call(edges_kernel, "edges", (tokens, valid), (), near_outs=outs, us=1, limit=2)


def call_front(
    heights, widths, valid, gain, tokens, cotangent, in_weight, out_weight, weights, reach,
):
    rows, width = tokens.shape
    inner = out_weight.shape[0]
    one = near(rows, inner)
    row = near(rows, width, dtype=BF16)
    return call(
        functools.partial(front_kernel, reach=reach, weights=len(weights)), "front", (valid, gain), (),
        [moves(len(weights))], weights, (),
        tuple(
            pltpu.with_memory_space_constraint(x, pltpu.VMEM)
            for x in (tokens, cotangent, in_weight, out_weight)
        ),
        [
            row, one, one, one, one, near(rows, LANES), near(2 * reach * rows, LANES), row,
            near(width, inner, dtype=BF16), near(2 * CHUNKS, LANES), near(CHUNKS, width),
        ] + like(*weights),
        (heights, widths), us=4, limit=12,
    )


def call_middle(handed, used, from_core, from_chip, arrays, reach, cols):
    x, a_log = arrays[0], arrays[-2]
    rows, inner = x.shape
    state, width = a_log.shape[1], from_core.shape[1]
    half = 2 * state
    both = near(2 * rows, inner)
    maps = near(half, CHUNKS, inner)
    ends = near(2 * CHUNKS, inner)
    n_hand = len(handed)

    def kernel(io, *refs):
        middle_kernel(io, *(refs[i] for i in used), *refs[n_hand:], reach=reach)

    return call(
        kernel, "middle", (), (),
        [
            scratch(2 * rows, inner, dtype=BF16), scratch(rows, half * LANES),
            scratch(state, CHUNKS, inner), scratch(state, CHUNKS, inner), scratch(CHUNKS, inner),
        ],
        near_args=(from_core, from_chip) + arrays,
        near_outs=[
            near(2 * half + CHUNKS + half, inner), near(2 * half + 2 * CHUNKS, inner, dtype=BF16),
            both, both, both, maps, maps, near(rows + 2 * reach * CHUNKS, inner),
            near(2 * rows, cols), ends, ends, near(half + CHUNKS, inner),
            near(4 * CHUNKS, width, dtype=BF16),
        ],
        handed=handed, us=20, limit=9,
    )


def call_join(got, summary, entered, state, bit, final):
    inner = summary.shape[1]
    half = 2 * state
    outs = [
        near(2 * half + CHUNKS, inner),
        near(half if final else 2 * half + 2 * CHUNKS, inner, dtype=BF16),
    ]
    if not final:
        outs = [near(2 * half + CHUNKS + half, inner)] + outs
    args = (got, summary) + (() if entered is None else (entered,))
    kernel = first_join if entered is None else join_kernel
    joined = call(
        functools.partial(kernel, state=state, bit=bit, final=final), "join", (), (),
        near_args=args, near_outs=outs, us=1, limit=4,
    )
    return joined if not final else [None] + list(joined)


def call_states(handed, used, before, tail, got, entered, zs, dgz, cotan, rank, reach, state, bit):
    rows, inner = zs.shape
    width = cotan.shape[1]
    half = 2 * state
    n_hand = len(handed)

    def kernel(io, *refs):
        states_kernel(
            io, *(refs[i] for i in used), *refs[n_hand:], reach=reach, rank=rank, state=state, bit=bit
        )

    grad = near(inner, width, dtype=BF16)
    one = near(rows, inner, dtype=BF16)
    held = near(inner // LANES, (rows // CHUNKS + 1) * state * CHUNKS, LANES)
    return call(
        kernel, "states", (), (),
        [scratch(rows, half * LANES), scratch(rows, inner)],
        near_args=(before, tail, got, entered, zs, dgz, cotan),
        near_outs=[grad, grad, near(2 * half, inner), one, held, held, one], handed=handed, us=12,
        limit=9,
    )


def adjoint_scratch(rows, inner, half, reach, small, cols, rank):
    return [
        scratch(rows, half * LANES), scratch(rows, half * LANES), scratch(rows, inner), scratch(rows, inner), scratch(small - cols - rank, inner),
        scratch(rows + reach * CHUNKS, inner),
    ]


def call_first_adjoint(handed, used, h, weights, small, reach, rank, state):
    rows, inner = handed[used[3]].shape
    cols = handed[used[6]].shape[1]
    n_hand = len(handed)

    def kernel(io, *refs):
        first_adjoint(
            io, *(refs[i] for i in used), *refs[n_hand:], d=0, reach=reach, rank=rank, state=state
        )

    return call(
        kernel, "adjoint_up", weights, (),
        adjoint_scratch(rows, inner, 2 * state, reach, small, cols, rank), near_outs=[
            near(CHUNKS, inner), near(small, inner), near(rows, inner),
        ], near_args=(h,), handed=handed, us=14, limit=13,
    )


def call_second_adjoint(handed, arrays, weights, in_weight, small, reach, rank, state):
    rows, inner = arrays[3].shape
    cols = arrays[6].shape[1]
    n_hand = len(handed)

    def kernel(io, *refs):
        second_adjoint(io, *refs[n_hand:], d=1, reach=reach, rank=rank, state=state)

    return call(
        kernel, "adjoint_down", weights, (),
        [moves(1)] + adjoint_scratch(rows, inner, 2 * state, reach, small, cols, rank),
        (in_weight,), (), arrays,
        [near(CHUNKS, inner), near(small, inner), near(rows, inner), near(*in_weight.shape, dtype=BF16)],
        handed=handed, us=14, limit=13,
    )


def call_last(handed, dx, rim0, rim1, small0, small1, normed, nhalo, live):
    rows, inner = dx.shape
    width = normed.shape[1]
    small = small0.shape[0]
    folds = inner // width
    edges = 2 * CHUNKS
    fold = -(-(width + 2 * small + edges) // 64) * 64
    n_hand = len(handed)

    def kernel(io, *refs):
        last_kernel(io, *refs[n_hand : n_hand + 8], refs[n_hand - 1], *refs[n_hand + 8 :])

    return call(
        kernel, "last", (), (),
        [
            scratch(rows + edges, inner, dtype=BF16), scratch(folds * fold, width, dtype=BF16),
        ],
        near_args=(dx, rim0, rim1, small0, small1, normed, nhalo, live),
        near_outs=[
            near(fold, width, dtype=BF16), near(fold, width, dtype=BF16),
            near(rows, inner, dtype=BF16),
        ],
        handed=handed, us=3, limit=8,
    )


def partner(axis, bit):
    return [(i, i ^ (1 << bit)) for i in range(lax.axis_size(axis))]


def bits_of(axis):
    return (lax.axis_size(axis) - 1).bit_length()


def other_core(values):
    return lax.ppermute(values, "seq", partner("seq", 0))


def next_chip(values):
    count = lax.axis_size("seq")
    pairs = [(i, i + 1) for i in range(1, count - 1, 2)]
    return lax.ppermute(values, "seq", pairs + [(j, i) for i, j in pairs])


def split_kernel(io, kept, got, own, *sent, edges):
    if edges:
        at = got.shape[0] - edges[1]
        sent[-1][...] = got[at : at + edges[0], :]
        sent = sent[:-1]
    count = len(sent) + 1
    rows = own.shape[0]
    here = lax.axis_index("img")
    for k in range(count):
        at = pl.ds(pl.multiple_of((here ^ k) * rows, rows), rows)
        total = kept[at, :].astype(F32) + got[at, :].astype(F32)
        if k == 0:
            own[...] = total
        else:
            sent[k - 1][...] = total.astype(BF16)


def add_kernel(io, *refs, outs):
    total = refs[0][...].astype(F32)
    for ref in refs[1 : len(refs) - outs]:
        total = total + ref[...].astype(F32)
    for ref in refs[len(refs) - outs :]:
        ref[...] = total.astype(ref.dtype)


def add(values, whole=True):
    rows, width = values[0].shape
    outs = [near(rows, width)] * whole + [near(rows, width, dtype=BF16)]
    sums = call(
        functools.partial(add_kernel, outs=len(outs)), "add", (), (), near_args=values,
        near_outs=outs, us=1, limit=2,
    )
    return sums if whole else sums[0]


def add_rim_kernel(io, *refs, count, bit):
    values, moving, stay = refs[:count], refs[count], refs[count + 1]
    low_out, stay_out = refs[-2:]
    rows = values[0].shape[0]
    total = values[0][...]
    for ref in values[1:]:
        total = total + ref[0:rows, :].astype(F32)
    if len(refs) > count + 4:
        refs[-3][...] = total
    low_out[0:rows, :] = total.astype(BF16)
    if bit is None:
        low_out[rows:, :] = moving[...]
        stay_out[...] = jnp.zeros_like(stay_out)
        return
    came = values[-1][rows:, :]
    if low_out.shape[0] > rows:
        low_out[rows:, :] = came
    position = lax.axis_index("seq")
    chip = position >> 1
    chip = jnp.where((position & 1) == 0, chip, lax.axis_size("seq") // 2 - 1 - chip)
    lowest = chip & ((2 << bit) - 1)
    stay_out[...] = jnp.where(lowest == (1 << bit), came, stay[...])


def add_rim(values, moving, stay, bit, final=False):
    rows, width = values[0].shape
    edge = moving.shape[0]
    sent = rows if final else rows + edge
    outs = [near(rows, width)] * (not final)
    outs += [near(sent, width, dtype=BF16), near(edge, width, dtype=BF16)]
    sums = call(
        functools.partial(add_rim_kernel, count=len(values), bit=bit), "add", (), (),
        near_args=tuple(values) + (moving, stay), near_outs=outs, us=1, limit=2,
    )
    return [None] * final + list(sums)


def stack_kernel(io, *refs):
    for k, ref in enumerate(refs[:-1]):
        refs[-1][k] = ref[...]


def plane_pairs(k):
    return [(i, i ^ k) for i in range(lax.axis_size("img"))]


def chips_sum(kept, sent, edges=()):
    count = lax.axis_size("img")
    rows, width = kept.shape
    block = (rows // count, width)
    got = other_core(sent)
    own, *parts = call(
        functools.partial(split_kernel, edges=edges), "split", (), (), near_args=(kept, got),
        near_outs=[near(*block)] + [near(*block, dtype=BF16)] * (count - 1)
        + [near(rim_rows, width, dtype=BF16) for rim_rows in edges[:1]],
        us=1, limit=2,
    )
    rim = parts.pop() if edges else None
    blocks = [own] + [
        lax.ppermute(part, "img", plane_pairs(k + 1)) for k, part in enumerate(parts)
    ]
    return blocks, rim


def line_steps(total, low):
    bits = bits_of("seq")
    for bit in range(1, bits):
        got = lax.ppermute(low, "seq", partner("seq", bit))
        if bit < bits - 1:
            total, low = add([total, got])
        else:
            low = add([total, got], whole=False)
    return low


def line_steps_with_rims(blocks, rim, first_low, beside):
    stay = rim
    total, low, stay = add_rim(blocks, rim, stay, None)
    low, first_low = tied(low, first_low)
    bits = bits_of("seq")
    for bit in range(1, bits):
        got = lax.ppermute(low, "seq", partner("seq", bit))
        if bit == 1:
            first_blocks = plane_blocks(first_low)
        if bit == bits - 1:
            got, beside, *first_blocks = lax.optimization_barrier((got, beside, *first_blocks))
        total, low, stay = add_rim([total, got], rim, stay, bit - 1, bit == bits - 1)
    return low, stay, first_blocks, beside


def plane_blocks(low):
    count = lax.axis_size("img")
    return [low] + [lax.ppermute(low, "img", plane_pairs(k)) for k in range(1, count)]


def stacked(blocks):
    low, count = blocks[0], len(blocks)
    return call(
        stack_kernel, "stack", (), (), near_args=blocks,
        near_outs=[near(count, *low.shape, dtype=BF16)], us=1, limit=2,
    )[0]


def tied(first, second):
    return lax.optimization_barrier((first, second))


def body(
    tokens, cotangent, heights, widths, valid, norm_gain, in_weight, conv_weight, conv_bias,
    xproj_weight, dt_weight, dt_bias, a_log, skip, out_weight,
):
    rows, width = tokens.shape[1:]
    inner = out_weight.shape[0]
    state = a_log.shape[1]
    rank = dt_weight.shape[1]
    cols = xproj_weight.shape[2]
    taps = conv_weight.shape[1]
    reach = taps - 1
    count = bits_of("seq")
    tokens, cotangent = tokens[0], cotangent[0]
    xproj = xproj_weight.transpose(0, 2, 1)

    to_core, to_chip = call_edges(tokens, valid)
    from_core, from_chip = other_core(to_core), next_chip(to_chip)
    weights = (conv_weight, conv_bias, xproj, dt_weight, dt_bias, a_log, skip)
    normed, x, zs, dgz, dy, live, same, cotan, in_x, halo_live, gains, *near_weights = call_front(
        heights, widths, valid, norm_gain, tokens, cotangent, in_weight, out_weight, weights, reach
    )
    (
        summary, sent, delta, s, dsilu, tail, head, xext, proj, before, after, rate, nhalo,
        dy, live, same, normed, zs, dgz, cotan,
    ) = call_middle(
        (dy, live, same, normed, zs, dgz, cotan), (0, 1, 2), from_core, from_chip,
        (x, in_x, halo_live, gains) + tuple(near_weights), reach, cols,
    )
    entered = None
    for bit in range(count - 1):
        got = lax.ppermute(sent, "seq", partner("seq", bit))
        summary, entered, sent = call_join(got, summary, entered, state, bit, bit == count - 2)
    got = lax.ppermute(sent, "seq", partner("seq", count - 1))
    handed = (
        delta, s, dsilu, dy, head, xext, proj, after, rate, same, live, normed, nhalo,
    )
    kept, sent, carry, dz, h0, h1, gated, *handed = call_states(
        handed, (0, 1, 6, 8, 9, 11), before, tail, got, entered, zs, dgz, cotan, rank, reach, state,
        count - 1,
    )

    blocks, _ = chips_sum(kept, sent)
    small = -(-(cols + rank + state + 2 + taps + 1) // CHUNKS) * CHUNKS
    weights = (dt_weight, xproj, conv_weight)
    handed = tuple(handed[:10]) + (carry,) + tuple(handed[10:]) + (dz, gated, h1)
    rim0, small0, dx, *handed = call_first_adjoint(
        handed, tuple(range(11)), h0, weights, small, reach, rank, state
    )
    *blocks, dx = lax.optimization_barrier((*blocks, dx))
    first_sum, first_low = add(blocks)
    first_sum, first_low, dx = lax.optimization_barrier((first_sum, first_low, dx))
    arrays, passed, h1 = tuple(handed[:11]), tuple(handed[11:-1]), handed[-1]
    if bits_of("seq") > 3:
        first_low = line_steps(first_sum, first_low)
    else:
        devices = lax.axis_size("seq")
        blocks = [first_sum] + [
            lax.ppermute(first_low, "seq", [(i, i ^ k) for i in range(devices)])
            for k in range(2, devices, 2)
        ]
    rim1, small1, dx, in_near, *passed = call_second_adjoint(
        passed, arrays + (h1, dx), weights, in_weight, small, reach, rank, state
    )
    live, normed, nhalo, dz, gated = passed
    if bits_of("seq") <= 3:
        *blocks, dx = lax.optimization_barrier((*blocks, dx))
        first_low = add(blocks, whole=False)
    kept, sent, dx_low, dz, gated, in_near = call_last(
        (dz, gated, in_near), dx, rim0, rim1, small0, small1, normed, nhalo, live
    )

    edges = (2 * CHUNKS, kept.shape[0] - width - 2 * small)
    blocks, rim = chips_sum(kept, sent, edges)


    output = call(
        output_kernel, "output", (tokens, out_weight), [low(rows, width)], near_args=(gated,), us=2,
        limit=6,
    )[0]
    second_low, chip_rim, first_blocks, output = line_steps_with_rims(blocks, rim, first_low, output)
    blocks = plane_blocks(second_low)
    _, *first_blocks = lax.optimization_barrier((blocks[1], *first_blocks))
    first_mine = stacked(first_blocks)
    first_other = other_core(first_mine)
    input_grad = call(
        finish_kernel, "finish", (tokens, cotangent, valid, norm_gain), [shape(rows, width)],
        near_args=(dx_low, dz, in_near, rim, chip_rim), scalars=(heights, widths), us=3, limit=8,
    )[0]
    blocks, input_grad = lax.optimization_barrier((blocks, input_grad))
    second_mine = stacked(blocks)
    second_other = other_core(second_mine)
    parts, in_total, out_total = call(
        first_unpack, "unpack_first", (), (),
        [scratch(inner, width), scratch(width, inner), moves(2)],
        far_outs=[shape(width, 2 * inner), shape(inner, width)],
        near_args=(first_mine, first_other, in_near), near_outs=[near(width, LANES)], us=2, limit=8,
    )
    second_other, parts = tied(second_other, parts)
    fold = kept.shape[0]
    (
        conv_total, bias_total, xproj_total, dtw_total, dtb_total, a_total, skip_total, in_total,
        gain_total,
    ) = call(
        functools.partial(
            second_unpack, count=small, state=state, rank=rank, cols=cols, taps=taps
        ),
        "unpack_second", (norm_gain,),
        [
            shape(2, taps, inner), shape(2, inner), shape(2, cols, inner), shape(2, rank, inner),
            shape(2, inner), shape(2, state, inner), shape(2, inner),
        ],
        [
            scratch(fold, width), scratch(fold, width), scratch(width, inner), scratch(width),
            moves(2),
        ],
        (in_total,), [shape(width, 2 * inner), shape(width)], (second_mine, second_other, in_near, parts),
        aliases=((0, 0),), us=2, limit=10,
    )
    return (
        output[None], input_grad[None], gain_total, in_total, conv_total, bias_total,
        xproj_total.transpose(0, 2, 1), dtw_total, dtb_total, a_total, skip_total, out_total,
    )


def solution(mesh):
    split = P("img", "seq", None)
    placed = (split, split, P("img", None), P("img", None), P("img", "seq")) + (P(),) * 10
    return jax.shard_map(
        body,
        mesh=mesh,
        in_specs=placed,
        out_specs=(split, split) + (P(),) * 10,
        check_vma=False,
    )
```

```python
import functools

import jax
import jax.numpy as jnp
from jax import lax
from jax.experimental import pallas as pl
from jax.experimental.pallas import tpu as pltpu
from jax.sharding import PartitionSpec as P

NORM_EPS = 1e-05
CONTRACT_ROWS = (((0,), (0,)), ((), ()))
CONTRACT_COLS = (((1,), (1,)), ((), ()))
LOG2E = 1.4426950408889634
LN2 = 0.6931471805599453
BREAK = 1e30
CHUNKS = 8
LANES = 128
SUMMARY_STATES = 8
SUMMARY_UNROLL = 16
STATES_UNROLL = 32
ADJOINT_STATES = 8
ADJOINT_UNROLL = 16
F32 = jnp.float32
BF16 = jnp.bfloat16


def dot(a, b):
    return jnp.dot(a, b, preferred_element_type=F32)


def dot_rows(a, b):
    return lax.dot_general(a, b, CONTRACT_ROWS, preferred_element_type=F32)


def dot_cols(a, b):
    return lax.dot_general(a, b, CONTRACT_COLS, preferred_element_type=F32)


def sigmoid(v):
    return 1.0 / (1.0 + jnp.exp(-v))


def fetch(source, target, semaphore):
    copy = pltpu.make_async_copy(source, target, semaphore)
    copy.start()
    return copy


def lanes_of(tile):
    return pl.ds(pl.multiple_of(tile * LANES, LANES), LANES)


def rows_of(j, count=CHUNKS):
    return pl.ds(pl.multiple_of(j * CHUNKS, CHUNKS), count)


def chunk_order(rows):
    row = lax.broadcasted_iota(jnp.int32, (rows, rows), 0)
    slot = lax.broadcasted_iota(jnp.int32, (rows, rows), 1)
    return slot == (row & (CHUNKS - 1)) * (rows // CHUNKS) + (row >> 3)


def image_ends(heights, widths):
    ends, total = [], 0
    for i in range(heights.shape[1]):
        total = total + heights[0, i] * widths[0, i]
        ends.append(total)
    return ends


def segment_of(places, ends):
    found = jnp.zeros_like(places)
    for end in ends:
        found = found + (places >= end).astype(jnp.int32)
    return found


def places_of(first, rows):
    row = lax.broadcasted_iota(jnp.int32, (rows, LANES), 0)
    return first + (row & (CHUNKS - 1)) * (rows // CHUNKS) + (row >> 3)


def edges_kernel(io, tokens, valid, to_core, to_chip):
    rows = tokens.shape[0]
    edge = to_core.shape[0]
    io.ready()
    row = lax.broadcasted_iota(jnp.int32, (edge, rows), 0)
    slot = lax.broadcasted_iota(jnp.int32, (edge, rows), 1)
    held = jnp.broadcast_to(valid[...].astype(F32), (edge, rows))
    first = jnp.where(slot == row, held, 0.0).astype(BF16)
    last = jnp.where(slot == rows - edge + row, held, 0.0).astype(BF16)
    first = dot(first, tokens[...]).astype(BF16)
    last = dot(last, tokens[...]).astype(BF16)
    even = (lax.axis_index("seq") & 1) == 0
    to_core[...] = jnp.where(even, last, first)
    to_chip[...] = jnp.where(even, first, last)


def spread(values, target):
    count = values.shape[1]
    high = values.astype(BF16)
    low = (values - high.astype(F32)).astype(BF16)
    both = jnp.concatenate([high, low], axis=1)
    row = lax.broadcasted_iota(jnp.int32, (2 * count, LANES), 0)
    row = jnp.where(row < count, row, row - count)
    for at in range(0, count, 2):
        pick = jnp.concatenate([(row == at).astype(BF16), (row == at + 1).astype(BF16)], axis=1)
        target[:, at * LANES : (at + 2) * LANES] = dot(both, pick)


def windows(span, up, sublane):
    sign = 1 if up else -1

    def from_before(value, by, fill):
        moved = pltpu.roll(value, (sign * by) % CHUNKS, axis=0)
        kept = sublane >= by if up else sublane < CHUNKS - by
        return jnp.where(kept, moved, fill)

    two = span + from_before(span, 1, 0.0)
    four = two + from_before(two, 2, 0.0)
    eight = four + from_before(four, 4, 0.0)
    edge = [jnp.where(sublane >= by if up else sublane < CHUNKS - by, 0.0, BREAK) for by in (1, 2, 4)]
    return (span + edge[0], two + edge[1], four + edge[2]), from_before(eight, 1, 0.0)


def chain(rate, sums, tail, up, sublane):
    sign = 1 if up else -1
    for by, span in zip((1, 2, 4), sums):
        tail = jnp.exp2(rate * span) * pltpu.roll(tail, (sign * by) % CHUNKS, axis=0) + tail
    end = CHUNKS - 1 if up else 0
    kept = sublane >= 1 if up else sublane < CHUNKS - 1
    return jnp.where(kept, pltpu.roll(tail, sign % CHUNKS, axis=0), 0.0), tail[end : end + 1]


def front_kernel(
    io, tokens, cotangent, in_weight, out_weight, heights, widths, valid, gain, *refs, reach, weights,
):
    (
        normed_out, x_out, zs_out, dgz_out, dy, live, same_out, cotan, in_x, halo_live, gains_out,
    ) = refs[weights : weights + 11]
    near_weights = refs[weights + 11 : 2 * weights + 11]
    ins = refs[2 * weights + 11]
    rows, width = tokens.shape
    inner = out_weight.shape[0]
    tiles = inner // LANES
    arriving = [
        fetch(source, target, ins.at[i])
        for i, (source, target) in enumerate(zip(refs[:weights], near_weights))
    ]
    order = chunk_order(rows)
    order_low = order.astype(BF16)
    inputs = dot(order_low, tokens[...])
    inv_rms = lax.rsqrt(jnp.mean(inputs * inputs, axis=-1, keepdims=True) + NORM_EPS)
    cotan[...] = dot(order_low, cotangent[...]).astype(BF16)
    step = 2 * LANES
    for at in range(0, inner, step):
        lanes = slice(at, at + step)
        dgz_out[:, lanes] = dot_cols(cotan[...], out_weight[lanes, :])
    in_x[...] = in_weight[:, 0:inner]

    io.ready()
    start = lax.axis_index("seq") * rows
    slots = lax.axis_size("seq") * rows
    ends = image_ends(heights, widths)
    images = heights.shape[1]
    picked = jnp.where(order, jnp.broadcast_to(valid[...].astype(F32), order.shape), 0.0)
    alive = dot(picked.astype(BF16), jnp.ones((rows, LANES), BF16))
    places = places_of(start, rows)
    segment = segment_of(places, ends)
    live[...] = jnp.where(segment < images, alive, 0.0)
    for k in range(1, reach + 1):
        same = (segment_of(places - k, ends) == segment) & (places >= k)
        same_out[(k - 1) * rows : k * rows, :] = same.astype(F32)
        same = (segment_of(places + k, ends) == segment) & (places + k < slots)
        same_out[(reach + k - 1) * rows : (reach + k) * rows, :] = same.astype(F32)
    near_row = lax.broadcasted_iota(jnp.int32, (2 * CHUNKS, LANES), 0)
    near_place = jnp.where(
        near_row < CHUNKS, start - CHUNKS + near_row, start + rows + near_row - CHUNKS
    )
    halo_live[...] = (segment_of(near_place, ends) < images).astype(F32)

    gains = gain[...].astype(F32).reshape(1, width)
    gains_out[...] = jnp.broadcast_to(gains, gains_out.shape)
    scaled = inputs * inv_rms * gains
    normed = scaled.astype(BF16)
    normed_out[...] = normed
    live_wide = jnp.concatenate([live[...]] * (width // LANES), axis=1)
    normed_live = (scaled * live_wide).astype(BF16)
    for at in range(0, inner, step):
        lanes = slice(at, at + step)
        x_out[:, lanes] = dot(normed_live, in_x[:, lanes]).astype(BF16).astype(F32)
        zs_out[:, lanes] = dot(normed, in_weight[:, inner + at : inner + at + step])
    block = 32

    def gate_block(b, _):
        here = pl.ds(pl.multiple_of(b * block, block), block)
        alive = live[here, :]
        for tile in range(tiles):
            lanes = slice(tile * LANES, (tile + 1) * LANES)
            z = zs_out[here, lanes]
            grad = dgz_out[here, lanes] * alive
            gate = sigmoid(z)
            zs = z * gate * alive
            zs_out[here, lanes] = zs
            dy[here, lanes] = 0.5 * grad * zs
            dgz_out[here, lanes] = grad * (gate * (1.0 + z * (1.0 - gate)))
        return 0

    lax.fori_loop(0, rows // block, gate_block, 0, unroll=8)
    for copy in arriving:
        copy.wait()


def middle_kernel(
    io, dy, live, same_out, from_core, from_chip, x, in_x, halo_live, gains, conv_weight, conv_bias,
    xproj, dt_weight, dt_bias, a_log, skip,
    sum_out, sent_out, delta_out, s_out, dsilu_out, tail_out, head_out, xext_out, proj_out,
    before_out, after_out, rate_out, nhalo_out,
    low_out, bc, tails, heads, spans,
    *, reach,
):
    rows, inner = x.shape
    width = in_x.shape[0]
    steps = rows // CHUNKS
    state = a_log.shape[1]
    rank = dt_weight.shape[1]
    tiles = inner // LANES
    even = (lax.axis_index("seq") & 1) == 0
    sublane = lax.broadcasted_iota(jnp.int32, (CHUNKS, LANES), 0)
    wide = lax.broadcasted_iota(jnp.int32, (CHUNKS, inner), 0)
    xext_out[reach * CHUNKS : (reach + steps) * CHUNKS, :] = x[...]

    core, chip = from_core[...].astype(F32), from_chip[...].astype(F32)
    before = jnp.where(even, chip, core)
    after = jnp.where(even, core, chip)
    htok = jnp.concatenate([before[CHUNKS:], after[:CHUNKS]], axis=0)
    htok = htok * jnp.concatenate([halo_live[...]] * (width // LANES), axis=1)
    hinv = lax.rsqrt(jnp.mean(htok * htok, axis=-1, keepdims=True) + NORM_EPS)
    scaled = htok * hinv
    nhalo = (scaled * gains[0:1, :]).astype(BF16)
    nhalo_out[...] = jnp.concatenate([nhalo, scaled.astype(BF16)], axis=0)
    hx = dot(nhalo, in_x[...]).astype(BF16).astype(F32)
    for i in range(reach):
        to = steps - reach + i
        moved = pltpu.roll(x[to * CHUNKS : (to + 1) * CHUNKS, :], 1, axis=0)
        of = CHUNKS - reach + i
        xext_out[i * CHUNKS : (i + 1) * CHUNKS, :] = jnp.where(wide == 0, hx[of : of + 1], moved)
        moved = pltpu.roll(x[i * CHUNKS : (i + 1) * CHUNKS, :], CHUNKS - 1, axis=0)
        to = reach + steps + i
        of = CHUNKS + i
        xext_out[to * CHUNKS : (to + 1) * CHUNKS, :] = jnp.where(
            wide == CHUNKS - 1, hx[of : of + 1], moved
        )

    block = 64
    step = 2 * LANES
    taps = reach + 1
    conv_w = [conv_weight[d].astype(F32) for d in range(2)]
    conv_b = conv_bias[...].astype(F32)
    for tile in range(tiles):
        lanes = slice(tile * LANES, (tile + 1) * LANES)

        def conv_block(b, _, lanes=lanes):
            at = pl.multiple_of(b * block, block)
            for d in range(2):
                total = conv_b[d : d + 1, lanes] + conv_w[d][reach:taps, lanes] * (
                    xext_out[pl.ds(at + reach * CHUNKS, block), lanes]
                )
                for k in range(1, taps):
                    move = reach - k if d == 0 else reach + k
                    mask = same_out[pl.ds((d * reach + k - 1) * rows + at, block), :]
                    total = total + conv_w[d][reach - k : taps - k, lanes] * (
                        xext_out[pl.ds(at + move * CHUNKS, block), lanes] * mask
                    )
                gate = sigmoid(total)
                value = total * gate
                s_out[pl.ds(d * rows + at, block), lanes] = value
                low_out[pl.ds(d * rows + at, block), lanes] = value.astype(BF16)
                dsilu_out[pl.ds(d * rows + at, block), lanes] = gate * (1.0 + total * (1.0 - gate))
            return 0

        lax.fori_loop(0, rows // block, conv_block, 0, unroll=4)

    dt_b = dt_bias[...].astype(F32)
    for d in range(2):
        rate_out[d * state : (d + 1) * state, :] = jnp.minimum(
            -LOG2E * jnp.exp(a_log[d].astype(F32)), -1e-20
        )
        here = slice(d * rows, (d + 1) * rows)
        proj = dot_cols(low_out[here, :], xproj[d])
        proj_out[here, :] = proj
        dt_low = proj[:, :rank].astype(BF16)
        for at in range(0, inner, step):
            lanes = slice(at, at + step)
            delta_out[here, lanes] = dot(dt_low, dt_weight[d, :, lanes])
        spread(proj[:, rank:], bc)

        def delta_block(b, _, d=d):
            alive = live[pl.ds(pl.multiple_of(b * block, block), block), :]
            here = pl.ds(pl.multiple_of(d * rows + b * block, block), block)
            for tile in range(tiles):
                lanes = slice(tile * LANES, (tile + 1) * LANES)
                pre = delta_out[here, lanes] + dt_b[d : d + 1, lanes]
                small = jnp.exp(-jnp.abs(pre))
                log1p = jnp.where(small < 1e-4, small * (1.0 - 0.5 * small), jnp.log(1.0 + small))
                delta_out[here, lanes] = (jnp.maximum(pre, 0.0) + log1p) * alive
            return 0

        lax.fori_loop(0, rows // block, delta_block, 0, unroll=4)
        some = SUMMARY_STATES

        def scan_tile(tile, _, d=d):
            lanes = lanes_of(tile)
            for low in range(0, state, some):
                rates = [
                    jnp.broadcast_to(
                        rate_out[d * state + low + m : d * state + low + m + 1, lanes],
                        (CHUNKS, LANES),
                    )
                    for m in range(some)
                ]

                def scan_step(i, carried, d=d, low=low, rates=rates):
                    tail, lead, head, span = carried
                    j = i if d == 0 else steps - 1 - i
                    at = pl.multiple_of(j * CHUNKS, CHUNKS)
                    keep = same_out[pl.ds(d * reach * rows + at, CHUNKS), :]
                    delta = delta_out[pl.ds(d * rows + at, CHUNKS), lanes]
                    drive = delta * s_out[pl.ds(d * rows + at, CHUNKS), lanes]
                    back = dy[pl.ds(at, CHUNKS), lanes]
                    delta = jnp.maximum(delta, BREAK - keep * BREAK)
                    tail, lead, head = list(tail), list(lead), list(head)
                    for m in range(some):
                        b = bc[pl.ds(at, CHUNKS), (low + m) * LANES : (low + m + 1) * LANES]
                        n = state + low + m
                        c = bc[pl.ds(at, CHUNKS), n * LANES : (n + 1) * LANES]
                        decay = jnp.exp2(delta * rates[m])
                        tail[m] = decay * tail[m] + b * drive
                        lead[m] = lead[m] * decay
                        head[m] = head[m] + lead[m] * (c * back)
                    return tuple(tail), tuple(lead), tuple(head), span + delta

                zeros = tuple(jnp.zeros((CHUNKS, LANES), F32) for _ in range(some))
                ones = tuple(jnp.ones((CHUNKS, LANES), F32) for _ in range(some))
                tail, lead, head, span = lax.fori_loop(
                    0, steps, scan_step, (zeros, ones, zeros, zeros[0]), unroll=SUMMARY_UNROLL
                )
                for m in range(some):
                    tails[low + m, :, lanes] = tail[m]
                    heads[low + m, :, lanes] = head[m]
                spans[:, lanes] = span
            return 0

        lax.fori_loop(0, tiles, scan_tile, 0)

        tail_row = 0 if d == 0 else 2 * state
        head_row = 3 * state if d == 0 else state

        def chain_tile(tile, _, d=d, tail_row=tail_row, head_row=head_row):
            lanes = lanes_of(tile)
            span = spans[:, lanes]
            sums, before = windows(span, d == 0, sublane)
            sums_back, after = windows(span, d == 1, sublane)
            before_out[d * CHUNKS : (d + 1) * CHUNKS, lanes] = before
            after_out[d * CHUNKS : (d + 1) * CHUNKS, lanes] = after
            for n in range(state):
                rate = jnp.broadcast_to(
                    rate_out[d * state + n : d * state + n + 1, lanes], (CHUNKS, LANES)
                )
                carried, total = chain(rate, sums, tails[n, :, lanes], d == 0, sublane)
                tail_out[d * state + n, :, lanes] = carried
                sum_out[tail_row + n : tail_row + n + 1, lanes] = total
                carried, total = chain(rate, sums_back, heads[n, :, lanes], d == 1, sublane)
                head_out[d * state + n, :, lanes] = carried
                sum_out[head_row + n : head_row + n + 1, lanes] = total
            return 0

        lax.fori_loop(0, tiles, chain_tile, 0)
        sum_out[4 * state + d : 4 * state + d + 1, :] = jnp.sum(spans[...], axis=0, keepdims=True)
    at = 4 * state + CHUNKS
    sum_out[4 * state + 2 : at, :] = jnp.zeros((CHUNKS - 2, inner), F32)
    sum_out[at:, :] = rate_out[0 : 2 * state, :]
    sent_out[...] = packed(sum_out[0:at, :], state)
    rate_out[2 * state : 2 * state + 2, :] = skip[...].astype(F32)


def packed(summary, state):
    rest = summary[4 * state :]
    high = rest.astype(BF16).astype(F32)
    return jnp.concatenate([summary[: 4 * state], high, rest - high], axis=0).astype(BF16)


def leads(rate, spans, state, flip):
    parts = [jnp.exp2(rate[d * state : (d + 1) * state] * spans[d : d + 1]) for d in range(2)]
    return jnp.concatenate(parts[::-1] if flip else parts, axis=0)


def join_kernel(io, got, summary, entered, *outs, state, bit, final):
    half = 2 * state
    upper = ((lax.axis_index("seq") >> bit) & 1) == 1
    mine = summary[0 : 2 * half + CHUNKS, :]
    rates = summary[2 * half + CHUNKS :, :]
    entered_out, sent_out = outs[-2], outs[-1]
    values = got[...].astype(F32)
    spans = mine[4 * state : 4 * state + 2]
    other = values[4 * state : 4 * state + 2] + values[4 * state + CHUNKS : 4 * state + CHUNKS + 2]
    if entered is None:
        entered_up = jnp.where(upper, values[:half], 0.0)
        entered_down = jnp.where(upper, 0.0, values[half : 2 * half])
        span_up = jnp.where(upper, other, 0.0)
        span_down = jnp.where(upper, 0.0, other)
    else:
        held = entered[...]
        span_up, span_down = held[2 * half : 2 * half + 2], held[2 * half + 2 : 2 * half + 4]
        entered_up = held[:half] + jnp.where(
            upper, leads(rates, span_up, state, False) * values[:half], 0.0
        )
        entered_down = held[half : 2 * half] + jnp.where(
            upper, 0.0, leads(rates, span_down, state, True) * values[half : 2 * half]
        )
        span_up = span_up + jnp.where(upper, other, 0.0)
        span_down = span_down + jnp.where(upper, 0.0, other)
    entered_out[0:half, :] = entered_up
    entered_out[half : 2 * half, :] = entered_down
    entered_out[2 * half :, :] = jnp.concatenate(
        [span_up, span_down, jnp.zeros((CHUNKS - 4, mine.shape[1]), F32)], axis=0
    )
    low_up = jnp.where(upper, values[:half], mine[:half])
    high_up = jnp.where(upper, mine[:half], values[:half])
    low_down = jnp.where(upper, values[half : 2 * half], mine[half : 2 * half])
    high_down = jnp.where(upper, mine[half : 2 * half], values[half : 2 * half])
    low_span, high_span = jnp.where(upper, other, spans), jnp.where(upper, spans, other)
    up = leads(rates, high_span, state, False) * low_up + high_up
    down = leads(rates, low_span, state, True) * high_down + low_down
    if final:
        next_upper = ((lax.axis_index("seq") >> (bit + 1)) & 1) == 1
        sent_out[...] = jnp.where(next_upper, down, up).astype(BF16)
    else:
        total = jnp.concatenate(
            [up, down, spans + other, jnp.zeros((CHUNKS - 2, mine.shape[1]), F32)], axis=0
        )
        outs[0][0 : 2 * half + CHUNKS, :] = total
        outs[0][2 * half + CHUNKS :, :] = rates
        sent_out[...] = packed(total, state)


def first_join(io, got, summary, *outs, state, bit, final):
    join_kernel(io, got, summary, None, *outs, state=state, bit=bit, final=final)


def state_block(j, state):
    return pl.multiple_of(j * state * CHUNKS, CHUNKS)


def states_pass(d, steps, state, rates, begin, delta, s, keep, bc, h_out, y):
    start = state_block(0 if d == 0 else steps, state)
    for n in range(state):
        h_out[pl.ds(start + n * CHUNKS, CHUNKS), :] = begin[n]

    def step(i, h):
        j = i if d == 0 else steps - 1 - i
        here = pl.ds(pl.multiple_of(j * CHUNKS, CHUNKS), CHUNKS)
        to = state_block(j + 1 if d == 0 else j, state)
        size = delta[here, :]
        drive = size * s[here, :]
        size = jnp.maximum(size, BREAK - keep[here, :] * BREAK)
        h = list(h)
        parts = [None if d == 0 else y[here, :], None]
        for n in range(state):
            b = bc[here, n * LANES : (n + 1) * LANES]
            c = bc[here, (state + n) * LANES : (state + n + 1) * LANES]
            h[n] = jnp.exp2(size * rates[n]) * h[n] + b * drive
            h_out[pl.ds(to + n * CHUNKS, CHUNKS), :] = h[n]
            part = parts[n % 2]
            parts[n % 2] = c * h[n] if part is None else part + c * h[n]
        y[here, :] = parts[0] + parts[1]
        return tuple(h)

    lax.fori_loop(0, steps, step, tuple(begin), unroll=STATES_UNROLL)


def adjoint_pass(
    d, steps, state, rates, back, delta, s, dy, keep, skip, bc, h_in, sums,
    dpre_out, ds_out, rows_out,
):
    some = ADJOINT_STATES
    edge = steps - 1
    skip = skip[...]
    zeros = jnp.zeros((CHUNKS, LANES), F32)
    grads = []
    for low in range(0, state, some):
        final = low + some == state

        def step(i, carried, low=low, final=final):
            g, acc, h, skip_acc, bias_acc = carried
            j = edge - i if d == 0 else i
            here = pl.ds(pl.multiple_of(j * CHUNKS, CHUNKS), CHUNKS)
            size = delta[here, :]
            value = s[here, :]
            grad = dy[here, :]
            drive = size * value
            masked = jnp.maximum(size, BREAK - keep[here, :] * BREAK)
            prev = state_block(j if d == 0 else j + 1, state)
            g, acc, h = list(g), list(acc), list(h)
            weighted = zeros if low == 0 else ds_out[here, :]
            rate_sum = zeros if low == 0 else dpre_out[here, :]
            for m in range(some):
                n = low + m
                b = bc[here, n * LANES : (n + 1) * LANES]
                c = bc[here, (state + n) * LANES : (state + n + 1) * LANES]
                adjoint = c * grad + g[m]
                before = h_in[pl.ds(prev + n * CHUNKS, CHUNKS), :]
                sums[here, n * LANES : (n + 1) * LANES] += adjoint * drive
                sums[here, (state + n) * LANES : (state + n + 1) * LANES] += grad * h[m]
                g[m] = adjoint * jnp.exp2(masked * rates[n])
                held = g[m] * before
                weighted = weighted + adjoint * b
                rate_sum = rate_sum + held * rates[n]
                acc[m] = acc[m] + held * masked
                h[m] = before
            if final:
                ds_out[here, :] = skip * grad + size * weighted
                gate = jnp.where(
                    size < 0.01, size * (1.0 - size * (0.5 - size * (1.0 / 6.0))), 1.0 - jnp.exp(-size)
                )
                pre = ((LN2 * rate_sum + weighted * value) * gate).astype(BF16).astype(F32)
                dpre_out[here, :] = pre
                bias_acc = bias_acc + pre
                skip_acc = skip_acc + grad * value
            else:
                dpre_out[here, :] = rate_sum
                ds_out[here, :] = weighted
            return tuple(g), tuple(acc), tuple(h), skip_acc, bias_acc

        last = state_block(steps if d == 0 else 0, state)
        h_last = tuple(h_in[pl.ds(last + (low + m) * CHUNKS, CHUNKS), :] for m in range(some))
        none = tuple(zeros for _ in range(some))
        _, acc, _, skip_acc, bias_acc = lax.fori_loop(
            0, steps, step, (tuple(back[low : low + some]), none, h_last, zeros, zeros),
            unroll=ADJOINT_UNROLL,
        )
        grads.extend(acc)
    for n in range(state):
        rows_out[n : n + 1, :] = jnp.sum(grads[n], axis=0, keepdims=True) * rates[n][0:1] * LN2
    rows_out[state : state + 1, :] = jnp.sum(bias_acc, axis=0, keepdims=True)
    rows_out[state + 1 : state + 2, :] = jnp.sum(skip_acc, axis=0, keepdims=True)


def lane_sums(sums, state):
    column = lax.broadcasted_iota(jnp.int32, (2 * CHUNKS, LANES), 1)
    picks = [(column == n).astype(BF16) for n in range(2 * state)]
    pick = jnp.concatenate([p for p in picks for _ in range(LANES // (2 * CHUNKS))], axis=0)
    return dot(sums.astype(BF16), pick)[:, : 2 * state]


def rate_tiles(rate, d, state, lanes):
    return [
        jnp.broadcast_to(rate[d * state + n : d * state + n + 1, lanes], (CHUNKS, LANES))
        for n in range(state)
    ]


def begin_tiles(rates, passed, maps, carry, at, d, state, lanes):
    passed = passed[d * CHUNKS : (d + 1) * CHUNKS, lanes]
    return [
        jnp.exp2(rates[n] * passed) * carry[at + n : at + n + 1, lanes]
        + maps[d * state + n, :, lanes]
        for n in range(state)
    ]


def slot_order(rows):
    row = lax.broadcasted_iota(jnp.int32, (rows, rows), 1)
    slot = lax.broadcasted_iota(jnp.int32, (rows, rows), 0)
    return (slot == (row & (CHUNKS - 1)) * (rows // CHUNKS) + (row >> 3)).astype(BF16)


def states_kernel(
    io, delta, s, proj, rate, same, normed, before, tail, got, entered, zs, dgz, cotan,
    kept, sent, carry_out, dz, h0, h1, gated,
    bc, y,
    *, reach, rank, state, bit,
):
    rows, inner = zs.shape
    width = cotan.shape[1]
    steps = rows // CHUNKS
    half = 2 * state
    tiles = inner // LANES
    upper = ((lax.axis_index("seq") >> bit) & 1) == 1
    values = got[...].astype(F32)
    held = entered[...]
    rates = rate[0:half, :]
    carry_out[0:half, :] = held[:half] + jnp.where(
        upper, leads(rates, held[2 * half : 2 * half + 2], state, False) * values, 0.0
    )
    carry_out[half : 2 * half, :] = held[half : 2 * half] + jnp.where(
        upper, 0.0, leads(rates, held[2 * half + 2 : 2 * half + 4], state, True) * values
    )
    for d, h in enumerate((h0, h1)):
        mine = slice(d * rows, (d + 1) * rows)
        spread(proj[mine, rank:], bc)
        keep = same.at[d * reach * rows : (d * reach + 1) * rows, :]

        def scan_tile(tile, _, d=d, h=h, mine=mine, keep=keep):
            lanes = lanes_of(tile)
            rates = rate_tiles(rate, d, state, lanes)
            begin = begin_tiles(rates, before, tail, carry_out, d * half, d, state, lanes)
            states_pass(
                d, steps, state, rates, begin, delta.at[mine, lanes], s.at[mine, lanes],
                keep, bc, h.at[tile], y.at[:, lanes],
            )
            return 0

        lax.fori_loop(0, tiles, scan_tile, 0)
    block = 32

    def gate_block(b, _):
        here = pl.ds(pl.multiple_of(b * block, block), block)
        there = pl.ds(pl.multiple_of(rows + b * block, block), block)
        for tile in range(tiles):
            lanes = slice(tile * LANES, (tile + 1) * LANES)
            total = 0.5 * (
                y[here, lanes] + rate[half : half + 1, lanes] * s[here, lanes]
                + rate[half + 1 : half + 2, lanes] * s[there, lanes]
            )
            gated[here, lanes] = (total * zs[here, lanes]).astype(BF16)
            dz[here, lanes] = (total * dgz[here, lanes]).astype(BF16)
        return 0

    lax.fori_loop(0, rows // block, gate_block, 0, unroll=8)
    even = (lax.axis_index("seq") & 1) == 0
    out_grad = dot_rows(gated[...], cotan[...]).astype(BF16)
    z_grad = jnp.concatenate(
        [dot_rows(normed[...], dz[:, at : at + width]) for at in range(0, inner, width)], axis=0
    ).astype(BF16)
    sent[...] = jnp.where(even, z_grad, out_grad)
    kept[...] = jnp.where(even, out_grad, z_grad)


def output_kernel(io, gated, tokens, out_weight, output):
    ordered = dot(slot_order(gated.shape[0]), gated[...]).astype(BF16)
    io.ready()
    output[...] = (tokens[...].astype(F32) + dot(ordered, out_weight[...])).astype(BF16)


def adjoint_kernel(
    io, delta, s, dsilu, dy, head, xext, proj, after, rate, same, carry, h, dx_in,
    dt_weight, xproj, conv_weight,
    dc_rim, small_out, dx_out,
    bc, sums, dpre, ds, rows_out, ext,
    *, d, reach, rank, state,
):
    rows, inner = dy.shape
    steps = rows // CHUNKS
    half = 2 * state
    tiles = inner // LANES
    taps = reach + 1
    cols = proj.shape[1]
    mine = slice(d * rows, (d + 1) * rows)
    keep = same.at[d * reach * rows : (d * reach + 1) * rows, :]
    spread(proj[mine, rank:], bc)
    sums[...] = jnp.zeros_like(sums)
    rows_out[...] = jnp.zeros_like(rows_out)
    grad_at = (half if d == 0 else 0) + state

    def scan_tile(tile, _):
        lanes = lanes_of(tile)
        rates = rate_tiles(rate, d, state, lanes)
        back = begin_tiles(rates, after, head, carry, grad_at, d, state, lanes)
        adjoint_pass(
            d, steps, state, rates, back, delta.at[mine, lanes], s.at[mine, lanes],
            dy.at[:, lanes], keep, rate.at[half + d : half + d + 1, lanes], bc,
            h.at[tile], sums, dpre.at[:, lanes], ds.at[:, lanes], rows_out.at[:, lanes],
        )
        return 0

    lax.fori_loop(0, tiles, scan_tile, 0)
    io.ready()
    dpre_low = dpre[...].astype(BF16)
    dt_grad = dot_rows(proj[mine, :rank].astype(BF16), dpre_low)
    dt_back = dot_cols(dpre_low, dt_weight[d])
    dproj = jnp.concatenate([dt_back, lane_sums(sums[...], state)], axis=1).astype(BF16)
    small_out[0:cols, :] = dot_rows(dproj, s[mine, :].astype(BF16))
    small_out[cols : cols + rank, :] = dt_grad
    base = 0 if d == 0 else reach * CHUNKS
    step = 2 * LANES
    for lane in range(0, inner, step):
        lanes = slice(lane, lane + step)
        total = ds[:, lanes] + dot(dproj, xproj[d, :, lanes])
        ext[base : base + rows, lanes] = (total * dsilu[mine, lanes]).astype(BF16).astype(F32)
    wide = lax.broadcasted_iota(jnp.int32, (CHUNKS, inner), 0)
    for i in range(reach):
        if d == 0:
            moved = pltpu.roll(ext[i * CHUNKS : (i + 1) * CHUNKS, :], CHUNKS - 1, axis=0)
            ext[rows + i * CHUNKS : rows + (i + 1) * CHUNKS, :] = jnp.where(
                wide == CHUNKS - 1, 0.0, moved
            )
        else:
            moved = pltpu.roll(ext[rows + i * CHUNKS : rows + (i + 1) * CHUNKS, :], 1, axis=0)
            ext[i * CHUNKS : (i + 1) * CHUNKS, :] = jnp.where(wide == 0, 0.0, moved)

    conv_w = conv_weight[d].astype(F32)
    block = 64
    zeros = jnp.zeros((CHUNKS, LANES), F32)

    def folded(values):
        return functools.reduce(
            lambda a, b: a + b, [values[i : i + CHUNKS] for i in range(0, block, CHUNKS)]
        )

    base_row = cols + rank
    for tile in range(tiles):
        lanes = slice(tile * LANES, (tile + 1) * LANES)
        weight = conv_w[:, lanes]

        def conv_block(b, totals, lanes=lanes, weight=weight):
            here = pl.multiple_of(b * block, block)
            totals = list(totals)
            mid = ext[pl.ds(here + base, block), lanes]
            total = weight[reach:taps] * mid
            totals[reach] = totals[reach] + folded(mid * xext[pl.ds(here + reach * CHUNKS, block), lanes])
            totals[taps] = totals[taps] + folded(mid)
            for k in range(1, taps):
                past = same[pl.ds((k - 1) * rows + here, block), :]
                ahead = same[pl.ds((reach + k - 1) * rows + here, block), :]
                if d == 0:
                    given = ext[pl.ds(here + k * CHUNKS, block), lanes] * ahead
                    taken = xext[pl.ds(here + (reach - k) * CHUNKS, block), lanes] * past
                else:
                    given = ext[pl.ds(here + (reach - k) * CHUNKS, block), lanes] * past
                    taken = xext[pl.ds(here + (reach + k) * CHUNKS, block), lanes] * ahead
                total = total + weight[reach - k : taps - k] * given
                totals[reach - k] = totals[reach - k] + folded(mid * taken)
            if dx_in is not None:
                total = total + dx_in[pl.ds(here, block), lanes]
            dx_out[pl.ds(here, block), lanes] = total
            return tuple(totals)

        totals = lax.fori_loop(0, rows // block, conv_block, (zeros,) * (taps + 1), unroll=4)
        for i in range(taps + 1):
            at = state + 2 + i
            rows_out[at : at + 1, lanes] = jnp.sum(totals[i], axis=0, keepdims=True)

    edge = []
    for i in range(CHUNKS):
        row = jnp.zeros((1, inner), F32)
        for k in range(1, taps):
            j = i - CHUNKS + k if d == 0 else steps + i - k
            if (d == 0 and j >= 0) or (d == 1 and j < steps):
                sub = 0 if d == 0 else CHUNKS - 1
                at = (d * reach + k - 1) * rows + j * CHUNKS + sub
                mask = jnp.concatenate([same[at : at + 1, :]] * tiles, axis=1)
                at = base + j * CHUNKS + sub
                row = row + conv_w[reach - k : taps - k] * ext[at : at + 1, :] * mask
        edge.append(row)
    dc_rim[...] = jnp.concatenate(edge, axis=0)
    small_out[base_row:, :] = rows_out[0 : small_out.shape[0] - base_row, :]


def first_adjoint(io, *refs, **static):
    adjoint_kernel(io, *refs[:12], None, *refs[12:], **static)


def second_adjoint(io, *refs, **static):
    in_far, in_near, moves = refs[16], refs[20], refs[21]
    copy = fetch(in_far, in_near, moves.at[0])
    adjoint_kernel(io, *refs[:16], *refs[17:20], *refs[22:], **static)
    copy.wait()


def last_kernel(
    io, dx, rim0, rim1, small0, small1, normed, nhalo, live, in_weight,
    kept, sent, low,
    lines, grads,
):
    rows, inner = dx.shape
    width = normed.shape[1]
    folds = inner // width
    fold = kept.shape[0]
    edges = 2 * CHUNKS
    for tile in range(inner // LANES):
        lanes = slice(tile * LANES, (tile + 1) * LANES)
        lines[0:rows, lanes] = (dx[:, lanes] * live[...]).astype(BF16)
    low[...] = lines[0:rows, :]
    lines[rows : rows + edges, :] = jnp.concatenate([rim0[...], rim1[...]], axis=0).astype(BF16)
    both = jnp.concatenate([normed[...], nhalo[0:edges, :]], axis=0)
    size = small0.shape[0]
    for i in range(folds):
        lanes = slice(i * width, (i + 1) * width)
        at = i * fold
        grads[at : at + width, :] = dot_rows(both, lines[:, lanes]).astype(BF16)
        at += width
        grads[at : at + 2 * size, :] = jnp.concatenate(
            [small0[:, lanes], small1[:, lanes]], axis=0
        ).astype(BF16)
        at += 2 * size
        grads[at : (i + 1) * fold, :] = jnp.zeros(((i + 1) * fold - at, width), BF16)
    rim = dot_cols(lines[rows : rows + edges, :], in_weight[:, 0:inner])
    even = (lax.axis_index("seq") & 1) == 0
    turned = jnp.concatenate([rim[CHUNKS:], rim[:CHUNKS]], axis=0)
    left, right = grads[0:fold, :], grads[fold : 2 * fold, :]
    kept[...] = jnp.where(even, left, right)
    sent[...] = jnp.where(even, right, left)
    at = width + 2 * size
    sent[at : at + edges, :] = jnp.where(even, turned, rim).astype(BF16)


def finish_kernel(
    io, low, dz, in_weight, rims, chip_rim, heights, widths, tokens, cotangent, valid, gain,
    input_grad,
):
    rows, width = tokens.shape
    inner = low.shape[1]
    even = (lax.axis_index("seq") & 1) == 0
    start = lax.axis_index("seq") * rows
    back = slot_order(rows)
    dn = dot_cols(dot(back, low[...]).astype(BF16), in_weight[:, 0:inner]) + dot_cols(
        dot(back, dz[...]).astype(BF16), in_weight[:, inner : 2 * inner]
    )
    io.ready()
    from_core = rims[...].astype(F32)[:CHUNKS]
    from_chip = chip_rim[...].astype(F32)[CHUNKS:]
    before = jnp.where(even, from_chip, from_core)
    after = jnp.where(even, from_core, from_chip)
    end = image_ends(heights, widths)[-1]
    row = lax.broadcasted_iota(jnp.int32, (CHUNKS, rows), 0)
    slot = lax.broadcasted_iota(jnp.int32, (CHUNKS, rows), 1)
    alive = jnp.broadcast_to(valid[...].astype(F32), (CHUNKS, rows))
    alive = jnp.where(start + slot < end, alive, 0.0)
    first = jnp.sum(jnp.where(slot == row, alive, 0.0), axis=1, keepdims=True)
    last = jnp.sum(jnp.where(slot == rows - CHUNKS + row, alive, 0.0), axis=1, keepdims=True)
    values = jnp.concatenate(
        [
            dn[0:CHUNKS, :] + first * before, dn[CHUNKS : rows - CHUNKS, :],
            dn[rows - CHUNKS : rows, :] + last * after,
        ],
        axis=0,
    )
    inputs = tokens[...].astype(F32)
    inv_rms = lax.rsqrt(jnp.mean(inputs * inputs, axis=-1, keepdims=True) + NORM_EPS)
    scaled = values * gain[...].astype(F32).reshape(1, width)
    mean = jnp.mean(scaled * inputs, axis=-1, keepdims=True)
    input_grad[...] = (
        cotangent[...].astype(F32) + inv_rms * scaled - inputs * (inv_rms * inv_rms * inv_rms) * mean
    )


def blocks_in_order(mine, other, into_first, into_second):
    size = mine.shape[1]
    is_even = (lax.axis_index("seq") & 1) == 0
    here = lax.axis_index("img")
    for k in range(mine.shape[0]):
        a, b = mine[here ^ k].astype(F32), other[here ^ k].astype(F32)
        into_first(k * size, jnp.where(is_even, a, b))
        into_second(k * size, jnp.where(is_even, b, a))


def weighted_rows(values, weights):
    total = None
    for at in range(0, values.shape[1], LANES):
        part = values[:, at : at + LANES] * weights[:, at : at + LANES].astype(F32)
        total = part if total is None else total + part
    return total


def first_unpack(io, mine, other, in_weight, parts, in_far, out_far, out_w, z_half, moves):
    width = out_w.shape[1]
    inner = out_w.shape[0]

    def put_out(at, values):
        out_w[at : at + values.shape[0], :] = values

    def put_z(at, values):
        size = values.shape[0]
        column = at // width * width
        z_half[at % width : at % width + size, column : column + width] = values

    blocks_in_order(mine, other, put_out, put_z)
    leaving = [
        fetch(out_w, out_far, moves.at[0]),
        fetch(z_half, in_far.at[:, inner : 2 * inner], moves.at[1]),
    ]
    parts[...] = weighted_rows(z_half[...], in_weight[:, inner : 2 * inner])
    for copy in leaving:
        copy.wait()


def second_unpack(
    io, mine, other, in_weight, parts, gain_in, in_before,
    conv_w, conv_b, xproj, dt_w, dt_b, a_log, skip, in_far, gain_far,
    left, right, x_half, gain, moves,
    *, count, state, rank, cols, taps,
):
    width = left.shape[1]
    inner = x_half.shape[1]

    def put(target, lane):
        def at_rows(at, values):
            size = values.shape[0]
            target[at : at + size, :] = values
            top = min(width - at, size)
            if top > 0:
                x_half[at : at + top, lane : lane + width] = values[:top]

        return at_rows

    blocks_in_order(mine, other, put(left, 0), put(right, width))
    leaving = fetch(x_half, in_far.at[:, 0:inner], moves.at[0])
    for i, half in enumerate((left, right)):
        lanes = slice(i * width, (i + 1) * width)
        for d in range(2):
            at = width + d * count
            xproj[d, :, lanes] = half[at : at + cols, :]
            at += cols
            dt_w[d, :, lanes] = half[at : at + rank, :]
            at += rank
            a_log[d, :, lanes] = half[at : at + state, :]
            dt_b[d : d + 1, lanes] = half[at + state : at + state + 1, :]
            skip[d : d + 1, lanes] = half[at + state + 1 : at + state + 2, :]
            at += state + 2
            conv_w[d, :, lanes] = half[at : at + taps, :]
            conv_b[d : d + 1, lanes] = half[at + taps : at + taps + 1, :]
    io.ready()
    io.done()
    total = parts[...] + weighted_rows(x_half[...], in_weight[:, 0:inner])
    high = total.astype(BF16)
    rest = (total - high.astype(F32)).astype(BF16)
    ones = jnp.ones((2 * CHUNKS, LANES), BF16)
    sums = (dot_cols(ones, high) + dot_cols(ones, rest))[0:1]
    gain[...] = (sums / gain_in[...].astype(F32).reshape(1, width)).reshape(width)
    last = fetch(gain, gain_far, moves.at[1])
    leaving.wait()
    last.wait()


IN_VMEM = pl.BlockSpec(memory_space=pltpu.VMEM)
IN_SMEM = pl.BlockSpec(memory_space=pltpu.SMEM)
FAR = pl.BlockSpec(memory_space=pltpu.HBM)


def shape(*dims, dtype=F32):
    return jax.ShapeDtypeStruct(dims, dtype)


def low(*dims):
    return jax.ShapeDtypeStruct(dims, BF16)


def near(*dims, dtype=F32):
    return pltpu.VMEM(dims, dtype)


def scratch(*dims, dtype=F32):
    return pltpu.VMEM(dims, dtype)


def like(*outs):
    return [pltpu.VMEM(out.shape, out.dtype) for out in outs]


def moves(*dims):
    return pltpu.SemaphoreType.DMA(dims)


class Moves:
    def __init__(self, arrive, leave):
        self.arrive, self.leave, self.left = arrive, leave, False
        for copy in arrive:
            copy.start()

    def ready(self):
        for copy in self.arrive:
            copy.wait()

    def done(self):
        self.left = True
        for copy in self.leave:
            copy.start()


def call(
    kernel, name, args, outs, scratches=(), far=(), far_outs=(), near_args=(), near_outs=(),
    scalars=(), handed=(), aliases=(), us=4, limit=4,
):
    small = tuple(scalars) + tuple(args)
    small, far = (
        tuple(pltpu.with_memory_space_constraint(x, pltpu.HBM) for x in arrays)
        for arrays in (small, far)
    )
    n_hand = len(handed)
    near_args = tuple(handed) + tuple(near_args)
    n_near, n_small, n_far = len(near_args), len(small), len(far)
    n_near_outs, n_outs, n_far_outs = len(near_outs), len(outs), len(far_outs)

    def wrapped(*refs):
        refs = list(refs)

        def take(count):
            taken = refs[:count]
            del refs[:count]
            return taken

        near_in, small_in, far_in = take(n_near), take(n_small), take(n_far)
        near_out, out, far_out = take(n_near_outs), take(n_outs), take(n_far_outs)
        take(n_hand)
        small_here, out_here = take(n_small), take(n_outs)
        in_moves, out_moves = take(2)
        io = Moves(
            [pltpu.make_async_copy(a, b, in_moves.at[i]) for i, (a, b) in enumerate(zip(small_in, small_here))],
            [pltpu.make_async_copy(a, b, out_moves.at[i]) for i, (a, b) in enumerate(zip(out_here, out))],
        )
        kernel(io, *near_in, *small_here, *far_in, *near_out, *out_here, *far_out, *refs)
        if not io.left:
            io.done()
        for copy in io.leave:
            copy.wait()

    return pl.pallas_call(
        wrapped,
        out_shape=list(near_outs) + [
            pltpu.HBM(out.shape, out.dtype) for out in tuple(outs) + tuple(far_outs)
        ] + [pltpu.VMEM(x.shape, x.dtype) for x in handed],
        in_specs=[IN_VMEM] * n_near + [FAR] * (n_small + n_far),
        out_specs=[IN_VMEM] * n_near_outs + [FAR] * (n_outs + n_far_outs) + [IN_VMEM] * n_hand,
        input_output_aliases={
            **{i: n_near_outs + n_outs + n_far_outs + i for i in range(n_hand)},
            **{n_near + n_small + i: n_near_outs + n_outs + o for i, o in aliases},
        },
        scratch_shapes=(
            [pltpu.SMEM(a.shape, a.dtype) for a in scalars] + like(*args) + like(*outs)
            + [moves(max(n_small, 1)), moves(max(n_outs, 1))] + list(scratches)
        ),
        compiler_params=pltpu.CompilerParams(vmem_limit_bytes=limit * 2**20),
        cost_estimate=pl.CostEstimate(flops=us * 2000000000, bytes_accessed=0, transcendentals=0),
        name=name,
    )(*near_args, *small, *far)


def call_edges(tokens, valid):
    edge = 2 * CHUNKS
    width = tokens.shape[1]
    outs = [near(edge, width, dtype=BF16), near(edge, width, dtype=BF16)]
    return call(edges_kernel, "edges", (tokens, valid), (), near_outs=outs, us=1, limit=2)


def call_front(
    heights, widths, valid, gain, tokens, cotangent, in_weight, out_weight, weights, reach,
):
    rows, width = tokens.shape
    inner = out_weight.shape[0]
    one = near(rows, inner)
    row = near(rows, width, dtype=BF16)
    return call(
        functools.partial(front_kernel, reach=reach, weights=len(weights)), "front", (valid, gain), (),
        [moves(len(weights))], weights, (),
        tuple(
            pltpu.with_memory_space_constraint(x, pltpu.VMEM)
            for x in (tokens, cotangent, in_weight, out_weight)
        ),
        [
            row, one, one, one, one, near(rows, LANES), near(2 * reach * rows, LANES), row,
            near(width, inner, dtype=BF16), near(2 * CHUNKS, LANES), near(CHUNKS, width),
        ] + like(*weights),
        (heights, widths), us=4, limit=12,
    )


def call_middle(handed, used, from_core, from_chip, arrays, reach, cols):
    x, a_log = arrays[0], arrays[-2]
    rows, inner = x.shape
    state, width = a_log.shape[1], from_core.shape[1]
    half = 2 * state
    both = near(2 * rows, inner)
    maps = near(half, CHUNKS, inner)
    ends = near(2 * CHUNKS, inner)
    n_hand = len(handed)

    def kernel(io, *refs):
        middle_kernel(io, *(refs[i] for i in used), *refs[n_hand:], reach=reach)

    return call(
        kernel, "middle", (), (),
        [
            scratch(2 * rows, inner, dtype=BF16), scratch(rows, half * LANES),
            scratch(state, CHUNKS, inner), scratch(state, CHUNKS, inner), scratch(CHUNKS, inner),
        ],
        near_args=(from_core, from_chip) + arrays,
        near_outs=[
            near(2 * half + CHUNKS + half, inner), near(2 * half + 2 * CHUNKS, inner, dtype=BF16),
            both, both, both, maps, maps, near(rows + 2 * reach * CHUNKS, inner),
            near(2 * rows, cols), ends, ends, near(half + CHUNKS, inner),
            near(4 * CHUNKS, width, dtype=BF16),
        ],
        handed=handed, us=20, limit=9,
    )


def call_join(got, summary, entered, state, bit, final):
    inner = summary.shape[1]
    half = 2 * state
    outs = [
        near(2 * half + CHUNKS, inner),
        near(half if final else 2 * half + 2 * CHUNKS, inner, dtype=BF16),
    ]
    if not final:
        outs = [near(2 * half + CHUNKS + half, inner)] + outs
    args = (got, summary) + (() if entered is None else (entered,))
    kernel = first_join if entered is None else join_kernel
    joined = call(
        functools.partial(kernel, state=state, bit=bit, final=final), "join", (), (),
        near_args=args, near_outs=outs, us=1, limit=4,
    )
    return joined if not final else [None] + list(joined)


def call_states(handed, used, before, tail, got, entered, zs, dgz, cotan, rank, reach, state, bit):
    rows, inner = zs.shape
    width = cotan.shape[1]
    half = 2 * state
    n_hand = len(handed)

    def kernel(io, *refs):
        states_kernel(
            io, *(refs[i] for i in used), *refs[n_hand:], reach=reach, rank=rank, state=state, bit=bit
        )

    grad = near(inner, width, dtype=BF16)
    one = near(rows, inner, dtype=BF16)
    held = near(inner // LANES, (rows // CHUNKS + 1) * state * CHUNKS, LANES)
    return call(
        kernel, "states", (), (),
        [scratch(rows, half * LANES), scratch(rows, inner)],
        near_args=(before, tail, got, entered, zs, dgz, cotan),
        near_outs=[grad, grad, near(2 * half, inner), one, held, held, one], handed=handed, us=12,
        limit=9,
    )


def adjoint_scratch(rows, inner, half, reach, small, cols, rank):
    return [
        scratch(rows, half * LANES), scratch(rows, half * LANES), scratch(rows, inner), scratch(rows, inner), scratch(small - cols - rank, inner),
        scratch(rows + reach * CHUNKS, inner),
    ]


def call_first_adjoint(handed, used, h, weights, small, reach, rank, state):
    rows, inner = handed[used[3]].shape
    cols = handed[used[6]].shape[1]
    n_hand = len(handed)

    def kernel(io, *refs):
        first_adjoint(
            io, *(refs[i] for i in used), *refs[n_hand:], d=0, reach=reach, rank=rank, state=state
        )

    return call(
        kernel, "adjoint_up", weights, (),
        adjoint_scratch(rows, inner, 2 * state, reach, small, cols, rank), near_outs=[
            near(CHUNKS, inner), near(small, inner), near(rows, inner),
        ], near_args=(h,), handed=handed, us=14, limit=13,
    )


def call_second_adjoint(handed, arrays, weights, in_weight, small, reach, rank, state):
    rows, inner = arrays[3].shape
    cols = arrays[6].shape[1]
    n_hand = len(handed)

    def kernel(io, *refs):
        second_adjoint(io, *refs[n_hand:], d=1, reach=reach, rank=rank, state=state)

    return call(
        kernel, "adjoint_down", weights, (),
        [moves(1)] + adjoint_scratch(rows, inner, 2 * state, reach, small, cols, rank),
        (in_weight,), (), arrays,
        [near(CHUNKS, inner), near(small, inner), near(rows, inner), near(*in_weight.shape, dtype=BF16)],
        handed=handed, us=14, limit=13,
    )


def call_last(handed, dx, rim0, rim1, small0, small1, normed, nhalo, live):
    rows, inner = dx.shape
    width = normed.shape[1]
    small = small0.shape[0]
    folds = inner // width
    edges = 2 * CHUNKS
    fold = -(-(width + 2 * small + edges) // 64) * 64
    n_hand = len(handed)

    def kernel(io, *refs):
        last_kernel(io, *refs[n_hand : n_hand + 8], refs[n_hand - 1], *refs[n_hand + 8 :])

    return call(
        kernel, "last", (), (),
        [
            scratch(rows + edges, inner, dtype=BF16), scratch(folds * fold, width, dtype=BF16),
        ],
        near_args=(dx, rim0, rim1, small0, small1, normed, nhalo, live),
        near_outs=[
            near(fold, width, dtype=BF16), near(fold, width, dtype=BF16),
            near(rows, inner, dtype=BF16),
        ],
        handed=handed, us=3, limit=8,
    )


def partner(axis, bit):
    return [(i, i ^ (1 << bit)) for i in range(lax.axis_size(axis))]


def bits_of(axis):
    return (lax.axis_size(axis) - 1).bit_length()


def other_core(values):
    return lax.ppermute(values, "seq", partner("seq", 0))


def next_chip(values):
    count = lax.axis_size("seq")
    pairs = [(i, i + 1) for i in range(1, count - 1, 2)]
    return lax.ppermute(values, "seq", pairs + [(j, i) for i, j in pairs])


def split_kernel(io, kept, got, own, *sent, edges):
    if edges:
        at = got.shape[0] - edges[1]
        sent[-1][...] = got[at : at + edges[0], :]
        sent = sent[:-1]
    count = len(sent) + 1
    rows = own.shape[0]
    here = lax.axis_index("img")
    for k in range(count):
        at = pl.ds(pl.multiple_of((here ^ k) * rows, rows), rows)
        total = kept[at, :].astype(F32) + got[at, :].astype(F32)
        if k == 0:
            own[...] = total
        else:
            sent[k - 1][...] = total.astype(BF16)


def add_kernel(io, *refs, outs):
    total = refs[0][...].astype(F32)
    for ref in refs[1 : len(refs) - outs]:
        total = total + ref[...].astype(F32)
    for ref in refs[len(refs) - outs :]:
        ref[...] = total.astype(ref.dtype)


def add(values, whole=True):
    rows, width = values[0].shape
    outs = [near(rows, width)] * whole + [near(rows, width, dtype=BF16)]
    sums = call(
        functools.partial(add_kernel, outs=len(outs)), "add", (), (), near_args=values,
        near_outs=outs, us=1, limit=2,
    )
    return sums if whole else sums[0]


def add_rim_kernel(io, *refs, count, bit):
    values, moving, stay = refs[:count], refs[count], refs[count + 1]
    low_out, stay_out = refs[-2:]
    rows = values[0].shape[0]
    total = values[0][...]
    for ref in values[1:]:
        total = total + ref[0:rows, :].astype(F32)
    if len(refs) > count + 4:
        refs[-3][...] = total
    low_out[0:rows, :] = total.astype(BF16)
    if bit is None:
        low_out[rows:, :] = moving[...]
        stay_out[...] = jnp.zeros_like(stay_out)
        return
    came = values[-1][rows:, :]
    if low_out.shape[0] > rows:
        low_out[rows:, :] = came
    position = lax.axis_index("seq")
    chip = position >> 1
    chip = jnp.where((position & 1) == 0, chip, lax.axis_size("seq") // 2 - 1 - chip)
    lowest = chip & ((2 << bit) - 1)
    stay_out[...] = jnp.where(lowest == (1 << bit), came, stay[...])


def add_rim(values, moving, stay, bit, final=False):
    rows, width = values[0].shape
    edge = moving.shape[0]
    sent = rows if final else rows + edge
    outs = [near(rows, width)] * (not final)
    outs += [near(sent, width, dtype=BF16), near(edge, width, dtype=BF16)]
    sums = call(
        functools.partial(add_rim_kernel, count=len(values), bit=bit), "add", (), (),
        near_args=tuple(values) + (moving, stay), near_outs=outs, us=1, limit=2,
    )
    return [None] * final + list(sums)


def stack_kernel(io, *refs):
    for k, ref in enumerate(refs[:-1]):
        refs[-1][k] = ref[...]


def plane_pairs(k):
    return [(i, i ^ k) for i in range(lax.axis_size("img"))]


def chips_sum(kept, sent, edges=()):
    count = lax.axis_size("img")
    rows, width = kept.shape
    block = (rows // count, width)
    got = other_core(sent)
    own, *parts = call(
        functools.partial(split_kernel, edges=edges), "split", (), (), near_args=(kept, got),
        near_outs=[near(*block)] + [near(*block, dtype=BF16)] * (count - 1)
        + [near(rim_rows, width, dtype=BF16) for rim_rows in edges[:1]],
        us=1, limit=2,
    )
    rim = parts.pop() if edges else None
    blocks = [own] + [
        lax.ppermute(part, "img", plane_pairs(k + 1)) for k, part in enumerate(parts)
    ]
    return blocks, rim


def line_steps(total, low):
    bits = bits_of("seq")
    for bit in range(1, bits):
        got = lax.ppermute(low, "seq", partner("seq", bit))
        if bit < bits - 1:
            total, low = add([total, got])
        else:
            low = add([total, got], whole=False)
    return low


def line_steps_with_rims(blocks, rim, first_low, beside):
    stay = rim
    total, low, stay = add_rim(blocks, rim, stay, None)
    low, first_low = tied(low, first_low)
    bits = bits_of("seq")
    for bit in range(1, bits):
        got = lax.ppermute(low, "seq", partner("seq", bit))
        if bit == 1:
            first_blocks = plane_blocks(first_low)
        if bit == bits - 1:
            got, beside, *first_blocks = lax.optimization_barrier((got, beside, *first_blocks))
        total, low, stay = add_rim([total, got], rim, stay, bit - 1, bit == bits - 1)
    return low, stay, first_blocks, beside


def plane_blocks(low):
    count = lax.axis_size("img")
    return [low] + [lax.ppermute(low, "img", plane_pairs(k)) for k in range(1, count)]


def stacked(blocks):
    low, count = blocks[0], len(blocks)
    return call(
        stack_kernel, "stack", (), (), near_args=blocks,
        near_outs=[near(count, *low.shape, dtype=BF16)], us=1, limit=2,
    )[0]


def tied(first, second):
    return lax.optimization_barrier((first, second))


def body(
    tokens, cotangent, heights, widths, valid, norm_gain, in_weight, conv_weight, conv_bias,
    xproj_weight, dt_weight, dt_bias, a_log, skip, out_weight,
):
    rows, width = tokens.shape[1:]
    inner = out_weight.shape[0]
    state = a_log.shape[1]
    rank = dt_weight.shape[1]
    cols = xproj_weight.shape[2]
    taps = conv_weight.shape[1]
    reach = taps - 1
    count = bits_of("seq")
    tokens, cotangent = tokens[0], cotangent[0]
    xproj = xproj_weight.transpose(0, 2, 1)

    to_core, to_chip = call_edges(tokens, valid)
    from_core, from_chip = other_core(to_core), next_chip(to_chip)
    weights = (conv_weight, conv_bias, xproj, dt_weight, dt_bias, a_log, skip)
    normed, x, zs, dgz, dy, live, same, cotan, in_x, halo_live, gains, *near_weights = call_front(
        heights, widths, valid, norm_gain, tokens, cotangent, in_weight, out_weight, weights, reach
    )
    (
        summary, sent, delta, s, dsilu, tail, head, xext, proj, before, after, rate, nhalo,
        dy, live, same, normed, zs, dgz, cotan,
    ) = call_middle(
        (dy, live, same, normed, zs, dgz, cotan), (0, 1, 2), from_core, from_chip,
        (x, in_x, halo_live, gains) + tuple(near_weights), reach, cols,
    )
    entered = None
    for bit in range(count - 1):
        got = lax.ppermute(sent, "seq", partner("seq", bit))
        summary, entered, sent = call_join(got, summary, entered, state, bit, bit == count - 2)
    got = lax.ppermute(sent, "seq", partner("seq", count - 1))
    handed = (
        delta, s, dsilu, dy, head, xext, proj, after, rate, same, live, normed, nhalo,
    )
    kept, sent, carry, dz, h0, h1, gated, *handed = call_states(
        handed, (0, 1, 6, 8, 9, 11), before, tail, got, entered, zs, dgz, cotan, rank, reach, state,
        count - 1,
    )

    blocks, _ = chips_sum(kept, sent)
    small = -(-(cols + rank + state + 2 + taps + 1) // CHUNKS) * CHUNKS
    weights = (dt_weight, xproj, conv_weight)
    handed = tuple(handed[:10]) + (carry,) + tuple(handed[10:]) + (dz, gated, h1)
    rim0, small0, dx, *handed = call_first_adjoint(
        handed, tuple(range(11)), h0, weights, small, reach, rank, state
    )
    *blocks, dx = lax.optimization_barrier((*blocks, dx))
    first_sum, first_low = add(blocks)
    first_sum, first_low, dx = lax.optimization_barrier((first_sum, first_low, dx))
    arrays, passed, h1 = tuple(handed[:11]), tuple(handed[11:-1]), handed[-1]
    if bits_of("seq") > 3:
        first_low = line_steps(first_sum, first_low)
    else:
        devices = lax.axis_size("seq")
        blocks = [first_sum] + [
            lax.ppermute(first_low, "seq", [(i, i ^ k) for i in range(devices)])
            for k in range(2, devices, 2)
        ]
    rim1, small1, dx, in_near, *passed = call_second_adjoint(
        passed, arrays + (h1, dx), weights, in_weight, small, reach, rank, state
    )
    live, normed, nhalo, dz, gated = passed
    if bits_of("seq") <= 3:
        *blocks, dx = lax.optimization_barrier((*blocks, dx))
        first_low = add(blocks, whole=False)
    kept, sent, dx_low, dz, gated, in_near = call_last(
        (dz, gated, in_near), dx, rim0, rim1, small0, small1, normed, nhalo, live
    )

    edges = (2 * CHUNKS, kept.shape[0] - width - 2 * small)
    blocks, rim = chips_sum(kept, sent, edges)


    output = call(
        output_kernel, "output", (tokens, out_weight), [low(rows, width)], near_args=(gated,), us=2,
        limit=6,
    )[0]
    second_low, chip_rim, first_blocks, output = line_steps_with_rims(blocks, rim, first_low, output)
    blocks = plane_blocks(second_low)
    _, *first_blocks = lax.optimization_barrier((blocks[1], *first_blocks))
    first_mine = stacked(first_blocks)
    first_other = other_core(first_mine)
    input_grad = call(
        finish_kernel, "finish", (tokens, cotangent, valid, norm_gain), [shape(rows, width)],
        near_args=(dx_low, dz, in_near, rim, chip_rim), scalars=(heights, widths), us=3, limit=8,
    )[0]
    blocks, input_grad = lax.optimization_barrier((blocks, input_grad))
    second_mine = stacked(blocks)
    second_other = other_core(second_mine)
    parts, in_total, out_total = call(
        first_unpack, "unpack_first", (), (),
        [scratch(inner, width), scratch(width, inner), moves(2)],
        far_outs=[shape(width, 2 * inner), shape(inner, width)],
        near_args=(first_mine, first_other, in_near), near_outs=[near(width, LANES)], us=2, limit=8,
    )
    second_other, parts = tied(second_other, parts)
    fold = kept.shape[0]
    (
        conv_total, bias_total, xproj_total, dtw_total, dtb_total, a_total, skip_total, in_total,
        gain_total,
    ) = call(
        functools.partial(
            second_unpack, count=small, state=state, rank=rank, cols=cols, taps=taps
        ),
        "unpack_second", (norm_gain,),
        [
            shape(2, taps, inner), shape(2, inner), shape(2, cols, inner), shape(2, rank, inner),
            shape(2, inner), shape(2, state, inner), shape(2, inner),
        ],
        [
            scratch(fold, width), scratch(fold, width), scratch(width, inner), scratch(width),
            moves(2),
        ],
        (in_total,), [shape(width, 2 * inner), shape(width)], (second_mine, second_other, in_near, parts),
        aliases=((0, 0),), us=2, limit=10,
    )
    return (
        output[None], input_grad[None], gain_total, in_total, conv_total, bias_total,
        xproj_total.transpose(0, 2, 1), dtw_total, dtb_total, a_total, skip_total, out_total,
    )


def solution(mesh):
    split = P("img", "seq", None)
    placed = (split, split, P("img", None), P("img", None), P("img", "seq")) + (P(),) * 10
    return jax.shard_map(
        body,
        mesh=mesh,
        in_specs=placed,
        out_specs=(split, split) + (P(),) * 10,
        check_vma=False,
    )
```

```python
import functools

import jax
import jax.numpy as jnp
from jax import lax
from jax.experimental import pallas as pl
from jax.experimental.pallas import tpu as pltpu
from jax.sharding import PartitionSpec as P

NORM_EPS = 1e-05
CONTRACT_ROWS = (((0,), (0,)), ((), ()))
CONTRACT_COLS = (((1,), (1,)), ((), ()))
LOG2E = 1.4426950408889634
LN2 = 0.6931471805599453
BREAK = 1e30
CHUNKS = 8
LANES = 128
SUMMARY_STATES = 8
SUMMARY_UNROLL = 16
STATES_UNROLL = 32
ADJOINT_STATES = 8
ADJOINT_UNROLL = 16
F32 = jnp.float32
BF16 = jnp.bfloat16


def dot(a, b):
    return jnp.dot(a, b, preferred_element_type=F32)


def dot_rows(a, b):
    return lax.dot_general(a, b, CONTRACT_ROWS, preferred_element_type=F32)


def dot_cols(a, b):
    return lax.dot_general(a, b, CONTRACT_COLS, preferred_element_type=F32)


def sigmoid(v):
    return 1.0 / (1.0 + jnp.exp(-v))


def fetch(source, target, semaphore):
    copy = pltpu.make_async_copy(source, target, semaphore)
    copy.start()
    return copy


def lanes_of(tile):
    return pl.ds(pl.multiple_of(tile * LANES, LANES), LANES)


def rows_of(j, count=CHUNKS):
    return pl.ds(pl.multiple_of(j * CHUNKS, CHUNKS), count)


def chunk_order(rows):
    row = lax.broadcasted_iota(jnp.int32, (rows, rows), 0)
    slot = lax.broadcasted_iota(jnp.int32, (rows, rows), 1)
    return slot == (row & (CHUNKS - 1)) * (rows // CHUNKS) + (row >> 3)


def image_ends(heights, widths):
    ends, total = [], 0
    for i in range(heights.shape[1]):
        total = total + heights[0, i] * widths[0, i]
        ends.append(total)
    return ends


def segment_of(places, ends):
    found = jnp.zeros_like(places)
    for end in ends:
        found = found + (places >= end).astype(jnp.int32)
    return found


def places_of(first, rows):
    row = lax.broadcasted_iota(jnp.int32, (rows, LANES), 0)
    return first + (row & (CHUNKS - 1)) * (rows // CHUNKS) + (row >> 3)


def edges_kernel(io, valid, tokens_far, to_core, to_chip, top, bottom, moves):
    rows = tokens_far.shape[0]
    edge = to_core.shape[0]
    arriving = [
        fetch(tokens_far.at[0:edge, :], top, moves.at[0]),
        fetch(tokens_far.at[rows - edge : rows, :], bottom, moves.at[1]),
    ]
    row = lax.broadcasted_iota(jnp.int32, (edge, rows), 0)
    slot = lax.broadcasted_iota(jnp.int32, (edge, rows), 1)
    io.ready()
    held = jnp.broadcast_to(valid[...].astype(F32), (edge, rows))
    kept_top = jnp.sum(jnp.where(slot == row, held, 0.0), axis=1, keepdims=True)
    kept_bottom = jnp.sum(jnp.where(slot == rows - edge + row, held, 0.0), axis=1, keepdims=True)
    for copy in arriving:
        copy.wait()
    first = (top[...].astype(F32) * kept_top).astype(BF16)
    last = (bottom[...].astype(F32) * kept_bottom).astype(BF16)
    even = (lax.axis_index("seq") & 1) == 0
    to_core[...] = jnp.where(even, last, first)
    to_chip[...] = jnp.where(even, first, last)


def spread(values, target):
    count = values.shape[1]
    high = values.astype(BF16)
    low = (values - high.astype(F32)).astype(BF16)
    both = jnp.concatenate([high, low], axis=1)
    row = lax.broadcasted_iota(jnp.int32, (2 * count, LANES), 0)
    row = jnp.where(row < count, row, row - count)
    for at in range(0, count, 2):
        pick = jnp.concatenate([(row == at).astype(BF16), (row == at + 1).astype(BF16)], axis=1)
        target[:, at * LANES : (at + 2) * LANES] = dot(both, pick)


def windows(span, up, sublane):
    sign = 1 if up else -1

    def from_before(value, by, fill):
        moved = pltpu.roll(value, (sign * by) % CHUNKS, axis=0)
        kept = sublane >= by if up else sublane < CHUNKS - by
        return jnp.where(kept, moved, fill)

    two = span + from_before(span, 1, 0.0)
    four = two + from_before(two, 2, 0.0)
    eight = four + from_before(four, 4, 0.0)
    edge = [jnp.where(sublane >= by if up else sublane < CHUNKS - by, 0.0, BREAK) for by in (1, 2, 4)]
    return (span + edge[0], two + edge[1], four + edge[2]), from_before(eight, 1, 0.0)


def chain(rate, sums, tail, up, sublane):
    sign = 1 if up else -1
    for by, span in zip((1, 2, 4), sums):
        tail = jnp.exp2(rate * span) * pltpu.roll(tail, (sign * by) % CHUNKS, axis=0) + tail
    end = CHUNKS - 1 if up else 0
    kept = sublane >= 1 if up else sublane < CHUNKS - 1
    return jnp.where(kept, pltpu.roll(tail, sign % CHUNKS, axis=0), 0.0), tail[end : end + 1]


def front_kernel(
    io, tokens, cotangent, in_weight, out_weight, heights, widths, valid, gain, *refs, reach, weights,
):
    (
        normed_out, x_out, zs_out, dgz_out, dy, live, same_out, cotan, in_x, halo_live, gains_out,
    ) = refs[weights : weights + 11]
    near_weights = refs[weights + 11 : 2 * weights + 11]
    ins = refs[2 * weights + 11]
    rows, width = tokens.shape
    inner = out_weight.shape[0]
    tiles = inner // LANES
    arriving = [
        fetch(source, target, ins.at[i])
        for i, (source, target) in enumerate(zip(refs[:weights], near_weights))
    ]
    order = chunk_order(rows)
    order_low = order.astype(BF16)
    inputs = dot(order_low, tokens[...])
    inv_rms = lax.rsqrt(jnp.mean(inputs * inputs, axis=-1, keepdims=True) + NORM_EPS)
    cotan[...] = dot(order_low, cotangent[...]).astype(BF16)
    step = 2 * LANES
    for at in range(0, inner, step):
        lanes = slice(at, at + step)
        dgz_out[:, lanes] = dot_cols(cotan[...], out_weight[lanes, :])
    in_x[...] = in_weight[:, 0:inner]

    io.ready()
    start = lax.axis_index("seq") * rows
    slots = lax.axis_size("seq") * rows
    ends = image_ends(heights, widths)
    images = heights.shape[1]
    picked = jnp.where(order, jnp.broadcast_to(valid[...].astype(F32), order.shape), 0.0)
    alive = dot(picked.astype(BF16), jnp.ones((rows, LANES), BF16))
    places = places_of(start, rows)
    segment = segment_of(places, ends)
    live[...] = jnp.where(segment < images, alive, 0.0)
    for k in range(1, reach + 1):
        same = (segment_of(places - k, ends) == segment) & (places >= k)
        same_out[(k - 1) * rows : k * rows, :] = same.astype(F32)
        same = (segment_of(places + k, ends) == segment) & (places + k < slots)
        same_out[(reach + k - 1) * rows : (reach + k) * rows, :] = same.astype(F32)
    near_row = lax.broadcasted_iota(jnp.int32, (2 * CHUNKS, LANES), 0)
    near_place = jnp.where(
        near_row < CHUNKS, start - CHUNKS + near_row, start + rows + near_row - CHUNKS
    )
    halo_live[...] = (segment_of(near_place, ends) < images).astype(F32)

    gains = gain[...].astype(F32).reshape(1, width)
    gains_out[...] = jnp.broadcast_to(gains, gains_out.shape)
    scaled = inputs * inv_rms * gains
    normed = scaled.astype(BF16)
    normed_out[...] = normed
    live_wide = jnp.concatenate([live[...]] * (width // LANES), axis=1)
    normed_live = (scaled * live_wide).astype(BF16)
    for at in range(0, inner, step):
        lanes = slice(at, at + step)
        x_out[:, lanes] = dot(normed_live, in_x[:, lanes]).astype(BF16).astype(F32)
        zs_out[:, lanes] = dot(normed, in_weight[:, inner + at : inner + at + step])
    block = 32

    def gate_block(b, _):
        here = pl.ds(pl.multiple_of(b * block, block), block)
        alive = live[here, :]
        for tile in range(tiles):
            lanes = slice(tile * LANES, (tile + 1) * LANES)
            z = zs_out[here, lanes]
            grad = dgz_out[here, lanes] * alive
            gate = sigmoid(z)
            zs = z * gate * alive
            zs_out[here, lanes] = zs
            dy[here, lanes] = 0.5 * grad * zs
            dgz_out[here, lanes] = grad * (gate * (1.0 + z * (1.0 - gate)))
        return 0

    lax.fori_loop(0, rows // block, gate_block, 0, unroll=8)
    for copy in arriving:
        copy.wait()


def middle_kernel(
    io, dy, live, same_out, from_core, from_chip, x, in_x, halo_live, gains, conv_weight, conv_bias,
    xproj, dt_weight, dt_bias, a_log, skip,
    sum_out, sent_out, delta_out, s_out, dsilu_out, tail_out, head_out, xext_out, proj_out,
    before_out, after_out, rate_out, nhalo_out,
    low_out, bc, tails, heads, spans,
    *, reach,
):
    rows, inner = x.shape
    width = in_x.shape[0]
    steps = rows // CHUNKS
    state = a_log.shape[1]
    rank = dt_weight.shape[1]
    tiles = inner // LANES
    even = (lax.axis_index("seq") & 1) == 0
    sublane = lax.broadcasted_iota(jnp.int32, (CHUNKS, LANES), 0)
    wide = lax.broadcasted_iota(jnp.int32, (CHUNKS, inner), 0)
    xext_out[reach * CHUNKS : (reach + steps) * CHUNKS, :] = x[...]

    core, chip = from_core[...].astype(F32), from_chip[...].astype(F32)
    before = jnp.where(even, chip, core)
    after = jnp.where(even, core, chip)
    htok = jnp.concatenate([before[CHUNKS:], after[:CHUNKS]], axis=0)
    htok = htok * jnp.concatenate([halo_live[...]] * (width // LANES), axis=1)
    hinv = lax.rsqrt(jnp.mean(htok * htok, axis=-1, keepdims=True) + NORM_EPS)
    scaled = htok * hinv
    nhalo = (scaled * gains[0:1, :]).astype(BF16)
    nhalo_out[...] = jnp.concatenate([nhalo, scaled.astype(BF16)], axis=0)
    hx = dot(nhalo, in_x[...]).astype(BF16).astype(F32)
    for i in range(reach):
        to = steps - reach + i
        moved = pltpu.roll(x[to * CHUNKS : (to + 1) * CHUNKS, :], 1, axis=0)
        of = CHUNKS - reach + i
        xext_out[i * CHUNKS : (i + 1) * CHUNKS, :] = jnp.where(wide == 0, hx[of : of + 1], moved)
        moved = pltpu.roll(x[i * CHUNKS : (i + 1) * CHUNKS, :], CHUNKS - 1, axis=0)
        to = reach + steps + i
        of = CHUNKS + i
        xext_out[to * CHUNKS : (to + 1) * CHUNKS, :] = jnp.where(
            wide == CHUNKS - 1, hx[of : of + 1], moved
        )

    block = 64
    step = 2 * LANES
    taps = reach + 1
    conv_w = [conv_weight[d].astype(F32) for d in range(2)]
    conv_b = conv_bias[...].astype(F32)
    for tile in range(tiles):
        lanes = slice(tile * LANES, (tile + 1) * LANES)

        def conv_block(b, _, lanes=lanes):
            at = pl.multiple_of(b * block, block)
            for d in range(2):
                total = conv_b[d : d + 1, lanes] + conv_w[d][reach:taps, lanes] * (
                    xext_out[pl.ds(at + reach * CHUNKS, block), lanes]
                )
                for k in range(1, taps):
                    move = reach - k if d == 0 else reach + k
                    mask = same_out[pl.ds((d * reach + k - 1) * rows + at, block), :]
                    total = total + conv_w[d][reach - k : taps - k, lanes] * (
                        xext_out[pl.ds(at + move * CHUNKS, block), lanes] * mask
                    )
                gate = sigmoid(total)
                value = total * gate
                s_out[pl.ds(d * rows + at, block), lanes] = value
                low_out[pl.ds(d * rows + at, block), lanes] = value.astype(BF16)
                dsilu_out[pl.ds(d * rows + at, block), lanes] = gate * (1.0 + total * (1.0 - gate))
            return 0

        lax.fori_loop(0, rows // block, conv_block, 0, unroll=4)

    dt_b = dt_bias[...].astype(F32)
    for d in range(2):
        rate_out[d * state : (d + 1) * state, :] = jnp.minimum(
            -LOG2E * jnp.exp(a_log[d].astype(F32)), -1e-20
        )
        here = slice(d * rows, (d + 1) * rows)
        proj = dot_cols(low_out[here, :], xproj[d])
        proj_out[here, :] = proj
        dt_low = proj[:, :rank].astype(BF16)
        for at in range(0, inner, step):
            lanes = slice(at, at + step)
            delta_out[here, lanes] = dot(dt_low, dt_weight[d, :, lanes])
        spread(proj[:, rank:], bc)

        def delta_block(b, _, d=d):
            alive = live[pl.ds(pl.multiple_of(b * block, block), block), :]
            here = pl.ds(pl.multiple_of(d * rows + b * block, block), block)
            for tile in range(tiles):
                lanes = slice(tile * LANES, (tile + 1) * LANES)
                pre = delta_out[here, lanes] + dt_b[d : d + 1, lanes]
                small = jnp.exp(-jnp.abs(pre))
                log1p = jnp.where(small < 1e-4, small * (1.0 - 0.5 * small), jnp.log(1.0 + small))
                delta_out[here, lanes] = (jnp.maximum(pre, 0.0) + log1p) * alive
            return 0

        lax.fori_loop(0, rows // block, delta_block, 0, unroll=4)
        some = SUMMARY_STATES

        def scan_tile(tile, _, d=d):
            lanes = lanes_of(tile)
            for low in range(0, state, some):
                rates = [
                    jnp.broadcast_to(
                        rate_out[d * state + low + m : d * state + low + m + 1, lanes],
                        (CHUNKS, LANES),
                    )
                    for m in range(some)
                ]

                def scan_step(i, carried, d=d, low=low, rates=rates):
                    tail, lead, head, span = carried
                    j = i if d == 0 else steps - 1 - i
                    at = pl.multiple_of(j * CHUNKS, CHUNKS)
                    keep = same_out[pl.ds(d * reach * rows + at, CHUNKS), :]
                    delta = delta_out[pl.ds(d * rows + at, CHUNKS), lanes]
                    drive = delta * s_out[pl.ds(d * rows + at, CHUNKS), lanes]
                    back = dy[pl.ds(at, CHUNKS), lanes]
                    delta = jnp.maximum(delta, BREAK - keep * BREAK)
                    tail, lead, head = list(tail), list(lead), list(head)
                    for m in range(some):
                        b = bc[pl.ds(at, CHUNKS), (low + m) * LANES : (low + m + 1) * LANES]
                        n = state + low + m
                        c = bc[pl.ds(at, CHUNKS), n * LANES : (n + 1) * LANES]
                        decay = jnp.exp2(delta * rates[m])
                        tail[m] = decay * tail[m] + b * drive
                        lead[m] = lead[m] * decay
                        head[m] = head[m] + lead[m] * (c * back)
                    return tuple(tail), tuple(lead), tuple(head), span + delta

                zeros = tuple(jnp.zeros((CHUNKS, LANES), F32) for _ in range(some))
                ones = tuple(jnp.ones((CHUNKS, LANES), F32) for _ in range(some))
                tail, lead, head, span = lax.fori_loop(
                    0, steps, scan_step, (zeros, ones, zeros, zeros[0]), unroll=SUMMARY_UNROLL
                )
                for m in range(some):
                    tails[low + m, :, lanes] = tail[m]
                    heads[low + m, :, lanes] = head[m]
                spans[:, lanes] = span
            return 0

        lax.fori_loop(0, tiles, scan_tile, 0)

        tail_row = 0 if d == 0 else 2 * state
        head_row = 3 * state if d == 0 else state

        def chain_tile(tile, _, d=d, tail_row=tail_row, head_row=head_row):
            lanes = lanes_of(tile)
            span = spans[:, lanes]
            sums, before = windows(span, d == 0, sublane)
            sums_back, after = windows(span, d == 1, sublane)
            before_out[d * CHUNKS : (d + 1) * CHUNKS, lanes] = before
            after_out[d * CHUNKS : (d + 1) * CHUNKS, lanes] = after
            for n in range(state):
                rate = jnp.broadcast_to(
                    rate_out[d * state + n : d * state + n + 1, lanes], (CHUNKS, LANES)
                )
                carried, total = chain(rate, sums, tails[n, :, lanes], d == 0, sublane)
                tail_out[d * state + n, :, lanes] = carried
                sum_out[tail_row + n : tail_row + n + 1, lanes] = total
                carried, total = chain(rate, sums_back, heads[n, :, lanes], d == 1, sublane)
                head_out[d * state + n, :, lanes] = carried
                sum_out[head_row + n : head_row + n + 1, lanes] = total
            return 0

        lax.fori_loop(0, tiles, chain_tile, 0, unroll=2)
        sum_out[4 * state + d : 4 * state + d + 1, :] = jnp.sum(spans[...], axis=0, keepdims=True)
    at = 4 * state + CHUNKS
    sum_out[4 * state + 2 : at, :] = jnp.zeros((CHUNKS - 2, inner), F32)
    sum_out[at:, :] = rate_out[0 : 2 * state, :]
    sent_out[...] = packed(sum_out[0:at, :], state)
    rate_out[2 * state : 2 * state + 2, :] = skip[...].astype(F32)


def packed(summary, state):
    rest = summary[4 * state :]
    high = rest.astype(BF16).astype(F32)
    return jnp.concatenate([summary[: 4 * state], high, rest - high], axis=0).astype(BF16)


def leads(rate, spans, state, flip):
    parts = [jnp.exp2(rate[d * state : (d + 1) * state] * spans[d : d + 1]) for d in range(2)]
    return jnp.concatenate(parts[::-1] if flip else parts, axis=0)


def join_kernel(io, got, summary, entered, *outs, state, bit, final):
    half = 2 * state
    upper = ((lax.axis_index("seq") >> bit) & 1) == 1
    mine = summary[0 : 2 * half + CHUNKS, :]
    rates = summary[2 * half + CHUNKS :, :]
    entered_out, sent_out = outs[-2], outs[-1]
    values = got[...].astype(F32)
    spans = mine[4 * state : 4 * state + 2]
    other = values[4 * state : 4 * state + 2] + values[4 * state + CHUNKS : 4 * state + CHUNKS + 2]
    if entered is None:
        entered_up = jnp.where(upper, values[:half], 0.0)
        entered_down = jnp.where(upper, 0.0, values[half : 2 * half])
        span_up = jnp.where(upper, other, 0.0)
        span_down = jnp.where(upper, 0.0, other)
    else:
        held = entered[...]
        span_up, span_down = held[2 * half : 2 * half + 2], held[2 * half + 2 : 2 * half + 4]
        entered_up = held[:half] + jnp.where(
            upper, leads(rates, span_up, state, False) * values[:half], 0.0
        )
        entered_down = held[half : 2 * half] + jnp.where(
            upper, 0.0, leads(rates, span_down, state, True) * values[half : 2 * half]
        )
        span_up = span_up + jnp.where(upper, other, 0.0)
        span_down = span_down + jnp.where(upper, 0.0, other)
    entered_out[0:half, :] = entered_up
    entered_out[half : 2 * half, :] = entered_down
    entered_out[2 * half :, :] = jnp.concatenate(
        [span_up, span_down, jnp.zeros((CHUNKS - 4, mine.shape[1]), F32)], axis=0
    )
    low_up = jnp.where(upper, values[:half], mine[:half])
    high_up = jnp.where(upper, mine[:half], values[:half])
    low_down = jnp.where(upper, values[half : 2 * half], mine[half : 2 * half])
    high_down = jnp.where(upper, mine[half : 2 * half], values[half : 2 * half])
    low_span, high_span = jnp.where(upper, other, spans), jnp.where(upper, spans, other)
    up = leads(rates, high_span, state, False) * low_up + high_up
    down = leads(rates, low_span, state, True) * high_down + low_down
    if final:
        next_upper = ((lax.axis_index("seq") >> (bit + 1)) & 1) == 1
        sent_out[...] = jnp.where(next_upper, down, up).astype(BF16)
    else:
        total = jnp.concatenate(
            [up, down, spans + other, jnp.zeros((CHUNKS - 2, mine.shape[1]), F32)], axis=0
        )
        outs[0][0 : 2 * half + CHUNKS, :] = total
        outs[0][2 * half + CHUNKS :, :] = rates
        sent_out[...] = packed(total, state)


def first_join(io, got, summary, *outs, state, bit, final):
    join_kernel(io, got, summary, None, *outs, state=state, bit=bit, final=final)


def state_block(j, state):
    return pl.multiple_of(j * state * CHUNKS, CHUNKS)


def states_pass(d, steps, state, rates, begin, delta, s, keep, bc, h_out, y):
    start = state_block(0 if d == 0 else steps, state)
    for n in range(state):
        h_out[pl.ds(start + n * CHUNKS, CHUNKS), :] = begin[n]

    def step(i, h):
        j = i if d == 0 else steps - 1 - i
        here = pl.ds(pl.multiple_of(j * CHUNKS, CHUNKS), CHUNKS)
        to = state_block(j + 1 if d == 0 else j, state)
        size = delta[here, :]
        drive = size * s[here, :]
        size = jnp.maximum(size, BREAK - keep[here, :] * BREAK)
        h = list(h)
        parts = [None if d == 0 else y[here, :], None]
        for n in range(state):
            b = bc[here, n * LANES : (n + 1) * LANES]
            c = bc[here, (state + n) * LANES : (state + n + 1) * LANES]
            h[n] = jnp.exp2(size * rates[n]) * h[n] + b * drive
            h_out[pl.ds(to + n * CHUNKS, CHUNKS), :] = h[n]
            part = parts[n % 2]
            parts[n % 2] = c * h[n] if part is None else part + c * h[n]
        y[here, :] = parts[0] + parts[1]
        return tuple(h)

    lax.fori_loop(0, steps, step, tuple(begin), unroll=STATES_UNROLL)


def adjoint_pass(
    d, steps, state, rates, back, delta, s, dy, keep, skip, bc, h_in, sums,
    dpre_out, ds_out, rows_out,
):
    some = ADJOINT_STATES
    edge = steps - 1
    skip = skip[...]
    zeros = jnp.zeros((CHUNKS, LANES), F32)
    grads = []
    for low in range(0, state, some):
        final = low + some == state

        def step(i, carried, low=low, final=final):
            g, acc, h, skip_acc, bias_acc = carried
            j = edge - i if d == 0 else i
            here = pl.ds(pl.multiple_of(j * CHUNKS, CHUNKS), CHUNKS)
            size = delta[here, :]
            value = s[here, :]
            grad = dy[here, :]
            drive = size * value
            masked = jnp.maximum(size, BREAK - keep[here, :] * BREAK)
            prev = state_block(j if d == 0 else j + 1, state)
            g, acc, h = list(g), list(acc), list(h)
            weighted = zeros if low == 0 else ds_out[here, :]
            rate_sum = zeros if low == 0 else dpre_out[here, :]
            for m in range(some):
                n = low + m
                b = bc[here, n * LANES : (n + 1) * LANES]
                c = bc[here, (state + n) * LANES : (state + n + 1) * LANES]
                adjoint = c * grad + g[m]
                before = h_in[pl.ds(prev + n * CHUNKS, CHUNKS), :]
                sums[here, n * LANES : (n + 1) * LANES] += adjoint * drive
                sums[here, (state + n) * LANES : (state + n + 1) * LANES] += grad * h[m]
                g[m] = adjoint * jnp.exp2(masked * rates[n])
                held = g[m] * before
                weighted = weighted + adjoint * b
                rate_sum = rate_sum + held * rates[n]
                acc[m] = acc[m] + held * masked
                h[m] = before
            if final:
                ds_out[here, :] = skip * grad + size * weighted
                gate = jnp.where(
                    size < 0.01, size * (1.0 - size * (0.5 - size * (1.0 / 6.0))), 1.0 - jnp.exp(-size)
                )
                pre = ((LN2 * rate_sum + weighted * value) * gate).astype(BF16).astype(F32)
                dpre_out[here, :] = pre
                bias_acc = bias_acc + pre
                skip_acc = skip_acc + grad * value
            else:
                dpre_out[here, :] = rate_sum
                ds_out[here, :] = weighted
            return tuple(g), tuple(acc), tuple(h), skip_acc, bias_acc

        last = state_block(steps if d == 0 else 0, state)
        h_last = tuple(h_in[pl.ds(last + (low + m) * CHUNKS, CHUNKS), :] for m in range(some))
        none = tuple(zeros for _ in range(some))
        _, acc, _, skip_acc, bias_acc = lax.fori_loop(
            0, steps, step, (tuple(back[low : low + some]), none, h_last, zeros, zeros),
            unroll=ADJOINT_UNROLL,
        )
        grads.extend(acc)
    for n in range(state):
        rows_out[n : n + 1, :] = jnp.sum(grads[n], axis=0, keepdims=True) * rates[n][0:1] * LN2
    rows_out[state : state + 1, :] = jnp.sum(bias_acc, axis=0, keepdims=True)
    rows_out[state + 1 : state + 2, :] = jnp.sum(skip_acc, axis=0, keepdims=True)


def lane_sums(sums, state):
    column = lax.broadcasted_iota(jnp.int32, (2 * CHUNKS, LANES), 1)
    picks = [(column == n).astype(BF16) for n in range(2 * state)]
    pick = jnp.concatenate([p for p in picks for _ in range(LANES // (2 * CHUNKS))], axis=0)
    return dot(sums.astype(BF16), pick)[:, : 2 * state]


def rate_tiles(rate, d, state, lanes):
    return [
        jnp.broadcast_to(rate[d * state + n : d * state + n + 1, lanes], (CHUNKS, LANES))
        for n in range(state)
    ]


def begin_tiles(rates, passed, maps, carry, at, d, state, lanes):
    passed = passed[d * CHUNKS : (d + 1) * CHUNKS, lanes]
    return [
        jnp.exp2(rates[n] * passed) * carry[at + n : at + n + 1, lanes]
        + maps[d * state + n, :, lanes]
        for n in range(state)
    ]


def slot_order(rows):
    row = lax.broadcasted_iota(jnp.int32, (rows, rows), 1)
    slot = lax.broadcasted_iota(jnp.int32, (rows, rows), 0)
    return (slot == (row & (CHUNKS - 1)) * (rows // CHUNKS) + (row >> 3)).astype(BF16)


def states_kernel(
    io, delta, s, proj, rate, same, normed, before, tail, got, entered, zs, dgz, cotan,
    kept, sent, carry_out, dz, h0, h1, gated,
    bc, y,
    *, reach, rank, state, bit,
):
    rows, inner = zs.shape
    width = cotan.shape[1]
    steps = rows // CHUNKS
    half = 2 * state
    tiles = inner // LANES
    upper = ((lax.axis_index("seq") >> bit) & 1) == 1
    values = got[...].astype(F32)
    held = entered[...]
    rates = rate[0:half, :]
    carry_out[0:half, :] = held[:half] + jnp.where(
        upper, leads(rates, held[2 * half : 2 * half + 2], state, False) * values, 0.0
    )
    carry_out[half : 2 * half, :] = held[half : 2 * half] + jnp.where(
        upper, 0.0, leads(rates, held[2 * half + 2 : 2 * half + 4], state, True) * values
    )
    for d, h in enumerate((h0, h1)):
        mine = slice(d * rows, (d + 1) * rows)
        spread(proj[mine, rank:], bc)
        keep = same.at[d * reach * rows : (d * reach + 1) * rows, :]

        def scan_tile(tile, _, d=d, h=h, mine=mine, keep=keep):
            lanes = lanes_of(tile)
            rates = rate_tiles(rate, d, state, lanes)
            begin = begin_tiles(rates, before, tail, carry_out, d * half, d, state, lanes)
            states_pass(
                d, steps, state, rates, begin, delta.at[mine, lanes], s.at[mine, lanes],
                keep, bc, h.at[tile], y.at[:, lanes],
            )
            return 0

        lax.fori_loop(0, tiles, scan_tile, 0)
    block = 32

    def gate_block(b, _):
        here = pl.ds(pl.multiple_of(b * block, block), block)
        there = pl.ds(pl.multiple_of(rows + b * block, block), block)
        for tile in range(tiles):
            lanes = slice(tile * LANES, (tile + 1) * LANES)
            total = 0.5 * (
                y[here, lanes] + rate[half : half + 1, lanes] * s[here, lanes]
                + rate[half + 1 : half + 2, lanes] * s[there, lanes]
            )
            gated[here, lanes] = (total * zs[here, lanes]).astype(BF16)
            dz[here, lanes] = (total * dgz[here, lanes]).astype(BF16)
        return 0

    lax.fori_loop(0, rows // block, gate_block, 0, unroll=8)
    even = (lax.axis_index("seq") & 1) == 0
    out_grad = dot_rows(gated[...], cotan[...]).astype(BF16)
    z_grad = jnp.concatenate(
        [dot_rows(normed[...], dz[:, at : at + width]) for at in range(0, inner, width)], axis=0
    ).astype(BF16)
    sent[...] = jnp.where(even, z_grad, out_grad)
    kept[...] = jnp.where(even, out_grad, z_grad)


def output_kernel(io, gated, tokens, out_weight, output):
    ordered = dot(slot_order(gated.shape[0]), gated[...]).astype(BF16)
    io.ready()
    output[...] = (tokens[...].astype(F32) + dot(ordered, out_weight[...])).astype(BF16)


def adjoint_kernel(
    io, delta, s, dsilu, dy, head, xext, proj, after, rate, same, carry, h, dx_in,
    dt_weight, xproj, conv_weight,
    dc_rim, small_out, dx_out,
    bc, sums, dpre, ds, rows_out, ext,
    *, d, reach, rank, state,
):
    rows, inner = dy.shape
    steps = rows // CHUNKS
    half = 2 * state
    tiles = inner // LANES
    taps = reach + 1
    cols = proj.shape[1]
    mine = slice(d * rows, (d + 1) * rows)
    keep = same.at[d * reach * rows : (d * reach + 1) * rows, :]
    spread(proj[mine, rank:], bc)
    sums[...] = jnp.zeros_like(sums)
    rows_out[...] = jnp.zeros_like(rows_out)
    grad_at = (half if d == 0 else 0) + state

    def scan_tile(tile, _):
        lanes = lanes_of(tile)
        rates = rate_tiles(rate, d, state, lanes)
        back = begin_tiles(rates, after, head, carry, grad_at, d, state, lanes)
        adjoint_pass(
            d, steps, state, rates, back, delta.at[mine, lanes], s.at[mine, lanes],
            dy.at[:, lanes], keep, rate.at[half + d : half + d + 1, lanes], bc,
            h.at[tile], sums, dpre.at[:, lanes], ds.at[:, lanes], rows_out.at[:, lanes],
        )
        return 0

    lax.fori_loop(0, tiles, scan_tile, 0)
    io.ready()
    dpre_low = dpre[...].astype(BF16)
    dt_grad = dot_rows(proj[mine, :rank].astype(BF16), dpre_low)
    dt_back = dot_cols(dpre_low, dt_weight[d])
    dproj = jnp.concatenate([dt_back, lane_sums(sums[...], state)], axis=1).astype(BF16)
    small_out[0:cols, :] = dot_rows(dproj, s[mine, :].astype(BF16))
    small_out[cols : cols + rank, :] = dt_grad
    base = 0 if d == 0 else reach * CHUNKS
    step = 2 * LANES
    for lane in range(0, inner, step):
        lanes = slice(lane, lane + step)
        total = ds[:, lanes] + dot(dproj, xproj[d, :, lanes])
        ext[base : base + rows, lanes] = (total * dsilu[mine, lanes]).astype(BF16).astype(F32)
    wide = lax.broadcasted_iota(jnp.int32, (CHUNKS, inner), 0)
    for i in range(reach):
        if d == 0:
            moved = pltpu.roll(ext[i * CHUNKS : (i + 1) * CHUNKS, :], CHUNKS - 1, axis=0)
            ext[rows + i * CHUNKS : rows + (i + 1) * CHUNKS, :] = jnp.where(
                wide == CHUNKS - 1, 0.0, moved
            )
        else:
            moved = pltpu.roll(ext[rows + i * CHUNKS : rows + (i + 1) * CHUNKS, :], 1, axis=0)
            ext[i * CHUNKS : (i + 1) * CHUNKS, :] = jnp.where(wide == 0, 0.0, moved)

    conv_w = conv_weight[d].astype(F32)
    block = 64
    zeros = jnp.zeros((CHUNKS, LANES), F32)

    def folded(values):
        return functools.reduce(
            lambda a, b: a + b, [values[i : i + CHUNKS] for i in range(0, block, CHUNKS)]
        )

    base_row = cols + rank
    for tile in range(tiles):
        lanes = slice(tile * LANES, (tile + 1) * LANES)
        weight = conv_w[:, lanes]

        def conv_block(b, totals, lanes=lanes, weight=weight):
            here = pl.multiple_of(b * block, block)
            totals = list(totals)
            mid = ext[pl.ds(here + base, block), lanes]
            total = weight[reach:taps] * mid
            totals[reach] = totals[reach] + folded(mid * xext[pl.ds(here + reach * CHUNKS, block), lanes])
            totals[taps] = totals[taps] + folded(mid)
            for k in range(1, taps):
                past = same[pl.ds((k - 1) * rows + here, block), :]
                ahead = same[pl.ds((reach + k - 1) * rows + here, block), :]
                if d == 0:
                    given = ext[pl.ds(here + k * CHUNKS, block), lanes] * ahead
                    taken = xext[pl.ds(here + (reach - k) * CHUNKS, block), lanes] * past
                else:
                    given = ext[pl.ds(here + (reach - k) * CHUNKS, block), lanes] * past
                    taken = xext[pl.ds(here + (reach + k) * CHUNKS, block), lanes] * ahead
                total = total + weight[reach - k : taps - k] * given
                totals[reach - k] = totals[reach - k] + folded(mid * taken)
            if dx_in is not None:
                total = total + dx_in[pl.ds(here, block), lanes]
            dx_out[pl.ds(here, block), lanes] = total
            return tuple(totals)

        totals = lax.fori_loop(0, rows // block, conv_block, (zeros,) * (taps + 1), unroll=4)
        for i in range(taps + 1):
            at = state + 2 + i
            rows_out[at : at + 1, lanes] = jnp.sum(totals[i], axis=0, keepdims=True)

    edge = []
    for i in range(CHUNKS):
        row = jnp.zeros((1, inner), F32)
        for k in range(1, taps):
            j = i - CHUNKS + k if d == 0 else steps + i - k
            if (d == 0 and j >= 0) or (d == 1 and j < steps):
                sub = 0 if d == 0 else CHUNKS - 1
                at = (d * reach + k - 1) * rows + j * CHUNKS + sub
                mask = jnp.concatenate([same[at : at + 1, :]] * tiles, axis=1)
                at = base + j * CHUNKS + sub
                row = row + conv_w[reach - k : taps - k] * ext[at : at + 1, :] * mask
        edge.append(row)
    dc_rim[...] = jnp.concatenate(edge, axis=0)
    small_out[base_row:, :] = rows_out[0 : small_out.shape[0] - base_row, :]


def first_adjoint(io, *refs, **static):
    adjoint_kernel(io, *refs[:12], None, *refs[12:], **static)


def second_adjoint(io, *refs, **static):
    in_far, in_near, moves = refs[16], refs[20], refs[21]
    copy = fetch(in_far, in_near, moves.at[0])
    adjoint_kernel(io, *refs[:16], *refs[17:20], *refs[22:], **static)
    copy.wait()


def last_kernel(
    io, dx, rim0, rim1, small0, small1, normed, nhalo, live, in_weight,
    kept, sent, low,
    lines, grads,
):
    rows, inner = dx.shape
    width = normed.shape[1]
    folds = inner // width
    fold = kept.shape[0]
    edges = 2 * CHUNKS
    for tile in range(inner // LANES):
        lanes = slice(tile * LANES, (tile + 1) * LANES)
        lines[0:rows, lanes] = (dx[:, lanes] * live[...]).astype(BF16)
    low[...] = lines[0:rows, :]
    lines[rows : rows + edges, :] = jnp.concatenate([rim0[...], rim1[...]], axis=0).astype(BF16)
    both = jnp.concatenate([normed[...], nhalo[0:edges, :]], axis=0)
    size = small0.shape[0]
    for i in range(folds):
        lanes = slice(i * width, (i + 1) * width)
        at = i * fold
        grads[at : at + width, :] = dot_rows(both, lines[:, lanes]).astype(BF16)
        at += width
        grads[at : at + 2 * size, :] = jnp.concatenate(
            [small0[:, lanes], small1[:, lanes]], axis=0
        ).astype(BF16)
        at += 2 * size
        grads[at : (i + 1) * fold, :] = jnp.zeros(((i + 1) * fold - at, width), BF16)
    rim = dot_cols(lines[rows : rows + edges, :], in_weight[:, 0:inner])
    even = (lax.axis_index("seq") & 1) == 0
    turned = jnp.concatenate([rim[CHUNKS:], rim[:CHUNKS]], axis=0)
    left, right = grads[0:fold, :], grads[fold : 2 * fold, :]
    kept[...] = jnp.where(even, left, right)
    sent[...] = jnp.where(even, right, left)
    at = width + 2 * size
    sent[at : at + edges, :] = jnp.where(even, turned, rim).astype(BF16)


def finish_kernel(
    io, low, dz, in_weight, rims, chip_rim, heights, widths, tokens, cotangent, valid, gain,
    input_grad,
):
    rows, width = tokens.shape
    inner = low.shape[1]
    even = (lax.axis_index("seq") & 1) == 0
    start = lax.axis_index("seq") * rows
    back = slot_order(rows)
    dn = dot_cols(dot(back, low[...]).astype(BF16), in_weight[:, 0:inner]) + dot_cols(
        dot(back, dz[...]).astype(BF16), in_weight[:, inner : 2 * inner]
    )
    io.ready()
    from_core = rims[...].astype(F32)[:CHUNKS]
    from_chip = chip_rim[...].astype(F32)[CHUNKS:]
    before = jnp.where(even, from_chip, from_core)
    after = jnp.where(even, from_core, from_chip)
    end = image_ends(heights, widths)[-1]
    row = lax.broadcasted_iota(jnp.int32, (CHUNKS, rows), 0)
    slot = lax.broadcasted_iota(jnp.int32, (CHUNKS, rows), 1)
    alive = jnp.broadcast_to(valid[...].astype(F32), (CHUNKS, rows))
    alive = jnp.where(start + slot < end, alive, 0.0)
    first = jnp.sum(jnp.where(slot == row, alive, 0.0), axis=1, keepdims=True)
    last = jnp.sum(jnp.where(slot == rows - CHUNKS + row, alive, 0.0), axis=1, keepdims=True)
    values = jnp.concatenate(
        [
            dn[0:CHUNKS, :] + first * before, dn[CHUNKS : rows - CHUNKS, :],
            dn[rows - CHUNKS : rows, :] + last * after,
        ],
        axis=0,
    )
    inputs = tokens[...].astype(F32)
    inv_rms = lax.rsqrt(jnp.mean(inputs * inputs, axis=-1, keepdims=True) + NORM_EPS)
    scaled = values * gain[...].astype(F32).reshape(1, width)
    mean = jnp.mean(scaled * inputs, axis=-1, keepdims=True)
    input_grad[...] = (
        cotangent[...].astype(F32) + inv_rms * scaled - inputs * (inv_rms * inv_rms * inv_rms) * mean
    )


def blocks_in_order(mine, other, into_first, into_second):
    size = mine.shape[1]
    is_even = (lax.axis_index("seq") & 1) == 0
    here = lax.axis_index("img")
    for k in range(mine.shape[0]):
        a, b = mine[here ^ k].astype(F32), other[here ^ k].astype(F32)
        into_first(k * size, jnp.where(is_even, a, b))
        into_second(k * size, jnp.where(is_even, b, a))


def weighted_rows(values, weights):
    total = None
    for at in range(0, values.shape[1], LANES):
        part = values[:, at : at + LANES] * weights[:, at : at + LANES].astype(F32)
        total = part if total is None else total + part
    return total


def first_unpack(io, mine, other, in_weight, parts, in_far, out_far, out_w, z_half, moves):
    width = out_w.shape[1]
    inner = out_w.shape[0]

    def put_out(at, values):
        out_w[at : at + values.shape[0], :] = values

    def put_z(at, values):
        size = values.shape[0]
        column = at // width * width
        z_half[at % width : at % width + size, column : column + width] = values

    blocks_in_order(mine, other, put_out, put_z)
    leaving = [
        fetch(out_w, out_far, moves.at[0]),
        fetch(z_half, in_far.at[:, inner : 2 * inner], moves.at[1]),
    ]
    parts[...] = weighted_rows(z_half[...], in_weight[:, inner : 2 * inner])
    for copy in leaving:
        copy.wait()


def second_unpack(
    io, mine, other, in_weight, parts, gain_in, in_before,
    conv_w, conv_b, xproj, dt_w, dt_b, a_log, skip, in_far, gain_far,
    left, right, x_half, gain, moves,
    *, count, state, rank, cols, taps,
):
    width = left.shape[1]
    inner = x_half.shape[1]

    def put(target, lane):
        def at_rows(at, values):
            size = values.shape[0]
            target[at : at + size, :] = values
            top = min(width - at, size)
            if top > 0:
                x_half[at : at + top, lane : lane + width] = values[:top]

        return at_rows

    blocks_in_order(mine, other, put(left, 0), put(right, width))
    leaving = fetch(x_half, in_far.at[:, 0:inner], moves.at[0])
    for i, half in enumerate((left, right)):
        lanes = slice(i * width, (i + 1) * width)
        for d in range(2):
            at = width + d * count
            xproj[d, :, lanes] = half[at : at + cols, :]
            at += cols
            dt_w[d, :, lanes] = half[at : at + rank, :]
            at += rank
            a_log[d, :, lanes] = half[at : at + state, :]
            dt_b[d : d + 1, lanes] = half[at + state : at + state + 1, :]
            skip[d : d + 1, lanes] = half[at + state + 1 : at + state + 2, :]
            at += state + 2
            conv_w[d, :, lanes] = half[at : at + taps, :]
            conv_b[d : d + 1, lanes] = half[at + taps : at + taps + 1, :]
    io.ready()
    io.done()
    total = parts[...] + weighted_rows(x_half[...], in_weight[:, 0:inner])
    high = total.astype(BF16)
    rest = (total - high.astype(F32)).astype(BF16)
    ones = jnp.ones((2 * CHUNKS, LANES), BF16)
    sums = (dot_cols(ones, high) + dot_cols(ones, rest))[0:1]
    gain[...] = (sums / gain_in[...].astype(F32).reshape(1, width)).reshape(width)
    last = fetch(gain, gain_far, moves.at[1])
    leaving.wait()
    last.wait()


IN_VMEM = pl.BlockSpec(memory_space=pltpu.VMEM)
IN_SMEM = pl.BlockSpec(memory_space=pltpu.SMEM)
FAR = pl.BlockSpec(memory_space=pltpu.HBM)


def shape(*dims, dtype=F32):
    return jax.ShapeDtypeStruct(dims, dtype)


def low(*dims):
    return jax.ShapeDtypeStruct(dims, BF16)


def near(*dims, dtype=F32):
    return pltpu.VMEM(dims, dtype)


def scratch(*dims, dtype=F32):
    return pltpu.VMEM(dims, dtype)


def like(*outs):
    return [pltpu.VMEM(out.shape, out.dtype) for out in outs]


def moves(*dims):
    return pltpu.SemaphoreType.DMA(dims)


class Moves:
    def __init__(self, arrive, leave):
        self.arrive, self.leave, self.left = arrive, leave, False
        for copy in arrive:
            copy.start()

    def ready(self):
        for copy in self.arrive:
            copy.wait()

    def done(self):
        self.left = True
        for copy in self.leave:
            copy.start()


def call(
    kernel, name, args, outs, scratches=(), far=(), far_outs=(), near_args=(), near_outs=(),
    scalars=(), handed=(), aliases=(), us=4, limit=4,
):
    small = tuple(scalars) + tuple(args)
    small, far = (
        tuple(pltpu.with_memory_space_constraint(x, pltpu.HBM) for x in arrays)
        for arrays in (small, far)
    )
    n_hand = len(handed)
    near_args = tuple(handed) + tuple(near_args)
    n_near, n_small, n_far = len(near_args), len(small), len(far)
    n_near_outs, n_outs, n_far_outs = len(near_outs), len(outs), len(far_outs)

    def wrapped(*refs):
        refs = list(refs)

        def take(count):
            taken = refs[:count]
            del refs[:count]
            return taken

        near_in, small_in, far_in = take(n_near), take(n_small), take(n_far)
        near_out, out, far_out = take(n_near_outs), take(n_outs), take(n_far_outs)
        take(n_hand)
        small_here, out_here = take(n_small), take(n_outs)
        in_moves, out_moves = take(2)
        io = Moves(
            [pltpu.make_async_copy(a, b, in_moves.at[i]) for i, (a, b) in enumerate(zip(small_in, small_here))],
            [pltpu.make_async_copy(a, b, out_moves.at[i]) for i, (a, b) in enumerate(zip(out_here, out))],
        )
        kernel(io, *near_in, *small_here, *far_in, *near_out, *out_here, *far_out, *refs)
        if not io.left:
            io.done()
        for copy in io.leave:
            copy.wait()

    return pl.pallas_call(
        wrapped,
        out_shape=list(near_outs) + [
            pltpu.HBM(out.shape, out.dtype) for out in tuple(outs) + tuple(far_outs)
        ] + [pltpu.VMEM(x.shape, x.dtype) for x in handed],
        in_specs=[IN_VMEM] * n_near + [FAR] * (n_small + n_far),
        out_specs=[IN_VMEM] * n_near_outs + [FAR] * (n_outs + n_far_outs) + [IN_VMEM] * n_hand,
        input_output_aliases={
            **{i: n_near_outs + n_outs + n_far_outs + i for i in range(n_hand)},
            **{n_near + n_small + i: n_near_outs + n_outs + o for i, o in aliases},
        },
        scratch_shapes=(
            [pltpu.SMEM(a.shape, a.dtype) for a in scalars] + like(*args) + like(*outs)
            + [moves(max(n_small, 1)), moves(max(n_outs, 1))] + list(scratches)
        ),
        compiler_params=pltpu.CompilerParams(vmem_limit_bytes=limit * 2**20),
        cost_estimate=pl.CostEstimate(flops=us * 2000000000, bytes_accessed=0, transcendentals=0),
        name=name,
    )(*near_args, *small, *far)


def call_edges(tokens, valid):
    edge = 2 * CHUNKS
    width = tokens.shape[1]
    outs = [near(edge, width, dtype=BF16), near(edge, width, dtype=BF16)]
    ends = [scratch(edge, width, dtype=BF16), scratch(edge, width, dtype=BF16), moves(2)]
    return call(
        edges_kernel, "edges", (valid,), (), ends, (tokens,), near_outs=outs, us=1, limit=2
    )


def call_front(
    heights, widths, valid, gain, tokens, cotangent, in_weight, out_weight, weights, reach,
):
    rows, width = tokens.shape
    inner = out_weight.shape[0]
    one = near(rows, inner)
    row = near(rows, width, dtype=BF16)
    return call(
        functools.partial(front_kernel, reach=reach, weights=len(weights)), "front", (valid, gain), (),
        [moves(len(weights))], weights, (),
        tuple(
            pltpu.with_memory_space_constraint(x, pltpu.VMEM)
            for x in (tokens, cotangent, in_weight, out_weight)
        ),
        [
            row, one, one, one, one, near(rows, LANES), near(2 * reach * rows, LANES), row,
            near(width, inner, dtype=BF16), near(2 * CHUNKS, LANES), near(CHUNKS, width),
        ] + like(*weights),
        (heights, widths), us=4, limit=12,
    )


def call_middle(handed, used, from_core, from_chip, arrays, reach, cols):
    x, a_log = arrays[0], arrays[-2]
    rows, inner = x.shape
    state, width = a_log.shape[1], from_core.shape[1]
    half = 2 * state
    both = near(2 * rows, inner)
    maps = near(half, CHUNKS, inner)
    ends = near(2 * CHUNKS, inner)
    n_hand = len(handed)

    def kernel(io, *refs):
        middle_kernel(io, *(refs[i] for i in used), *refs[n_hand:], reach=reach)

    return call(
        kernel, "middle", (), (),
        [
            scratch(2 * rows, inner, dtype=BF16), scratch(rows, half * LANES),
            scratch(state, CHUNKS, inner), scratch(state, CHUNKS, inner), scratch(CHUNKS, inner),
        ],
        near_args=(from_core, from_chip) + arrays,
        near_outs=[
            near(2 * half + CHUNKS + half, inner), near(2 * half + 2 * CHUNKS, inner, dtype=BF16),
            both, both, both, maps, maps, near(rows + 2 * reach * CHUNKS, inner),
            near(2 * rows, cols), ends, ends, near(half + CHUNKS, inner),
            near(4 * CHUNKS, width, dtype=BF16),
        ],
        handed=handed, us=20, limit=9,
    )


def call_join(got, summary, entered, state, bit, final):
    inner = summary.shape[1]
    half = 2 * state
    outs = [
        near(2 * half + CHUNKS, inner),
        near(half if final else 2 * half + 2 * CHUNKS, inner, dtype=BF16),
    ]
    if not final:
        outs = [near(2 * half + CHUNKS + half, inner)] + outs
    args = (got, summary) + (() if entered is None else (entered,))
    kernel = first_join if entered is None else join_kernel
    joined = call(
        functools.partial(kernel, state=state, bit=bit, final=final), "join", (), (),
        near_args=args, near_outs=outs, us=1, limit=4,
    )
    return joined if not final else [None] + list(joined)


def call_states(handed, used, before, tail, got, entered, zs, dgz, cotan, rank, reach, state, bit):
    rows, inner = zs.shape
    width = cotan.shape[1]
    half = 2 * state
    n_hand = len(handed)

    def kernel(io, *refs):
        states_kernel(
            io, *(refs[i] for i in used), *refs[n_hand:], reach=reach, rank=rank, state=state, bit=bit
        )

    grad = near(inner, width, dtype=BF16)
    one = near(rows, inner, dtype=BF16)
    held = near(inner // LANES, (rows // CHUNKS + 1) * state * CHUNKS, LANES)
    return call(
        kernel, "states", (), (),
        [scratch(rows, half * LANES), scratch(rows, inner)],
        near_args=(before, tail, got, entered, zs, dgz, cotan),
        near_outs=[grad, grad, near(2 * half, inner), one, held, held, one], handed=handed, us=12,
        limit=9,
    )


def adjoint_scratch(rows, inner, half, reach, small, cols, rank):
    return [
        scratch(rows, half * LANES), scratch(rows, half * LANES), scratch(rows, inner), scratch(rows, inner), scratch(small - cols - rank, inner),
        scratch(rows + reach * CHUNKS, inner),
    ]


def call_first_adjoint(handed, used, h, weights, small, reach, rank, state):
    rows, inner = handed[used[3]].shape
    cols = handed[used[6]].shape[1]
    n_hand = len(handed)

    def kernel(io, *refs):
        first_adjoint(
            io, *(refs[i] for i in used), *refs[n_hand:], d=0, reach=reach, rank=rank, state=state
        )

    return call(
        kernel, "adjoint_up", weights, (),
        adjoint_scratch(rows, inner, 2 * state, reach, small, cols, rank), near_outs=[
            near(CHUNKS, inner), near(small, inner), near(rows, inner),
        ], near_args=(h,), handed=handed, us=14, limit=13,
    )


def call_second_adjoint(handed, arrays, weights, in_weight, small, reach, rank, state):
    rows, inner = arrays[3].shape
    cols = arrays[6].shape[1]
    n_hand = len(handed)

    def kernel(io, *refs):
        second_adjoint(io, *refs[n_hand:], d=1, reach=reach, rank=rank, state=state)

    return call(
        kernel, "adjoint_down", weights, (),
        [moves(1)] + adjoint_scratch(rows, inner, 2 * state, reach, small, cols, rank),
        (in_weight,), (), arrays,
        [near(CHUNKS, inner), near(small, inner), near(rows, inner), near(*in_weight.shape, dtype=BF16)],
        handed=handed, us=14, limit=13,
    )


def call_last(handed, dx, rim0, rim1, small0, small1, normed, nhalo, live):
    rows, inner = dx.shape
    width = normed.shape[1]
    small = small0.shape[0]
    folds = inner // width
    edges = 2 * CHUNKS
    fold = -(-(width + 2 * small + edges) // 64) * 64
    n_hand = len(handed)

    def kernel(io, *refs):
        last_kernel(io, *refs[n_hand : n_hand + 8], refs[n_hand - 1], *refs[n_hand + 8 :])

    return call(
        kernel, "last", (), (),
        [
            scratch(rows + edges, inner, dtype=BF16), scratch(folds * fold, width, dtype=BF16),
        ],
        near_args=(dx, rim0, rim1, small0, small1, normed, nhalo, live),
        near_outs=[
            near(fold, width, dtype=BF16), near(fold, width, dtype=BF16),
            near(rows, inner, dtype=BF16),
        ],
        handed=handed, us=3, limit=8,
    )


def partner(axis, bit):
    return [(i, i ^ (1 << bit)) for i in range(lax.axis_size(axis))]


def bits_of(axis):
    return (lax.axis_size(axis) - 1).bit_length()


def other_core(values):
    return lax.ppermute(values, "seq", partner("seq", 0))


def next_chip(values):
    count = lax.axis_size("seq")
    pairs = [(i, i + 1) for i in range(1, count - 1, 2)]
    return lax.ppermute(values, "seq", pairs + [(j, i) for i, j in pairs])


def split_kernel(io, kept, got, own, *sent, edges):
    if edges:
        at = got.shape[0] - edges[1]
        sent[-1][...] = got[at : at + edges[0], :]
        sent = sent[:-1]
    count = len(sent) + 1
    rows = own.shape[0]
    here = lax.axis_index("img")
    for k in range(count):
        at = pl.ds(pl.multiple_of((here ^ k) * rows, rows), rows)
        total = kept[at, :].astype(F32) + got[at, :].astype(F32)
        if k == 0:
            own[...] = total
        else:
            sent[k - 1][...] = total.astype(BF16)


def add_kernel(io, *refs, outs):
    total = refs[0][...].astype(F32)
    for ref in refs[1 : len(refs) - outs]:
        total = total + ref[...].astype(F32)
    for ref in refs[len(refs) - outs :]:
        ref[...] = total.astype(ref.dtype)


def add(values, whole=True):
    rows, width = values[0].shape
    outs = [near(rows, width)] * whole + [near(rows, width, dtype=BF16)]
    sums = call(
        functools.partial(add_kernel, outs=len(outs)), "add", (), (), near_args=values,
        near_outs=outs, us=1, limit=2,
    )
    return sums if whole else sums[0]


def add_rim_kernel(io, *refs, count, bit):
    values, moving, stay = refs[:count], refs[count], refs[count + 1]
    low_out, stay_out = refs[-2:]
    rows = values[0].shape[0]
    total = values[0][...]
    for ref in values[1:]:
        total = total + ref[0:rows, :].astype(F32)
    if len(refs) > count + 4:
        refs[-3][...] = total
    low_out[0:rows, :] = total.astype(BF16)
    if bit is None:
        low_out[rows:, :] = moving[...]
        stay_out[...] = jnp.zeros_like(stay_out)
        return
    came = values[-1][rows:, :]
    if low_out.shape[0] > rows:
        low_out[rows:, :] = came
    position = lax.axis_index("seq")
    chip = position >> 1
    chip = jnp.where((position & 1) == 0, chip, lax.axis_size("seq") // 2 - 1 - chip)
    lowest = chip & ((2 << bit) - 1)
    stay_out[...] = jnp.where(lowest == (1 << bit), came, stay[...])


def add_rim(values, moving, stay, bit, final=False):
    rows, width = values[0].shape
    edge = moving.shape[0]
    sent = rows if final else rows + edge
    outs = [near(rows, width)] * (not final)
    outs += [near(sent, width, dtype=BF16), near(edge, width, dtype=BF16)]
    sums = call(
        functools.partial(add_rim_kernel, count=len(values), bit=bit), "add", (), (),
        near_args=tuple(values) + (moving, stay), near_outs=outs, us=1, limit=2,
    )
    return [None] * final + list(sums)


def stack_kernel(io, *refs):
    for k, ref in enumerate(refs[:-1]):
        refs[-1][k] = ref[...]


def plane_pairs(k):
    return [(i, i ^ k) for i in range(lax.axis_size("img"))]


def chips_sum(kept, sent, edges=()):
    count = lax.axis_size("img")
    rows, width = kept.shape
    block = (rows // count, width)
    got = other_core(sent)
    own, *parts = call(
        functools.partial(split_kernel, edges=edges), "split", (), (), near_args=(kept, got),
        near_outs=[near(*block)] + [near(*block, dtype=BF16)] * (count - 1)
        + [near(rim_rows, width, dtype=BF16) for rim_rows in edges[:1]],
        us=1, limit=2,
    )
    rim = parts.pop() if edges else None
    blocks = [own] + [
        lax.ppermute(part, "img", plane_pairs(k + 1)) for k, part in enumerate(parts)
    ]
    return blocks, rim


def line_steps(total, low):
    bits = bits_of("seq")
    for bit in range(1, bits):
        got = lax.ppermute(low, "seq", partner("seq", bit))
        if bit < bits - 1:
            total, low = add([total, got])
        else:
            low = add([total, got], whole=False)
    return low


def line_steps_with_rims(blocks, rim, first_low, beside):
    stay = rim
    total, low, stay = add_rim(blocks, rim, stay, None)
    low, first_low = tied(low, first_low)
    bits = bits_of("seq")
    for bit in range(1, bits):
        got = lax.ppermute(low, "seq", partner("seq", bit))
        if bit == 1:
            first_blocks = plane_blocks(first_low)
        if bit == bits - 1:
            got, beside, *first_blocks = lax.optimization_barrier((got, beside, *first_blocks))
        total, low, stay = add_rim([total, got], rim, stay, bit - 1, bit == bits - 1)
    return low, stay, first_blocks, beside


def plane_blocks(low):
    count = lax.axis_size("img")
    return [low] + [lax.ppermute(low, "img", plane_pairs(k)) for k in range(1, count)]


def stacked(blocks):
    low, count = blocks[0], len(blocks)
    return call(
        stack_kernel, "stack", (), (), near_args=blocks,
        near_outs=[near(count, *low.shape, dtype=BF16)], us=1, limit=2,
    )[0]


def tied(first, second):
    return lax.optimization_barrier((first, second))


def body(
    tokens, cotangent, heights, widths, valid, norm_gain, in_weight, conv_weight, conv_bias,
    xproj_weight, dt_weight, dt_bias, a_log, skip, out_weight,
):
    rows, width = tokens.shape[1:]
    inner = out_weight.shape[0]
    state = a_log.shape[1]
    rank = dt_weight.shape[1]
    cols = xproj_weight.shape[2]
    taps = conv_weight.shape[1]
    reach = taps - 1
    count = bits_of("seq")
    tokens, cotangent = tokens[0], cotangent[0]
    xproj = xproj_weight.transpose(0, 2, 1)

    to_core, to_chip = call_edges(tokens, valid)
    from_core, from_chip = other_core(to_core), next_chip(to_chip)
    weights = (conv_weight, conv_bias, xproj, dt_weight, dt_bias, a_log, skip)
    normed, x, zs, dgz, dy, live, same, cotan, in_x, halo_live, gains, *near_weights = call_front(
        heights, widths, valid, norm_gain, tokens, cotangent, in_weight, out_weight, weights, reach
    )
    (
        summary, sent, delta, s, dsilu, tail, head, xext, proj, before, after, rate, nhalo,
        dy, live, same, normed, zs, dgz, cotan,
    ) = call_middle(
        (dy, live, same, normed, zs, dgz, cotan), (0, 1, 2), from_core, from_chip,
        (x, in_x, halo_live, gains) + tuple(near_weights), reach, cols,
    )
    entered = None
    for bit in range(count - 1):
        got = lax.ppermute(sent, "seq", partner("seq", bit))
        summary, entered, sent = call_join(got, summary, entered, state, bit, bit == count - 2)
    got = lax.ppermute(sent, "seq", partner("seq", count - 1))
    handed = (
        delta, s, dsilu, dy, head, xext, proj, after, rate, same, live, normed, nhalo,
    )
    kept, sent, carry, dz, h0, h1, gated, *handed = call_states(
        handed, (0, 1, 6, 8, 9, 11), before, tail, got, entered, zs, dgz, cotan, rank, reach, state,
        count - 1,
    )

    blocks, _ = chips_sum(kept, sent)
    small = -(-(cols + rank + state + 2 + taps + 1) // CHUNKS) * CHUNKS
    weights = (dt_weight, xproj, conv_weight)
    handed = tuple(handed[:10]) + (carry,) + tuple(handed[10:]) + (dz, gated, h1)
    rim0, small0, dx, *handed = call_first_adjoint(
        handed, tuple(range(11)), h0, weights, small, reach, rank, state
    )
    *blocks, dx = lax.optimization_barrier((*blocks, dx))
    first_sum, first_low = add(blocks)
    first_sum, first_low, dx = lax.optimization_barrier((first_sum, first_low, dx))
    arrays, passed, h1 = tuple(handed[:11]), tuple(handed[11:-1]), handed[-1]
    if bits_of("seq") > 3:
        first_low = line_steps(first_sum, first_low)
    else:
        devices = lax.axis_size("seq")
        blocks = [first_sum] + [
            lax.ppermute(first_low, "seq", [(i, i ^ k) for i in range(devices)])
            for k in range(2, devices, 2)
        ]
    rim1, small1, dx, in_near, *passed = call_second_adjoint(
        passed, arrays + (h1, dx), weights, in_weight, small, reach, rank, state
    )
    live, normed, nhalo, dz, gated = passed
    if bits_of("seq") <= 3:
        *blocks, dx = lax.optimization_barrier((*blocks, dx))
        first_low = add(blocks, whole=False)
    kept, sent, dx_low, dz, gated, in_near = call_last(
        (dz, gated, in_near), dx, rim0, rim1, small0, small1, normed, nhalo, live
    )

    edges = (2 * CHUNKS, kept.shape[0] - width - 2 * small)
    blocks, rim = chips_sum(kept, sent, edges)


    output = call(
        output_kernel, "output", (tokens, out_weight), [low(rows, width)], near_args=(gated,), us=2,
        limit=6,
    )[0]
    second_low, chip_rim, first_blocks, output = line_steps_with_rims(blocks, rim, first_low, output)
    blocks = plane_blocks(second_low)
    _, *first_blocks = lax.optimization_barrier((blocks[1], *first_blocks))
    first_mine = stacked(first_blocks)
    first_other = other_core(first_mine)
    input_grad = call(
        finish_kernel, "finish", (tokens, cotangent, valid, norm_gain), [shape(rows, width)],
        near_args=(dx_low, dz, in_near, rim, chip_rim), scalars=(heights, widths), us=3, limit=8,
    )[0]
    blocks, input_grad = lax.optimization_barrier((blocks, input_grad))
    second_mine = stacked(blocks)
    second_other = other_core(second_mine)
    parts, in_total, out_total = call(
        first_unpack, "unpack_first", (), (),
        [scratch(inner, width), scratch(width, inner), moves(2)],
        far_outs=[shape(width, 2 * inner), shape(inner, width)],
        near_args=(first_mine, first_other, in_near), near_outs=[near(width, LANES)], us=2, limit=8,
    )
    second_other, parts = tied(second_other, parts)
    fold = kept.shape[0]
    (
        conv_total, bias_total, xproj_total, dtw_total, dtb_total, a_total, skip_total, in_total,
        gain_total,
    ) = call(
        functools.partial(
            second_unpack, count=small, state=state, rank=rank, cols=cols, taps=taps
        ),
        "unpack_second", (norm_gain,),
        [
            shape(2, taps, inner), shape(2, inner), shape(2, cols, inner), shape(2, rank, inner),
            shape(2, inner), shape(2, state, inner), shape(2, inner),
        ],
        [
            scratch(fold, width), scratch(fold, width), scratch(width, inner), scratch(width),
            moves(2),
        ],
        (in_total,), [shape(width, 2 * inner), shape(width)], (second_mine, second_other, in_near, parts),
        aliases=((0, 0),), us=2, limit=10,
    )
    return (
        output[None], input_grad[None], gain_total, in_total, conv_total, bias_total,
        xproj_total.transpose(0, 2, 1), dtw_total, dtb_total, a_total, skip_total, out_total,
    )


def solution(mesh):
    split = P("img", "seq", None)
    placed = (split, split, P("img", None), P("img", None), P("img", "seq")) + (P(),) * 10
    return jax.shard_map(
        body,
        mesh=mesh,
        in_specs=placed,
        out_specs=(split, split) + (P(),) * 10,
        check_vma=False,
    )
```

```python
import functools

import jax
import jax.numpy as jnp
from jax import lax
from jax.experimental import pallas as pl
from jax.experimental.pallas import tpu as pltpu
from jax.sharding import PartitionSpec as P

NORM_EPS = 1e-05
CONTRACT_ROWS = (((0,), (0,)), ((), ()))
CONTRACT_COLS = (((1,), (1,)), ((), ()))
LOG2E = 1.4426950408889634
LN2 = 0.6931471805599453
BREAK = 1e30
CHUNKS = 8
LANES = 128
SUMMARY_STATES = 8
SUMMARY_UNROLL = 16
STATES_UNROLL = 32
ADJOINT_STATES = 8
ADJOINT_UNROLL = 16
F32 = jnp.float32
BF16 = jnp.bfloat16


def dot(a, b):
    return jnp.dot(a, b, preferred_element_type=F32)


def dot_rows(a, b):
    return lax.dot_general(a, b, CONTRACT_ROWS, preferred_element_type=F32)


def dot_cols(a, b):
    return lax.dot_general(a, b, CONTRACT_COLS, preferred_element_type=F32)


def sigmoid(v):
    return 1.0 / (1.0 + jnp.exp(-v))


def fetch(source, target, semaphore):
    copy = pltpu.make_async_copy(source, target, semaphore)
    copy.start()
    return copy


def lanes_of(tile):
    return pl.ds(pl.multiple_of(tile * LANES, LANES), LANES)


def rows_of(j, count=CHUNKS):
    return pl.ds(pl.multiple_of(j * CHUNKS, CHUNKS), count)


def chunk_order(rows):
    row = lax.broadcasted_iota(jnp.int32, (rows, rows), 0)
    slot = lax.broadcasted_iota(jnp.int32, (rows, rows), 1)
    return slot == (row & (CHUNKS - 1)) * (rows // CHUNKS) + (row >> 3)


def image_ends(heights, widths):
    ends, total = [], 0
    for i in range(heights.shape[1]):
        total = total + heights[0, i] * widths[0, i]
        ends.append(total)
    return ends


def segment_of(places, ends):
    found = jnp.zeros_like(places)
    for end in ends:
        found = found + (places >= end).astype(jnp.int32)
    return found


def places_of(first, rows):
    row = lax.broadcasted_iota(jnp.int32, (rows, LANES), 0)
    return first + (row & (CHUNKS - 1)) * (rows // CHUNKS) + (row >> 3)


def edges_kernel(io, valid, tokens_far, to_core, to_chip, top, bottom, moves):
    rows = tokens_far.shape[0]
    edge = to_core.shape[0]
    arriving = [
        fetch(tokens_far.at[0:edge, :], top, moves.at[0]),
        fetch(tokens_far.at[rows - edge : rows, :], bottom, moves.at[1]),
    ]
    row = lax.broadcasted_iota(jnp.int32, (edge, rows), 0)
    slot = lax.broadcasted_iota(jnp.int32, (edge, rows), 1)
    io.ready()
    held = jnp.broadcast_to(valid[...].astype(F32), (edge, rows))
    kept_top = jnp.sum(jnp.where(slot == row, held, 0.0), axis=1, keepdims=True)
    kept_bottom = jnp.sum(jnp.where(slot == rows - edge + row, held, 0.0), axis=1, keepdims=True)
    for copy in arriving:
        copy.wait()
    first = (top[...].astype(F32) * kept_top).astype(BF16)
    last = (bottom[...].astype(F32) * kept_bottom).astype(BF16)
    even = (lax.axis_index("seq") & 1) == 0
    to_core[...] = jnp.where(even, last, first)
    to_chip[...] = jnp.where(even, first, last)


def spread(values, target):
    count = values.shape[1]
    high = values.astype(BF16)
    low = (values - high.astype(F32)).astype(BF16)
    both = jnp.concatenate([high, low], axis=1)
    row = lax.broadcasted_iota(jnp.int32, (2 * count, LANES), 0)
    row = jnp.where(row < count, row, row - count)
    for at in range(0, count, 2):
        pick = jnp.concatenate([(row == at).astype(BF16), (row == at + 1).astype(BF16)], axis=1)
        target[:, at * LANES : (at + 2) * LANES] = dot(both, pick)


def windows(span, up, sublane):
    sign = 1 if up else -1

    def from_before(value, by, fill):
        moved = pltpu.roll(value, (sign * by) % CHUNKS, axis=0)
        kept = sublane >= by if up else sublane < CHUNKS - by
        return jnp.where(kept, moved, fill)

    two = span + from_before(span, 1, 0.0)
    four = two + from_before(two, 2, 0.0)
    eight = four + from_before(four, 4, 0.0)
    edge = [jnp.where(sublane >= by if up else sublane < CHUNKS - by, 0.0, BREAK) for by in (1, 2, 4)]
    return (span + edge[0], two + edge[1], four + edge[2]), from_before(eight, 1, 0.0)


def chain(rate, sums, tail, up, sublane):
    sign = 1 if up else -1
    for by, span in zip((1, 2, 4), sums):
        tail = jnp.exp2(rate * span) * pltpu.roll(tail, (sign * by) % CHUNKS, axis=0) + tail
    end = CHUNKS - 1 if up else 0
    kept = sublane >= 1 if up else sublane < CHUNKS - 1
    return jnp.where(kept, pltpu.roll(tail, sign % CHUNKS, axis=0), 0.0), tail[end : end + 1]


def front_kernel(
    io, tokens, cotangent, in_weight, out_weight, heights, widths, valid, gain, *refs, reach, weights,
):
    (
        normed_out, x_out, zs_out, dgz_out, dy, live, same_out, cotan, in_x, halo_live, gains_out,
    ) = refs[weights : weights + 11]
    near_weights = refs[weights + 11 : 2 * weights + 11]
    ins = refs[2 * weights + 11]
    rows, width = tokens.shape
    inner = out_weight.shape[0]
    tiles = inner // LANES
    arriving = [
        fetch(source, target, ins.at[i])
        for i, (source, target) in enumerate(zip(refs[:weights], near_weights))
    ]
    order = chunk_order(rows)
    order_low = order.astype(BF16)
    inputs = dot(order_low, tokens[...])
    inv_rms = lax.rsqrt(jnp.mean(inputs * inputs, axis=-1, keepdims=True) + NORM_EPS)
    cotan[...] = dot(order_low, cotangent[...]).astype(BF16)
    step = 2 * LANES
    for at in range(0, inner, step):
        lanes = slice(at, at + step)
        dgz_out[:, lanes] = dot_cols(cotan[...], out_weight[lanes, :])
    in_x[...] = in_weight[:, 0:inner]

    io.ready()
    start = lax.axis_index("seq") * rows
    slots = lax.axis_size("seq") * rows
    ends = image_ends(heights, widths)
    images = heights.shape[1]
    picked = jnp.where(order, jnp.broadcast_to(valid[...].astype(F32), order.shape), 0.0)
    alive = dot(picked.astype(BF16), jnp.ones((rows, LANES), BF16))
    places = places_of(start, rows)
    segment = segment_of(places, ends)
    live[...] = jnp.where(segment < images, alive, 0.0)
    for k in range(1, reach + 1):
        same = (segment_of(places - k, ends) == segment) & (places >= k)
        same_out[(k - 1) * rows : k * rows, :] = same.astype(F32)
        same = (segment_of(places + k, ends) == segment) & (places + k < slots)
        same_out[(reach + k - 1) * rows : (reach + k) * rows, :] = same.astype(F32)
    near_row = lax.broadcasted_iota(jnp.int32, (2 * CHUNKS, LANES), 0)
    near_place = jnp.where(
        near_row < CHUNKS, start - CHUNKS + near_row, start + rows + near_row - CHUNKS
    )
    halo_live[...] = (segment_of(near_place, ends) < images).astype(F32)

    gains = gain[...].astype(F32).reshape(1, width)
    gains_out[...] = jnp.broadcast_to(gains, gains_out.shape)
    scaled = inputs * inv_rms * gains
    normed = scaled.astype(BF16)
    normed_out[...] = normed
    live_wide = jnp.concatenate([live[...]] * (width // LANES), axis=1)
    normed_live = (scaled * live_wide).astype(BF16)
    for at in range(0, inner, step):
        lanes = slice(at, at + step)
        x_out[:, lanes] = dot(normed_live, in_x[:, lanes]).astype(BF16).astype(F32)
        zs_out[:, lanes] = dot(normed, in_weight[:, inner + at : inner + at + step])
    block = 32

    def gate_block(b, _):
        here = pl.ds(pl.multiple_of(b * block, block), block)
        alive = live[here, :]
        for tile in range(tiles):
            lanes = slice(tile * LANES, (tile + 1) * LANES)
            z = zs_out[here, lanes]
            grad = dgz_out[here, lanes] * alive
            gate = sigmoid(z)
            zs = z * gate * alive
            zs_out[here, lanes] = zs
            dy[here, lanes] = 0.5 * grad * zs
            dgz_out[here, lanes] = grad * (gate * (1.0 + z * (1.0 - gate)))
        return 0

    lax.fori_loop(0, rows // block, gate_block, 0, unroll=8)
    for copy in arriving:
        copy.wait()


def middle_kernel(
    io, dy, live, same_out, from_core, from_chip, x, in_x, halo_live, gains, conv_weight, conv_bias,
    xproj, dt_weight, dt_bias, a_log, skip,
    sum_out, sent_out, delta_out, s_out, dsilu_out, tail_out, head_out, xext_out, proj_out,
    before_out, after_out, rate_out, nhalo_out,
    low_out, bc, tails, heads, spans,
    *, reach,
):
    rows, inner = x.shape
    width = in_x.shape[0]
    steps = rows // CHUNKS
    state = a_log.shape[1]
    rank = dt_weight.shape[1]
    tiles = inner // LANES
    even = (lax.axis_index("seq") & 1) == 0
    sublane = lax.broadcasted_iota(jnp.int32, (CHUNKS, LANES), 0)
    wide = lax.broadcasted_iota(jnp.int32, (CHUNKS, inner), 0)
    xext_out[reach * CHUNKS : (reach + steps) * CHUNKS, :] = x[...]

    core, chip = from_core[...].astype(F32), from_chip[...].astype(F32)
    before = jnp.where(even, chip, core)
    after = jnp.where(even, core, chip)
    htok = jnp.concatenate([before[CHUNKS:], after[:CHUNKS]], axis=0)
    htok = htok * jnp.concatenate([halo_live[...]] * (width // LANES), axis=1)
    hinv = lax.rsqrt(jnp.mean(htok * htok, axis=-1, keepdims=True) + NORM_EPS)
    scaled = htok * hinv
    nhalo = (scaled * gains[0:1, :]).astype(BF16)
    nhalo_out[...] = jnp.concatenate([nhalo, scaled.astype(BF16)], axis=0)
    hx = dot(nhalo, in_x[...]).astype(BF16).astype(F32)
    for i in range(reach):
        to = steps - reach + i
        moved = pltpu.roll(x[to * CHUNKS : (to + 1) * CHUNKS, :], 1, axis=0)
        of = CHUNKS - reach + i
        xext_out[i * CHUNKS : (i + 1) * CHUNKS, :] = jnp.where(wide == 0, hx[of : of + 1], moved)
        moved = pltpu.roll(x[i * CHUNKS : (i + 1) * CHUNKS, :], CHUNKS - 1, axis=0)
        to = reach + steps + i
        of = CHUNKS + i
        xext_out[to * CHUNKS : (to + 1) * CHUNKS, :] = jnp.where(
            wide == CHUNKS - 1, hx[of : of + 1], moved
        )

    block = 64
    step = 2 * LANES
    taps = reach + 1
    conv_w = [conv_weight[d].astype(F32) for d in range(2)]
    conv_b = conv_bias[...].astype(F32)
    for tile in range(tiles):
        lanes = slice(tile * LANES, (tile + 1) * LANES)

        def conv_block(b, _, lanes=lanes):
            at = pl.multiple_of(b * block, block)
            for d in range(2):
                total = conv_b[d : d + 1, lanes] + conv_w[d][reach:taps, lanes] * (
                    xext_out[pl.ds(at + reach * CHUNKS, block), lanes]
                )
                for k in range(1, taps):
                    move = reach - k if d == 0 else reach + k
                    mask = same_out[pl.ds((d * reach + k - 1) * rows + at, block), :]
                    total = total + conv_w[d][reach - k : taps - k, lanes] * (
                        xext_out[pl.ds(at + move * CHUNKS, block), lanes] * mask
                    )
                gate = sigmoid(total)
                value = total * gate
                s_out[pl.ds(d * rows + at, block), lanes] = value
                low_out[pl.ds(d * rows + at, block), lanes] = value.astype(BF16)
                dsilu_out[pl.ds(d * rows + at, block), lanes] = gate * (1.0 + total * (1.0 - gate))
            return 0

        lax.fori_loop(0, rows // block, conv_block, 0, unroll=4)

    dt_b = dt_bias[...].astype(F32)
    for d in range(2):
        rate_out[d * state : (d + 1) * state, :] = jnp.minimum(
            -LOG2E * jnp.exp(a_log[d].astype(F32)), -1e-20
        )
        here = slice(d * rows, (d + 1) * rows)
        proj = dot_cols(low_out[here, :], xproj[d])
        proj_out[here, :] = proj
        dt_low = proj[:, :rank].astype(BF16)
        for at in range(0, inner, step):
            lanes = slice(at, at + step)
            delta_out[here, lanes] = dot(dt_low, dt_weight[d, :, lanes])
        spread(proj[:, rank:], bc)

        def delta_block(b, _, d=d):
            alive = live[pl.ds(pl.multiple_of(b * block, block), block), :]
            here = pl.ds(pl.multiple_of(d * rows + b * block, block), block)
            for tile in range(tiles):
                lanes = slice(tile * LANES, (tile + 1) * LANES)
                pre = delta_out[here, lanes] + dt_b[d : d + 1, lanes]
                small = jnp.exp(-jnp.abs(pre))
                log1p = jnp.where(small < 1e-4, small * (1.0 - 0.5 * small), jnp.log(1.0 + small))
                delta_out[here, lanes] = (jnp.maximum(pre, 0.0) + log1p) * alive
            return 0

        lax.fori_loop(0, rows // block, delta_block, 0, unroll=4)
        some = SUMMARY_STATES

        def scan_tile(tile, _, d=d):
            lanes = lanes_of(tile)
            for low in range(0, state, some):
                rates = [
                    jnp.broadcast_to(
                        rate_out[d * state + low + m : d * state + low + m + 1, lanes],
                        (CHUNKS, LANES),
                    )
                    for m in range(some)
                ]

                def scan_step(i, carried, d=d, low=low, rates=rates):
                    tail, lead, head, span = carried
                    j = i if d == 0 else steps - 1 - i
                    at = pl.multiple_of(j * CHUNKS, CHUNKS)
                    keep = same_out[pl.ds(d * reach * rows + at, CHUNKS), :]
                    delta = delta_out[pl.ds(d * rows + at, CHUNKS), lanes]
                    drive = delta * s_out[pl.ds(d * rows + at, CHUNKS), lanes]
                    back = dy[pl.ds(at, CHUNKS), lanes]
                    delta = jnp.maximum(delta, BREAK - keep * BREAK)
                    tail, lead, head = list(tail), list(lead), list(head)
                    for m in range(some):
                        b = bc[pl.ds(at, CHUNKS), (low + m) * LANES : (low + m + 1) * LANES]
                        n = state + low + m
                        c = bc[pl.ds(at, CHUNKS), n * LANES : (n + 1) * LANES]
                        decay = jnp.exp2(delta * rates[m])
                        tail[m] = decay * tail[m] + b * drive
                        lead[m] = lead[m] * decay
                        head[m] = head[m] + lead[m] * (c * back)
                    return tuple(tail), tuple(lead), tuple(head), span + delta

                zeros = tuple(jnp.zeros((CHUNKS, LANES), F32) for _ in range(some))
                ones = tuple(jnp.ones((CHUNKS, LANES), F32) for _ in range(some))
                tail, lead, head, span = lax.fori_loop(
                    0, steps, scan_step, (zeros, ones, zeros, zeros[0]), unroll=SUMMARY_UNROLL
                )
                for m in range(some):
                    tails[low + m, :, lanes] = tail[m]
                    heads[low + m, :, lanes] = head[m]
                spans[:, lanes] = span
            return 0

        lax.fori_loop(0, tiles, scan_tile, 0)

        tail_row = 0 if d == 0 else 2 * state
        head_row = 3 * state if d == 0 else state

        def chain_tile(tile, _, d=d, tail_row=tail_row, head_row=head_row):
            lanes = lanes_of(tile)
            span = spans[:, lanes]
            sums, before = windows(span, d == 0, sublane)
            sums_back, after = windows(span, d == 1, sublane)
            before_out[d * CHUNKS : (d + 1) * CHUNKS, lanes] = before
            after_out[d * CHUNKS : (d + 1) * CHUNKS, lanes] = after
            for n in range(state):
                rate = jnp.broadcast_to(
                    rate_out[d * state + n : d * state + n + 1, lanes], (CHUNKS, LANES)
                )
                carried, total = chain(rate, sums, tails[n, :, lanes], d == 0, sublane)
                tail_out[d * state + n, :, lanes] = carried
                sum_out[tail_row + n : tail_row + n + 1, lanes] = total
                carried, total = chain(rate, sums_back, heads[n, :, lanes], d == 1, sublane)
                head_out[d * state + n, :, lanes] = carried
                sum_out[head_row + n : head_row + n + 1, lanes] = total
            return 0

        lax.fori_loop(0, tiles, chain_tile, 0, unroll=2)
        sum_out[4 * state + d : 4 * state + d + 1, :] = jnp.sum(spans[...], axis=0, keepdims=True)
    at = 4 * state + CHUNKS
    sum_out[4 * state + 2 : at, :] = jnp.zeros((CHUNKS - 2, inner), F32)
    sum_out[at:, :] = rate_out[0 : 2 * state, :]
    sent_out[...] = packed(sum_out[0:at, :], state)
    rate_out[2 * state : 2 * state + 2, :] = skip[...].astype(F32)


def packed(summary, state):
    rest = summary[4 * state :]
    high = rest.astype(BF16).astype(F32)
    return jnp.concatenate([summary[: 4 * state], high, rest - high], axis=0).astype(BF16)


def leads(rate, spans, state, flip):
    parts = [jnp.exp2(rate[d * state : (d + 1) * state] * spans[d : d + 1]) for d in range(2)]
    return jnp.concatenate(parts[::-1] if flip else parts, axis=0)


def join_kernel(io, got, summary, entered, *outs, state, bit, final):
    half = 2 * state
    upper = ((lax.axis_index("seq") >> bit) & 1) == 1
    mine = summary[0 : 2 * half + CHUNKS, :]
    rates = summary[2 * half + CHUNKS :, :]
    entered_out, sent_out = outs[-2], outs[-1]
    values = got[...].astype(F32)
    spans = mine[4 * state : 4 * state + 2]
    other = values[4 * state : 4 * state + 2] + values[4 * state + CHUNKS : 4 * state + CHUNKS + 2]
    if entered is None:
        entered_up = jnp.where(upper, values[:half], 0.0)
        entered_down = jnp.where(upper, 0.0, values[half : 2 * half])
        span_up = jnp.where(upper, other, 0.0)
        span_down = jnp.where(upper, 0.0, other)
    else:
        held = entered[...]
        span_up, span_down = held[2 * half : 2 * half + 2], held[2 * half + 2 : 2 * half + 4]
        entered_up = held[:half] + jnp.where(
            upper, leads(rates, span_up, state, False) * values[:half], 0.0
        )
        entered_down = held[half : 2 * half] + jnp.where(
            upper, 0.0, leads(rates, span_down, state, True) * values[half : 2 * half]
        )
        span_up = span_up + jnp.where(upper, other, 0.0)
        span_down = span_down + jnp.where(upper, 0.0, other)
    entered_out[0:half, :] = entered_up
    entered_out[half : 2 * half, :] = entered_down
    entered_out[2 * half :, :] = jnp.concatenate(
        [span_up, span_down, jnp.zeros((CHUNKS - 4, mine.shape[1]), F32)], axis=0
    )
    low_up = jnp.where(upper, values[:half], mine[:half])
    high_up = jnp.where(upper, mine[:half], values[:half])
    low_down = jnp.where(upper, values[half : 2 * half], mine[half : 2 * half])
    high_down = jnp.where(upper, mine[half : 2 * half], values[half : 2 * half])
    low_span, high_span = jnp.where(upper, other, spans), jnp.where(upper, spans, other)
    up = leads(rates, high_span, state, False) * low_up + high_up
    down = leads(rates, low_span, state, True) * high_down + low_down
    if final:
        next_upper = ((lax.axis_index("seq") >> (bit + 1)) & 1) == 1
        sent_out[...] = jnp.where(next_upper, down, up).astype(BF16)
    else:
        total = jnp.concatenate(
            [up, down, spans + other, jnp.zeros((CHUNKS - 2, mine.shape[1]), F32)], axis=0
        )
        outs[0][0 : 2 * half + CHUNKS, :] = total
        outs[0][2 * half + CHUNKS :, :] = rates
        sent_out[...] = packed(total, state)


def first_join(io, got, summary, *outs, state, bit, final):
    join_kernel(io, got, summary, None, *outs, state=state, bit=bit, final=final)


def state_block(j, state):
    return pl.multiple_of(j * state * CHUNKS, CHUNKS)


def states_pass(d, steps, state, rates, begin, delta, s, keep, bc, h_out, y):
    start = state_block(0 if d == 0 else steps, state)
    for n in range(state):
        h_out[pl.ds(start + n * CHUNKS, CHUNKS), :] = begin[n]

    def step(i, h):
        j = i if d == 0 else steps - 1 - i
        here = pl.ds(pl.multiple_of(j * CHUNKS, CHUNKS), CHUNKS)
        to = state_block(j + 1 if d == 0 else j, state)
        size = delta[here, :]
        drive = size * s[here, :]
        size = jnp.maximum(size, BREAK - keep[here, :] * BREAK)
        h = list(h)
        parts = [None if d == 0 else y[here, :], None]
        for n in range(state):
            b = bc[here, n * LANES : (n + 1) * LANES]
            c = bc[here, (state + n) * LANES : (state + n + 1) * LANES]
            h[n] = jnp.exp2(size * rates[n]) * h[n] + b * drive
            h_out[pl.ds(to + n * CHUNKS, CHUNKS), :] = h[n]
            part = parts[n % 2]
            parts[n % 2] = c * h[n] if part is None else part + c * h[n]
        y[here, :] = parts[0] + parts[1]
        return tuple(h)

    lax.fori_loop(0, steps, step, tuple(begin), unroll=STATES_UNROLL)


def adjoint_pass(
    d, steps, state, rates, back, delta, s, dy, keep, skip, bc, h_in, sums,
    dpre_out, ds_out, rows_out, fresh,
):
    some = ADJOINT_STATES
    edge = steps - 1
    skip = skip[...]
    zeros = jnp.zeros((CHUNKS, LANES), F32)
    grads = []
    for low in range(0, state, some):
        final = low + some == state

        def step(i, carried, low=low, final=final):
            g, acc, h, skip_acc, bias_acc = carried
            j = edge - i if d == 0 else i
            here = pl.ds(pl.multiple_of(j * CHUNKS, CHUNKS), CHUNKS)
            size = delta[here, :]
            value = s[here, :]
            grad = dy[here, :]
            drive = size * value
            masked = jnp.maximum(size, BREAK - keep[here, :] * BREAK)
            prev = state_block(j if d == 0 else j + 1, state)
            g, acc, h = list(g), list(acc), list(h)
            weighted = zeros if low == 0 else ds_out[here, :]
            rate_sum = zeros if low == 0 else dpre_out[here, :]
            for m in range(some):
                n = low + m
                b = bc[here, n * LANES : (n + 1) * LANES]
                c = bc[here, (state + n) * LANES : (state + n + 1) * LANES]
                adjoint = c * grad + g[m]
                before = h_in[pl.ds(prev + n * CHUNKS, CHUNKS), :]
                for block, part in ((n, adjoint * drive), (state + n, grad * h[m])):
                    column = slice(block * LANES, (block + 1) * LANES)
                    sums[here, column] = part if fresh else sums[here, column] + part
                g[m] = adjoint * jnp.exp2(masked * rates[n])
                held = g[m] * before
                weighted = weighted + adjoint * b
                rate_sum = rate_sum + held * rates[n]
                acc[m] = acc[m] + held * masked
                h[m] = before
            if final:
                ds_out[here, :] = skip * grad + size * weighted
                gate = jnp.where(
                    size < 0.01, size * (1.0 - size * (0.5 - size * (1.0 / 6.0))), 1.0 - jnp.exp(-size)
                )
                pre = ((LN2 * rate_sum + weighted * value) * gate).astype(BF16).astype(F32)
                dpre_out[here, :] = pre
                bias_acc = bias_acc + pre
                skip_acc = skip_acc + grad * value
            else:
                dpre_out[here, :] = rate_sum
                ds_out[here, :] = weighted
            return tuple(g), tuple(acc), tuple(h), skip_acc, bias_acc

        last = state_block(steps if d == 0 else 0, state)
        h_last = tuple(h_in[pl.ds(last + (low + m) * CHUNKS, CHUNKS), :] for m in range(some))
        none = tuple(zeros for _ in range(some))
        _, acc, _, skip_acc, bias_acc = lax.fori_loop(
            0, steps, step, (tuple(back[low : low + some]), none, h_last, zeros, zeros),
            unroll=ADJOINT_UNROLL,
        )
        grads.extend(acc)
    for n in range(state):
        rows_out[n : n + 1, :] = jnp.sum(grads[n], axis=0, keepdims=True) * rates[n][0:1] * LN2
    rows_out[state : state + 1, :] = jnp.sum(bias_acc, axis=0, keepdims=True)
    rows_out[state + 1 : state + 2, :] = jnp.sum(skip_acc, axis=0, keepdims=True)


def lane_sums(sums, state):
    column = lax.broadcasted_iota(jnp.int32, (2 * CHUNKS, LANES), 1)
    picks = [(column == n).astype(BF16) for n in range(2 * state)]
    pick = jnp.concatenate([p for p in picks for _ in range(LANES // (2 * CHUNKS))], axis=0)
    return dot(sums.astype(BF16), pick)[:, : 2 * state]


def rate_tiles(rate, d, state, lanes):
    return [
        jnp.broadcast_to(rate[d * state + n : d * state + n + 1, lanes], (CHUNKS, LANES))
        for n in range(state)
    ]


def begin_tiles(rates, passed, maps, carry, at, d, state, lanes):
    passed = passed[d * CHUNKS : (d + 1) * CHUNKS, lanes]
    return [
        jnp.exp2(rates[n] * passed) * carry[at + n : at + n + 1, lanes]
        + maps[d * state + n, :, lanes]
        for n in range(state)
    ]


def slot_order(rows):
    row = lax.broadcasted_iota(jnp.int32, (rows, rows), 1)
    slot = lax.broadcasted_iota(jnp.int32, (rows, rows), 0)
    return (slot == (row & (CHUNKS - 1)) * (rows // CHUNKS) + (row >> 3)).astype(BF16)


def states_kernel(
    io, delta, s, proj, rate, same, normed, before, tail, got, entered, zs, dgz, cotan,
    kept, sent, carry_out, dz, h0, h1, gated,
    bc, y,
    *, reach, rank, state, bit,
):
    rows, inner = zs.shape
    width = cotan.shape[1]
    steps = rows // CHUNKS
    half = 2 * state
    tiles = inner // LANES
    upper = ((lax.axis_index("seq") >> bit) & 1) == 1
    values = got[...].astype(F32)
    held = entered[...]
    rates = rate[0:half, :]
    carry_out[0:half, :] = held[:half] + jnp.where(
        upper, leads(rates, held[2 * half : 2 * half + 2], state, False) * values, 0.0
    )
    carry_out[half : 2 * half, :] = held[half : 2 * half] + jnp.where(
        upper, 0.0, leads(rates, held[2 * half + 2 : 2 * half + 4], state, True) * values
    )
    for d, h in enumerate((h0, h1)):
        mine = slice(d * rows, (d + 1) * rows)
        spread(proj[mine, rank:], bc)
        keep = same.at[d * reach * rows : (d * reach + 1) * rows, :]

        def scan_tile(tile, _, d=d, h=h, mine=mine, keep=keep):
            lanes = lanes_of(tile)
            rates = rate_tiles(rate, d, state, lanes)
            begin = begin_tiles(rates, before, tail, carry_out, d * half, d, state, lanes)
            states_pass(
                d, steps, state, rates, begin, delta.at[mine, lanes], s.at[mine, lanes],
                keep, bc, h.at[tile], y.at[:, lanes],
            )
            return 0

        lax.fori_loop(0, tiles, scan_tile, 0)
    block = 32

    def gate_block(b, _):
        here = pl.ds(pl.multiple_of(b * block, block), block)
        there = pl.ds(pl.multiple_of(rows + b * block, block), block)
        for tile in range(tiles):
            lanes = slice(tile * LANES, (tile + 1) * LANES)
            total = 0.5 * (
                y[here, lanes] + rate[half : half + 1, lanes] * s[here, lanes]
                + rate[half + 1 : half + 2, lanes] * s[there, lanes]
            )
            gated[here, lanes] = (total * zs[here, lanes]).astype(BF16)
            dz[here, lanes] = (total * dgz[here, lanes]).astype(BF16)
        return 0

    lax.fori_loop(0, rows // block, gate_block, 0, unroll=8)
    even = (lax.axis_index("seq") & 1) == 0
    out_grad = dot_rows(gated[...], cotan[...]).astype(BF16)
    z_grad = jnp.concatenate(
        [dot_rows(normed[...], dz[:, at : at + width]) for at in range(0, inner, width)], axis=0
    ).astype(BF16)
    sent[...] = jnp.where(even, z_grad, out_grad)
    kept[...] = jnp.where(even, out_grad, z_grad)


def output_kernel(io, gated, tokens, out_weight, output):
    ordered = dot(slot_order(gated.shape[0]), gated[...]).astype(BF16)
    io.ready()
    output[...] = (tokens[...].astype(F32) + dot(ordered, out_weight[...])).astype(BF16)


def adjoint_kernel(
    io, delta, s, dsilu, dy, head, xext, proj, after, rate, same, carry, h, dx_in,
    dt_weight, xproj, conv_weight,
    dc_rim, small_out, dx_out,
    bc, sums, dpre, ds, rows_out, ext,
    *, d, reach, rank, state,
):
    rows, inner = dy.shape
    steps = rows // CHUNKS
    half = 2 * state
    tiles = inner // LANES
    taps = reach + 1
    cols = proj.shape[1]
    mine = slice(d * rows, (d + 1) * rows)
    keep = same.at[d * reach * rows : (d * reach + 1) * rows, :]
    spread(proj[mine, rank:], bc)
    rows_out[...] = jnp.zeros_like(rows_out)
    grad_at = (half if d == 0 else 0) + state

    def scan_tile(tile, _, fresh=False):
        lanes = lanes_of(tile)
        rates = rate_tiles(rate, d, state, lanes)
        back = begin_tiles(rates, after, head, carry, grad_at, d, state, lanes)
        adjoint_pass(
            d, steps, state, rates, back, delta.at[mine, lanes], s.at[mine, lanes],
            dy.at[:, lanes], keep, rate.at[half + d : half + d + 1, lanes], bc,
            h.at[tile], sums, dpre.at[:, lanes], ds.at[:, lanes], rows_out.at[:, lanes], fresh,
        )
        return 0

    scan_tile(0, 0, True)
    lax.fori_loop(1, tiles, scan_tile, 0)
    io.ready()
    dpre_low = dpre[...].astype(BF16)
    dt_grad = dot_rows(proj[mine, :rank].astype(BF16), dpre_low)
    dt_back = dot_cols(dpre_low, dt_weight[d])
    dproj = jnp.concatenate([dt_back, lane_sums(sums[...], state)], axis=1).astype(BF16)
    small_out[0:cols, :] = dot_rows(dproj, s[mine, :].astype(BF16))
    small_out[cols : cols + rank, :] = dt_grad
    base = 0 if d == 0 else reach * CHUNKS
    step = 2 * LANES
    for lane in range(0, inner, step):
        lanes = slice(lane, lane + step)
        total = ds[:, lanes] + dot(dproj, xproj[d, :, lanes])
        ext[base : base + rows, lanes] = (total * dsilu[mine, lanes]).astype(BF16).astype(F32)
    wide = lax.broadcasted_iota(jnp.int32, (CHUNKS, inner), 0)
    for i in range(reach):
        if d == 0:
            moved = pltpu.roll(ext[i * CHUNKS : (i + 1) * CHUNKS, :], CHUNKS - 1, axis=0)
            ext[rows + i * CHUNKS : rows + (i + 1) * CHUNKS, :] = jnp.where(
                wide == CHUNKS - 1, 0.0, moved
            )
        else:
            moved = pltpu.roll(ext[rows + i * CHUNKS : rows + (i + 1) * CHUNKS, :], 1, axis=0)
            ext[i * CHUNKS : (i + 1) * CHUNKS, :] = jnp.where(wide == 0, 0.0, moved)

    conv_w = conv_weight[d].astype(F32)
    block = 64
    zeros = jnp.zeros((CHUNKS, LANES), F32)

    def folded(values):
        return functools.reduce(
            lambda a, b: a + b, [values[i : i + CHUNKS] for i in range(0, block, CHUNKS)]
        )

    base_row = cols + rank
    for tile in range(tiles):
        lanes = slice(tile * LANES, (tile + 1) * LANES)
        weight = conv_w[:, lanes]

        def conv_block(b, totals, lanes=lanes, weight=weight):
            here = pl.multiple_of(b * block, block)
            totals = list(totals)
            mid = ext[pl.ds(here + base, block), lanes]
            total = weight[reach:taps] * mid
            totals[reach] = totals[reach] + folded(mid * xext[pl.ds(here + reach * CHUNKS, block), lanes])
            totals[taps] = totals[taps] + folded(mid)
            for k in range(1, taps):
                past = same[pl.ds((k - 1) * rows + here, block), :]
                ahead = same[pl.ds((reach + k - 1) * rows + here, block), :]
                if d == 0:
                    given = ext[pl.ds(here + k * CHUNKS, block), lanes] * ahead
                    taken = xext[pl.ds(here + (reach - k) * CHUNKS, block), lanes] * past
                else:
                    given = ext[pl.ds(here + (reach - k) * CHUNKS, block), lanes] * past
                    taken = xext[pl.ds(here + (reach + k) * CHUNKS, block), lanes] * ahead
                total = total + weight[reach - k : taps - k] * given
                totals[reach - k] = totals[reach - k] + folded(mid * taken)
            if dx_in is not None:
                total = total + dx_in[pl.ds(here, block), lanes]
            dx_out[pl.ds(here, block), lanes] = total
            return tuple(totals)

        totals = lax.fori_loop(0, rows // block, conv_block, (zeros,) * (taps + 1), unroll=4)
        for i in range(taps + 1):
            at = state + 2 + i
            rows_out[at : at + 1, lanes] = jnp.sum(totals[i], axis=0, keepdims=True)

    edge = []
    for i in range(CHUNKS):
        row = jnp.zeros((1, inner), F32)
        for k in range(1, taps):
            j = i - CHUNKS + k if d == 0 else steps + i - k
            if (d == 0 and j >= 0) or (d == 1 and j < steps):
                sub = 0 if d == 0 else CHUNKS - 1
                at = (d * reach + k - 1) * rows + j * CHUNKS + sub
                mask = jnp.concatenate([same[at : at + 1, :]] * tiles, axis=1)
                at = base + j * CHUNKS + sub
                row = row + conv_w[reach - k : taps - k] * ext[at : at + 1, :] * mask
        edge.append(row)
    dc_rim[...] = jnp.concatenate(edge, axis=0)
    small_out[base_row:, :] = rows_out[0 : small_out.shape[0] - base_row, :]


def first_adjoint(io, *refs, **static):
    adjoint_kernel(io, *refs[:12], None, *refs[12:], **static)


def second_adjoint(io, *refs, **static):
    in_far, in_near, moves = refs[16], refs[20], refs[21]
    copy = fetch(in_far, in_near, moves.at[0])
    adjoint_kernel(io, *refs[:16], *refs[17:20], *refs[22:], **static)
    copy.wait()


def last_kernel(
    io, dx, rim0, rim1, small0, small1, normed, nhalo, live, in_weight,
    kept, sent, low,
    lines, grads,
):
    rows, inner = dx.shape
    width = normed.shape[1]
    folds = inner // width
    fold = kept.shape[0]
    edges = 2 * CHUNKS
    for tile in range(inner // LANES):
        lanes = slice(tile * LANES, (tile + 1) * LANES)
        lines[0:rows, lanes] = (dx[:, lanes] * live[...]).astype(BF16)
    low[...] = lines[0:rows, :]
    lines[rows : rows + edges, :] = jnp.concatenate([rim0[...], rim1[...]], axis=0).astype(BF16)
    both = jnp.concatenate([normed[...], nhalo[0:edges, :]], axis=0)
    size = small0.shape[0]
    for i in range(folds):
        lanes = slice(i * width, (i + 1) * width)
        at = i * fold
        grads[at : at + width, :] = dot_rows(both, lines[:, lanes]).astype(BF16)
        at += width
        grads[at : at + 2 * size, :] = jnp.concatenate(
            [small0[:, lanes], small1[:, lanes]], axis=0
        ).astype(BF16)
        at += 2 * size
        grads[at : (i + 1) * fold, :] = jnp.zeros(((i + 1) * fold - at, width), BF16)
    rim = dot_cols(lines[rows : rows + edges, :], in_weight[:, 0:inner])
    even = (lax.axis_index("seq") & 1) == 0
    turned = jnp.concatenate([rim[CHUNKS:], rim[:CHUNKS]], axis=0)
    left, right = grads[0:fold, :], grads[fold : 2 * fold, :]
    kept[...] = jnp.where(even, left, right)
    sent[...] = jnp.where(even, right, left)
    at = width + 2 * size
    sent[at : at + edges, :] = jnp.where(even, turned, rim).astype(BF16)


def finish_kernel(
    io, low, dz, in_weight, rims, chip_rim, heights, widths, tokens, cotangent, valid, gain,
    input_grad,
):
    rows, width = tokens.shape
    inner = low.shape[1]
    even = (lax.axis_index("seq") & 1) == 0
    start = lax.axis_index("seq") * rows
    back = slot_order(rows)
    dn = dot_cols(dot(back, low[...]).astype(BF16), in_weight[:, 0:inner]) + dot_cols(
        dot(back, dz[...]).astype(BF16), in_weight[:, inner : 2 * inner]
    )
    io.ready()
    from_core = rims[...].astype(F32)[:CHUNKS]
    from_chip = chip_rim[...].astype(F32)[CHUNKS:]
    before = jnp.where(even, from_chip, from_core)
    after = jnp.where(even, from_core, from_chip)
    end = image_ends(heights, widths)[-1]
    row = lax.broadcasted_iota(jnp.int32, (CHUNKS, rows), 0)
    slot = lax.broadcasted_iota(jnp.int32, (CHUNKS, rows), 1)
    alive = jnp.broadcast_to(valid[...].astype(F32), (CHUNKS, rows))
    alive = jnp.where(start + slot < end, alive, 0.0)
    first = jnp.sum(jnp.where(slot == row, alive, 0.0), axis=1, keepdims=True)
    last = jnp.sum(jnp.where(slot == rows - CHUNKS + row, alive, 0.0), axis=1, keepdims=True)
    values = jnp.concatenate(
        [
            dn[0:CHUNKS, :] + first * before, dn[CHUNKS : rows - CHUNKS, :],
            dn[rows - CHUNKS : rows, :] + last * after,
        ],
        axis=0,
    )
    inputs = tokens[...].astype(F32)
    inv_rms = lax.rsqrt(jnp.mean(inputs * inputs, axis=-1, keepdims=True) + NORM_EPS)
    scaled = values * gain[...].astype(F32).reshape(1, width)
    mean = jnp.mean(scaled * inputs, axis=-1, keepdims=True)
    input_grad[...] = (
        cotangent[...].astype(F32) + inv_rms * scaled - inputs * (inv_rms * inv_rms * inv_rms) * mean
    )


def blocks_in_order(mine, other, into_first, into_second):
    size = mine.shape[1]
    is_even = (lax.axis_index("seq") & 1) == 0
    here = lax.axis_index("img")
    for k in range(mine.shape[0]):
        a, b = mine[here ^ k].astype(F32), other[here ^ k].astype(F32)
        into_first(k * size, jnp.where(is_even, a, b))
        into_second(k * size, jnp.where(is_even, b, a))


def weighted_rows(values, weights):
    total = None
    for at in range(0, values.shape[1], LANES):
        part = values[:, at : at + LANES] * weights[:, at : at + LANES].astype(F32)
        total = part if total is None else total + part
    return total


def first_unpack(io, mine, other, in_weight, parts, in_far, out_far, out_w, z_half, moves):
    width = out_w.shape[1]
    inner = out_w.shape[0]

    def put_out(at, values):
        out_w[at : at + values.shape[0], :] = values

    def put_z(at, values):
        size = values.shape[0]
        column = at // width * width
        z_half[at % width : at % width + size, column : column + width] = values

    blocks_in_order(mine, other, put_out, put_z)
    leaving = [
        fetch(out_w, out_far, moves.at[0]),
        fetch(z_half, in_far.at[:, inner : 2 * inner], moves.at[1]),
    ]
    parts[...] = weighted_rows(z_half[...], in_weight[:, inner : 2 * inner])
    for copy in leaving:
        copy.wait()


def second_unpack(
    io, mine, other, in_weight, parts, gain_in, in_before,
    conv_w, conv_b, xproj, dt_w, dt_b, a_log, skip, in_far, gain_far,
    left, right, x_half, gain, moves,
    *, count, state, rank, cols, taps,
):
    width = left.shape[1]
    inner = x_half.shape[1]

    def put(target, lane):
        def at_rows(at, values):
            size = values.shape[0]
            target[at : at + size, :] = values
            top = min(width - at, size)
            if top > 0:
                x_half[at : at + top, lane : lane + width] = values[:top]

        return at_rows

    blocks_in_order(mine, other, put(left, 0), put(right, width))
    leaving = fetch(x_half, in_far.at[:, 0:inner], moves.at[0])
    for i, half in enumerate((left, right)):
        lanes = slice(i * width, (i + 1) * width)
        for d in range(2):
            at = width + d * count
            xproj[d, :, lanes] = half[at : at + cols, :]
            at += cols
            dt_w[d, :, lanes] = half[at : at + rank, :]
            at += rank
            a_log[d, :, lanes] = half[at : at + state, :]
            dt_b[d : d + 1, lanes] = half[at + state : at + state + 1, :]
            skip[d : d + 1, lanes] = half[at + state + 1 : at + state + 2, :]
            at += state + 2
            conv_w[d, :, lanes] = half[at : at + taps, :]
            conv_b[d : d + 1, lanes] = half[at + taps : at + taps + 1, :]
    io.ready()
    io.done()
    total = parts[...] + weighted_rows(x_half[...], in_weight[:, 0:inner])
    high = total.astype(BF16)
    rest = (total - high.astype(F32)).astype(BF16)
    ones = jnp.ones((2 * CHUNKS, LANES), BF16)
    sums = (dot_cols(ones, high) + dot_cols(ones, rest))[0:1]
    gain[...] = (sums / gain_in[...].astype(F32).reshape(1, width)).reshape(width)
    last = fetch(gain, gain_far, moves.at[1])
    leaving.wait()
    last.wait()


IN_VMEM = pl.BlockSpec(memory_space=pltpu.VMEM)
IN_SMEM = pl.BlockSpec(memory_space=pltpu.SMEM)
FAR = pl.BlockSpec(memory_space=pltpu.HBM)


def shape(*dims, dtype=F32):
    return jax.ShapeDtypeStruct(dims, dtype)


def low(*dims):
    return jax.ShapeDtypeStruct(dims, BF16)


def near(*dims, dtype=F32):
    return pltpu.VMEM(dims, dtype)


def scratch(*dims, dtype=F32):
    return pltpu.VMEM(dims, dtype)


def like(*outs):
    return [pltpu.VMEM(out.shape, out.dtype) for out in outs]


def moves(*dims):
    return pltpu.SemaphoreType.DMA(dims)


class Moves:
    def __init__(self, arrive, leave):
        self.arrive, self.leave, self.left = arrive, leave, False
        for copy in arrive:
            copy.start()

    def ready(self):
        for copy in self.arrive:
            copy.wait()

    def done(self):
        self.left = True
        for copy in self.leave:
            copy.start()


def call(
    kernel, name, args, outs, scratches=(), far=(), far_outs=(), near_args=(), near_outs=(),
    scalars=(), handed=(), aliases=(), us=4, limit=4,
):
    small = tuple(scalars) + tuple(args)
    small, far = (
        tuple(pltpu.with_memory_space_constraint(x, pltpu.HBM) for x in arrays)
        for arrays in (small, far)
    )
    n_hand = len(handed)
    near_args = tuple(handed) + tuple(near_args)
    n_near, n_small, n_far = len(near_args), len(small), len(far)
    n_near_outs, n_outs, n_far_outs = len(near_outs), len(outs), len(far_outs)

    def wrapped(*refs):
        refs = list(refs)

        def take(count):
            taken = refs[:count]
            del refs[:count]
            return taken

        near_in, small_in, far_in = take(n_near), take(n_small), take(n_far)
        near_out, out, far_out = take(n_near_outs), take(n_outs), take(n_far_outs)
        take(n_hand)
        small_here, out_here = take(n_small), take(n_outs)
        in_moves, out_moves = take(2)
        io = Moves(
            [pltpu.make_async_copy(a, b, in_moves.at[i]) for i, (a, b) in enumerate(zip(small_in, small_here))],
            [pltpu.make_async_copy(a, b, out_moves.at[i]) for i, (a, b) in enumerate(zip(out_here, out))],
        )
        kernel(io, *near_in, *small_here, *far_in, *near_out, *out_here, *far_out, *refs)
        if not io.left:
            io.done()
        for copy in io.leave:
            copy.wait()

    return pl.pallas_call(
        wrapped,
        out_shape=list(near_outs) + [
            pltpu.HBM(out.shape, out.dtype) for out in tuple(outs) + tuple(far_outs)
        ] + [pltpu.VMEM(x.shape, x.dtype) for x in handed],
        in_specs=[IN_VMEM] * n_near + [FAR] * (n_small + n_far),
        out_specs=[IN_VMEM] * n_near_outs + [FAR] * (n_outs + n_far_outs) + [IN_VMEM] * n_hand,
        input_output_aliases={
            **{i: n_near_outs + n_outs + n_far_outs + i for i in range(n_hand)},
            **{n_near + n_small + i: n_near_outs + n_outs + o for i, o in aliases},
        },
        scratch_shapes=(
            [pltpu.SMEM(a.shape, a.dtype) for a in scalars] + like(*args) + like(*outs)
            + [moves(max(n_small, 1)), moves(max(n_outs, 1))] + list(scratches)
        ),
        compiler_params=pltpu.CompilerParams(vmem_limit_bytes=limit * 2**20),
        cost_estimate=pl.CostEstimate(flops=us * 2000000000, bytes_accessed=0, transcendentals=0),
        name=name,
    )(*near_args, *small, *far)


def call_edges(tokens, valid):
    edge = 2 * CHUNKS
    width = tokens.shape[1]
    outs = [near(edge, width, dtype=BF16), near(edge, width, dtype=BF16)]
    ends = [scratch(edge, width, dtype=BF16), scratch(edge, width, dtype=BF16), moves(2)]
    return call(
        edges_kernel, "edges", (valid,), (), ends, (tokens,), near_outs=outs, us=1, limit=2
    )


def call_front(
    heights, widths, valid, gain, tokens, cotangent, in_weight, out_weight, weights, reach,
):
    rows, width = tokens.shape
    inner = out_weight.shape[0]
    one = near(rows, inner)
    row = near(rows, width, dtype=BF16)
    return call(
        functools.partial(front_kernel, reach=reach, weights=len(weights)), "front", (valid, gain), (),
        [moves(len(weights))], weights, (),
        tuple(
            pltpu.with_memory_space_constraint(x, pltpu.VMEM)
            for x in (tokens, cotangent, in_weight, out_weight)
        ),
        [
            row, one, one, one, one, near(rows, LANES), near(2 * reach * rows, LANES), row,
            near(width, inner, dtype=BF16), near(2 * CHUNKS, LANES), near(CHUNKS, width),
        ] + like(*weights),
        (heights, widths), us=4, limit=12,
    )


def call_middle(handed, used, from_core, from_chip, arrays, reach, cols):
    x, a_log = arrays[0], arrays[-2]
    rows, inner = x.shape
    state, width = a_log.shape[1], from_core.shape[1]
    half = 2 * state
    both = near(2 * rows, inner)
    maps = near(half, CHUNKS, inner)
    ends = near(2 * CHUNKS, inner)
    n_hand = len(handed)

    def kernel(io, *refs):
        middle_kernel(io, *(refs[i] for i in used), *refs[n_hand:], reach=reach)

    return call(
        kernel, "middle", (), (),
        [
            scratch(2 * rows, inner, dtype=BF16), scratch(rows, half * LANES),
            scratch(state, CHUNKS, inner), scratch(state, CHUNKS, inner), scratch(CHUNKS, inner),
        ],
        near_args=(from_core, from_chip) + arrays,
        near_outs=[
            near(2 * half + CHUNKS + half, inner), near(2 * half + 2 * CHUNKS, inner, dtype=BF16),
            both, both, both, maps, maps, near(rows + 2 * reach * CHUNKS, inner),
            near(2 * rows, cols), ends, ends, near(half + CHUNKS, inner),
            near(4 * CHUNKS, width, dtype=BF16),
        ],
        handed=handed, us=20, limit=9,
    )


def call_join(got, summary, entered, state, bit, final):
    inner = summary.shape[1]
    half = 2 * state
    outs = [
        near(2 * half + CHUNKS, inner),
        near(half if final else 2 * half + 2 * CHUNKS, inner, dtype=BF16),
    ]
    if not final:
        outs = [near(2 * half + CHUNKS + half, inner)] + outs
    args = (got, summary) + (() if entered is None else (entered,))
    kernel = first_join if entered is None else join_kernel
    joined = call(
        functools.partial(kernel, state=state, bit=bit, final=final), "join", (), (),
        near_args=args, near_outs=outs, us=1, limit=4,
    )
    return joined if not final else [None] + list(joined)


def call_states(handed, used, before, tail, got, entered, zs, dgz, cotan, rank, reach, state, bit):
    rows, inner = zs.shape
    width = cotan.shape[1]
    half = 2 * state
    n_hand = len(handed)

    def kernel(io, *refs):
        states_kernel(
            io, *(refs[i] for i in used), *refs[n_hand:], reach=reach, rank=rank, state=state, bit=bit
        )

    grad = near(inner, width, dtype=BF16)
    one = near(rows, inner, dtype=BF16)
    held = near(inner // LANES, (rows // CHUNKS + 1) * state * CHUNKS, LANES)
    return call(
        kernel, "states", (), (),
        [scratch(rows, half * LANES), scratch(rows, inner)],
        near_args=(before, tail, got, entered, zs, dgz, cotan),
        near_outs=[grad, grad, near(2 * half, inner), one, held, held, one], handed=handed, us=12,
        limit=9,
    )


def adjoint_scratch(rows, inner, half, reach, small, cols, rank):
    return [
        scratch(rows, half * LANES), scratch(rows, half * LANES), scratch(rows, inner), scratch(rows, inner), scratch(small - cols - rank, inner),
        scratch(rows + reach * CHUNKS, inner),
    ]


def call_first_adjoint(handed, used, h, weights, small, reach, rank, state):
    rows, inner = handed[used[3]].shape
    cols = handed[used[6]].shape[1]
    n_hand = len(handed)

    def kernel(io, *refs):
        first_adjoint(
            io, *(refs[i] for i in used), *refs[n_hand:], d=0, reach=reach, rank=rank, state=state
        )

    return call(
        kernel, "adjoint_up", weights, (),
        adjoint_scratch(rows, inner, 2 * state, reach, small, cols, rank), near_outs=[
            near(CHUNKS, inner), near(small, inner), near(rows, inner),
        ], near_args=(h,), handed=handed, us=14, limit=13,
    )


def call_second_adjoint(handed, arrays, weights, in_weight, small, reach, rank, state):
    rows, inner = arrays[3].shape
    cols = arrays[6].shape[1]
    n_hand = len(handed)

    def kernel(io, *refs):
        second_adjoint(io, *refs[n_hand:], d=1, reach=reach, rank=rank, state=state)

    return call(
        kernel, "adjoint_down", weights, (),
        [moves(1)] + adjoint_scratch(rows, inner, 2 * state, reach, small, cols, rank),
        (in_weight,), (), arrays,
        [near(CHUNKS, inner), near(small, inner), near(rows, inner), near(*in_weight.shape, dtype=BF16)],
        handed=handed, us=14, limit=13,
    )


def call_last(handed, dx, rim0, rim1, small0, small1, normed, nhalo, live):
    rows, inner = dx.shape
    width = normed.shape[1]
    small = small0.shape[0]
    folds = inner // width
    edges = 2 * CHUNKS
    fold = -(-(width + 2 * small + edges) // 64) * 64
    n_hand = len(handed)

    def kernel(io, *refs):
        last_kernel(io, *refs[n_hand : n_hand + 8], refs[n_hand - 1], *refs[n_hand + 8 :])

    return call(
        kernel, "last", (), (),
        [
            scratch(rows + edges, inner, dtype=BF16), scratch(folds * fold, width, dtype=BF16),
        ],
        near_args=(dx, rim0, rim1, small0, small1, normed, nhalo, live),
        near_outs=[
            near(fold, width, dtype=BF16), near(fold, width, dtype=BF16),
            near(rows, inner, dtype=BF16),
        ],
        handed=handed, us=3, limit=8,
    )


def partner(axis, bit):
    return [(i, i ^ (1 << bit)) for i in range(lax.axis_size(axis))]


def bits_of(axis):
    return (lax.axis_size(axis) - 1).bit_length()


def other_core(values):
    return lax.ppermute(values, "seq", partner("seq", 0))


def next_chip(values):
    count = lax.axis_size("seq")
    pairs = [(i, i + 1) for i in range(1, count - 1, 2)]
    return lax.ppermute(values, "seq", pairs + [(j, i) for i, j in pairs])


def split_kernel(io, kept, got, own, *sent, edges):
    if edges:
        at = got.shape[0] - edges[1]
        sent[-1][...] = got[at : at + edges[0], :]
        sent = sent[:-1]
    count = len(sent) + 1
    rows = own.shape[0]
    here = lax.axis_index("img")
    for k in range(count):
        at = pl.ds(pl.multiple_of((here ^ k) * rows, rows), rows)
        total = kept[at, :].astype(F32) + got[at, :].astype(F32)
        if k == 0:
            own[...] = total
        else:
            sent[k - 1][...] = total.astype(BF16)


def add_kernel(io, *refs, outs):
    total = refs[0][...].astype(F32)
    for ref in refs[1 : len(refs) - outs]:
        total = total + ref[...].astype(F32)
    for ref in refs[len(refs) - outs :]:
        ref[...] = total.astype(ref.dtype)


def add(values, whole=True):
    rows, width = values[0].shape
    outs = [near(rows, width)] * whole + [near(rows, width, dtype=BF16)]
    sums = call(
        functools.partial(add_kernel, outs=len(outs)), "add", (), (), near_args=values,
        near_outs=outs, us=1, limit=2,
    )
    return sums if whole else sums[0]


def add_rim_kernel(io, *refs, count, bit):
    values, moving, stay = refs[:count], refs[count], refs[count + 1]
    low_out, stay_out = refs[-2:]
    rows = values[0].shape[0]
    total = values[0][...]
    for ref in values[1:]:
        total = total + ref[0:rows, :].astype(F32)
    if len(refs) > count + 4:
        refs[-3][...] = total
    low_out[0:rows, :] = total.astype(BF16)
    if bit is None:
        low_out[rows:, :] = moving[...]
        stay_out[...] = jnp.zeros_like(stay_out)
        return
    came = values[-1][rows:, :]
    if low_out.shape[0] > rows:
        low_out[rows:, :] = came
    position = lax.axis_index("seq")
    chip = position >> 1
    chip = jnp.where((position & 1) == 0, chip, lax.axis_size("seq") // 2 - 1 - chip)
    lowest = chip & ((2 << bit) - 1)
    stay_out[...] = jnp.where(lowest == (1 << bit), came, stay[...])


def add_rim(values, moving, stay, bit, final=False):
    rows, width = values[0].shape
    edge = moving.shape[0]
    sent = rows if final else rows + edge
    outs = [near(rows, width)] * (not final)
    outs += [near(sent, width, dtype=BF16), near(edge, width, dtype=BF16)]
    sums = call(
        functools.partial(add_rim_kernel, count=len(values), bit=bit), "add", (), (),
        near_args=tuple(values) + (moving, stay), near_outs=outs, us=1, limit=2,
    )
    return [None] * final + list(sums)


def stack_kernel(io, *refs):
    for k, ref in enumerate(refs[:-1]):
        refs[-1][k] = ref[...]


def plane_pairs(k):
    return [(i, i ^ k) for i in range(lax.axis_size("img"))]


def chips_sum(kept, sent, edges=()):
    count = lax.axis_size("img")
    rows, width = kept.shape
    block = (rows // count, width)
    got = other_core(sent)
    own, *parts = call(
        functools.partial(split_kernel, edges=edges), "split", (), (), near_args=(kept, got),
        near_outs=[near(*block)] + [near(*block, dtype=BF16)] * (count - 1)
        + [near(rim_rows, width, dtype=BF16) for rim_rows in edges[:1]],
        us=1, limit=2,
    )
    rim = parts.pop() if edges else None
    blocks = [own] + [
        lax.ppermute(part, "img", plane_pairs(k + 1)) for k, part in enumerate(parts)
    ]
    return blocks, rim


def line_steps(total, low):
    bits = bits_of("seq")
    for bit in range(1, bits):
        got = lax.ppermute(low, "seq", partner("seq", bit))
        if bit < bits - 1:
            total, low = add([total, got])
        else:
            low = add([total, got], whole=False)
    return low


def line_steps_with_rims(blocks, rim, first_low, beside):
    stay = rim
    total, low, stay = add_rim(blocks, rim, stay, None)
    low, first_low = tied(low, first_low)
    bits = bits_of("seq")
    for bit in range(1, bits):
        got = lax.ppermute(low, "seq", partner("seq", bit))
        if bit == 1:
            first_blocks = plane_blocks(first_low)
        if bit == bits - 1:
            got, beside, *first_blocks = lax.optimization_barrier((got, beside, *first_blocks))
        total, low, stay = add_rim([total, got], rim, stay, bit - 1, bit == bits - 1)
    return low, stay, first_blocks, beside


def plane_blocks(low):
    count = lax.axis_size("img")
    return [low] + [lax.ppermute(low, "img", plane_pairs(k)) for k in range(1, count)]


def stacked(blocks):
    low, count = blocks[0], len(blocks)
    return call(
        stack_kernel, "stack", (), (), near_args=blocks,
        near_outs=[near(count, *low.shape, dtype=BF16)], us=1, limit=2,
    )[0]


def tied(first, second):
    return lax.optimization_barrier((first, second))


def body(
    tokens, cotangent, heights, widths, valid, norm_gain, in_weight, conv_weight, conv_bias,
    xproj_weight, dt_weight, dt_bias, a_log, skip, out_weight,
):
    rows, width = tokens.shape[1:]
    inner = out_weight.shape[0]
    state = a_log.shape[1]
    rank = dt_weight.shape[1]
    cols = xproj_weight.shape[2]
    taps = conv_weight.shape[1]
    reach = taps - 1
    count = bits_of("seq")
    tokens, cotangent = tokens[0], cotangent[0]
    xproj = xproj_weight.transpose(0, 2, 1)

    to_core, to_chip = call_edges(tokens, valid)
    from_core, from_chip = other_core(to_core), next_chip(to_chip)
    weights = (conv_weight, conv_bias, xproj, dt_weight, dt_bias, a_log, skip)
    normed, x, zs, dgz, dy, live, same, cotan, in_x, halo_live, gains, *near_weights = call_front(
        heights, widths, valid, norm_gain, tokens, cotangent, in_weight, out_weight, weights, reach
    )
    (
        summary, sent, delta, s, dsilu, tail, head, xext, proj, before, after, rate, nhalo,
        dy, live, same, normed, zs, dgz, cotan,
    ) = call_middle(
        (dy, live, same, normed, zs, dgz, cotan), (0, 1, 2), from_core, from_chip,
        (x, in_x, halo_live, gains) + tuple(near_weights), reach, cols,
    )
    entered = None
    for bit in range(count - 1):
        got = lax.ppermute(sent, "seq", partner("seq", bit))
        summary, entered, sent = call_join(got, summary, entered, state, bit, bit == count - 2)
    got = lax.ppermute(sent, "seq", partner("seq", count - 1))
    handed = (
        delta, s, dsilu, dy, head, xext, proj, after, rate, same, live, normed, nhalo,
    )
    kept, sent, carry, dz, h0, h1, gated, *handed = call_states(
        handed, (0, 1, 6, 8, 9, 11), before, tail, got, entered, zs, dgz, cotan, rank, reach, state,
        count - 1,
    )

    blocks, _ = chips_sum(kept, sent)
    small = -(-(cols + rank + state + 2 + taps + 1) // CHUNKS) * CHUNKS
    weights = (dt_weight, xproj, conv_weight)
    handed = tuple(handed[:10]) + (carry,) + tuple(handed[10:]) + (dz, gated, h1)
    rim0, small0, dx, *handed = call_first_adjoint(
        handed, tuple(range(11)), h0, weights, small, reach, rank, state
    )
    *blocks, dx = lax.optimization_barrier((*blocks, dx))
    first_sum, first_low = add(blocks)
    first_sum, first_low, dx = lax.optimization_barrier((first_sum, first_low, dx))
    arrays, passed, h1 = tuple(handed[:11]), tuple(handed[11:-1]), handed[-1]
    if bits_of("seq") > 3:
        first_low = line_steps(first_sum, first_low)
    else:
        devices = lax.axis_size("seq")
        blocks = [first_sum] + [
            lax.ppermute(first_low, "seq", [(i, i ^ k) for i in range(devices)])
            for k in range(2, devices, 2)
        ]
    rim1, small1, dx, in_near, *passed = call_second_adjoint(
        passed, arrays + (h1, dx), weights, in_weight, small, reach, rank, state
    )
    live, normed, nhalo, dz, gated = passed
    if bits_of("seq") <= 3:
        *blocks, dx = lax.optimization_barrier((*blocks, dx))
        first_low = add(blocks, whole=False)
    kept, sent, dx_low, dz, gated, in_near = call_last(
        (dz, gated, in_near), dx, rim0, rim1, small0, small1, normed, nhalo, live
    )

    edges = (2 * CHUNKS, kept.shape[0] - width - 2 * small)
    blocks, rim = chips_sum(kept, sent, edges)


    output = call(
        output_kernel, "output", (tokens, out_weight), [low(rows, width)], near_args=(gated,), us=2,
        limit=6,
    )[0]
    second_low, chip_rim, first_blocks, output = line_steps_with_rims(blocks, rim, first_low, output)
    blocks = plane_blocks(second_low)
    _, *first_blocks = lax.optimization_barrier((blocks[1], *first_blocks))
    first_mine = stacked(first_blocks)
    first_other = other_core(first_mine)
    input_grad = call(
        finish_kernel, "finish", (tokens, cotangent, valid, norm_gain), [shape(rows, width)],
        near_args=(dx_low, dz, in_near, rim, chip_rim), scalars=(heights, widths), us=3, limit=8,
    )[0]
    blocks, input_grad = lax.optimization_barrier((blocks, input_grad))
    second_mine = stacked(blocks)
    second_other = other_core(second_mine)
    parts, in_total, out_total = call(
        first_unpack, "unpack_first", (), (),
        [scratch(inner, width), scratch(width, inner), moves(2)],
        far_outs=[shape(width, 2 * inner), shape(inner, width)],
        near_args=(first_mine, first_other, in_near), near_outs=[near(width, LANES)], us=2, limit=8,
    )
    second_other, parts = tied(second_other, parts)
    fold = kept.shape[0]
    (
        conv_total, bias_total, xproj_total, dtw_total, dtb_total, a_total, skip_total, in_total,
        gain_total,
    ) = call(
        functools.partial(
            second_unpack, count=small, state=state, rank=rank, cols=cols, taps=taps
        ),
        "unpack_second", (norm_gain,),
        [
            shape(2, taps, inner), shape(2, inner), shape(2, cols, inner), shape(2, rank, inner),
            shape(2, inner), shape(2, state, inner), shape(2, inner),
        ],
        [
            scratch(fold, width), scratch(fold, width), scratch(width, inner), scratch(width),
            moves(2),
        ],
        (in_total,), [shape(width, 2 * inner), shape(width)], (second_mine, second_other, in_near, parts),
        aliases=((0, 0),), us=2, limit=10,
    )
    return (
        output[None], input_grad[None], gain_total, in_total, conv_total, bias_total,
        xproj_total.transpose(0, 2, 1), dtw_total, dtb_total, a_total, skip_total, out_total,
    )


def solution(mesh):
    split = P("img", "seq", None)
    placed = (split, split, P("img", None), P("img", None), P("img", "seq")) + (P(),) * 10
    return jax.shard_map(
        body,
        mesh=mesh,
        in_specs=placed,
        out_specs=(split, split) + (P(),) * 10,
        check_vma=False,
    )
```
